32 devices in a mesh: seq: 8 (over y, x, core), mp: 4 (over z).
Axes of the slice: x: 2, y: 2, z: 4, core: 2. Of those that a mesh axis runs over, the one named last changes fastest.
Arguments:
- layer_in: bfloat16 [4, 2048, 2048], P(None, ('seq', 'mp')), may hold values from -6 to 6
- w_qkv: bfloat16 [3, 2048, 2048], P(None, None, 'mp'), may hold values from -0.125 to 0.125
- w_out: bfloat16 [2048, 2048], P('mp'), may hold values from -3 to 3
- w_gate_up: bfloat16 [2, 2048, 8192], P(None, None, 'mp'), may hold values from -0.125 to 0.125
- w_down: bfloat16 [8192, 2048], P('mp'), may hold values from -0.0625 to 0.0625
- a_in: bfloat16 [4, 5, 16, 2048], replicated, may hold values from -0.125 to 0.125
- b_qkv: bfloat16 [4, 3, 16, 2048], P(None, None, None, 'mp'), may hold values from -1.5 to 1.5
- b_gate_up: bfloat16 [4, 2, 16, 8192], P(None, None, None, 'mp'), may hold values from -1.5 to 1.5
- a_out: bfloat16 [4, 16, 2048], P(None, None, 'mp'), may hold values from -3 to 3
- a_down: bfloat16 [4, 16, 8192], P(None, None, 'mp'), may hold values from -0.0625 to 0.0625
- b_out_down: bfloat16 [4, 2, 16, 2048], replicated, may hold values from -1.5 to 1.5
- set_index: int32 [4], replicated, may hold values from 0 to 3
- positions: int32 [4, 2048], P(None, 'seq'), may hold values from 0 to 4094, as said below
- cotangent: bfloat16 [4, 2048, 2048], P(None, ('seq', 'mp')), may hold values from -6 to 6
Outputs:
- result: bfloat16 [4, 2048, 2048], P(None, ('seq', 'mp'))
- grad_in: bfloat16 [4, 2048, 2048], P(None, ('seq', 'mp'))
- grad_a_in: float32 [4, 5, 16, 2048], replicated
- grad_b_qkv: float32 [4, 3, 16, 2048], P(None, None, None, 'mp')
- grad_b_gate_up: float32 [4, 2, 16, 8192], P(None, None, None, 'mp')
- grad_a_out: float32 [4, 16, 2048], P(None, None, 'mp')
- grad_a_down: float32 [4, 16, 8192], P(None, None, 'mp')
- grad_b_out_down: float32 [4, 2, 16, 2048], replicated
The draws below stay inside these ranges and needn't reach their ends.
Inputs may be any that keep to these rules, and one draw needn't show every extreme that they name: Along each sequence the positions start at 0 and rise by one or two from each token to the next; in one sequence they rise by two throughout.
All inputs are finite; a program needn't handle non-finite values.
Results may differ from the reference program's by a relative error of at most 0.025.
Values may be sent and summed in bfloat16 or wider, within the bound.
A program may use at most 512 MiB of HBM per device.

```python
import math
import jax
import jax.numpy as jnp
from jax import lax

D = 2048
HDIM = 128
FF = 8192
RANK = 16
SETS = 4
SEQS = 4
LEN = 2048


def draw_positions(key, part):
    key = jax.random.fold_in(key, 11)
    step_key, pick_key = jax.random.split(key)
    increments = jax.random.randint(step_key, (SEQS, LEN), 1, 3).astype(jnp.int32)
    chosen_seq = jax.random.randint(pick_key, (), 0, SEQS).astype(jnp.int32)
    seq_ids = jnp.arange(SEQS, dtype=jnp.int32)[:, None]
    increments = jnp.where(seq_ids == chosen_seq, jnp.int32(2), increments).astype(jnp.int32)
    return (jnp.cumsum(increments, axis=1) - increments[:, :1]).astype(jnp.int32)


def place_ends(entries, rng, least, high):
    longest = entries.shape.index(max(entries.shape))
    spots = []
    for shift in (0, 1):
        where = [jax.random.randint(jax.random.fold_in(rng, axis), (), 0, length) for axis, length in enumerate(entries.shape)]
        where[longest] = (where[longest] + shift) % entries.shape[longest]
        spots.append(tuple(where))
    return entries.at[spots[0]].set(least).at[spots[1]].set(high)


def shard_levels(stream_key, shape, pieces, low, top_value):
    def one(axis_at, parts):
        steps = jax.random.uniform(jax.random.fold_in(jax.random.fold_in(stream_key, 6), axis_at), (parts,), jnp.float32, low / len(pieces), top_value / len(pieces))
        return jnp.repeat(jnp.exp(steps), shape[axis_at] // parts).reshape((-1,) + (1,) * (len(shape) - axis_at - 1))

    loudness = one(*pieces[0])
    for cut in pieces[1:]:
        loudness = loudness * one(*cut)
    return loudness


def scatter_about(stream_key, extent, spread, most, cuts=(), kind=jnp.bfloat16):
    entries = spread * jax.random.normal(stream_key, extent, jnp.float32)
    if cuts:
        entries = entries * shard_levels(stream_key, extent, cuts, -0.22, 0.18)
    return jnp.clip(entries, -most, most).astype(kind)


def setup_inputs(seed: int = 0) -> dict:
    key_of = jax.random.split(jax.random.key(seed), 15)
    return {
        "layer_in": scatter_about(key_of[0], (SEQS, LEN, D), 1.0, 6.0, ((1, 32),)),
        "w_qkv": scatter_about(key_of[1], (3, D, D), D ** -0.5, 0.125, ((2, 4),)),
        "w_out": scatter_about(key_of[2], (D, D), (max(1, 4 * D // LEN)) ** -0.5, 3.0, ((0, 4),)),
        "w_gate_up": scatter_about(key_of[3], (2, D, FF), D ** -0.5, 0.125, ((2, 4),)),
        "w_down": scatter_about(key_of[4], (FF, D), FF ** -0.5, 0.0625, ((0, 4),)),
        "a_in": scatter_about(key_of[5], (SETS, 5, RANK, D), D ** -0.5, 0.125),
        "b_qkv": scatter_about(key_of[6], (SETS, 3, RANK, D), RANK ** -0.5, 1.5, ((3, 4),)),
        "b_gate_up": scatter_about(key_of[7], (SETS, 2, RANK, FF), RANK ** -0.5, 1.5, ((3, 4),)),
        "a_out": scatter_about(key_of[8], (SETS, RANK, D), (max(1, 4 * D // LEN)) ** -0.5, 3.0, ((2, 4),)),
        "a_down": scatter_about(key_of[9], (SETS, RANK, FF), FF ** -0.5, 0.0625, ((2, 4),)),
        "b_out_down": scatter_about(key_of[10], (SETS, 2, RANK, D), RANK ** -0.5, 1.5),
        "set_index": place_ends(jax.random.randint(key_of[11], (SEQS,), 0, SETS), jax.random.fold_in(key_of[11], 1), 0, SETS - 1).astype(jnp.int32),
        "positions": draw_positions(jax.random.fold_in(key_of[14], 71), 0),
        "cotangent": scatter_about(key_of[13], (SEQS, LEN, D), 1.0, 6.0, ((1, 32),)),
    }


adapt_scale = 0.5
norm_eps = 1e-05
rope_base = 10000.0
far_below = -1e+30
highest = lax.Precision.HIGHEST

@jax.custom_vjp
def low(v):
    return lax.optimization_barrier(v.astype(jnp.bfloat16)).astype(jnp.float32)

@jax.custom_vjp
def low_back(v):
    return v

def low_keep(v):
    return (low(v), None)

def low_pass(kept, grad):
    return (grad,)

def back_keep(v):
    return (v, None)

def back_low(kept, grad):
    return (low(grad),)
low.defvjp(low_keep, low_pass)
low_back.defvjp(back_keep, back_low)

def product(left, right):
    return jnp.dot(left, right, precision=highest)

def layer_norm(values):
    centred = values - lax.optimization_barrier(jnp.mean(values, axis=-1, keepdims=True))
    return centred * lax.rsqrt(lax.optimization_barrier(jnp.mean(centred * centred, axis=-1, keepdims=True)) + norm_eps)

def rotate(values, cosine_table, sine_table):
    half_dim = values.shape[-1] // 2
    first_half = values[..., :half_dim]
    second_half = values[..., half_dim:]
    return jnp.concatenate([first_half * cosine_table - second_half * sine_table, second_half * cosine_table + first_half * sine_table], axis=-1)

def adapted(token_rows, weight, a_matrix, b_matrix):
    return product(token_rows, weight) + adapt_scale * product(product(token_rows, a_matrix.T), b_matrix)

def attention(queries, key_rows, value_rows):
    length = queries.shape[0]
    block_size = 512 if length % 512 == 0 else length
    score_scale = 1.0 / math.sqrt(queries.shape[-1])
    key_index = jnp.arange(length, dtype=jnp.int32)

    def query_block(operands):
        block_queries, first_row = operands
        raw_scores = jnp.einsum('qhd,khd->hqk', block_queries, key_rows, precision=highest) * score_scale
        scores = low_back(raw_scores)
        query_index = first_row + jnp.arange(block_size, dtype=jnp.int32)
        allowed = key_index[None, :] <= query_index[:, None]
        shifted = jnp.where(allowed, scores, far_below)
        row_max = lax.optimization_barrier(jnp.max(shifted, axis=-1, keepdims=True))
        exponent = jnp.where(allowed, jnp.exp(shifted - row_max), 0.0)
        attn_probs = low(exponent / lax.optimization_barrier(jnp.sum(exponent, axis=-1, keepdims=True)))
        return jnp.einsum('hqk,khd->qhd', attn_probs, value_rows, precision=highest)
    blocks = queries.reshape((length // block_size, block_size) + queries.shape[1:])
    firsts = jnp.arange(length // block_size, dtype=jnp.int32) * block_size
    output = lax.map(jax.checkpoint(query_block), (blocks, firsts))
    return output.reshape(queries.shape)

def full_layer(inputs, tables, weights, chosen, positions):
    a_in, b_qkv, b_gate_up, a_out, a_down, b_out_down = tables
    w_qkv, w_out, w_gate_up, w_down = weights
    length = inputs.shape[0]
    normed_attn = low(layer_norm(inputs))
    projected = [adapted(normed_attn, w_qkv[member], a_in[chosen, member], b_qkv[chosen, member]) for member in range(3)]
    half_dim = HDIM // 2
    frequency = jnp.exp(jnp.arange(half_dim, dtype=jnp.float32) * (-2.0 * math.log(rope_base) / HDIM))
    angles = positions.astype(jnp.float32)[:, None, None] * frequency
    cosine_table = jnp.cos(angles)
    sine_table = jnp.sin(angles)
    queries = low(rotate(low_back(projected[0]).reshape(length, -1, HDIM), cosine_table, sine_table))
    key_rows = low(rotate(low_back(projected[1]).reshape(length, -1, HDIM), cosine_table, sine_table))
    value_rows = low(low_back(projected[2]).reshape(length, -1, HDIM))
    mixed = low(low_back(attention(queries, key_rows, value_rows).reshape(length, -1)))
    residual = inputs + low_back(adapted(mixed, w_out, a_out[chosen], b_out_down[chosen, 0]))
    normed_mlp = low(layer_norm(residual))
    gate_proj = low_back(adapted(normed_mlp, w_gate_up[0], a_in[chosen, 3], b_gate_up[chosen, 0]))
    up_proj = low_back(adapted(normed_mlp, w_gate_up[1], a_in[chosen, 4], b_gate_up[chosen, 1]))
    activation = low(gate_proj * jax.nn.sigmoid(gate_proj) * up_proj)
    return residual + low_back(adapted(activation, w_down, a_down[chosen], b_out_down[chosen, 1]))

def reference(layer_in, w_qkv, w_out, w_gate_up, w_down, a_in, b_qkv, b_gate_up, a_out, a_down, b_out_down, set_index, positions, cotangent):
    weights = (w_qkv.astype(jnp.float32), w_out.astype(jnp.float32), w_gate_up.astype(jnp.float32), w_down.astype(jnp.float32))
    tables = (a_in.astype(jnp.float32), b_qkv.astype(jnp.float32), b_gate_up.astype(jnp.float32), a_out.astype(jnp.float32), a_down.astype(jnp.float32), b_out_down.astype(jnp.float32))
    zero_grads = tuple((jnp.zeros(table.shape, jnp.float32) for table in tables))

    def one_sequence(totals, seq_item):
        token_rows, seq_cotangent, chosen, seq_positions = seq_item

        def forward(inputs, params):
            return full_layer(inputs, params, weights, chosen, seq_positions)
        output, pullback = jax.vjp(forward, token_rows.astype(jnp.float32), tables)
        grad_rows, grad_tables = pullback(seq_cotangent.astype(jnp.float32))
        totals = tuple((running + update for running, update in zip(totals, grad_tables)))
        return (totals, (output.astype(jnp.bfloat16), grad_rows.astype(jnp.bfloat16)))
    totals, (outputs, grads_in) = lax.scan(one_sequence, zero_grads, (layer_in, cotangent, set_index, positions))
    return (outputs, grads_in, totals[0], totals[1], totals[2], totals[3], totals[4], totals[5])
```

```python
import math

import jax
import jax.numpy as jnp
from jax import lax
from jax.experimental import pallas as pl
from jax.experimental.pallas import tpu as pltpu
from jax.sharding import PartitionSpec as P

HDIM = 128


adapt_scale = 0.5
norm_eps = 1e-05
rope_base = 10000.0
far_below = -1e30
highest = lax.Precision.HIGHEST


def layer_norm(values):
    centred = values - jnp.mean(values, axis=-1, keepdims=True)
    inverse = lax.rsqrt(jnp.mean(centred * centred, axis=-1, keepdims=True) + norm_eps)
    return (centred * inverse, inverse)


def norm_back(gradient, normed, inverse):
    return inverse * (
        gradient
        - jnp.mean(gradient, axis=-1, keepdims=True)
        - normed * jnp.mean(gradient * normed, axis=-1, keepdims=True)
    )


def gather_rows(values):
    return lax.all_gather(values, "mp", axis=1, tiled=True)


def scatter_rows(values):
    return lax.psum_scatter(
        values.astype(jnp.bfloat16), "mp", scatter_dimension=1, tiled=True
    ).astype(jnp.float32)


def rope_tables(positions):
    half_dim = HDIM // 2
    frequency = jnp.exp(
        jnp.arange(half_dim, dtype=jnp.float32) * (-2.0 * math.log(rope_base) / HDIM)
    )
    angles = jnp.transpose(positions).astype(jnp.float32)[:, :, None, None] * frequency
    return (jnp.cos(angles), jnp.sin(angles))


def rotate(values, cosine_table, sine_table):
    half_dim = values.shape[-1] // 2
    first_half = values[..., :half_dim]
    second_half = values[..., half_dim:]
    return jnp.concatenate(
        [
            first_half * cosine_table - second_half * sine_table,
            second_half * cosine_table + first_half * sine_table,
        ],
        axis=-1,
    )


def rotate_back(gradient, cosine_table, sine_table):
    half_dim = gradient.shape[-1] // 2
    first_half = gradient[..., :half_dim]
    second_half = gradient[..., half_dim:]
    return jnp.concatenate(
        [
            first_half * cosine_table + second_half * sine_table,
            second_half * cosine_table - first_half * sine_table,
        ],
        axis=-1,
    )


def masked_scores(queries, key_rows, query_first, key_first, score_scale):
    raw_scores = (
        jnp.einsum("qshd,kshd->shqk", queries, key_rows, preferred_element_type=jnp.float32)
        * score_scale
    )
    query_index = query_first + jnp.arange(queries.shape[0])
    key_index = key_first + jnp.arange(key_rows.shape[0])
    return (raw_scores, key_index[None, :] <= query_index[:, None])


def blockwise(fold_step, state_carry, pieces, start_row):
    row_count = pieces[0].shape[0]
    block_size = 512

    def block_turn(block_id, running):
        blocks = tuple(
            (
                lax.dynamic_slice_in_dim(shard_piece, block_id * block_size, block_size, 0)
                for shard_piece in pieces
            )
        )
        return fold_step(running, blocks, start_row + block_id * block_size)

    return lax.fori_loop(0, row_count // block_size, block_turn, state_carry)


def forward_step(queries, query_first, score_scale):
    query_last = query_first + queries.shape[0] - 1

    def fold_step(state_carry, blocks, key_first):
        key_rows, value_rows = blocks

        def compute(running):
            running_max, running_sum, weighted = running
            scores, allowed = masked_scores(queries, key_rows, query_first, key_first, score_scale)
            new_max = jnp.maximum(
                running_max, jnp.max(jnp.where(allowed, scores, far_below), axis=-1)
            )
            exponent = jnp.where(allowed, jnp.exp(scores - new_max[..., None]), 0.0)
            factor = jnp.exp(running_max - new_max)
            running_sum = running_sum * factor + jnp.sum(exponent, axis=-1)
            weighted = weighted * factor[..., None] + jnp.einsum(
                "shqk,kshd->shqd",
                exponent.astype(jnp.bfloat16),
                value_rows,
                preferred_element_type=jnp.float32,
            )
            return (new_max, running_sum, weighted)

        return lax.cond(key_first <= query_last, compute, lambda running: running, state_carry)

    return fold_step


def query_grad_step(queries, grad_heads, log_total, row_dots, query_first, score_scale):
    query_last = query_first + queries.shape[0] - 1

    def fold_step(state_carry, blocks, key_first):
        key_rows, value_rows = blocks

        def compute(running):
            scores, allowed = masked_scores(queries, key_rows, query_first, key_first, score_scale)
            attn_probs = jnp.where(allowed, jnp.exp(scores - log_total[..., None]), 0.0)
            grad_probs = jnp.einsum(
                "qshd,kshd->shqk", grad_heads, value_rows, preferred_element_type=jnp.float32
            )
            grad_scores = (attn_probs * (grad_probs - row_dots[..., None])).astype(jnp.bfloat16)
            return running + score_scale * jnp.einsum(
                "shqk,kshd->qshd", grad_scores, key_rows, preferred_element_type=jnp.float32
            )

        return lax.cond(key_first <= query_last, compute, lambda running: running, state_carry)

    return fold_step


def key_grad_step(key_rows, value_rows, key_first, score_scale):

    def fold_step(state_carry, blocks, query_first):
        queries, grad_heads, log_total_tok, row_dots_tok = blocks
        query_last = query_first + queries.shape[0] - 1

        def compute(running):
            scores, allowed = masked_scores(queries, key_rows, query_first, key_first, score_scale)
            log_total = jnp.transpose(log_total_tok, (1, 2, 0))
            row_dots = jnp.transpose(row_dots_tok, (1, 2, 0))
            attn_probs = jnp.where(allowed, jnp.exp(scores - log_total[..., None]), 0.0)
            grad_value_rows = jnp.einsum(
                "shqk,qshd->kshd",
                attn_probs.astype(jnp.bfloat16),
                grad_heads,
                preferred_element_type=jnp.float32,
            )
            grad_probs = jnp.einsum(
                "qshd,kshd->shqk", grad_heads, value_rows, preferred_element_type=jnp.float32
            )
            grad_scores = (attn_probs * (grad_probs - row_dots[..., None])).astype(jnp.bfloat16)
            grad_key_rows = score_scale * jnp.einsum(
                "shqk,qshd->kshd", grad_scores, queries, preferred_element_type=jnp.float32
            )
            return (grad_key_rows, grad_value_rows)

        return lax.cond(key_first <= query_last, compute, lambda running: running, state_carry)

    return fold_step


def project_in(token_rows, weight, a_chosen, b_chosen):
    main_term = jnp.einsum("scd,dw->csw", token_rows, weight, preferred_element_type=jnp.float32)
    low_rank = jnp.einsum("scd,srd->scr", token_rows, a_chosen, preferred_element_type=jnp.float32)
    side_term = jnp.einsum(
        "scr,srw->csw", low_rank, b_chosen.astype(jnp.float32), precision=highest
    )
    return (main_term + adapt_scale * side_term, low_rank)


def project_out(middle, weight, a_chosen, b_chosen):
    main_term = jnp.einsum("csw,wd->scd", middle, weight, preferred_element_type=jnp.float32)
    low_rank = jnp.einsum("csw,srw->scr", middle, a_chosen, preferred_element_type=jnp.float32)
    side_term = jnp.einsum(
        "scr,srd->scd", low_rank, b_chosen.astype(jnp.float32), precision=highest
    )
    return (main_term + adapt_scale * side_term, low_rank)


def back_in(gradient, weight, a_chosen, b_chosen, token_rows, low_rank):
    back_rank = jnp.einsum("csw,srw->scr", gradient, b_chosen, preferred_element_type=jnp.float32)
    grad_rows = jnp.einsum("csw,dw->scd", gradient, weight, preferred_element_type=jnp.float32)
    grad_rows = grad_rows + adapt_scale * jnp.einsum(
        "scr,srd->scd", back_rank, a_chosen.astype(jnp.float32), precision=highest
    )
    grad_a = adapt_scale * jnp.einsum("scr,scd->srd", back_rank, token_rows, precision=highest)
    grad_b = adapt_scale * jnp.einsum("scr,csw->srw", low_rank, gradient, precision=highest)
    return (grad_rows, grad_a, grad_b)


def back_out(gradient, weight, a_chosen, b_chosen, middle, low_rank):
    back_rank = jnp.einsum("scd,srd->scr", gradient, b_chosen, preferred_element_type=jnp.float32)
    grad_middle = jnp.einsum("scd,wd->csw", gradient, weight, preferred_element_type=jnp.float32)
    grad_middle = grad_middle + adapt_scale * jnp.einsum(
        "scr,srw->csw", back_rank, a_chosen.astype(jnp.float32), precision=highest
    )
    grad_a = adapt_scale * jnp.einsum("scr,csw->srw", back_rank, middle, precision=highest)
    grad_b = adapt_scale * jnp.einsum("scr,scd->srd", low_rank, gradient, precision=highest)
    return (grad_middle, grad_a, grad_b)


def pick_set(onehot, set_table):
    flattened = set_table.reshape(set_table.shape[0], -1)
    chosen = jnp.dot(onehot, flattened, preferred_element_type=jnp.float32).astype(jnp.bfloat16)
    return chosen.reshape((onehot.shape[0],) + set_table.shape[1:])


def spread_sets(onehot, per_sequence):
    flattened = per_sequence.reshape(per_sequence.shape[0], -1)
    summed = jnp.dot(onehot.astype(jnp.float32).T, flattened, precision=highest)
    return summed.reshape((onehot.shape[1],) + per_sequence.shape[1:])


def per_device(
    layer_in,
    w_qkv,
    w_out,
    w_gate_up,
    w_down,
    a_in,
    b_qkv,
    b_gate_up,
    a_out,
    a_down,
    b_out_down,
    set_index,
    positions,
    cotangent,
):
    local_len = positions.shape[1]
    seq_count = positions.shape[0]
    score_scale = 1.0 / math.sqrt(HDIM)
    my_first = lax.axis_index("seq") * local_len
    onehot = (set_index[:, None] == jnp.arange(a_in.shape[0])[None, :]).astype(jnp.bfloat16)
    chosen_a_in = pick_set(onehot, a_in)
    chosen_b_qkv = pick_set(onehot, b_qkv)
    chosen_b_gate_up = pick_set(onehot, b_gate_up)
    chosen_a_out = pick_set(onehot, a_out)
    chosen_a_down = pick_set(onehot, a_down)
    chosen_b_out_down = pick_set(onehot, b_out_down)

    def to_heads(values):
        return values.reshape(local_len, seq_count, -1, HDIM)

    residual_in = layer_in.astype(jnp.float32)
    normed_attn, inverse_attn = layer_norm(residual_in)
    rows_attn = gather_rows(normed_attn.astype(jnp.bfloat16))
    projected = [
        project_in(rows_attn, w_qkv[member], chosen_a_in[:, member], chosen_b_qkv[:, member])
        for member in range(3)
    ]
    cosine_table, sine_table = rope_tables(positions)
    queries = rotate(to_heads(projected[0][0]), cosine_table, sine_table).astype(jnp.bfloat16)
    key_rows = rotate(to_heads(projected[1][0]), cosine_table, sine_table).astype(jnp.bfloat16)
    value_rows = to_heads(projected[2][0]).astype(jnp.bfloat16)
    stat_shape = (seq_count, queries.shape[2], local_len)
    initial = (
        jnp.full(stat_shape, far_below, jnp.float32),
        jnp.zeros(stat_shape, jnp.float32),
        jnp.zeros(stat_shape + (HDIM,), jnp.float32),
    )
    attend = forward_step(queries, my_first, score_scale)
    running_max, running_sum, weighted = blockwise(
        attend,
        initial,
        (
            lax.all_gather(key_rows, "seq", axis=0, tiled=True),
            lax.all_gather(value_rows, "seq", axis=0, tiled=True),
        ),
        jnp.int32(0),
    )
    log_total = running_max + jnp.log(running_sum)
    attn_output = jnp.transpose(weighted / running_sum[..., None], (2, 0, 1, 3))
    mixed = attn_output.reshape(local_len, seq_count, -1).astype(jnp.bfloat16)
    attn_term, rank_out = project_out(mixed, w_out, chosen_a_out, chosen_b_out_down[:, 0])
    residual = residual_in + scatter_rows(attn_term)
    normed_mlp, inverse_mlp = layer_norm(residual)
    rows_mlp = gather_rows(normed_mlp.astype(jnp.bfloat16))
    gate_proj, rank_gate = project_in(
        rows_mlp, w_gate_up[0], chosen_a_in[:, 3], chosen_b_gate_up[:, 0]
    )
    up_proj, rank_up = project_in(rows_mlp, w_gate_up[1], chosen_a_in[:, 4], chosen_b_gate_up[:, 1])
    sigmoid_gate = jax.nn.sigmoid(gate_proj)
    activation = (gate_proj * sigmoid_gate * up_proj).astype(jnp.bfloat16)
    down_term, rank_down = project_out(activation, w_down, chosen_a_down, chosen_b_out_down[:, 1])
    result = (residual + scatter_rows(down_term)).astype(jnp.bfloat16)
    grad_down = gather_rows(cotangent)
    grad_activation, grad_a_down, grad_b_down = back_out(
        grad_down, w_down, chosen_a_down, chosen_b_out_down[:, 1], activation, rank_down
    )
    grad_up = (grad_activation * gate_proj * sigmoid_gate).astype(jnp.bfloat16)
    grad_gate = (
        grad_activation * up_proj * sigmoid_gate * (1.0 + gate_proj * (1.0 - sigmoid_gate))
    ).astype(jnp.bfloat16)
    rows_from_gate, grad_a_gate, grad_b_gate = back_in(
        grad_gate, w_gate_up[0], chosen_a_in[:, 3], chosen_b_gate_up[:, 0], rows_mlp, rank_gate
    )
    rows_from_up, grad_a_up, grad_b_up = back_in(
        grad_up, w_gate_up[1], chosen_a_in[:, 4], chosen_b_gate_up[:, 1], rows_mlp, rank_up
    )
    grad_residual = cotangent.astype(jnp.float32) + norm_back(
        scatter_rows(rows_from_gate + rows_from_up), normed_mlp, inverse_mlp
    )
    grad_attn_rows = gather_rows(grad_residual.astype(jnp.bfloat16))
    grad_mixed, grad_a_out, grad_b_out = back_out(
        grad_attn_rows, w_out, chosen_a_out, chosen_b_out_down[:, 0], mixed, rank_out
    )
    grad_heads = to_heads(grad_mixed.astype(jnp.bfloat16))
    row_dots_tok = jnp.sum(grad_heads.astype(jnp.float32) * attn_output, axis=-1)
    row_dots = jnp.transpose(row_dots_tok, (1, 2, 0))
    log_total_tok = jnp.transpose(log_total, (2, 0, 1))
    query_step = query_grad_step(queries, grad_heads, log_total, row_dots, my_first, score_scale)
    zero_heads = jnp.zeros(queries.shape, jnp.float32)
    every_key, every_value = (
        lax.all_gather(key_rows, "seq", axis=0, tiled=True),
        lax.all_gather(value_rows, "seq", axis=0, tiled=True),
    )
    grad_queries = blockwise(query_step, zero_heads, (every_key, every_value), 0)
    block_size = 512

    def one_block(block_id):
        first_key = block_id * block_size
        block_keys = lax.dynamic_slice_in_dim(every_key, first_key, block_size, 0)
        block_values = lax.dynamic_slice_in_dim(every_value, first_key, block_size, 0)
        zero_block = jnp.zeros(block_keys.shape, jnp.float32)
        block_step = key_grad_step(block_keys, block_values, first_key, score_scale)
        grad_key_block, grad_value_block = block_step(
            (zero_block, zero_block), (queries, grad_heads, log_total_tok, row_dots_tok), my_first
        )
        return jnp.concatenate([grad_key_block, grad_value_block], axis=-1)

    stacked = lax.map(one_block, jnp.arange(local_len * lax.axis_size("seq") // block_size))
    stacked_terms = lax.psum_scatter(
        stacked.reshape((local_len * lax.axis_size("seq"),) + stacked.shape[2:]).astype(
            jnp.bfloat16
        ),
        "seq",
        scatter_dimension=0,
        tiled=True,
    ).astype(jnp.float32)
    grad_keys = stacked_terms[..., :HDIM]
    grad_values = stacked_terms[..., HDIM:]
    grad_query_raw = (
        rotate_back(grad_queries, cosine_table, sine_table)
        .astype(jnp.bfloat16)
        .reshape(local_len, seq_count, -1)
    )
    grad_key_raw = (
        rotate_back(grad_keys, cosine_table, sine_table)
        .astype(jnp.bfloat16)
        .reshape(local_len, seq_count, -1)
    )
    grad_value_raw = grad_values.astype(jnp.bfloat16).reshape(local_len, seq_count, -1)
    back_parts = [
        back_in(
            gradient,
            w_qkv[member],
            chosen_a_in[:, member],
            chosen_b_qkv[:, member],
            rows_attn,
            projected[member][1],
        )
        for member, gradient in enumerate((grad_query_raw, grad_key_raw, grad_value_raw))
    ]
    grad_rows_attn = back_parts[0][0] + back_parts[1][0] + back_parts[2][0]
    grad_in = (
        grad_residual + norm_back(scatter_rows(grad_rows_attn), normed_attn, inverse_attn)
    ).astype(jnp.bfloat16)
    per_seq_a_in = jnp.stack(
        [back_parts[0][1], back_parts[1][1], back_parts[2][1], grad_a_gate, grad_a_up], axis=1
    )
    per_seq_b_qkv = jnp.stack([bundle[2] for bundle in back_parts], axis=1)
    per_seq_b_gate_up = jnp.stack([grad_b_gate, grad_b_up], axis=1)
    per_seq_b_out_down = jnp.stack([grad_b_out, grad_b_down], axis=1)
    sums_seq = (
        lax.psum(spread_sets(onehot, per_seq_b_qkv).astype(jnp.bfloat16), "seq").astype(
            jnp.float32
        ),
        lax.psum(spread_sets(onehot, per_seq_b_gate_up).astype(jnp.bfloat16), "seq").astype(
            jnp.float32
        ),
        lax.psum(spread_sets(onehot, grad_a_out).astype(jnp.bfloat16), "seq").astype(jnp.float32),
        lax.psum(spread_sets(onehot, grad_a_down).astype(jnp.bfloat16), "seq").astype(jnp.float32),
    )
    sums_all = lax.psum(
        (spread_sets(onehot, per_seq_a_in), spread_sets(onehot, per_seq_b_out_down)), ("seq", "mp")
    )
    return (
        result,
        grad_in,
        sums_all[0],
        sums_seq[0],
        sums_seq[1],
        sums_seq[2],
        sums_seq[3],
        sums_all[1],
    )


log2e = 1.4426950408889634
attn_tile = 512
hidden_tile = 512


def dot_nt(a, b):
    return lax.dot_general(a, b, (((1,), (1,)), ((), ())), preferred_element_type=jnp.float32)


def dot_tn(a, b):
    return lax.dot_general(a, b, (((0,), (0,)), ((), ())), preferred_element_type=jnp.float32)


def dot_nn(a, b):
    return jnp.dot(a, b, preferred_element_type=jnp.float32)


def causal(block_t, first_row, first_col):
    rows = first_row + lax.broadcasted_iota(jnp.int32, block_t.shape, 0)
    cols = first_col + lax.broadcasted_iota(jnp.int32, block_t.shape, 1)
    return rows <= cols


def attend_kernel(q_ref, k_ref, v_ref, o_ref, lse_ref):
    i = pl.program_id(1)
    tile = q_ref.shape[0]
    factor = log2e / math.sqrt(HDIM)
    q = q_ref[...]

    def fold(j, carry, diagonal):
        top, total, acc = carry
        at = pl.ds(pl.multiple_of(j * tile, tile), tile)
        scores = dot_nt(k_ref[at, :], q)
        if diagonal:
            scores = jnp.where(causal(scores, 0, 0), scores, far_below)
        new_top = jnp.maximum(top, jnp.max(scores, axis=0, keepdims=True))
        weight = jnp.exp2(scores * factor - new_top * factor)
        keep = jnp.exp2((top - new_top) * factor)
        total = total * keep + jnp.sum(weight, axis=0, keepdims=True)
        acc = acc * keep + dot_tn(v_ref[at, :], weight.astype(jnp.bfloat16))
        return (new_top, total, acc)

    carry = (
        jnp.full((1, tile), far_below, jnp.float32),
        jnp.zeros((1, tile), jnp.float32),
        jnp.zeros((HDIM, tile), jnp.float32),
    )
    carry = lax.fori_loop(0, i, lambda j, c: fold(j, c, False), carry)
    top, total, acc = fold(i, carry, True)
    o_ref[...] = jnp.transpose(acc / total).astype(o_ref.dtype)
    lse_ref[0] = top * factor + jnp.log2(total)


def attend(q, k, v):
    length = q.shape[0]
    heads = q.shape[1] // HDIM
    tile = attn_tile
    return pl.pallas_call(
        attend_kernel,
        grid=(heads, length // tile),
        in_specs=[
            pl.BlockSpec((tile, HDIM), lambda h, i: (i, h)),
            pl.BlockSpec((length, HDIM), lambda h, i: (0, h)),
            pl.BlockSpec((length, HDIM), lambda h, i: (0, h)),
        ],
        out_specs=[
            pl.BlockSpec((tile, HDIM), lambda h, i: (i, h)),
            pl.BlockSpec((1, 1, tile), lambda h, i: (h, 0, i)),
        ],
        out_shape=[
            jax.ShapeDtypeStruct(q.shape, jnp.bfloat16),
            jax.ShapeDtypeStruct((heads, 1, length), jnp.float32),
        ],
        cost_estimate=pl.CostEstimate(
            flops=2 * heads * length * length * HDIM,
            bytes_accessed=8 * length * heads * HDIM,
            transcendentals=heads * length * length // 2,
        ),
        compiler_params=pltpu.CompilerParams(vmem_limit_bytes=32 << 20),
    )(q, k, v)


def turn_back(gradient, cos, sin):
    return gradient * cos + pltpu.roll(gradient, HDIM // 2, 1) * sin


def attend_back_kernel(
    q_ref, k_ref, v_ref, go_ref, lse_ref, dots_ref, cos_ref, sin_ref, dq_ref, dk_ref, dv_ref, acc_ref
):
    j = pl.program_id(1)
    tile = k_ref.shape[0]
    length = q_ref.shape[0]
    scale = 1.0 / math.sqrt(HDIM)
    factor = log2e * scale
    k = k_ref[...]
    v = v_ref[...]

    @pl.when(j == 0)
    def _():
        acc_ref[...] = jnp.zeros_like(acc_ref)

    def fold(i, carry, diagonal):
        dk, dv = carry
        at = pl.ds(pl.multiple_of(i * tile, tile), tile)
        q = q_ref[at, :]
        go = go_ref[at, :]
        scores = dot_nt(k, q)
        weight = jnp.exp2(scores * factor - lse_ref[0, :, at])
        if diagonal:
            weight = jnp.where(causal(scores, 0, 0), weight, 0.0)
        grad_weight = dot_nt(v, go)
        grad_scores = (weight * (grad_weight - dots_ref[0, :, at])).astype(jnp.bfloat16)
        dv = dv + dot_nn(weight.astype(jnp.bfloat16), go)
        dk = dk + dot_nn(grad_scores, q)
        acc_ref[at, :] += dot_tn(grad_scores, k)
        return (dk, dv)

    zero = jnp.zeros((tile, HDIM), jnp.float32)
    carry = fold(j, (zero, zero), True)
    dk, dv = lax.fori_loop(j + 1, length // tile, lambda i, c: fold(i, c, False), carry)
    at = pl.ds(pl.multiple_of(j * tile, tile), tile)
    dk_ref[...] = turn_back(dk * scale, cos_ref[at, :], sin_ref[at, :]).astype(dk_ref.dtype)
    dv_ref[...] = dv.astype(dv_ref.dtype)
    dq_ref[...] = turn_back(acc_ref[at, :] * scale, cos_ref[at, :], sin_ref[at, :]).astype(dq_ref.dtype)


def attend_back(q, k, v, go, lse, dots, cos, sin):
    length = q.shape[0]
    heads = q.shape[1] // HDIM
    tile = attn_tile
    whole = pl.BlockSpec((length, HDIM), lambda h, j: (0, h))
    part = pl.BlockSpec((tile, HDIM), lambda h, j: (j, h))
    row = pl.BlockSpec((1, 1, length), lambda h, j: (h, 0, 0))
    table = pl.BlockSpec((length, HDIM), lambda h, j: (0, 0))
    return pl.pallas_call(
        attend_back_kernel,
        grid=(heads, length // tile),
        in_specs=[whole, part, part, whole, row, row, table, table],
        out_specs=[part, part, part],
        out_shape=[jax.ShapeDtypeStruct(q.shape, jnp.bfloat16)] * 3,
        scratch_shapes=[pltpu.VMEM((length, HDIM), jnp.float32)],
        cost_estimate=pl.CostEstimate(
            flops=5 * heads * length * length * HDIM,
            bytes_accessed=14 * length * heads * HDIM,
            transcendentals=heads * length * length // 2,
        ),
        compiler_params=pltpu.CompilerParams(vmem_limit_bytes=32 << 20),
    )(q, k, v, go, lse, dots, cos, sin)


mesh_ids = pl.DeviceIdType.MESH


def remote(src, dst, send, recv, target):
    return pltpu.make_async_remote_copy(
        src_ref=src, dst_ref=dst, send_sem=send, recv_sem=recv, device_id=target, device_id_type=mesh_ids
    )


def meet(partners):
    barrier = pltpu.get_barrier_semaphore()
    for condition, device in partners:
        if condition is None:
            pl.semaphore_signal(barrier, inc=1, device_id=device, device_id_type=mesh_ids)
        else:

            @pl.when(condition)
            def _():
                pl.semaphore_signal(barrier, inc=1, device_id=device, device_id_type=mesh_ids)

    count = 0
    for condition, device in partners:
        count = count + (1 if condition is None else condition.astype(jnp.int32))
    pl.semaphore_wait(barrier, count)


def flip(index, bit):
    return index + bit - 2 * bit * ((index // bit) % 2)


def places():
    s = lax.axis_index("seq")
    z = lax.axis_index("mp")
    return s, z


class Gather:
    def __init__(self, blocks, s, z, send, recv, half):
        self.at = blocks
        self.s = s
        self.z = z
        self.send = send
        self.recv = recv
        self.half = half

    def rows(self, part):
        return pl.ds(part * self.half, self.half)

    def copy(self, index, span, part, target):
        ref = self.at.at[span] if part is None else self.at.at[span, self.rows(part)]
        return remote(ref, ref, self.send.at[index], self.recv.at[index], (target, self.z))

    def begin(self):
        s, x, y, other = self.s, flip(self.s, 2), flip(self.s, 4), flip(self.s, 1)
        self.copies = [
            self.copy(0, s, 0, x),
            self.copy(1, s, 1, y),
            self.copy(2, s, 1, x),
            self.copy(3, s, 0, y),
            self.copy(6, s, None, other),
        ]
        for one in self.copies:
            one.start()

    def arrive_first(self):
        s, x, y = self.s, flip(self.s, 2), flip(self.s, 4)
        self.copy(0, x, 0, x).wait_recv()
        one = self.copy(4, x, 0, y)
        one.start()
        self.copy(1, y, 1, y).wait_recv()
        two = self.copy(5, y, 1, x)
        two.start()
        self.copies += [one, two]

    def arrive_neighbours(self):
        s, x, y, other = self.s, flip(self.s, 2), flip(self.s, 4), flip(self.s, 1)
        self.copy(2, x, 1, x).wait_recv()
        one = self.copy(7, x, None, other)
        one.start()
        self.copy(3, y, 0, y).wait_recv()
        two = self.copy(8, y, None, other)
        two.start()
        self.copies += [one, two]

    def arrive_diagonal(self):
        s, other = self.s, flip(self.s, 1)
        diagonal = flip(flip(s, 2), 4)
        self.copy(4, diagonal, 0, other).wait_recv()
        self.copy(5, diagonal, 1, other).wait_recv()
        one = self.copy(9, diagonal, None, other)
        one.start()
        self.copies += [one]

    def arrive_core(self, index):
        s = self.s
        other = flip(s, 1)
        span = (other, flip(other, 2), flip(other, 4), flip(flip(other, 2), 4))[index]
        self.copy(6 + index, span, None, other).wait_recv()
        return span

    def end(self):
        for one in self.copies:
            one.wait_send()


gather_sems = 10


def spend(microseconds):
    return pl.CostEstimate(flops=microseconds * 10**9, bytes_accessed=10**6, transcendentals=0)


class Line:
    def __init__(self, blocks, core, s, z, send, recv):
        self.at = blocks
        self.core = core
        self.s = s
        self.z = z
        self.send = send
        self.recv = recv

    def ref(self, j):
        return self.at.at[j, self.core]

    def up(self, hop, j):
        ref = self.ref(j)
        return remote(ref, ref, self.send.at[hop], self.recv.at[hop], (self.s, self.z + 1))

    def down(self, hop, j):
        ref = self.ref(j)
        return remote(ref, ref, self.send.at[3 + hop], self.recv.at[3 + hop], (self.s, self.z - 1))

    def across(self, index, j):
        ref = self.ref(j)
        return remote(ref, ref, self.send.at[6 + index], self.recv.at[6 + index], (flip(self.s, 1), self.z))

    def begin(self):
        z = self.z

        @pl.when(z < 3)
        def _():
            self.up(0, z).start()

        @pl.when(z > 0)
        def _():
            self.down(0, z).start()

        self.across(0, z).start()

    def hop(self, t):
        z = self.z

        @pl.when(z >= t)
        def _():
            self.up(t - 1, z - t).wait_recv()
            self.across(t, z - t).start()
            if t < 3:

                @pl.when(z < 3)
                def _():
                    self.up(t, z - t).start()

        @pl.when(z + t <= 3)
        def _():
            self.down(t - 1, z + t).wait_recv()
            self.across(3 + t, z + t).start()
            if t < 3:

                @pl.when(z > 0)
                def _():
                    self.down(t, z + t).start()

    def arrive_core(self):
        z = self.z
        other = 1 - self.core

        def wait(index, j):
            ref = self.at.at[j, other]
            remote(ref, ref, self.send.at[6 + index], self.recv.at[6 + index], (flip(self.s, 1), z)).wait_recv()

        wait(0, z)
        for t in (1, 2, 3):

            @pl.when(z >= t)
            def _():
                wait(t, z - t)

            @pl.when(z + t <= 3)
            def _():
                wait(3 + t, z + t)

    def end(self):
        z = self.z

        @pl.when(z < 3)
        def _():
            self.up(0, z).wait_send()

        @pl.when(z > 0)
        def _():
            self.down(0, z).wait_send()

        self.across(0, z).wait_send()
        for t in (1, 2, 3):

            @pl.when(z >= t)
            def _():
                self.across(t, z - t).wait_send()
                if t < 3:

                    @pl.when(z < 3)
                    def _():
                        self.up(t, z - t).wait_send()

            @pl.when(z + t <= 3)
            def _():
                self.across(3 + t, z + t).wait_send()
                if t < 3:

                    @pl.when(z > 0)
                    def _():
                        self.down(t, z + t).wait_send()


line_sems = 13


def norm_rows(values):
    centred = values - jnp.mean(values, axis=-1, keepdims=True)
    inverse = lax.rsqrt(jnp.mean(centred * centred, axis=-1, keepdims=True) + norm_eps)
    return (centred * inverse, inverse)


def start_kernel(
    x_ref, w_ref, o_ref, cos_ref, sin_ref, a_ref, set_ref,
    x_own_ref, n_own_ref, u_out, w_all, o_all, q_ref, k_ref, v_ref, low_ref, b_sel_ref, a_sel_ref,
    u_ref, w_buf, w_big, a2a_send, a2a_recv, ag_send, ag_recv, w_send, w_recv, o_send, o_recv, local_sem,
):
    s, z = places()
    core = s % 2
    other = flip(s, 1)
    zs = [flip(z, 1), flip(z, 2), 3 - z]
    meet([(None, (other, z)), (None, (flip(s, 2), z)), (None, (flip(s, 4), z))] + [(None, (s, j)) for j in zs])

    swaps = [
        remote(x_ref.at[j], x_own_ref.at[z], a2a_send.at[d], a2a_recv.at[d], (s, j)) for d, j in enumerate(zs)
    ]
    for one in swaps:
        one.start()
    x_own_ref[z] = x_ref[z]
    w_buf[z, core] = w_ref[...]
    own_o = pltpu.make_async_copy(o_ref, o_all.at[z, core], local_sem.at[8])
    own_o.start()
    for d, j in enumerate(zs):
        remote(x_ref.at[j], x_own_ref.at[j], a2a_send.at[d], a2a_recv.at[d], (s, j)).wait_recv()
    line = Line(w_buf, core, s, z, w_send, w_recv)
    line.begin()
    for part in range(4):
        normed, _ = norm_rows(x_own_ref[part].astype(jnp.float32))
        normed = normed.astype(jnp.bfloat16)
        n_own_ref[pl.ds(part * 64, 64), :] = normed
        u_ref[s, pl.ds(part * 64, 64), :] = normed
    gather = Gather(u_ref, s, z, ag_send, ag_recv, 128)
    gather.begin()
    gather.arrive_first()
    line.hop(1)
    gather.arrive_neighbours()
    line.hop(2)
    gather.arrive_diagonal()
    for index in range(4):
        gather.arrive_core(index)
    stores = [pltpu.make_async_copy(u_ref.at[t], u_out.at[t], local_sem.at[t]) for t in range(8)]
    for one in stores:
        one.start()
    a48 = a_ref[...]

    def lows(t, _):
        low_ref[t] = (adapt_scale * dot_nt(u_ref[t], a48)).astype(jnp.bfloat16)
        return 0

    lax.fori_loop(0, 8, lows, 0)
    line.hop(3)
    own_o.wait()
    o_line = Line(o_all, core, s, z, o_send, o_recv)
    o_line.begin()
    line.arrive_core()
    keep = pltpu.make_async_copy(w_buf, w_all, local_sem.at[9])
    keep.start()
    mine = set_ref[0]
    for j in range(4):
        table = w_buf[j, 0, 3072:, :]
        picked = jnp.zeros((48, HDIM), jnp.bfloat16)
        picked_a = jnp.zeros((16, HDIM), jnp.bfloat16)
        for member in range(4):
            picked = jnp.where(mine == member, table[48 * member : 48 * member + 48], picked)
            picked_a = jnp.where(mine == member, table[192 + 16 * member : 208 + 16 * member], picked_a)
        b_sel_ref[j] = picked
        a_sel_ref[j] = picked_a
    for part in range(3):
        for head in range(2):
            columns = pl.ds((2 * part + head) * HDIM, HDIM)
            for side in range(2):
                w_big[pl.ds(side * 1024, 1024), columns] = w_buf[
                    2 * core + head, side, pl.ds(part * 1024, 1024), :
                ]
    b_two = [
        jnp.concatenate(
            [b_sel_ref[2 * core, 16 * part : 16 * part + 16], b_sel_ref[2 * core + 1, 16 * part : 16 * part + 16]],
            axis=1,
        )
        for part in range(3)
    ]

    def project(t, _):
        u = u_ref[t]
        low = low_ref[t]
        cos = cos_ref[pl.ds(pl.multiple_of(t * 256, 256), 256), :]
        sin = sin_ref[pl.ds(pl.multiple_of(t * 256, 256), 256), :]
        for part, out in enumerate((q_ref, k_ref, v_ref)):
            raw = dot_nn(u, w_big[:, 256 * part : 256 * part + 256]) + dot_nn(
                low[:, 16 * part : 16 * part + 16], b_two[part]
            )
            for head in range(2):
                piece = raw[:, HDIM * head : HDIM * head + HDIM]
                if part < 2:
                    piece = piece * cos - pltpu.roll(piece, HDIM // 2, 1) * sin
                out[t, :, pl.ds(HDIM * head, HDIM)] = piece.astype(jnp.bfloat16)
        return 0

    lax.fori_loop(0, 3, project, 0)
    o_line.hop(1)
    lax.fori_loop(3, 6, project, 0)
    o_line.hop(2)
    lax.fori_loop(6, 8, project, 0)
    o_line.hop(3)
    o_line.arrive_core()
    for one in stores:
        one.wait()
    keep.wait()
    for one in swaps:
        one.wait_send()
    line.end()
    o_line.end()
    gather.end()


def start_layer(x, w_pack, o_pack, cos, sin, a48, my_set):
    bf16 = jnp.bfloat16
    vmem = pl.BlockSpec(memory_space=pltpu.VMEM)
    anywhere = pl.BlockSpec(memory_space=pl.ANY)
    width = x.shape[2]
    rows = w_pack.shape[0]
    shape = jax.ShapeDtypeStruct
    dma = pltpu.SemaphoreType.DMA
    return pl.pallas_call(
        start_kernel,
        in_specs=[vmem, vmem, anywhere, vmem, vmem, vmem, pl.BlockSpec(memory_space=pltpu.SMEM)],
        out_specs=[vmem, vmem, anywhere, anywhere, anywhere, vmem, vmem, vmem, vmem, vmem, vmem],
        out_shape=[
            shape((4, 64, width), bf16),
            shape((256, width), bf16),
            shape((8, 256, width), bf16),
            shape((4, 2, rows, HDIM), bf16),
            shape((4, 2, HDIM, width // 2), bf16),
            shape((8, 256, 256), bf16),
            shape((8, 256, 256), bf16),
            shape((8, 256, 256), bf16),
            shape((8, 256, 48), bf16),
            shape((4, 48, HDIM), bf16),
            shape((4, 16, HDIM), bf16),
        ],
        scratch_shapes=[
            pltpu.VMEM((8, 256, width), bf16),
            pltpu.VMEM((4, 2, rows, HDIM), bf16),
            pltpu.VMEM((width, 768), bf16),
            dma((3,)),
            dma((3,)),
            dma((gather_sems,)),
            dma((gather_sems,)),
            dma((line_sems,)),
            dma((line_sems,)),
            dma((line_sems,)),
            dma((line_sems,)),
            dma((10,)),
        ],
        cost_estimate=spend(80),
        compiler_params=pltpu.CompilerParams(
            collective_id=1, has_side_effects=True, vmem_limit_bytes=56 << 20
        ),
    )(x, w_pack, o_pack, cos, sin, a48, my_set)


class Reduce:
    def __init__(self, product, s, z, out, inn, send, recv):
        self.product = product
        self.s = s
        self.z = z
        self.out = out
        self.inn = inn
        self.send = send
        self.recv = recv
        chip = s // 2
        self.chip = chip
        self.cx = flip(chip, 1)
        self.cy = flip(chip, 2)
        self.cd = flip(self.cx, 2)

    def copy(self, index):
        target = flip(self.s, 2) if index in (0, 2, 5) else flip(self.s, 4)
        return remote(
            self.out.at[index], self.inn.at[index], self.send.at[index], self.recv.at[index], (target, self.z)
        )

    def give(self, index, chip, half, extra=None):
        value = self.product(chip, half)
        if extra is not None:
            self.copy(extra).wait_recv()
            value = value + self.inn[extra].astype(jnp.float32)
        self.out[index] = value.astype(jnp.bfloat16)
        self.copy(index).start()

    def begin(self):
        self.give(0, self.cd, 0)
        self.give(1, self.cd, 1)
        self.give(2, self.cx, 0)
        self.give(3, self.cy, 1)

    def middle(self):
        self.give(4, self.cy, 0, 0)
        self.give(5, self.cx, 1, 1)

    def finish(self, half):
        indices = (2, 4) if half == 0 else (3, 5)
        total = self.product(self.chip, half)
        for index in indices:
            self.copy(index).wait_recv()
            total = total + self.inn[index].astype(jnp.float32)
        return total

    def end(self):
        for index in range(6):
            self.copy(index).wait_send()


def out_kernel(
    mixed_ref, o_all, a_sel_ref, b_ref, w_all, a48_ref, b_sel_ref, x_own_ref,
    residual_ref, m_own_ref, o_eff_ref, w_cat_ref,
    sib_ref, out_buf, in_buf, o_big, w_buf, sib_send, sib_recv, send, recv, local_sem,
):
    s, z = places()
    core = s % 2
    other = flip(s, 1)
    meet([(None, (other, z)), (None, (flip(s, 2), z)), (None, (flip(s, 4), z))])
    swaps = [
        remote(
            mixed_ref.at[2 * c + 1 - core], sib_ref.at[c], sib_send.at[c], sib_recv.at[c], (other, z)
        )
        for c in range(4)
    ]
    for one in swaps:
        one.start()
    load_w = pltpu.make_async_copy(w_all, w_buf, local_sem.at[0])
    load_w.start()
    for j in range(4):
        head = (2 * core + j) % 4
        merged = adapt_scale * dot_tn(a_sel_ref[head], b_ref[...])
        for side in range(2):
            o_big[pl.ds(j * HDIM, HDIM), pl.ds(side * 1024, 1024)] = (
                o_all[head, side].astype(jnp.float32) + merged[:, side * 1024 : side * 1024 + 1024]
            ).astype(jnp.bfloat16)
    o_eff_ref[...] = o_big[0 : 2 * HDIM, :]
    for one in swaps:
        one.wait_recv()

    def product(chip, half):
        rows = pl.ds(half * 128, 128)
        both = jnp.concatenate([mixed_ref[2 * chip + core, rows, :], sib_ref[chip, rows, :]], axis=1)
        return dot_nn(both, o_big[...])

    reduce = Reduce(product, s, z, out_buf, in_buf, send, recv)
    reduce.begin()
    load_w.wait()

    def merge(index, _):
        j = index // 3
        part = index % 3
        head = (2 * core + j) % 4
        b_part = b_sel_ref[head, pl.ds(pl.multiple_of(part * 16, 16), 16), :]
        a_part = a48_ref[pl.ds(pl.multiple_of(part * 16, 16), 16), :]
        column = pl.multiple_of(((j // 2) * 6 + part * 2 + j % 2) * HDIM, HDIM)
        for side in range(2):
            merged = adapt_scale * dot_tn(a_part[:, side * 1024 : side * 1024 + 1024], b_part)
            w_cat_ref[pl.ds(side * 1024, 1024), pl.ds(column, HDIM)] = (
                w_buf[head, side, pl.ds(pl.multiple_of(part * 1024, 1024), 1024), :].astype(jnp.float32)
                + merged
            ).astype(jnp.bfloat16)
        return 0

    lax.fori_loop(0, 4, merge, 0)
    reduce.middle()
    lax.fori_loop(4, 12, merge, 0)
    for half in range(2):
        total = reduce.finish(half)
        x = x_own_ref[2 * half : 2 * half + 2].reshape(128, -1).astype(jnp.float32)
        residual = x + total
        residual_ref[pl.ds(half * 128, 128), :] = residual
        normed, _ = norm_rows(residual)
        m_own_ref[pl.ds(half * 128, 128), :] = normed.astype(jnp.bfloat16)
    for one in swaps:
        one.wait_send()
    reduce.end()


def out_layer(mixed, o_all, a_sel, b_row, w_all, a48, b_sel, x_own):
    bf16 = jnp.bfloat16
    vmem = pl.BlockSpec(memory_space=pltpu.VMEM)
    width = x_own.shape[2]
    shape = jax.ShapeDtypeStruct
    dma = pltpu.SemaphoreType.DMA
    return pl.pallas_call(
        out_kernel,
        in_specs=[vmem, vmem, vmem, vmem, pl.BlockSpec(memory_space=pl.ANY), vmem, vmem, vmem],
        out_specs=[vmem, vmem, vmem, vmem],
        out_shape=[
            shape((256, width), jnp.float32),
            shape((256, width), bf16),
            shape((256, width), bf16),
            shape((width, 1536), bf16),
        ],
        scratch_shapes=[
            pltpu.VMEM((4, 256, 256), bf16),
            pltpu.VMEM((6, 128, width), bf16),
            pltpu.VMEM((6, 128, width), bf16),
            pltpu.VMEM((512, width), bf16),
            pltpu.VMEM(w_all.shape, bf16),
            dma((4,)),
            dma((4,)),
            dma((6,)),
            dma((6,)),
            dma((1,)),
        ],
        cost_estimate=spend(45),
        compiler_params=pltpu.CompilerParams(
            collective_id=2, has_side_effects=True, vmem_limit_bytes=56 << 20
        ),
    )(mixed, o_all, a_sel, b_row, w_all, a48, b_sel, x_own)


def spread_kernel(
    g_ref, o_eff_ref, mixed_ref, b_ref, g_out, gm_ref, dots_ref, rank_ref, g_buf, send, recv, local_sem
):
    s, z = places()
    meet([(None, (flip(s, 1), z)), (None, (flip(s, 2), z)), (None, (flip(s, 4), z))])
    g_buf[s] = g_ref[...]
    gather = Gather(g_buf, s, z, send, recv, 128)
    gather.begin()

    def store(t):
        return pltpu.make_async_copy(g_buf.at[t], g_out.at[t], local_sem.at[0])

    def work(t):
        g = g_buf[t]
        store(t).start()
        back = dot_nt(g, o_eff_ref[...]).astype(jnp.bfloat16)
        gm_ref[t] = back
        product = back.astype(jnp.float32) * mixed_ref[t].astype(jnp.float32)
        for head in range(2):
            turned = jnp.transpose(product[:, HDIM * head : HDIM * head + HDIM])
            dots_ref[head, t] = jnp.sum(turned, axis=0, keepdims=True)
        rank_ref[t] = (adapt_scale * dot_nt(g, b_ref[...])).astype(jnp.bfloat16)
        store(t).wait()

    work(s)
    gather.arrive_first()
    work(gather.arrive_core(0))
    gather.arrive_neighbours()
    work(flip(s, 2))
    work(flip(s, 4))
    work(gather.arrive_core(1))
    work(gather.arrive_core(2))
    gather.arrive_diagonal()
    work(flip(flip(s, 2), 4))
    work(gather.arrive_core(3))
    gather.end()


def spread_layer(g_own, o_eff, mixed, b_row):
    bf16 = jnp.bfloat16
    vmem = pl.BlockSpec(memory_space=pltpu.VMEM)
    width = g_own.shape[1]
    shape = jax.ShapeDtypeStruct
    dma = pltpu.SemaphoreType.DMA
    return pl.pallas_call(
        spread_kernel,
        in_specs=[vmem, vmem, vmem, vmem],
        out_specs=[pl.BlockSpec(memory_space=pl.ANY), vmem, vmem, vmem],
        out_shape=[
            shape((8, 256, width), bf16),
            shape((8, 256, 256), bf16),
            shape((2, 8, 1, 256), jnp.float32),
            shape((8, 256, 16), bf16),
        ],
        scratch_shapes=[
            pltpu.VMEM((8, 256, width), bf16),
            dma((gather_sems,)),
            dma((gather_sems,)),
            dma((1,)),
        ],
        cost_estimate=spend(40),
        compiler_params=pltpu.CompilerParams(
            collective_id=3, has_side_effects=True, vmem_limit_bytes=48 << 20
        ),
    )(g_own, o_eff, mixed, b_row)


def in_kernel(
    dq_ref, dk_ref, dv_ref, w_ref, x_own_ref, residual_ref,
    grad_ref, own_ref, sib_q, sib_k, sib_v, out_buf, in_buf, a2a_send, a2a_recv, sib_send, sib_recv, send, recv,
):
    s, z = places()
    core = s % 2
    other = flip(s, 1)
    zs = [flip(z, 1), flip(z, 2), 3 - z]
    meet([(None, (other, z)), (None, (flip(s, 2), z)), (None, (flip(s, 4), z))] + [(None, (s, j)) for j in zs])
    mine = (dq_ref, dk_ref, dv_ref)
    theirs = (sib_q, sib_k, sib_v)
    swaps = [
        remote(
            mine[p].at[2 * c + 1 - core], theirs[p].at[c], sib_send.at[4 * p + c], sib_recv.at[4 * p + c], (other, z)
        )
        for c in range(4)
        for p in range(3)
    ]
    for one in swaps:
        one.start()
    for one in swaps:
        one.wait_recv()

    def product(chip, half):
        rows = pl.ds(half * 128, 128)
        both = jnp.concatenate(
            [ref[2 * chip + core, rows, :] for ref in mine] + [ref[chip, rows, :] for ref in theirs], axis=1
        )
        return dot_nt(both, w_ref[...])

    reduce = Reduce(product, s, z, out_buf, in_buf, send, recv)
    reduce.begin()
    reduce.middle()
    for half in range(2):
        total = reduce.finish(half)
        x = x_own_ref[2 * half : 2 * half + 2].reshape(128, -1).astype(jnp.float32)
        normed, inverse = norm_rows(x)
        value = residual_ref[pl.ds(half * 128, 128), :] + norm_back(total, normed, inverse)
        own_ref[2 * half : 2 * half + 2] = value.astype(jnp.bfloat16).reshape(2, 64, -1)
    backs = [
        remote(own_ref.at[j], grad_ref.at[z], a2a_send.at[d], a2a_recv.at[d], (s, j)) for d, j in enumerate(zs)
    ]
    for one in backs:
        one.start()
    grad_ref[z] = own_ref[z]
    for one in swaps:
        one.wait_send()
    reduce.end()
    for d, j in enumerate(zs):
        remote(own_ref.at[j], grad_ref.at[j], a2a_send.at[d], a2a_recv.at[d], (s, j)).wait_recv()
    for one in backs:
        one.wait_send()


def in_layer(dq, dk, dv, w_cat, x_own, grad_residual):
    bf16 = jnp.bfloat16
    vmem = pl.BlockSpec(memory_space=pltpu.VMEM)
    width = x_own.shape[2]
    dma = pltpu.SemaphoreType.DMA

    return pl.pallas_call(
        in_kernel,
        in_specs=[vmem] * 6,
        out_specs=vmem,
        out_shape=jax.ShapeDtypeStruct((4, 64, width), bf16),
        scratch_shapes=[
            pltpu.VMEM((4, 64, width), bf16),
            pltpu.VMEM((4, 256, 256), bf16),
            pltpu.VMEM((4, 256, 256), bf16),
            pltpu.VMEM((4, 256, 256), bf16),
            pltpu.VMEM((6, 128, width), bf16),
            pltpu.VMEM((6, 128, width), bf16),
            dma((3,)),
            dma((3,)),
            dma((12,)),
            dma((12,)),
            dma((6,)),
            dma((6,)),
        ],
        cost_estimate=spend(80),
        compiler_params=pltpu.CompilerParams(
            collective_id=4, has_side_effects=True, vmem_limit_bytes=48 << 20
        ),
    )(dq, dk, dv, w_cat, x_own, grad_residual)


def mlp_line_kernel(
    m_ref, residual_ref, cot0_ref, cot1_ref, cot2_ref, cot3_ref, w_gu_ref, w_d_ref, a_ref, b_ref, ad_ref, bd_ref,
    g_ref, grad_res_ref, down0_ref, down1_ref, down2_ref, down3_ref, grad_b_ref, grad_ad_ref, grad_a_ref, grad_bd_ref,
    m_buf, wg, wu, wd, cot_buf, back_acc, down_acc, ranks, slots, r1, r2, r3, r4, r5, stage,
    up_send, up_recv, dn_send, dn_recv, send1, recv1, send4, recv4, send5, recv5, send23, recv23,
    weight_sem, cot_sem, stage_sem,
):
    s, z = places()
    tiles = wg.shape[0]
    tile = wg.shape[2]
    f32 = jnp.float32
    bf16 = jnp.bfloat16
    middle = z * (3 - z) == 2
    at_end = z * (3 - z) == 0
    pair = flip(z, 1)
    opposite = 3 - z
    inner = 1 + z // 2
    high = z // 2
    ids = [z, pair, 2 - high, 3 - 3 * high]
    far = 3 - 3 * high

    loads = []
    for h in range(tiles):
        columns = pl.ds(h * tile, tile)
        loads.append(
            [
                pltpu.make_async_copy(w_gu_ref.at[0, :, columns], wg.at[h], weight_sem.at[3 * h]),
                pltpu.make_async_copy(w_gu_ref.at[1, :, columns], wu.at[h], weight_sem.at[3 * h + 1]),
                pltpu.make_async_copy(w_d_ref.at[columns, :], wd.at[h], weight_sem.at[3 * h + 2]),
            ]
        )
        for one in loads[-1]:
            one.start()

    others = [z, pair, flip(z, 2), opposite]
    cot_refs = (cot0_ref, cot1_ref, cot2_ref, cot3_ref)
    down_refs = (down0_ref, down1_ref, down2_ref, down3_ref)

    def load_cot(seq):
        return [
            pltpu.make_async_copy(cot_refs[d].at[seq], cot_buf.at[others[d]], cot_sem.at[d]) for d in range(4)
        ]

    for one in load_cot(z):
        one.start()

    meet([(z < 3, (s, z + 1)), (z > 0, (s, z - 1)), (None, (s, flip(z, 2)))])
    m_buf[z] = m_ref[...]

    def up(hop, j):
        return remote(m_buf.at[j], m_buf.at[j], up_send.at[hop], up_recv.at[hop], (s, z + 1))

    def down(hop, j):
        return remote(m_buf.at[j], m_buf.at[j], dn_send.at[hop], dn_recv.at[hop], (s, z - 1))

    def begin():
        @pl.when(z < 3)
        def _():
            up(0, z).start()

        @pl.when(z > 0)
        def _():
            down(0, z).start()

    def hop(t):
        @pl.when(z >= t)
        def _():
            up(t - 1, z - t).wait_recv()
            if t < 3:

                @pl.when(z < 3)
                def _():
                    up(t, z - t).start()

        @pl.when(z + t <= 3)
        def _():
            down(t - 1, z + t).wait_recv()
            if t < 3:

                @pl.when(z > 0)
                def _():
                    down(t, z + t).start()

    def hop_end():
        @pl.when(z < 3)
        def _():
            up(0, z).wait_send()

        @pl.when(z > 0)
        def _():
            down(0, z).wait_send()

        for t in (1, 2):

            @pl.when((z >= t) & (z < 3))
            def _():
                up(t, z - t).wait_send()

            @pl.when((z + t <= 3) & (z > 0))
            def _():
                down(t, z + t).wait_send()

    def piece(p):
        return pl.ds(p * 64, 64)

    def copy1():
        return remote(slots.at[1], r1, send1.at[0], recv1.at[0], (s, pair))

    def copy2():
        return remote(slots.at[2], r2, send23.at[0], recv23.at[0], (s, opposite))

    def copy3():
        return remote(slots.at[2], r3, send23.at[1], recv23.at[1], (s, inner))

    def copy4(p):
        return remote(slots.at[3, piece(p)], r4.at[piece(p)], send4.at[p], recv4.at[p], (s, far))

    def copy5(p):
        return remote(slots.at[3, piece(p)], r5.at[piece(p)], send5.at[p], recv5.at[p], (s, inner))

    def stage_copies(seq):
        return [
            pltpu.make_async_copy(stage.at[others[d]], down_refs[d].at[seq], stage_sem.at[d]) for d in range(4)
        ]

    def compute(slot):
        seq = ids[slot]
        rows = m_buf[seq]
        for one in load_cot(seq):
            one.wait()
        ranks[:, 0:32] = adapt_scale * dot_nt(rows, a_ref[seq])
        cot = cot_buf[...].reshape(256, -1)
        ranks[:, 32:48] = adapt_scale * dot_nt(cot, bd_ref[seq])
        ranks[:, 48:96] = jnp.zeros((256, 48), f32)
        back_acc[...] = jnp.zeros_like(back_acc)
        down_acc[...] = jnp.zeros_like(down_acc)

        def step(h, _):
            columns = pl.ds(pl.multiple_of(h * tile, tile), tile)
            low = ranks[...].astype(bf16)
            low_gate = low[:, 0:16]
            low_up = low[:, 16:32]
            low_cot = low[:, 32:48]
            bg = b_ref[seq, 0, :, columns]
            bu = b_ref[seq, 1, :, columns]
            ad = ad_ref[seq, :, columns]
            rows = m_buf[seq]
            cot = cot_buf[...].reshape(256, -1)
            gate = dot_nn(rows, wg[h]) + dot_nn(low_gate, bg)
            up_value = dot_nn(rows, wu[h]) + dot_nn(low_up, bu)
            grad_act = dot_nt(cot, wd[h]) + dot_nn(low_cot, ad)
            sig = jax.nn.sigmoid(gate)
            act = (gate * sig * up_value).astype(bf16)
            grad_up = (grad_act * gate * sig).astype(bf16)
            grad_gate = (grad_act * up_value * sig * (1.0 + gate * (1.0 - sig))).astype(bf16)
            for part in range(4):
                wide = pl.ds(part * 512, 512)
                back_acc[:, wide] += dot_nt(grad_gate, wg[h, wide, :]) + dot_nt(grad_up, wu[h, wide, :])
                down_acc[:, wide] += dot_nn(act, wd[h, :, wide])
            ranks[:, 48:64] += dot_nt(act, ad)
            ranks[:, 64:80] += dot_nt(grad_gate, bg)
            ranks[:, 80:96] += dot_nt(grad_up, bu)
            grad_b_ref[seq, 0, :, columns] = dot_tn(low_gate, grad_gate)
            grad_b_ref[seq, 1, :, columns] = dot_tn(low_up, grad_up)
            grad_ad_ref[seq, :, columns] = dot_tn(low_cot, act)
            return 0

        if slot == 0:
            for h in range(tiles):
                for one in loads[h]:
                    one.wait()
        lax.fori_loop(0, tiles, step, 0)
        back_rank = (adapt_scale * ranks[:, 64:96]).astype(bf16)
        slots[slot] = (back_acc[...] + dot_nn(back_rank, a_ref[seq])).astype(bf16)

    def rest(slot):
        seq = ids[slot]
        back_rank = (adapt_scale * ranks[:, 64:96]).astype(bf16)
        low_down = (adapt_scale * ranks[:, 48:64]).astype(bf16)
        grad_a_ref[seq] = dot_tn(back_rank, m_buf[seq])
        grad_bd_ref[seq] = dot_tn(low_down, cot_buf[...].reshape(256, -1))
        if slot > 0:
            for one in stage_copies(ids[slot - 1]):
                one.wait()
        value = down_acc[...] + dot_nn(low_down, bd_ref[seq])
        if slot == 0:
            value = value + residual_ref[...]
        stage[...] = value.astype(bf16).reshape(4, 64, -1)
        for one in stage_copies(seq):
            one.start()
        following = ids[slot + 1] if slot < 3 else z
        for one in load_cot(following):
            one.start()

    def add(slot, p, extra):
        slots[slot, piece(p), :] = (
            slots[slot, piece(p), :].astype(f32) + extra[piece(p), :].astype(f32)
        ).astype(bf16)

    begin()
    compute(0)
    rest(0)
    hop(1)
    compute(1)

    @pl.when(at_end)
    def _():
        copy1().start()

    rest(1)
    hop(2)
    compute(2)

    @pl.when(at_end)
    def _():
        copy3().start()

    @pl.when(middle)
    def _():
        copy1().start()

    rest(2)
    hop(3)
    compute(3)

    @pl.when(at_end)
    def _():
        copy5(0).start()
        copy5(1).start()

    @pl.when(middle)
    def _():
        copy3().wait_recv()
        for p in range(4):
            add(2, p, r3)
        copy2().start()

    rest(3)

    @pl.when(at_end)
    def _():
        for p in (2, 3):
            copy5(p - 2).wait_send()
            copy5(p).start()

    @pl.when(middle)
    def _():
        for p in range(4):
            copy5(p).wait_recv()
            add(3, p, r5)
            copy4(p).start()

    copy1().wait_recv()
    for p in range(4):
        add(0, p, r1)

    @pl.when(middle)
    def _():
        copy2().wait_recv()
        for p in range(4):
            add(0, p, r2)

    for one in load_cot(z):
        one.wait()
    for p in range(4):

        @pl.when(at_end)
        def _():
            copy4(p).wait_recv()
            add(0, p, r4)

        grad = slots[0, piece(p), :].astype(f32)
        normed, inverse = norm_rows(residual_ref[piece(p), :])
        value = cot_buf[p].astype(f32) + norm_back(grad, normed, inverse)
        grad_res_ref[piece(p), :] = value
        g_ref[piece(p), :] = value.astype(bf16)
    for one in stage_copies(ids[3]):
        one.wait()
    hop_end()
    copy1().wait_send()

    @pl.when(at_end)
    def _():
        copy3().wait_send()
        for p in (2, 3):
            copy5(p).wait_send()

    @pl.when(middle)
    def _():
        copy2().wait_send()
        for p in range(4):
            copy4(p).wait_send()


def mlp_line(m_own, residual, cots, w_gate_up, w_down, a_sel, b_sel, ad_sel, bd_sel):
    bf16 = jnp.bfloat16
    f32 = jnp.float32
    vmem = pl.BlockSpec(memory_space=pltpu.VMEM)
    anywhere = pl.BlockSpec(memory_space=pl.ANY)
    width = m_own.shape[1]
    hidden = w_down.shape[0]
    tile = hidden_tile
    tiles = hidden // tile
    shape = jax.ShapeDtypeStruct
    dma = pltpu.SemaphoreType.DMA
    vm = pltpu.VMEM
    return pl.pallas_call(
        mlp_line_kernel,
        in_specs=[vmem, vmem] + [anywhere] * 6 + [vmem] * 4,
        out_specs=[vmem, vmem] + [anywhere] * 4 + [vmem, vmem, vmem, vmem],
        out_shape=[
            shape((256, width), bf16),
            shape((256, width), f32),
        ]
        + [shape((4, 64, width), bf16)] * 4
        + [
            shape((4, 2, 16, hidden), f32),
            shape((4, 16, hidden), f32),
            shape((4, 32, width), f32),
            shape((4, 16, width), f32),
        ],
        scratch_shapes=[
            vm((4, 256, width), bf16),
            vm((tiles, width, tile), bf16),
            vm((tiles, width, tile), bf16),
            vm((tiles, tile, width), bf16),
            vm((4, 64, width), bf16),
            vm((256, width), f32),
            vm((256, width), f32),
            vm((256, 96), f32),
            vm((4, 256, width), bf16),
            vm((256, width), bf16),
            vm((256, width), bf16),
            vm((256, width), bf16),
            vm((256, width), bf16),
            vm((256, width), bf16),
            vm((4, 64, width), bf16),
        ]
        + [dma((3,))] * 4
        + [dma((4,))] * 6
        + [dma((2,))] * 2
        + [dma((3 * tiles,)), dma((4,)), dma((4,))],
        cost_estimate=spend(110),
        compiler_params=pltpu.CompilerParams(
            collective_id=5, has_side_effects=True, vmem_limit_bytes=60 << 20
        ),
    )(m_own, residual, *cots, w_gate_up, w_down, a_sel, b_sel, ad_sel, bd_sel)


def swap_mp(values, d):
    pairs = [(s * 4 + z, s * 4 + (z ^ d)) for s in range(lax.axis_size("seq")) for z in range(4)]
    return lax.ppermute(values, ("seq", "mp"), pairs)


def full_tables(positions):
    half_dim = HDIM // 2
    frequency = jnp.exp(
        jnp.arange(half_dim, dtype=jnp.float32) * (-2.0 * math.log(rope_base) / HDIM)
    )
    angles = positions.astype(jnp.float32)[:, None] * frequency
    cos = jnp.cos(angles)
    sin = jnp.sin(angles)
    return (jnp.concatenate([cos, cos], axis=1), jnp.concatenate([sin, -sin], axis=1))


def by_sets(set_ids, grads, sets):
    return jnp.stack(
        [
            sum(jnp.where(one == member, grad, 0.0) for one, grad in zip(set_ids, grads))
            for member in range(sets)
        ]
    )


def pick(values, index, axis=0):
    return lax.dynamic_index_in_dim(values, index, axis, keepdims=False)


def per_device_layers(
    layer_in, w_qkv, w_out, w_gate_up, w_down, a_in, b_qkv, b_gate_up, a_out, a_down, b_out_down,
    set_index, positions, cotangent,
):
    bf16 = jnp.bfloat16
    f32 = jnp.float32
    s = lax.axis_index("seq")
    z = lax.axis_index("mp")
    chip = s // 2
    core = s % 2
    sets = a_in.shape[0]
    width = layer_in.shape[2]
    rank = a_in.shape[2]
    length = 8 * 256

    my_set = pick(set_index, z)
    a48 = pick(a_in, my_set)[:3].reshape(3 * rank, width)
    bo_set = pick(b_out_down, my_set)
    a_sel = jnp.stack([pick(a_in, set_index[q])[3:].reshape(2 * rank, width) for q in range(4)])
    b_sel_mlp = jnp.stack([pick(b_gate_up, set_index[q]) for q in range(4)])
    ad_sel = jnp.stack([pick(a_down, set_index[q]) for q in range(4)])
    bd_sel = jnp.stack([pick(b_out_down, set_index[q])[1] for q in range(4)])
    half = width // 2
    w_half = lax.dynamic_slice(w_qkv, (0, core * half, chip * HDIM), (3, half, HDIM)).reshape(-1, HDIM)
    b_own = lax.dynamic_slice_in_dim(b_qkv, chip * HDIM, HDIM, 3).reshape(-1, HDIM)
    a_own = lax.dynamic_slice_in_dim(a_out, chip * HDIM, HDIM, 2).reshape(-1, HDIM)
    w_pack = jnp.concatenate([w_half, b_own, a_own], axis=0)
    o_pack = lax.dynamic_slice(w_out, (chip * HDIM, core * half), (HDIM, half))
    positions_z = lax.all_gather(pick(positions, z), "seq", axis=0, tiled=True)
    cos, sin = full_tables(positions_z)

    (x_own, n_own, u, w_all, o_all, q, k, v, low, b_sel, a_out_sel) = start_layer(
        layer_in, w_pack, o_pack, cos, sin, a48, my_set[None]
    )
    del n_own
    cot_late, _ = lax.optimization_barrier((cotangent, x_own))
    cots = [cot_late] + [swap_mp(cot_late, d) for d in (1, 2, 3)]

    def flat(values):
        return values.reshape(length, values.shape[-1])

    mixed, lse = attend(flat(q), flat(k), flat(v))
    residual, m_own, o_eff, w_cat = out_layer(
        mixed.reshape(8, 256, 256), o_all, a_out_sel, bo_set[0], w_all, a48, b_sel, x_own
    )
    g_own, grad_residual, down0, down1, down2, down3, grad_b_mlp, grad_ad, grad_a_mlp, grad_bd = mlp_line(
        m_own, residual, cots, w_gate_up, w_down, a_sel, b_sel_mlp, ad_sel, bd_sel
    )
    result = down0.astype(f32)
    for d, part in ((1, down1), (2, down2), (3, down3)):
        result = result + swap_mp(part, d).astype(f32)
    result = result.astype(bf16)

    set_ids = [set_index[q_] for q_ in range(4)]
    sum_b_gate_up = by_sets(set_ids, [grad_b_mlp[q_] for q_ in range(4)], sets).astype(bf16)
    sum_a_down = by_sets(set_ids, [grad_ad[q_] for q_ in range(4)], sets).astype(bf16)
    sum_a_mlp = by_sets(set_ids, [grad_a_mlp[q_].reshape(2, rank, width) for q_ in range(4)], sets).astype(bf16)
    sum_b_down = by_sets(set_ids, [grad_bd[q_] for q_ in range(4)], sets).astype(bf16)
    sum_b_gate_up, sum_a_down = lax.psum((sum_b_gate_up, sum_a_down), "seq")
    sum_a_mlp, sum_b_down = lax.psum((sum_a_mlp, sum_b_down), ("seq", "mp"))

    g, grad_mixed, dots, out_rank = spread_layer(g_own, o_eff, mixed.reshape(8, 256, 256), bo_set[0])
    dq, dk, dv = attend_back(
        flat(q), flat(k), flat(v), flat(grad_mixed), lse, dots.reshape(2, 1, length), cos, sin
    )

    def spans(values):
        return values.reshape(8, 256, 256)

    grad_in = in_layer(spans(dq), spans(dk), spans(dv), w_cat, x_own, grad_residual)

    my_b = lax.dynamic_slice_in_dim(b_sel.reshape(4, 3, rank, HDIM), 2 * core, 2, 0)
    my_a = lax.dynamic_slice_in_dim(a_out_sel, 2 * core, 2, 0)
    d_parts = [d.reshape(length, 2, HDIM) for d in (dq, dk, dv)]
    back_rank = jnp.concatenate(
        [
            adapt_scale * jnp.einsum("thk,hrk->tr", d_parts[p], my_b[:, p], preferred_element_type=f32)
            for p in range(3)
        ],
        axis=1,
    ).astype(bf16)
    grad_a_qkv = dot_tn(back_rank, flat(u)).reshape(3, rank, width)
    low = flat(low)
    grad_b_qkv = jnp.stack(
        [dot_tn(low[:, rank * p : rank * p + rank], d) for p, d in enumerate((dq, dk, dv))]
    )
    grad_a_out = dot_tn(flat(out_rank), mixed)
    out_low = (
        adapt_scale
        * jnp.einsum("thk,hrk->tr", mixed.reshape(length, 2, HDIM), my_a, preferred_element_type=f32)
    ).astype(bf16)
    grad_b_out = dot_tn(out_low, flat(g))

    def in_set(values):
        return jnp.stack([jnp.where(my_set == member, values, 0.0) for member in range(sets)]).astype(bf16)

    def in_heads(values):
        pairs = values.reshape(values.shape[:-1] + (2, HDIM))
        out = jnp.zeros(values.shape[:-1] + (4, 4 * HDIM), values.dtype)
        start = (0,) * (values.ndim - 1) + (2 * core, chip * HDIM)
        return lax.dynamic_update_slice(out, pairs, start)

    grad_b_out, _ = lax.optimization_barrier((grad_b_out, sum_b_down))
    sum_a_qkv, sum_b_out, sum_b_qkv, sum_a_out = lax.psum(
        (in_set(grad_a_qkv), in_set(grad_b_out), in_set(in_heads(grad_b_qkv)), in_set(in_heads(grad_a_out))),
        ("seq", "mp"),
    )
    return (
        result,
        grad_in,
        jnp.concatenate([sum_a_qkv, sum_a_mlp], axis=1).astype(f32),
        pick(sum_b_qkv, z, 3).astype(f32),
        sum_b_gate_up.astype(f32),
        pick(sum_a_out, z, 2).astype(f32),
        sum_a_down.astype(f32),
        jnp.stack([sum_b_out, sum_b_down], axis=1).astype(f32),
    )


def solution(mesh):
    by_layers = mesh.shape["seq"] == 8 and mesh.shape["mp"] == 4
    body = per_device_layers if by_layers else per_device
    placed = (
        P(None, ("seq", "mp"), None),
        P(None, None, "mp"),
        P("mp", None),
        P(None, None, "mp"),
        P("mp", None),
        P(),
        P(None, None, None, "mp"),
        P(None, None, None, "mp"),
        P(None, None, "mp"),
        P(None, None, "mp"),
        P(),
        P(),
        P(None, "seq"),
        P(None, ("seq", "mp"), None),
    )
    return jax.shard_map(
        body,
        mesh=mesh,
        in_specs=placed,
        out_specs=(
            P(None, ("seq", "mp"), None),
            P(None, ("seq", "mp"), None),
            P(),
            P(None, None, None, "mp"),
            P(None, None, None, "mp"),
            P(None, None, "mp"),
            P(None, None, "mp"),
            P(),
        ),
        check_vma=False,
    )
```

```python
import math

import jax
import jax.numpy as jnp
from jax import lax
from jax.experimental import pallas as pl
from jax.experimental.pallas import tpu as pltpu
from jax.sharding import PartitionSpec as P

HDIM = 128


adapt_scale = 0.5
norm_eps = 1e-05
rope_base = 10000.0
far_below = -1e30
highest = lax.Precision.HIGHEST


def layer_norm(values):
    centred = values - jnp.mean(values, axis=-1, keepdims=True)
    inverse = lax.rsqrt(jnp.mean(centred * centred, axis=-1, keepdims=True) + norm_eps)
    return (centred * inverse, inverse)


def norm_back(gradient, normed, inverse):
    return inverse * (
        gradient
        - jnp.mean(gradient, axis=-1, keepdims=True)
        - normed * jnp.mean(gradient * normed, axis=-1, keepdims=True)
    )


def gather_rows(values):
    return lax.all_gather(values, "mp", axis=1, tiled=True)


def scatter_rows(values):
    return lax.psum_scatter(
        values.astype(jnp.bfloat16), "mp", scatter_dimension=1, tiled=True
    ).astype(jnp.float32)


def rope_tables(positions):
    half_dim = HDIM // 2
    frequency = jnp.exp(
        jnp.arange(half_dim, dtype=jnp.float32) * (-2.0 * math.log(rope_base) / HDIM)
    )
    angles = jnp.transpose(positions).astype(jnp.float32)[:, :, None, None] * frequency
    return (jnp.cos(angles), jnp.sin(angles))


def rotate(values, cosine_table, sine_table):
    half_dim = values.shape[-1] // 2
    first_half = values[..., :half_dim]
    second_half = values[..., half_dim:]
    return jnp.concatenate(
        [
            first_half * cosine_table - second_half * sine_table,
            second_half * cosine_table + first_half * sine_table,
        ],
        axis=-1,
    )


def rotate_back(gradient, cosine_table, sine_table):
    half_dim = gradient.shape[-1] // 2
    first_half = gradient[..., :half_dim]
    second_half = gradient[..., half_dim:]
    return jnp.concatenate(
        [
            first_half * cosine_table + second_half * sine_table,
            second_half * cosine_table - first_half * sine_table,
        ],
        axis=-1,
    )


def masked_scores(queries, key_rows, query_first, key_first, score_scale):
    raw_scores = (
        jnp.einsum("qshd,kshd->shqk", queries, key_rows, preferred_element_type=jnp.float32)
        * score_scale
    )
    query_index = query_first + jnp.arange(queries.shape[0])
    key_index = key_first + jnp.arange(key_rows.shape[0])
    return (raw_scores, key_index[None, :] <= query_index[:, None])


def blockwise(fold_step, state_carry, pieces, start_row):
    row_count = pieces[0].shape[0]
    block_size = 512

    def block_turn(block_id, running):
        blocks = tuple(
            (
                lax.dynamic_slice_in_dim(shard_piece, block_id * block_size, block_size, 0)
                for shard_piece in pieces
            )
        )
        return fold_step(running, blocks, start_row + block_id * block_size)

    return lax.fori_loop(0, row_count // block_size, block_turn, state_carry)


def forward_step(queries, query_first, score_scale):
    query_last = query_first + queries.shape[0] - 1

    def fold_step(state_carry, blocks, key_first):
        key_rows, value_rows = blocks

        def compute(running):
            running_max, running_sum, weighted = running
            scores, allowed = masked_scores(queries, key_rows, query_first, key_first, score_scale)
            new_max = jnp.maximum(
                running_max, jnp.max(jnp.where(allowed, scores, far_below), axis=-1)
            )
            exponent = jnp.where(allowed, jnp.exp(scores - new_max[..., None]), 0.0)
            factor = jnp.exp(running_max - new_max)
            running_sum = running_sum * factor + jnp.sum(exponent, axis=-1)
            weighted = weighted * factor[..., None] + jnp.einsum(
                "shqk,kshd->shqd",
                exponent.astype(jnp.bfloat16),
                value_rows,
                preferred_element_type=jnp.float32,
            )
            return (new_max, running_sum, weighted)

        return lax.cond(key_first <= query_last, compute, lambda running: running, state_carry)

    return fold_step


def query_grad_step(queries, grad_heads, log_total, row_dots, query_first, score_scale):
    query_last = query_first + queries.shape[0] - 1

    def fold_step(state_carry, blocks, key_first):
        key_rows, value_rows = blocks

        def compute(running):
            scores, allowed = masked_scores(queries, key_rows, query_first, key_first, score_scale)
            attn_probs = jnp.where(allowed, jnp.exp(scores - log_total[..., None]), 0.0)
            grad_probs = jnp.einsum(
                "qshd,kshd->shqk", grad_heads, value_rows, preferred_element_type=jnp.float32
            )
            grad_scores = (attn_probs * (grad_probs - row_dots[..., None])).astype(jnp.bfloat16)
            return running + score_scale * jnp.einsum(
                "shqk,kshd->qshd", grad_scores, key_rows, preferred_element_type=jnp.float32
            )

        return lax.cond(key_first <= query_last, compute, lambda running: running, state_carry)

    return fold_step


def key_grad_step(key_rows, value_rows, key_first, score_scale):

    def fold_step(state_carry, blocks, query_first):
        queries, grad_heads, log_total_tok, row_dots_tok = blocks
        query_last = query_first + queries.shape[0] - 1

        def compute(running):
            scores, allowed = masked_scores(queries, key_rows, query_first, key_first, score_scale)
            log_total = jnp.transpose(log_total_tok, (1, 2, 0))
            row_dots = jnp.transpose(row_dots_tok, (1, 2, 0))
            attn_probs = jnp.where(allowed, jnp.exp(scores - log_total[..., None]), 0.0)
            grad_value_rows = jnp.einsum(
                "shqk,qshd->kshd",
                attn_probs.astype(jnp.bfloat16),
                grad_heads,
                preferred_element_type=jnp.float32,
            )
            grad_probs = jnp.einsum(
                "qshd,kshd->shqk", grad_heads, value_rows, preferred_element_type=jnp.float32
            )
            grad_scores = (attn_probs * (grad_probs - row_dots[..., None])).astype(jnp.bfloat16)
            grad_key_rows = score_scale * jnp.einsum(
                "shqk,qshd->kshd", grad_scores, queries, preferred_element_type=jnp.float32
            )
            return (grad_key_rows, grad_value_rows)

        return lax.cond(key_first <= query_last, compute, lambda running: running, state_carry)

    return fold_step


def project_in(token_rows, weight, a_chosen, b_chosen):
    main_term = jnp.einsum("scd,dw->csw", token_rows, weight, preferred_element_type=jnp.float32)
    low_rank = jnp.einsum("scd,srd->scr", token_rows, a_chosen, preferred_element_type=jnp.float32)
    side_term = jnp.einsum(
        "scr,srw->csw", low_rank, b_chosen.astype(jnp.float32), precision=highest
    )
    return (main_term + adapt_scale * side_term, low_rank)


def project_out(middle, weight, a_chosen, b_chosen):
    main_term = jnp.einsum("csw,wd->scd", middle, weight, preferred_element_type=jnp.float32)
    low_rank = jnp.einsum("csw,srw->scr", middle, a_chosen, preferred_element_type=jnp.float32)
    side_term = jnp.einsum(
        "scr,srd->scd", low_rank, b_chosen.astype(jnp.float32), precision=highest
    )
    return (main_term + adapt_scale * side_term, low_rank)


def back_in(gradient, weight, a_chosen, b_chosen, token_rows, low_rank):
    back_rank = jnp.einsum("csw,srw->scr", gradient, b_chosen, preferred_element_type=jnp.float32)
    grad_rows = jnp.einsum("csw,dw->scd", gradient, weight, preferred_element_type=jnp.float32)
    grad_rows = grad_rows + adapt_scale * jnp.einsum(
        "scr,srd->scd", back_rank, a_chosen.astype(jnp.float32), precision=highest
    )
    grad_a = adapt_scale * jnp.einsum("scr,scd->srd", back_rank, token_rows, precision=highest)
    grad_b = adapt_scale * jnp.einsum("scr,csw->srw", low_rank, gradient, precision=highest)
    return (grad_rows, grad_a, grad_b)


def back_out(gradient, weight, a_chosen, b_chosen, middle, low_rank):
    back_rank = jnp.einsum("scd,srd->scr", gradient, b_chosen, preferred_element_type=jnp.float32)
    grad_middle = jnp.einsum("scd,wd->csw", gradient, weight, preferred_element_type=jnp.float32)
    grad_middle = grad_middle + adapt_scale * jnp.einsum(
        "scr,srw->csw", back_rank, a_chosen.astype(jnp.float32), precision=highest
    )
    grad_a = adapt_scale * jnp.einsum("scr,csw->srw", back_rank, middle, precision=highest)
    grad_b = adapt_scale * jnp.einsum("scr,scd->srd", low_rank, gradient, precision=highest)
    return (grad_middle, grad_a, grad_b)


def pick_set(onehot, set_table):
    flattened = set_table.reshape(set_table.shape[0], -1)
    chosen = jnp.dot(onehot, flattened, preferred_element_type=jnp.float32).astype(jnp.bfloat16)
    return chosen.reshape((onehot.shape[0],) + set_table.shape[1:])


def spread_sets(onehot, per_sequence):
    flattened = per_sequence.reshape(per_sequence.shape[0], -1)
    summed = jnp.dot(onehot.astype(jnp.float32).T, flattened, precision=highest)
    return summed.reshape((onehot.shape[1],) + per_sequence.shape[1:])


def per_device(
    layer_in,
    w_qkv,
    w_out,
    w_gate_up,
    w_down,
    a_in,
    b_qkv,
    b_gate_up,
    a_out,
    a_down,
    b_out_down,
    set_index,
    positions,
    cotangent,
):
    local_len = positions.shape[1]
    seq_count = positions.shape[0]
    score_scale = 1.0 / math.sqrt(HDIM)
    my_first = lax.axis_index("seq") * local_len
    onehot = (set_index[:, None] == jnp.arange(a_in.shape[0])[None, :]).astype(jnp.bfloat16)
    chosen_a_in = pick_set(onehot, a_in)
    chosen_b_qkv = pick_set(onehot, b_qkv)
    chosen_b_gate_up = pick_set(onehot, b_gate_up)
    chosen_a_out = pick_set(onehot, a_out)
    chosen_a_down = pick_set(onehot, a_down)
    chosen_b_out_down = pick_set(onehot, b_out_down)

    def to_heads(values):
        return values.reshape(local_len, seq_count, -1, HDIM)

    residual_in = layer_in.astype(jnp.float32)
    normed_attn, inverse_attn = layer_norm(residual_in)
    rows_attn = gather_rows(normed_attn.astype(jnp.bfloat16))
    projected = [
        project_in(rows_attn, w_qkv[member], chosen_a_in[:, member], chosen_b_qkv[:, member])
        for member in range(3)
    ]
    cosine_table, sine_table = rope_tables(positions)
    queries = rotate(to_heads(projected[0][0]), cosine_table, sine_table).astype(jnp.bfloat16)
    key_rows = rotate(to_heads(projected[1][0]), cosine_table, sine_table).astype(jnp.bfloat16)
    value_rows = to_heads(projected[2][0]).astype(jnp.bfloat16)
    stat_shape = (seq_count, queries.shape[2], local_len)
    initial = (
        jnp.full(stat_shape, far_below, jnp.float32),
        jnp.zeros(stat_shape, jnp.float32),
        jnp.zeros(stat_shape + (HDIM,), jnp.float32),
    )
    attend = forward_step(queries, my_first, score_scale)
    running_max, running_sum, weighted = blockwise(
        attend,
        initial,
        (
            lax.all_gather(key_rows, "seq", axis=0, tiled=True),
            lax.all_gather(value_rows, "seq", axis=0, tiled=True),
        ),
        jnp.int32(0),
    )
    log_total = running_max + jnp.log(running_sum)
    attn_output = jnp.transpose(weighted / running_sum[..., None], (2, 0, 1, 3))
    mixed = attn_output.reshape(local_len, seq_count, -1).astype(jnp.bfloat16)
    attn_term, rank_out = project_out(mixed, w_out, chosen_a_out, chosen_b_out_down[:, 0])
    residual = residual_in + scatter_rows(attn_term)
    normed_mlp, inverse_mlp = layer_norm(residual)
    rows_mlp = gather_rows(normed_mlp.astype(jnp.bfloat16))
    gate_proj, rank_gate = project_in(
        rows_mlp, w_gate_up[0], chosen_a_in[:, 3], chosen_b_gate_up[:, 0]
    )
    up_proj, rank_up = project_in(rows_mlp, w_gate_up[1], chosen_a_in[:, 4], chosen_b_gate_up[:, 1])
    sigmoid_gate = jax.nn.sigmoid(gate_proj)
    activation = (gate_proj * sigmoid_gate * up_proj).astype(jnp.bfloat16)
    down_term, rank_down = project_out(activation, w_down, chosen_a_down, chosen_b_out_down[:, 1])
    result = (residual + scatter_rows(down_term)).astype(jnp.bfloat16)
    grad_down = gather_rows(cotangent)
    grad_activation, grad_a_down, grad_b_down = back_out(
        grad_down, w_down, chosen_a_down, chosen_b_out_down[:, 1], activation, rank_down
    )
    grad_up = (grad_activation * gate_proj * sigmoid_gate).astype(jnp.bfloat16)
    grad_gate = (
        grad_activation * up_proj * sigmoid_gate * (1.0 + gate_proj * (1.0 - sigmoid_gate))
    ).astype(jnp.bfloat16)
    rows_from_gate, grad_a_gate, grad_b_gate = back_in(
        grad_gate, w_gate_up[0], chosen_a_in[:, 3], chosen_b_gate_up[:, 0], rows_mlp, rank_gate
    )
    rows_from_up, grad_a_up, grad_b_up = back_in(
        grad_up, w_gate_up[1], chosen_a_in[:, 4], chosen_b_gate_up[:, 1], rows_mlp, rank_up
    )
    grad_residual = cotangent.astype(jnp.float32) + norm_back(
        scatter_rows(rows_from_gate + rows_from_up), normed_mlp, inverse_mlp
    )
    grad_attn_rows = gather_rows(grad_residual.astype(jnp.bfloat16))
    grad_mixed, grad_a_out, grad_b_out = back_out(
        grad_attn_rows, w_out, chosen_a_out, chosen_b_out_down[:, 0], mixed, rank_out
    )
    grad_heads = to_heads(grad_mixed.astype(jnp.bfloat16))
    row_dots_tok = jnp.sum(grad_heads.astype(jnp.float32) * attn_output, axis=-1)
    row_dots = jnp.transpose(row_dots_tok, (1, 2, 0))
    log_total_tok = jnp.transpose(log_total, (2, 0, 1))
    query_step = query_grad_step(queries, grad_heads, log_total, row_dots, my_first, score_scale)
    zero_heads = jnp.zeros(queries.shape, jnp.float32)
    every_key, every_value = (
        lax.all_gather(key_rows, "seq", axis=0, tiled=True),
        lax.all_gather(value_rows, "seq", axis=0, tiled=True),
    )
    grad_queries = blockwise(query_step, zero_heads, (every_key, every_value), 0)
    block_size = 512

    def one_block(block_id):
        first_key = block_id * block_size
        block_keys = lax.dynamic_slice_in_dim(every_key, first_key, block_size, 0)
        block_values = lax.dynamic_slice_in_dim(every_value, first_key, block_size, 0)
        zero_block = jnp.zeros(block_keys.shape, jnp.float32)
        block_step = key_grad_step(block_keys, block_values, first_key, score_scale)
        grad_key_block, grad_value_block = block_step(
            (zero_block, zero_block), (queries, grad_heads, log_total_tok, row_dots_tok), my_first
        )
        return jnp.concatenate([grad_key_block, grad_value_block], axis=-1)

    stacked = lax.map(one_block, jnp.arange(local_len * lax.axis_size("seq") // block_size))
    stacked_terms = lax.psum_scatter(
        stacked.reshape((local_len * lax.axis_size("seq"),) + stacked.shape[2:]).astype(
            jnp.bfloat16
        ),
        "seq",
        scatter_dimension=0,
        tiled=True,
    ).astype(jnp.float32)
    grad_keys = stacked_terms[..., :HDIM]
    grad_values = stacked_terms[..., HDIM:]
    grad_query_raw = (
        rotate_back(grad_queries, cosine_table, sine_table)
        .astype(jnp.bfloat16)
        .reshape(local_len, seq_count, -1)
    )
    grad_key_raw = (
        rotate_back(grad_keys, cosine_table, sine_table)
        .astype(jnp.bfloat16)
        .reshape(local_len, seq_count, -1)
    )
    grad_value_raw = grad_values.astype(jnp.bfloat16).reshape(local_len, seq_count, -1)
    back_parts = [
        back_in(
            gradient,
            w_qkv[member],
            chosen_a_in[:, member],
            chosen_b_qkv[:, member],
            rows_attn,
            projected[member][1],
        )
        for member, gradient in enumerate((grad_query_raw, grad_key_raw, grad_value_raw))
    ]
    grad_rows_attn = back_parts[0][0] + back_parts[1][0] + back_parts[2][0]
    grad_in = (
        grad_residual + norm_back(scatter_rows(grad_rows_attn), normed_attn, inverse_attn)
    ).astype(jnp.bfloat16)
    per_seq_a_in = jnp.stack(
        [back_parts[0][1], back_parts[1][1], back_parts[2][1], grad_a_gate, grad_a_up], axis=1
    )
    per_seq_b_qkv = jnp.stack([bundle[2] for bundle in back_parts], axis=1)
    per_seq_b_gate_up = jnp.stack([grad_b_gate, grad_b_up], axis=1)
    per_seq_b_out_down = jnp.stack([grad_b_out, grad_b_down], axis=1)
    sums_seq = (
        lax.psum(spread_sets(onehot, per_seq_b_qkv).astype(jnp.bfloat16), "seq").astype(
            jnp.float32
        ),
        lax.psum(spread_sets(onehot, per_seq_b_gate_up).astype(jnp.bfloat16), "seq").astype(
            jnp.float32
        ),
        lax.psum(spread_sets(onehot, grad_a_out).astype(jnp.bfloat16), "seq").astype(jnp.float32),
        lax.psum(spread_sets(onehot, grad_a_down).astype(jnp.bfloat16), "seq").astype(jnp.float32),
    )
    sums_all = lax.psum(
        (spread_sets(onehot, per_seq_a_in), spread_sets(onehot, per_seq_b_out_down)), ("seq", "mp")
    )
    return (
        result,
        grad_in,
        sums_all[0],
        sums_seq[0],
        sums_seq[1],
        sums_seq[2],
        sums_seq[3],
        sums_all[1],
    )


log2e = 1.4426950408889634
attn_tile = 512
hidden_tile = 512


def dot_nt(a, b):
    return lax.dot_general(a, b, (((1,), (1,)), ((), ())), preferred_element_type=jnp.float32)


def dot_tn(a, b):
    return lax.dot_general(a, b, (((0,), (0,)), ((), ())), preferred_element_type=jnp.float32)


def dot_nn(a, b):
    return jnp.dot(a, b, preferred_element_type=jnp.float32)


def causal(block_t, first_row, first_col):
    rows = first_row + lax.broadcasted_iota(jnp.int32, block_t.shape, 0)
    cols = first_col + lax.broadcasted_iota(jnp.int32, block_t.shape, 1)
    return rows <= cols


def attend_kernel(q_ref, k_ref, v_ref, o_ref, lse_ref):
    i = pl.program_id(1)
    tile = q_ref.shape[0]
    factor = log2e / math.sqrt(HDIM)
    q = q_ref[...]

    def fold(j, carry, diagonal):
        top, total, acc = carry
        at = pl.ds(pl.multiple_of(j * tile, tile), tile)
        scores = dot_nt(k_ref[at, :], q)
        if diagonal:
            scores = jnp.where(causal(scores, 0, 0), scores, far_below)
        new_top = jnp.maximum(top, jnp.max(scores, axis=0, keepdims=True))
        weight = jnp.exp2(scores * factor - new_top * factor)
        keep = jnp.exp2((top - new_top) * factor)
        total = total * keep + jnp.sum(weight, axis=0, keepdims=True)
        acc = acc * keep + dot_tn(v_ref[at, :], weight.astype(jnp.bfloat16))
        return (new_top, total, acc)

    carry = (
        jnp.full((1, tile), far_below, jnp.float32),
        jnp.zeros((1, tile), jnp.float32),
        jnp.zeros((HDIM, tile), jnp.float32),
    )
    carry = lax.fori_loop(0, i, lambda j, c: fold(j, c, False), carry)
    top, total, acc = fold(i, carry, True)
    o_ref[...] = jnp.transpose(acc / total).astype(o_ref.dtype)
    lse_ref[0] = top * factor + jnp.log2(total)


def attend(q, k, v):
    length = q.shape[0]
    heads = q.shape[1] // HDIM
    tile = attn_tile
    return pl.pallas_call(
        attend_kernel,
        grid=(heads, length // tile),
        in_specs=[
            pl.BlockSpec((tile, HDIM), lambda h, i: (i, h)),
            pl.BlockSpec((length, HDIM), lambda h, i: (0, h)),
            pl.BlockSpec((length, HDIM), lambda h, i: (0, h)),
        ],
        out_specs=[
            pl.BlockSpec((tile, HDIM), lambda h, i: (i, h)),
            pl.BlockSpec((1, 1, tile), lambda h, i: (h, 0, i)),
        ],
        out_shape=[
            jax.ShapeDtypeStruct(q.shape, jnp.bfloat16),
            jax.ShapeDtypeStruct((heads, 1, length), jnp.float32),
        ],
        cost_estimate=pl.CostEstimate(
            flops=2 * heads * length * length * HDIM,
            bytes_accessed=8 * length * heads * HDIM,
            transcendentals=heads * length * length // 2,
        ),
        compiler_params=pltpu.CompilerParams(vmem_limit_bytes=32 << 20),
    )(q, k, v)


def turn_back(gradient, cos, sin):
    return gradient * cos + pltpu.roll(gradient, HDIM // 2, 1) * sin


def attend_back_kernel(
    q_ref, k_ref, v_ref, go_ref, lse_ref, dots_ref, cos_ref, sin_ref, dq_ref, dk_ref, dv_ref, acc_ref
):
    j = pl.program_id(1)
    tile = k_ref.shape[0]
    length = q_ref.shape[0]
    scale = 1.0 / math.sqrt(HDIM)
    factor = log2e * scale
    k = k_ref[...]
    v = v_ref[...]

    @pl.when(j == 0)
    def _():
        acc_ref[...] = jnp.zeros_like(acc_ref)

    def fold(i, carry, diagonal):
        dk, dv = carry
        at = pl.ds(pl.multiple_of(i * tile, tile), tile)
        q = q_ref[at, :]
        go = go_ref[at, :]
        scores = dot_nt(k, q)
        weight = jnp.exp2(scores * factor - lse_ref[0, :, at])
        if diagonal:
            weight = jnp.where(causal(scores, 0, 0), weight, 0.0)
        grad_weight = dot_nt(v, go)
        grad_scores = (weight * (grad_weight - dots_ref[0, :, at])).astype(jnp.bfloat16)
        dv = dv + dot_nn(weight.astype(jnp.bfloat16), go)
        dk = dk + dot_nn(grad_scores, q)
        acc_ref[at, :] += dot_tn(grad_scores, k)
        return (dk, dv)

    zero = jnp.zeros((tile, HDIM), jnp.float32)
    carry = fold(j, (zero, zero), True)
    dk, dv = lax.fori_loop(j + 1, length // tile, lambda i, c: fold(i, c, False), carry)
    at = pl.ds(pl.multiple_of(j * tile, tile), tile)
    dk_ref[...] = turn_back(dk * scale, cos_ref[at, :], sin_ref[at, :]).astype(dk_ref.dtype)
    dv_ref[...] = dv.astype(dv_ref.dtype)
    dq_ref[...] = turn_back(acc_ref[at, :] * scale, cos_ref[at, :], sin_ref[at, :]).astype(dq_ref.dtype)


def attend_back(q, k, v, go, lse, dots, cos, sin):
    length = q.shape[0]
    heads = q.shape[1] // HDIM
    tile = attn_tile
    whole = pl.BlockSpec((length, HDIM), lambda h, j: (0, h))
    part = pl.BlockSpec((tile, HDIM), lambda h, j: (j, h))
    row = pl.BlockSpec((1, 1, length), lambda h, j: (h, 0, 0))
    table = pl.BlockSpec((length, HDIM), lambda h, j: (0, 0))
    return pl.pallas_call(
        attend_back_kernel,
        grid=(heads, length // tile),
        in_specs=[whole, part, part, whole, row, row, table, table],
        out_specs=[part, part, part],
        out_shape=[jax.ShapeDtypeStruct(q.shape, jnp.bfloat16)] * 3,
        scratch_shapes=[pltpu.VMEM((length, HDIM), jnp.float32)],
        cost_estimate=pl.CostEstimate(
            flops=5 * heads * length * length * HDIM,
            bytes_accessed=14 * length * heads * HDIM,
            transcendentals=heads * length * length // 2,
        ),
        compiler_params=pltpu.CompilerParams(vmem_limit_bytes=32 << 20),
    )(q, k, v, go, lse, dots, cos, sin)


mesh_ids = pl.DeviceIdType.MESH


def remote(src, dst, send, recv, target):
    return pltpu.make_async_remote_copy(
        src_ref=src, dst_ref=dst, send_sem=send, recv_sem=recv, device_id=target, device_id_type=mesh_ids
    )


def meet(partners):
    barrier = pltpu.get_barrier_semaphore()
    for condition, device in partners:
        if condition is None:
            pl.semaphore_signal(barrier, inc=1, device_id=device, device_id_type=mesh_ids)
        else:

            @pl.when(condition)
            def _():
                pl.semaphore_signal(barrier, inc=1, device_id=device, device_id_type=mesh_ids)

    count = 0
    for condition, device in partners:
        count = count + (1 if condition is None else condition.astype(jnp.int32))
    pl.semaphore_wait(barrier, count)


def flip(index, bit):
    return index + bit - 2 * bit * ((index // bit) % 2)


def places():
    s = lax.axis_index("seq")
    z = lax.axis_index("mp")
    return s, z


class Gather:
    def __init__(self, blocks, s, z, send, recv, half):
        self.at = blocks
        self.s = s
        self.z = z
        self.send = send
        self.recv = recv
        self.half = half

    def rows(self, part):
        return pl.ds(part * self.half, self.half)

    def copy(self, index, span, part, target):
        ref = self.at.at[span] if part is None else self.at.at[span, self.rows(part)]
        return remote(ref, ref, self.send.at[index], self.recv.at[index], (target, self.z))

    def begin(self):
        s, x, y, other = self.s, flip(self.s, 2), flip(self.s, 4), flip(self.s, 1)
        self.copies = [
            self.copy(0, s, 0, x),
            self.copy(1, s, 1, y),
            self.copy(2, s, 1, x),
            self.copy(3, s, 0, y),
            self.copy(6, s, None, other),
        ]
        for one in self.copies:
            one.start()

    def arrive_first(self):
        s, x, y = self.s, flip(self.s, 2), flip(self.s, 4)
        self.copy(0, x, 0, x).wait_recv()
        one = self.copy(4, x, 0, y)
        one.start()
        self.copy(1, y, 1, y).wait_recv()
        two = self.copy(5, y, 1, x)
        two.start()
        self.copies += [one, two]

    def arrive_neighbours(self):
        s, x, y, other = self.s, flip(self.s, 2), flip(self.s, 4), flip(self.s, 1)
        self.copy(2, x, 1, x).wait_recv()
        one = self.copy(7, x, None, other)
        one.start()
        self.copy(3, y, 0, y).wait_recv()
        two = self.copy(8, y, None, other)
        two.start()
        self.copies += [one, two]

    def arrive_diagonal(self):
        s, other = self.s, flip(self.s, 1)
        diagonal = flip(flip(s, 2), 4)
        self.copy(4, diagonal, 0, other).wait_recv()
        self.copy(5, diagonal, 1, other).wait_recv()
        one = self.copy(9, diagonal, None, other)
        one.start()
        self.copies += [one]

    def arrive_core(self, index):
        s = self.s
        other = flip(s, 1)
        span = (other, flip(other, 2), flip(other, 4), flip(flip(other, 2), 4))[index]
        self.copy(6 + index, span, None, other).wait_recv()
        return span

    def end(self):
        for one in self.copies:
            one.wait_send()


gather_sems = 10


def spend(microseconds):
    return pl.CostEstimate(flops=microseconds * 10**9, bytes_accessed=10**6, transcendentals=0)


class Line:
    def __init__(self, blocks, core, s, z, send, recv):
        self.at = blocks
        self.core = core
        self.s = s
        self.z = z
        self.send = send
        self.recv = recv

    def ref(self, j):
        return self.at.at[j, self.core]

    def up(self, hop, j):
        ref = self.ref(j)
        return remote(ref, ref, self.send.at[hop], self.recv.at[hop], (self.s, self.z + 1))

    def down(self, hop, j):
        ref = self.ref(j)
        return remote(ref, ref, self.send.at[3 + hop], self.recv.at[3 + hop], (self.s, self.z - 1))

    def across(self, index, j):
        ref = self.ref(j)
        return remote(ref, ref, self.send.at[6 + index], self.recv.at[6 + index], (flip(self.s, 1), self.z))

    def begin(self):
        z = self.z

        @pl.when(z < 3)
        def _():
            self.up(0, z).start()

        @pl.when(z > 0)
        def _():
            self.down(0, z).start()

        self.across(0, z).start()

    def hop(self, t):
        z = self.z

        @pl.when(z >= t)
        def _():
            self.up(t - 1, z - t).wait_recv()
            self.across(t, z - t).start()
            if t < 3:

                @pl.when(z < 3)
                def _():
                    self.up(t, z - t).start()

        @pl.when(z + t <= 3)
        def _():
            self.down(t - 1, z + t).wait_recv()
            self.across(3 + t, z + t).start()
            if t < 3:

                @pl.when(z > 0)
                def _():
                    self.down(t, z + t).start()

    def arrive_core(self):
        z = self.z
        other = 1 - self.core

        def wait(index, j):
            ref = self.at.at[j, other]
            remote(ref, ref, self.send.at[6 + index], self.recv.at[6 + index], (flip(self.s, 1), z)).wait_recv()

        wait(0, z)
        for t in (1, 2, 3):

            @pl.when(z >= t)
            def _():
                wait(t, z - t)

            @pl.when(z + t <= 3)
            def _():
                wait(3 + t, z + t)

    def end(self):
        z = self.z

        @pl.when(z < 3)
        def _():
            self.up(0, z).wait_send()

        @pl.when(z > 0)
        def _():
            self.down(0, z).wait_send()

        self.across(0, z).wait_send()
        for t in (1, 2, 3):

            @pl.when(z >= t)
            def _():
                self.across(t, z - t).wait_send()
                if t < 3:

                    @pl.when(z < 3)
                    def _():
                        self.up(t, z - t).wait_send()

            @pl.when(z + t <= 3)
            def _():
                self.across(3 + t, z + t).wait_send()
                if t < 3:

                    @pl.when(z > 0)
                    def _():
                        self.down(t, z + t).wait_send()


line_sems = 13


def norm_rows(values):
    centred = values - jnp.mean(values, axis=-1, keepdims=True)
    inverse = lax.rsqrt(jnp.mean(centred * centred, axis=-1, keepdims=True) + norm_eps)
    return (centred * inverse, inverse)


def start_kernel(
    x_ref, w_ref, o_ref, cos_ref, sin_ref, a_ref, set_ref,
    x_own_ref, n_own_ref, u_out, w_all, o_all, q_ref, k_ref, v_ref, low_ref, b_sel_ref, a_sel_ref,
    u_ref, w_buf, w_big, a2a_send, a2a_recv, ag_send, ag_recv, w_send, w_recv, o_send, o_recv, local_sem,
):
    s, z = places()
    core = s % 2
    other = flip(s, 1)
    zs = [flip(z, 1), flip(z, 2), 3 - z]
    meet([(None, (other, z)), (None, (flip(s, 2), z)), (None, (flip(s, 4), z))] + [(None, (s, j)) for j in zs])

    swaps = [
        remote(x_ref.at[j], x_own_ref.at[z], a2a_send.at[d], a2a_recv.at[d], (s, j)) for d, j in enumerate(zs)
    ]
    for one in swaps:
        one.start()
    x_own_ref[z] = x_ref[z]
    w_buf[z, core] = w_ref[...]
    own_o = pltpu.make_async_copy(o_ref, o_all.at[z, core], local_sem.at[8])
    own_o.start()
    for d, j in enumerate(zs):
        remote(x_ref.at[j], x_own_ref.at[j], a2a_send.at[d], a2a_recv.at[d], (s, j)).wait_recv()
    line = Line(w_buf, core, s, z, w_send, w_recv)
    line.begin()
    for part in range(4):
        normed, _ = norm_rows(x_own_ref[part].astype(jnp.float32))
        normed = normed.astype(jnp.bfloat16)
        n_own_ref[pl.ds(part * 64, 64), :] = normed
        u_ref[s, pl.ds(part * 64, 64), :] = normed
    gather = Gather(u_ref, s, z, ag_send, ag_recv, 128)
    gather.begin()
    gather.arrive_first()
    line.hop(1)
    gather.arrive_neighbours()
    line.hop(2)
    gather.arrive_diagonal()
    for index in range(4):
        gather.arrive_core(index)
    stores = [pltpu.make_async_copy(u_ref.at[t], u_out.at[t], local_sem.at[t]) for t in range(8)]
    for one in stores:
        one.start()
    a48 = a_ref[...]

    def lows(t, _):
        low_ref[t] = (adapt_scale * dot_nt(u_ref[t], a48)).astype(jnp.bfloat16)
        return 0

    lax.fori_loop(0, 8, lows, 0)
    line.hop(3)
    own_o.wait()
    o_line = Line(o_all, core, s, z, o_send, o_recv)
    o_line.begin()
    line.arrive_core()
    keep = pltpu.make_async_copy(w_buf, w_all, local_sem.at[9])
    keep.start()
    mine = set_ref[0]
    for j in range(4):
        table = w_buf[j, 0, 3072:, :]
        picked = jnp.zeros((48, HDIM), jnp.bfloat16)
        picked_a = jnp.zeros((16, HDIM), jnp.bfloat16)
        for member in range(4):
            picked = jnp.where(mine == member, table[48 * member : 48 * member + 48], picked)
            picked_a = jnp.where(mine == member, table[192 + 16 * member : 208 + 16 * member], picked_a)
        b_sel_ref[j] = picked
        a_sel_ref[j] = picked_a
    for part in range(3):
        for head in range(2):
            columns = pl.ds((2 * part + head) * HDIM, HDIM)
            for side in range(2):
                w_big[pl.ds(side * 1024, 1024), columns] = w_buf[
                    2 * core + head, side, pl.ds(part * 1024, 1024), :
                ]
    b_two = [
        jnp.concatenate(
            [b_sel_ref[2 * core, 16 * part : 16 * part + 16], b_sel_ref[2 * core + 1, 16 * part : 16 * part + 16]],
            axis=1,
        )
        for part in range(3)
    ]

    def project(t, _):
        u = u_ref[t]
        low = low_ref[t]
        cos = cos_ref[pl.ds(pl.multiple_of(t * 256, 256), 256), :]
        sin = sin_ref[pl.ds(pl.multiple_of(t * 256, 256), 256), :]
        for part, out in enumerate((q_ref, k_ref, v_ref)):
            raw = dot_nn(u, w_big[:, 256 * part : 256 * part + 256]) + dot_nn(
                low[:, 16 * part : 16 * part + 16], b_two[part]
            )
            for head in range(2):
                piece = raw[:, HDIM * head : HDIM * head + HDIM]
                if part < 2:
                    piece = piece * cos - pltpu.roll(piece, HDIM // 2, 1) * sin
                out[t, :, pl.ds(HDIM * head, HDIM)] = piece.astype(jnp.bfloat16)
        return 0

    lax.fori_loop(0, 3, project, 0)
    o_line.hop(1)
    lax.fori_loop(3, 6, project, 0)
    o_line.hop(2)
    lax.fori_loop(6, 8, project, 0)
    o_line.hop(3)
    o_line.arrive_core()
    for one in stores:
        one.wait()
    keep.wait()
    for one in swaps:
        one.wait_send()
    line.end()
    o_line.end()
    gather.end()


def start_layer(x, w_pack, o_pack, cos, sin, a48, my_set):
    bf16 = jnp.bfloat16
    vmem = pl.BlockSpec(memory_space=pltpu.VMEM)
    anywhere = pl.BlockSpec(memory_space=pl.ANY)
    width = x.shape[2]
    rows = w_pack.shape[0]
    shape = jax.ShapeDtypeStruct
    dma = pltpu.SemaphoreType.DMA
    return pl.pallas_call(
        start_kernel,
        in_specs=[vmem, vmem, anywhere, vmem, vmem, vmem, pl.BlockSpec(memory_space=pltpu.SMEM)],
        out_specs=[vmem, vmem, anywhere, anywhere, anywhere, vmem, vmem, vmem, vmem, vmem, vmem],
        out_shape=[
            shape((4, 64, width), bf16),
            shape((256, width), bf16),
            shape((8, 256, width), bf16),
            shape((4, 2, rows, HDIM), bf16),
            shape((4, 2, HDIM, width // 2), bf16),
            shape((8, 256, 256), bf16),
            shape((8, 256, 256), bf16),
            shape((8, 256, 256), bf16),
            shape((8, 256, 48), bf16),
            shape((4, 48, HDIM), bf16),
            shape((4, 16, HDIM), bf16),
        ],
        scratch_shapes=[
            pltpu.VMEM((8, 256, width), bf16),
            pltpu.VMEM((4, 2, rows, HDIM), bf16),
            pltpu.VMEM((width, 768), bf16),
            dma((3,)),
            dma((3,)),
            dma((gather_sems,)),
            dma((gather_sems,)),
            dma((line_sems,)),
            dma((line_sems,)),
            dma((line_sems,)),
            dma((line_sems,)),
            dma((10,)),
        ],
        cost_estimate=spend(80),
        compiler_params=pltpu.CompilerParams(
            collective_id=1, has_side_effects=True, vmem_limit_bytes=56 << 20
        ),
    )(x, w_pack, o_pack, cos, sin, a48, my_set)


class Reduce:
    def __init__(self, product, s, z, out, inn, send, recv):
        self.product = product
        self.s = s
        self.z = z
        self.out = out
        self.inn = inn
        self.send = send
        self.recv = recv
        chip = s // 2
        self.chip = chip
        self.cx = flip(chip, 1)
        self.cy = flip(chip, 2)
        self.cd = flip(self.cx, 2)

    def copy(self, index):
        target = flip(self.s, 2) if index in (0, 2, 5) else flip(self.s, 4)
        return remote(
            self.out.at[index], self.inn.at[index], self.send.at[index], self.recv.at[index], (target, self.z)
        )

    def give(self, index, chip, half, extra=None):
        value = self.product(chip, half)
        if extra is not None:
            self.copy(extra).wait_recv()
            value = value + self.inn[extra].astype(jnp.float32)
        self.out[index] = value.astype(jnp.bfloat16)
        self.copy(index).start()

    def begin(self):
        self.give(0, self.cd, 0)
        self.give(1, self.cd, 1)
        self.give(2, self.cx, 0)
        self.give(3, self.cy, 1)

    def middle(self):
        self.give(4, self.cy, 0, 0)
        self.give(5, self.cx, 1, 1)

    def finish(self, half):
        indices = (2, 4) if half == 0 else (3, 5)
        total = self.product(self.chip, half)
        for index in indices:
            self.copy(index).wait_recv()
            total = total + self.inn[index].astype(jnp.float32)
        return total

    def end(self):
        for index in range(6):
            self.copy(index).wait_send()


def out_kernel(
    mixed_ref, o_all, a_sel_ref, b_ref, w_all, a48_ref, b_sel_ref, x_own_ref,
    residual_ref, m_own_ref, o_eff_ref, w_cat_ref,
    sib_ref, out_buf, in_buf, o_big, w_buf, sib_send, sib_recv, send, recv, local_sem,
):
    s, z = places()
    core = s % 2
    other = flip(s, 1)
    meet([(None, (other, z)), (None, (flip(s, 2), z)), (None, (flip(s, 4), z))])
    swaps = [
        remote(
            mixed_ref.at[2 * c + 1 - core], sib_ref.at[c], sib_send.at[c], sib_recv.at[c], (other, z)
        )
        for c in range(4)
    ]
    for one in swaps:
        one.start()
    load_w = pltpu.make_async_copy(w_all, w_buf, local_sem.at[0])
    load_w.start()
    for j in range(4):
        head = (2 * core + j) % 4
        merged = adapt_scale * dot_tn(a_sel_ref[head], b_ref[...])
        for side in range(2):
            o_big[pl.ds(j * HDIM, HDIM), pl.ds(side * 1024, 1024)] = (
                o_all[head, side].astype(jnp.float32) + merged[:, side * 1024 : side * 1024 + 1024]
            ).astype(jnp.bfloat16)
    o_eff_ref[...] = o_big[0 : 2 * HDIM, :]
    for one in swaps:
        one.wait_recv()

    def product(chip, half):
        rows = pl.ds(half * 128, 128)
        both = jnp.concatenate([mixed_ref[2 * chip + core, rows, :], sib_ref[chip, rows, :]], axis=1)
        return dot_nn(both, o_big[...])

    reduce = Reduce(product, s, z, out_buf, in_buf, send, recv)
    reduce.begin()
    load_w.wait()

    def merge(index, _):
        j = index // 3
        part = index % 3
        head = (2 * core + j) % 4
        b_part = b_sel_ref[head, pl.ds(pl.multiple_of(part * 16, 16), 16), :]
        a_part = a48_ref[pl.ds(pl.multiple_of(part * 16, 16), 16), :]
        column = pl.multiple_of(((j // 2) * 6 + part * 2 + j % 2) * HDIM, HDIM)
        for side in range(2):
            merged = adapt_scale * dot_tn(a_part[:, side * 1024 : side * 1024 + 1024], b_part)
            w_cat_ref[pl.ds(side * 1024, 1024), pl.ds(column, HDIM)] = (
                w_buf[head, side, pl.ds(pl.multiple_of(part * 1024, 1024), 1024), :].astype(jnp.float32)
                + merged
            ).astype(jnp.bfloat16)
        return 0

    lax.fori_loop(0, 4, merge, 0)
    reduce.middle()
    lax.fori_loop(4, 12, merge, 0)
    for half in range(2):
        total = reduce.finish(half)
        x = x_own_ref[2 * half : 2 * half + 2].reshape(128, -1).astype(jnp.float32)
        residual = x + total
        residual_ref[pl.ds(half * 128, 128), :] = residual
        normed, _ = norm_rows(residual)
        m_own_ref[pl.ds(half * 128, 128), :] = normed.astype(jnp.bfloat16)
    for one in swaps:
        one.wait_send()
    reduce.end()


def out_layer(mixed, o_all, a_sel, b_row, w_all, a48, b_sel, x_own):
    bf16 = jnp.bfloat16
    vmem = pl.BlockSpec(memory_space=pltpu.VMEM)
    width = x_own.shape[2]
    shape = jax.ShapeDtypeStruct
    dma = pltpu.SemaphoreType.DMA
    return pl.pallas_call(
        out_kernel,
        in_specs=[vmem, vmem, vmem, vmem, pl.BlockSpec(memory_space=pl.ANY), vmem, vmem, vmem],
        out_specs=[vmem, vmem, vmem, vmem],
        out_shape=[
            shape((256, width), jnp.float32),
            shape((256, width), bf16),
            shape((256, width), bf16),
            shape((width, 1536), bf16),
        ],
        scratch_shapes=[
            pltpu.VMEM((4, 256, 256), bf16),
            pltpu.VMEM((6, 128, width), bf16),
            pltpu.VMEM((6, 128, width), bf16),
            pltpu.VMEM((512, width), bf16),
            pltpu.VMEM(w_all.shape, bf16),
            dma((4,)),
            dma((4,)),
            dma((6,)),
            dma((6,)),
            dma((1,)),
        ],
        cost_estimate=spend(45),
        compiler_params=pltpu.CompilerParams(
            collective_id=2, has_side_effects=True, vmem_limit_bytes=56 << 20
        ),
    )(mixed, o_all, a_sel, b_row, w_all, a48, b_sel, x_own)


def spread_kernel(
    g_ref, o_eff_ref, mixed_ref, b_ref, down1_ref, down2_ref,
    g_out, gm_ref, dots_ref, rank_ref, got1_ref, got2_ref, g_buf, send, recv, local_sem, down_send, down_recv,
):
    s, z = places()
    meet(
        [(None, (flip(s, 1), z)), (None, (flip(s, 2), z)), (None, (flip(s, 4), z))]
        + [(None, (s, flip(z, 1))), (None, (s, flip(z, 2)))]
    )
    results = [
        remote(down1_ref, got1_ref, down_send.at[0], down_recv.at[0], (s, flip(z, 1))),
        remote(down2_ref, got2_ref, down_send.at[1], down_recv.at[1], (s, flip(z, 2))),
    ]
    for one in results:
        one.start()
    g_buf[s] = g_ref[...]
    gather = Gather(g_buf, s, z, send, recv, 128)
    gather.begin()

    def store(t):
        return pltpu.make_async_copy(g_buf.at[t], g_out.at[t], local_sem.at[0])

    def work(t):
        g = g_buf[t]
        store(t).start()
        back = dot_nt(g, o_eff_ref[...]).astype(jnp.bfloat16)
        gm_ref[t] = back
        product = back.astype(jnp.float32) * mixed_ref[t].astype(jnp.float32)
        for head in range(2):
            turned = jnp.transpose(product[:, HDIM * head : HDIM * head + HDIM])
            dots_ref[head, t] = jnp.sum(turned, axis=0, keepdims=True)
        rank_ref[t] = (adapt_scale * dot_nt(g, b_ref[...])).astype(jnp.bfloat16)
        store(t).wait()

    work(s)
    gather.arrive_first()
    work(gather.arrive_core(0))
    gather.arrive_neighbours()
    work(flip(s, 2))
    work(flip(s, 4))
    work(gather.arrive_core(1))
    work(gather.arrive_core(2))
    gather.arrive_diagonal()
    work(flip(flip(s, 2), 4))
    work(gather.arrive_core(3))
    gather.end()
    for one in results:
        one.wait()


def spread_layer(g_own, o_eff, mixed, b_row, down1, down2):
    bf16 = jnp.bfloat16
    vmem = pl.BlockSpec(memory_space=pltpu.VMEM)
    anywhere = pl.BlockSpec(memory_space=pl.ANY)
    width = g_own.shape[1]
    shape = jax.ShapeDtypeStruct
    dma = pltpu.SemaphoreType.DMA
    return pl.pallas_call(
        spread_kernel,
        in_specs=[vmem] * 4 + [anywhere] * 2,
        out_specs=[anywhere, vmem, vmem, vmem, anywhere, anywhere],
        out_shape=[
            shape((8, 256, width), bf16),
            shape((8, 256, 256), bf16),
            shape((2, 8, 1, 256), jnp.float32),
            shape((8, 256, 16), bf16),
            shape(down1.shape, bf16),
            shape(down2.shape, bf16),
        ],
        scratch_shapes=[
            pltpu.VMEM((8, 256, width), bf16),
            dma((gather_sems,)),
            dma((gather_sems,)),
            dma((1,)),
            dma((2,)),
            dma((2,)),
        ],
        cost_estimate=spend(40),
        compiler_params=pltpu.CompilerParams(
            collective_id=3, has_side_effects=True, vmem_limit_bytes=48 << 20
        ),
    )(g_own, o_eff, mixed, b_row, down1, down2)


def mlp_line_kernel(
    m_ref, residual_ref, cot0_ref, cot1_ref, cot2_ref, cot3_ref, w_gu_ref, w_d_ref, a_ref, b_ref, ad_ref, bd_ref,
    g_ref, grad_res_ref, down0_ref, down1_ref, down2_ref, down3_ref, grad_b_ref, grad_ad_ref, grad_a_ref, grad_bd_ref,
    m_buf, wg, wu, wd, cot_buf, back_acc, down_acc, ranks, slots, r1, r2, r3, r4, r5, stage,
    up_send, up_recv, dn_send, dn_recv, send1, recv1, send4, recv4, send5, recv5, send23, recv23,
    weight_sem, cot_sem, stage_sem,
):
    s, z = places()
    tiles = wg.shape[0]
    tile = wg.shape[2]
    f32 = jnp.float32
    bf16 = jnp.bfloat16
    middle = z * (3 - z) == 2
    at_end = z * (3 - z) == 0
    pair = flip(z, 1)
    opposite = 3 - z
    inner = 1 + z // 2
    high = z // 2
    ids = [z, pair, 2 - high, 3 - 3 * high]
    far = 3 - 3 * high

    loads = []
    for h in range(tiles):
        columns = pl.ds(h * tile, tile)
        loads.append(
            [
                pltpu.make_async_copy(w_gu_ref.at[0, :, columns], wg.at[h], weight_sem.at[3 * h]),
                pltpu.make_async_copy(w_gu_ref.at[1, :, columns], wu.at[h], weight_sem.at[3 * h + 1]),
                pltpu.make_async_copy(w_d_ref.at[columns, :], wd.at[h], weight_sem.at[3 * h + 2]),
            ]
        )
        for one in loads[-1]:
            one.start()

    others = [z, pair, flip(z, 2), opposite]
    cot_refs = (cot0_ref, cot1_ref, cot2_ref, cot3_ref)
    down_refs = (down0_ref, down1_ref, down2_ref, down3_ref)

    def load_cot(seq):
        return [
            pltpu.make_async_copy(cot_refs[d].at[seq], cot_buf.at[others[d]], cot_sem.at[d]) for d in range(4)
        ]

    for one in load_cot(z):
        one.start()

    meet([(z < 3, (s, z + 1)), (z > 0, (s, z - 1)), (None, (s, flip(z, 2)))])
    m_buf[z] = m_ref[...]

    def up(hop, j):
        return remote(m_buf.at[j], m_buf.at[j], up_send.at[hop], up_recv.at[hop], (s, z + 1))

    def down(hop, j):
        return remote(m_buf.at[j], m_buf.at[j], dn_send.at[hop], dn_recv.at[hop], (s, z - 1))

    def begin():
        @pl.when(z < 3)
        def _():
            up(0, z).start()

        @pl.when(z > 0)
        def _():
            down(0, z).start()

    def hop(t):
        @pl.when(z >= t)
        def _():
            up(t - 1, z - t).wait_recv()
            if t < 3:

                @pl.when(z < 3)
                def _():
                    up(t, z - t).start()

        @pl.when(z + t <= 3)
        def _():
            down(t - 1, z + t).wait_recv()
            if t < 3:

                @pl.when(z > 0)
                def _():
                    down(t, z + t).start()

    def hop_end():
        @pl.when(z < 3)
        def _():
            up(0, z).wait_send()

        @pl.when(z > 0)
        def _():
            down(0, z).wait_send()

        for t in (1, 2):

            @pl.when((z >= t) & (z < 3))
            def _():
                up(t, z - t).wait_send()

            @pl.when((z + t <= 3) & (z > 0))
            def _():
                down(t, z + t).wait_send()

    def piece(p):
        return pl.ds(p * 64, 64)

    def copy1():
        return remote(slots.at[1], r1, send1.at[0], recv1.at[0], (s, pair))

    def copy2():
        return remote(slots.at[2], r2, send23.at[0], recv23.at[0], (s, opposite))

    def copy3():
        return remote(slots.at[2], r3, send23.at[1], recv23.at[1], (s, inner))

    def copy4(p):
        return remote(slots.at[3, piece(p)], r4.at[piece(p)], send4.at[p], recv4.at[p], (s, far))

    def copy5(p):
        return remote(slots.at[3, piece(p)], r5.at[piece(p)], send5.at[p], recv5.at[p], (s, inner))

    def stage_copies(seq):
        return [
            pltpu.make_async_copy(stage.at[others[d]], down_refs[d].at[seq], stage_sem.at[d]) for d in range(4)
        ]

    def compute(slot):
        seq = ids[slot]
        rows = m_buf[seq]
        for one in load_cot(seq):
            one.wait()
        ranks[:, 0:32] = adapt_scale * dot_nt(rows, a_ref[seq])
        cot = cot_buf[...].reshape(256, -1)
        ranks[:, 32:48] = adapt_scale * dot_nt(cot, bd_ref[seq])
        ranks[:, 48:96] = jnp.zeros((256, 48), f32)
        back_acc[...] = jnp.zeros_like(back_acc)
        down_acc[...] = jnp.zeros_like(down_acc)

        def step(h, _):
            columns = pl.ds(pl.multiple_of(h * tile, tile), tile)
            low = ranks[...].astype(bf16)
            low_gate = low[:, 0:16]
            low_up = low[:, 16:32]
            low_cot = low[:, 32:48]
            bg = b_ref[seq, 0, :, columns]
            bu = b_ref[seq, 1, :, columns]
            ad = ad_ref[seq, :, columns]
            rows = m_buf[seq]
            cot = cot_buf[...].reshape(256, -1)
            gate = dot_nn(rows, wg[h]) + dot_nn(low_gate, bg)
            up_value = dot_nn(rows, wu[h]) + dot_nn(low_up, bu)
            grad_act = dot_nt(cot, wd[h]) + dot_nn(low_cot, ad)
            sig = jax.nn.sigmoid(gate)
            act = (gate * sig * up_value).astype(bf16)
            grad_up = (grad_act * gate * sig).astype(bf16)
            grad_gate = (grad_act * up_value * sig * (1.0 + gate * (1.0 - sig))).astype(bf16)
            for part in range(4):
                wide = pl.ds(part * 512, 512)
                back_acc[:, wide] += dot_nt(grad_gate, wg[h, wide, :]) + dot_nt(grad_up, wu[h, wide, :])
                down_acc[:, wide] += dot_nn(act, wd[h, :, wide])
            ranks[:, 48:64] += dot_nt(act, ad)
            ranks[:, 64:80] += dot_nt(grad_gate, bg)
            ranks[:, 80:96] += dot_nt(grad_up, bu)
            grad_b_ref[seq, 0, :, columns] = dot_tn(low_gate, grad_gate)
            grad_b_ref[seq, 1, :, columns] = dot_tn(low_up, grad_up)
            grad_ad_ref[seq, :, columns] = dot_tn(low_cot, act)
            return 0

        if slot == 0:
            for h in range(tiles):
                for one in loads[h]:
                    one.wait()
        lax.fori_loop(0, tiles, step, 0)
        back_rank = (adapt_scale * ranks[:, 64:96]).astype(bf16)
        slots[slot] = (back_acc[...] + dot_nn(back_rank, a_ref[seq])).astype(bf16)

    def rest(slot):
        seq = ids[slot]
        back_rank = (adapt_scale * ranks[:, 64:96]).astype(bf16)
        low_down = (adapt_scale * ranks[:, 48:64]).astype(bf16)
        grad_a_ref[seq] = dot_tn(back_rank, m_buf[seq])
        grad_bd_ref[seq] = dot_tn(low_down, cot_buf[...].reshape(256, -1))
        if slot > 0:
            for one in stage_copies(ids[slot - 1]):
                one.wait()
        value = down_acc[...] + dot_nn(low_down, bd_ref[seq])
        if slot == 0:
            value = value + residual_ref[...]
        stage[...] = value.astype(bf16).reshape(4, 64, -1)
        for one in stage_copies(seq):
            one.start()
        following = ids[slot + 1] if slot < 3 else z
        for one in load_cot(following):
            one.start()

    def add(slot, p, extra):
        slots[slot, piece(p), :] = (
            slots[slot, piece(p), :].astype(f32) + extra[piece(p), :].astype(f32)
        ).astype(bf16)

    begin()
    compute(0)
    rest(0)
    hop(1)
    compute(1)

    @pl.when(at_end)
    def _():
        copy1().start()

    rest(1)
    hop(2)
    compute(2)

    @pl.when(at_end)
    def _():
        copy3().start()

    @pl.when(middle)
    def _():
        copy1().start()

    rest(2)
    hop(3)
    compute(3)

    @pl.when(at_end)
    def _():
        copy5(0).start()
        copy5(1).start()

    @pl.when(middle)
    def _():
        copy3().wait_recv()
        for p in range(4):
            add(2, p, r3)
        copy2().start()

    rest(3)

    @pl.when(at_end)
    def _():
        for p in (2, 3):
            copy5(p - 2).wait_send()
            copy5(p).start()

    @pl.when(middle)
    def _():
        for p in range(4):
            copy5(p).wait_recv()
            add(3, p, r5)
            copy4(p).start()

    copy1().wait_recv()
    for p in range(4):
        add(0, p, r1)

    @pl.when(middle)
    def _():
        copy2().wait_recv()
        for p in range(4):
            add(0, p, r2)

    for one in load_cot(z):
        one.wait()
    for p in range(4):

        @pl.when(at_end)
        def _():
            copy4(p).wait_recv()
            add(0, p, r4)

        grad = slots[0, piece(p), :].astype(f32)
        normed, inverse = norm_rows(residual_ref[piece(p), :])
        value = cot_buf[p].astype(f32) + norm_back(grad, normed, inverse)
        grad_res_ref[piece(p), :] = value
        g_ref[piece(p), :] = value.astype(bf16)
    for one in stage_copies(ids[3]):
        one.wait()
    hop_end()
    copy1().wait_send()

    @pl.when(at_end)
    def _():
        copy3().wait_send()
        for p in (2, 3):
            copy5(p).wait_send()

    @pl.when(middle)
    def _():
        copy2().wait_send()
        for p in range(4):
            copy4(p).wait_send()


def mlp_line(m_own, residual, cots, w_gate_up, w_down, a_sel, b_sel, ad_sel, bd_sel):
    bf16 = jnp.bfloat16
    f32 = jnp.float32
    vmem = pl.BlockSpec(memory_space=pltpu.VMEM)
    anywhere = pl.BlockSpec(memory_space=pl.ANY)
    width = m_own.shape[1]
    hidden = w_down.shape[0]
    tile = hidden_tile
    tiles = hidden // tile
    shape = jax.ShapeDtypeStruct
    dma = pltpu.SemaphoreType.DMA
    vm = pltpu.VMEM
    return pl.pallas_call(
        mlp_line_kernel,
        in_specs=[vmem, vmem] + [anywhere] * 6 + [vmem] * 4,
        out_specs=[vmem, vmem] + [anywhere] * 4 + [vmem, vmem, vmem, vmem],
        out_shape=[
            shape((256, width), bf16),
            shape((256, width), f32),
        ]
        + [shape((4, 64, width), bf16)] * 4
        + [
            shape((4, 2, 16, hidden), f32),
            shape((4, 16, hidden), f32),
            shape((4, 32, width), f32),
            shape((4, 16, width), f32),
        ],
        scratch_shapes=[
            vm((4, 256, width), bf16),
            vm((tiles, width, tile), bf16),
            vm((tiles, width, tile), bf16),
            vm((tiles, tile, width), bf16),
            vm((4, 64, width), bf16),
            vm((256, width), f32),
            vm((256, width), f32),
            vm((256, 96), f32),
            vm((4, 256, width), bf16),
            vm((256, width), bf16),
            vm((256, width), bf16),
            vm((256, width), bf16),
            vm((256, width), bf16),
            vm((256, width), bf16),
            vm((4, 64, width), bf16),
        ]
        + [dma((3,))] * 4
        + [dma((4,))] * 6
        + [dma((2,))] * 2
        + [dma((3 * tiles,)), dma((4,)), dma((4,))],
        cost_estimate=spend(110),
        compiler_params=pltpu.CompilerParams(
            collective_id=5, has_side_effects=True, vmem_limit_bytes=60 << 20
        ),
    )(m_own, residual, *cots, w_gate_up, w_down, a_sel, b_sel, ad_sel, bd_sel)


def finish_kernel(
    dq_ref, dk_ref, dv_ref, w_ref, x_own_ref, residual_ref, u_ref, g_ref, low_ref, rank_ref, mixed_ref,
    b_sel_ref, a_sel_ref, grad_b_ref, grad_ad_ref, grad_a_ref, grad_bd_ref, down0_ref, got1_ref, got2_ref, down3_ref,
    set_ref,
    result_ref, grad_ref, pool_ref, heads_ref, got3_ref,
    own_ref, sib_q, sib_k, sib_v, out_buf, in_buf, u_buf, g_buf, a_acc, b_acc, chunk_src, chunk_sib, chunk_sum,
    chunk_in, z_src, z_in, head_src, head_in,
    a2a_send, a2a_recv, sib_send, sib_recv, send, recv, load_sem, cs_send, cs_recv, cx_send, cx_recv,
    cz_send, cz_recv, cg_send, cg_recv, hz_send, hz_recv, hg_send, hg_recv, down_send, down_recv,
):
    f32 = jnp.float32
    bf16 = jnp.bfloat16
    s, z = places()
    core = s % 2
    chip = s // 2
    other = flip(s, 1)
    sx = flip(s, 2)
    sy = flip(s, 4)
    sd = flip(sx, 4)
    zs = [flip(z, 1), flip(z, 2), 3 - z]
    meet([(None, (t, z)) for t in (other, sx, sy, sd)] + [(None, (s, j)) for j in zs])
    last_down = remote(down3_ref, got3_ref, down_send.at[0], down_recv.at[0], (s, 3 - z))
    last_down.start()
    mine = (dq_ref, dk_ref, dv_ref)
    theirs = (sib_q, sib_k, sib_v)
    swaps = [
        remote(
            mine[p].at[2 * c + 1 - core], theirs[p].at[c], sib_send.at[4 * p + c], sib_recv.at[4 * p + c], (other, z)
        )
        for c in range(4)
        for p in range(3)
    ]
    for one in swaps:
        one.start()

    def load(t):
        return [
            pltpu.make_async_copy(u_ref.at[t], u_buf.at[t % 2], load_sem.at[t % 2]),
            pltpu.make_async_copy(g_ref.at[t], g_buf.at[t % 2], load_sem.at[2 + t % 2]),
        ]

    for one in load(0):
        one.start()
    for one in swaps:
        one.wait_recv()

    def product(c, half):
        rows = pl.ds(half * 128, 128)
        both = jnp.concatenate(
            [ref[2 * c + core, rows, :] for ref in mine] + [ref[c, rows, :] for ref in theirs], axis=1
        )
        return dot_nt(both, w_ref[...])

    reduce = Reduce(product, s, z, out_buf, in_buf, send, recv)
    reduce.begin()

    b_two = [
        jnp.concatenate(
            [b_sel_ref[2 * core, 16 * p : 16 * p + 16], b_sel_ref[2 * core + 1, 16 * p : 16 * p + 16]], axis=1
        )
        for p in range(3)
    ]
    a_two = jnp.concatenate([a_sel_ref[2 * core], a_sel_ref[2 * core + 1]], axis=1)

    def adapt(t, first):
        for one in load(t):
            one.wait()
        if t < 7:
            for one in load(t + 1):
                one.start()
        back = jnp.concatenate([dot_nt(mine[p][t], b_two[p]) for p in range(3)], axis=1)
        back = (adapt_scale * back).astype(bf16)
        a_part = dot_tn(back, u_buf[t % 2])
        lows = (adapt_scale * dot_nt(mixed_ref[t], a_two)).astype(bf16)
        b_part = dot_tn(lows, g_buf[t % 2])
        if first:
            a_acc[...] = a_part
            b_acc[...] = b_part
        else:
            a_acc[...] += a_part
            b_acc[...] += b_part

    for t in range(3):
        adapt(t, t == 0)
    reduce.middle()
    for t in range(3, 8):
        adapt(t, False)
    per_head = [
        dot_tn(low_ref[...].reshape(2048, 48)[:, 16 * p : 16 * p + 16], mine[p][...].reshape(2048, 256))
        for p in range(3)
    ] + [dot_tn(rank_ref[...].reshape(2048, 16), mixed_ref[...].reshape(2048, 256))]
    for head in range(2):
        columns = slice(HDIM * head, HDIM * head + HDIM)
        head_src[head] = jnp.concatenate([part[:, columns] for part in per_head], axis=0).astype(bf16)

    keeper = (z // 2) == core

    def head_copy(head):
        return remote(head_src.at[head], head_in.at[z], hz_send.at[head], hz_recv.at[z], (s, 2 * core + head))

    for head in range(2):

        @pl.when(2 * core + head != z)
        def _():
            head_copy(head).start()

        @pl.when(2 * core + head == z)
        def _():
            head_in[z] = head_src[head]

    for member in range(4):
        whole = jnp.zeros((48, a_acc.shape[1]), f32)
        split = jnp.zeros((48, a_acc.shape[1]), f32)
        for seq in range(4):
            used = (set_ref[seq] == member).astype(f32)
            whole += used * jnp.concatenate([grad_a_ref[seq], grad_bd_ref[seq]], axis=0)
            split += used * jnp.concatenate([grad_b_ref[seq, 0], grad_b_ref[seq, 1], grad_ad_ref[seq]], axis=0)
        for part in range(2):
            i = 2 * member + part
            sequence = a_acc[8 * i : 8 * i + 8] if i < 6 else b_acc[8 * i - 48 : 8 * i - 40]
            chunk_src[i] = jnp.concatenate(
                [
                    whole[24 * part : 24 * part + 24],
                    sequence,
                    split[24 * part : 24 * part + 24],
                    jnp.zeros((8, a_acc.shape[1]), f32),
                ],
                axis=0,
            ).astype(bf16)
    crosses = [
        remote(chunk_src.at[2 * c + 1 - core], chunk_sib.at[c], cs_send.at[c], cs_recv.at[c], (other, z))
        for c in range(4)
    ]
    for one in crosses:
        one.start()
    for one in crosses:
        one.wait_recv()
    for c in range(4):
        chunk_sum[c] = (chunk_src[2 * c + core].astype(f32) + chunk_sib[c].astype(f32)).astype(bf16)
    around = [
        remote(chunk_sum.at[t // 2], chunk_in.at[d], cx_send.at[d], cx_recv.at[d], (t, z))
        for d, t in enumerate((sx, sy, sd))
    ]
    for one in around:
        one.start()

    for half in range(2):
        total = reduce.finish(half)
        x = x_own_ref[2 * half : 2 * half + 2].reshape(128, -1).astype(f32)
        normed, inverse = norm_rows(x)
        value = residual_ref[pl.ds(half * 128, 128), :] + norm_back(total, normed, inverse)
        own_ref[2 * half : 2 * half + 2] = value.astype(bf16).reshape(2, 64, -1)
    backs = [
        remote(own_ref.at[j], grad_ref.at[z], a2a_send.at[d], a2a_recv.at[d], (s, j)) for d, j in enumerate(zs)
    ]
    for one in backs:
        one.start()
    grad_ref[z] = own_ref[z]

    last_down.wait_recv()
    for part in range(4):
        result_ref[part] = (
            down0_ref[part].astype(f32)
            + got1_ref[part].astype(f32)
            + got2_ref[part].astype(f32)
            + got3_ref[part].astype(f32)
        ).astype(bf16)
    for one in around:
        one.wait_recv()
    chunk = chunk_sum[chip].astype(f32)
    for d in range(3):
        chunk += chunk_in[d].astype(f32)
    z_src[...] = chunk[0:32].astype(bf16)
    along = [remote(z_src, z_in.at[d], cz_send.at[d], cz_recv.at[d], (s, j)) for d, j in enumerate(zs)]
    for one in along:
        one.start()

    def head_spread(target, index):
        return remote(heads_ref.at[chip], heads_ref.at[chip], hg_send.at[index], hg_recv.at[index], (target, z))

    def head_pass(t, index):
        c = t // 2
        return remote(heads_ref.at[c], heads_ref.at[c], hg_send.at[index], hg_recv.at[index], (other, z))

    @pl.when(keeper)
    def _():
        for j in range(4):

            @pl.when(z != j)
            def _():
                remote(head_src.at[0], head_in.at[j], hz_send.at[0], hz_recv.at[j], (s, j)).wait_recv()

        for member in range(4):
            total = jnp.zeros((64, HDIM), f32)
            for seq in range(4):
                total += (set_ref[seq] == member).astype(f32) * head_in[seq].astype(f32)
            heads_ref[chip, pl.ds(64 * member, 64)] = total.astype(bf16)
        for index, target in enumerate((sx, sy, sd, other)):
            head_spread(target, index).start()

    for one in along:
        one.wait_recv()
    whole = chunk[0:24]
    places_z = [z] + zs
    parts = [chunk[24:32]] + [z_in[d, 24:32].astype(f32) for d in range(3)]
    for d in range(3):
        whole += z_in[d, 0:24].astype(f32)
    by_member = [
        sum((set_ref[places_z[d]] == member).astype(f32) * parts[d] for d in range(4)) for member in range(4)
    ]
    pool_ref[s] = jnp.concatenate([whole] + by_member + [chunk[32:56]], axis=0).astype(bf16)

    def pool_copy(t, index, target):
        return remote(pool_ref.at[t], pool_ref.at[t], cg_send.at[index], cg_recv.at[index], (target, z))

    gives = [pool_copy(s, index, target) for index, target in enumerate((sx, sy, sd, other))]
    for one in gives:
        one.start()

    @pl.when(keeper)
    def _():
        for index, t in enumerate((sx, sy, sd)):
            head_pass(t, index).wait_recv()
            head_pass(t, 4 + index).start()

    for index, t in enumerate((sx, sy, sd)):
        pool_copy(t, index, other).wait_recv()
        pool_copy(t, 4 + index, other).start()
    pool_copy(other, 3, other).wait_recv()
    for index, t in enumerate((sx, sy, sd)):
        pool_copy(flip(t, 1), 4 + index, other).wait_recv()

    @pl.when(z // 2 != core)
    def _():
        head_spread(other, 3).wait_recv()
        for index, t in enumerate((sx, sy, sd)):
            head_pass(t, 4 + index).wait_recv()

    for d, j in enumerate(zs):
        remote(own_ref.at[j], grad_ref.at[j], a2a_send.at[d], a2a_recv.at[d], (s, j)).wait_recv()
    for one in swaps + crosses + around + backs + along + gives + [last_down]:
        one.wait_send()
    for index, t in enumerate((sx, sy, sd)):
        pool_copy(t, 4 + index, other).wait_send()
    reduce.end()
    for head in range(2):

        @pl.when(2 * core + head != z)
        def _():
            head_copy(head).wait_send()

    @pl.when(keeper)
    def _():
        for index, target in enumerate((sx, sy, sd, other)):
            head_spread(target, index).wait_send()
        for index, t in enumerate((sx, sy, sd)):
            head_pass(t, 4 + index).wait_send()


def finish_layer(*operands):
    bf16 = jnp.bfloat16
    f32 = jnp.float32
    vmem = pl.BlockSpec(memory_space=pltpu.VMEM)
    anywhere = pl.BlockSpec(memory_space=pl.ANY)
    width = operands[4].shape[2]
    dma = pltpu.SemaphoreType.DMA
    vm = pltpu.VMEM
    shape = jax.ShapeDtypeStruct
    return pl.pallas_call(
        finish_kernel,
        in_specs=[vmem] * 6 + [anywhere] * 2 + [vmem] * 13 + [pl.BlockSpec(memory_space=pltpu.SMEM)],
        out_specs=[vmem] * 5,
        out_shape=[
            shape((4, 64, width), bf16),
            shape((4, 64, width), bf16),
            shape((8, 80, width), bf16),
            shape((4, 256, HDIM), bf16),
            shape((4, 64, width), bf16),
        ],
        scratch_shapes=[
            vm((4, 64, width), bf16),
            vm((4, 256, 256), bf16),
            vm((4, 256, 256), bf16),
            vm((4, 256, 256), bf16),
            vm((6, 128, width), bf16),
            vm((6, 128, width), bf16),
            vm((2, 256, width), bf16),
            vm((2, 256, width), bf16),
            vm((48, width), f32),
            vm((16, width), f32),
            vm((8, 64, width), bf16),
            vm((4, 64, width), bf16),
            vm((4, 64, width), bf16),
            vm((3, 64, width), bf16),
            vm((32, width), bf16),
            vm((3, 32, width), bf16),
            vm((2, 64, HDIM), bf16),
            vm((4, 64, HDIM), bf16),
        ]
        + [
            dma((count,))
            for count in (3, 3, 12, 12, 6, 6, 4, 4, 4, 3, 3, 3, 3, 7, 7, 2, 4, 7, 7, 1, 1)
        ],
        cost_estimate=spend(80),
        compiler_params=pltpu.CompilerParams(
            collective_id=4, has_side_effects=True, vmem_limit_bytes=58 << 20
        ),
    )(*operands)


def swap_mp(values, d):
    pairs = [(s * 4 + z, s * 4 + (z ^ d)) for s in range(lax.axis_size("seq")) for z in range(4)]
    return lax.ppermute(values, ("seq", "mp"), pairs)


def full_tables(positions):
    half_dim = HDIM // 2
    frequency = jnp.exp(
        jnp.arange(half_dim, dtype=jnp.float32) * (-2.0 * math.log(rope_base) / HDIM)
    )
    angles = positions.astype(jnp.float32)[:, None] * frequency
    cos = jnp.cos(angles)
    sin = jnp.sin(angles)
    return (jnp.concatenate([cos, cos], axis=1), jnp.concatenate([sin, -sin], axis=1))


def pick(values, index, axis=0):
    return lax.dynamic_index_in_dim(values, index, axis, keepdims=False)


def per_device_layers(
    layer_in, w_qkv, w_out, w_gate_up, w_down, a_in, b_qkv, b_gate_up, a_out, a_down, b_out_down,
    set_index, positions, cotangent,
):
    bf16 = jnp.bfloat16
    f32 = jnp.float32
    s = lax.axis_index("seq")
    z = lax.axis_index("mp")
    chip = s // 2
    core = s % 2
    sets = a_in.shape[0]
    width = layer_in.shape[2]
    rank = a_in.shape[2]
    length = 8 * 256

    my_set = pick(set_index, z)
    a48 = pick(a_in, my_set)[:3].reshape(3 * rank, width)
    bo_set = pick(b_out_down, my_set)
    a_sel = jnp.stack([pick(a_in, set_index[q])[3:].reshape(2 * rank, width) for q in range(4)])
    b_sel_mlp = jnp.stack([pick(b_gate_up, set_index[q]) for q in range(4)])
    ad_sel = jnp.stack([pick(a_down, set_index[q]) for q in range(4)])
    bd_sel = jnp.stack([pick(b_out_down, set_index[q])[1] for q in range(4)])
    half = width // 2
    w_half = lax.dynamic_slice(w_qkv, (0, core * half, chip * HDIM), (3, half, HDIM)).reshape(-1, HDIM)
    b_own = lax.dynamic_slice_in_dim(b_qkv, chip * HDIM, HDIM, 3).reshape(-1, HDIM)
    a_own = lax.dynamic_slice_in_dim(a_out, chip * HDIM, HDIM, 2).reshape(-1, HDIM)
    w_pack = jnp.concatenate([w_half, b_own, a_own], axis=0)
    o_pack = lax.dynamic_slice(w_out, (chip * HDIM, core * half), (HDIM, half))
    positions_z = lax.all_gather(pick(positions, z), "seq", axis=0, tiled=True)
    cos, sin = full_tables(positions_z)

    (x_own, n_own, u, w_all, o_all, q, k, v, low, b_sel, a_out_sel) = start_layer(
        layer_in, w_pack, o_pack, cos, sin, a48, my_set[None]
    )
    del n_own
    cot_late, _ = lax.optimization_barrier((cotangent, x_own))
    cots = [cot_late] + [swap_mp(cot_late, d) for d in (1, 2, 3)]

    def flat(values):
        return values.reshape(length, values.shape[-1])

    mixed, lse = attend(flat(q), flat(k), flat(v))
    residual, m_own, o_eff, w_cat = out_layer(
        mixed.reshape(8, 256, 256), o_all, a_out_sel, bo_set[0], w_all, a48, b_sel, x_own
    )
    g_own, grad_residual, down0, down1, down2, down3, grad_b_mlp, grad_ad, grad_a_mlp, grad_bd = mlp_line(
        m_own, residual, cots, w_gate_up, w_down, a_sel, b_sel_mlp, ad_sel, bd_sel
    )
    g, grad_mixed, dots, out_rank, got1, got2 = spread_layer(
        g_own, o_eff, mixed.reshape(8, 256, 256), bo_set[0], down1, down2
    )
    dq, dk, dv = attend_back(
        flat(q), flat(k), flat(v), flat(grad_mixed), lse, dots.reshape(2, 1, length), cos, sin
    )

    def spans(values):
        return values.reshape(8, 256, 256)

    result, grad_in, pool, heads, _ = finish_layer(
        spans(dq), spans(dk), spans(dv), w_cat, x_own, grad_residual, u, g, low, out_rank, spans(mixed),
        b_sel, a_out_sel, grad_b_mlp, grad_ad, grad_a_mlp, grad_bd, down0, got1, got2, down3, set_index,
    )
    pool = pool.astype(f32)
    whole = pool[:, 0:24].reshape(sets, 48, width)
    sequence = jnp.transpose(pool[:, 24:56].reshape(8, sets, 8, width), (1, 0, 2, 3)).reshape(sets, 64, width)
    split = pool[:, 56:80].reshape(sets, 48, width)
    heads = heads.astype(f32).reshape(4, sets, 64, HDIM)
    heads = jnp.transpose(heads, (1, 2, 0, 3)).reshape(sets, 4, rank, 4 * HDIM)
    return (
        result,
        grad_in,
        jnp.concatenate([sequence[:, :48], whole[:, :32]], axis=1).reshape(sets, 5, rank, width),
        heads[:, :3],
        split[:, :32].reshape(sets, 2, rank, width),
        heads[:, 3],
        split[:, 32:],
        jnp.stack([sequence[:, 48:], whole[:, 32:]], axis=1),
    )


def solution(mesh):
    by_layers = mesh.shape["seq"] == 8 and mesh.shape["mp"] == 4
    body = per_device_layers if by_layers else per_device
    placed = (
        P(None, ("seq", "mp"), None),
        P(None, None, "mp"),
        P("mp", None),
        P(None, None, "mp"),
        P("mp", None),
        P(),
        P(None, None, None, "mp"),
        P(None, None, None, "mp"),
        P(None, None, "mp"),
        P(None, None, "mp"),
        P(),
        P(),
        P(None, "seq"),
        P(None, ("seq", "mp"), None),
    )
    return jax.shard_map(
        body,
        mesh=mesh,
        in_specs=placed,
        out_specs=(
            P(None, ("seq", "mp"), None),
            P(None, ("seq", "mp"), None),
            P(),
            P(None, None, None, "mp"),
            P(None, None, None, "mp"),
            P(None, None, "mp"),
            P(None, None, "mp"),
            P(),
        ),
        check_vma=False,
    )
```

```python
import math

import jax
import jax.numpy as jnp
from jax import lax
from jax.experimental import pallas as pl
from jax.experimental.pallas import tpu as pltpu
from jax.sharding import PartitionSpec as P

HDIM = 128


adapt_scale = 0.5
norm_eps = 1e-05
rope_base = 10000.0
far_below = -1e30
highest = lax.Precision.HIGHEST


def layer_norm(values):
    centred = values - jnp.mean(values, axis=-1, keepdims=True)
    inverse = lax.rsqrt(jnp.mean(centred * centred, axis=-1, keepdims=True) + norm_eps)
    return (centred * inverse, inverse)


def norm_back(gradient, normed, inverse):
    return inverse * (
        gradient
        - jnp.mean(gradient, axis=-1, keepdims=True)
        - normed * jnp.mean(gradient * normed, axis=-1, keepdims=True)
    )


def gather_rows(values):
    return lax.all_gather(values, "mp", axis=1, tiled=True)


def scatter_rows(values):
    return lax.psum_scatter(
        values.astype(jnp.bfloat16), "mp", scatter_dimension=1, tiled=True
    ).astype(jnp.float32)


def rope_tables(positions):
    half_dim = HDIM // 2
    frequency = jnp.exp(
        jnp.arange(half_dim, dtype=jnp.float32) * (-2.0 * math.log(rope_base) / HDIM)
    )
    angles = jnp.transpose(positions).astype(jnp.float32)[:, :, None, None] * frequency
    return (jnp.cos(angles), jnp.sin(angles))


def rotate(values, cosine_table, sine_table):
    half_dim = values.shape[-1] // 2
    first_half = values[..., :half_dim]
    second_half = values[..., half_dim:]
    return jnp.concatenate(
        [
            first_half * cosine_table - second_half * sine_table,
            second_half * cosine_table + first_half * sine_table,
        ],
        axis=-1,
    )


def rotate_back(gradient, cosine_table, sine_table):
    half_dim = gradient.shape[-1] // 2
    first_half = gradient[..., :half_dim]
    second_half = gradient[..., half_dim:]
    return jnp.concatenate(
        [
            first_half * cosine_table + second_half * sine_table,
            second_half * cosine_table - first_half * sine_table,
        ],
        axis=-1,
    )


def masked_scores(queries, key_rows, query_first, key_first, score_scale):
    raw_scores = (
        jnp.einsum("qshd,kshd->shqk", queries, key_rows, preferred_element_type=jnp.float32)
        * score_scale
    )
    query_index = query_first + jnp.arange(queries.shape[0])
    key_index = key_first + jnp.arange(key_rows.shape[0])
    return (raw_scores, key_index[None, :] <= query_index[:, None])


def blockwise(fold_step, state_carry, pieces, start_row):
    row_count = pieces[0].shape[0]
    block_size = 512

    def block_turn(block_id, running):
        blocks = tuple(
            (
                lax.dynamic_slice_in_dim(shard_piece, block_id * block_size, block_size, 0)
                for shard_piece in pieces
            )
        )
        return fold_step(running, blocks, start_row + block_id * block_size)

    return lax.fori_loop(0, row_count // block_size, block_turn, state_carry)


def forward_step(queries, query_first, score_scale):
    query_last = query_first + queries.shape[0] - 1

    def fold_step(state_carry, blocks, key_first):
        key_rows, value_rows = blocks

        def compute(running):
            running_max, running_sum, weighted = running
            scores, allowed = masked_scores(queries, key_rows, query_first, key_first, score_scale)
            new_max = jnp.maximum(
                running_max, jnp.max(jnp.where(allowed, scores, far_below), axis=-1)
            )
            exponent = jnp.where(allowed, jnp.exp(scores - new_max[..., None]), 0.0)
            factor = jnp.exp(running_max - new_max)
            running_sum = running_sum * factor + jnp.sum(exponent, axis=-1)
            weighted = weighted * factor[..., None] + jnp.einsum(
                "shqk,kshd->shqd",
                exponent.astype(jnp.bfloat16),
                value_rows,
                preferred_element_type=jnp.float32,
            )
            return (new_max, running_sum, weighted)

        return lax.cond(key_first <= query_last, compute, lambda running: running, state_carry)

    return fold_step


def query_grad_step(queries, grad_heads, log_total, row_dots, query_first, score_scale):
    query_last = query_first + queries.shape[0] - 1

    def fold_step(state_carry, blocks, key_first):
        key_rows, value_rows = blocks

        def compute(running):
            scores, allowed = masked_scores(queries, key_rows, query_first, key_first, score_scale)
            attn_probs = jnp.where(allowed, jnp.exp(scores - log_total[..., None]), 0.0)
            grad_probs = jnp.einsum(
                "qshd,kshd->shqk", grad_heads, value_rows, preferred_element_type=jnp.float32
            )
            grad_scores = (attn_probs * (grad_probs - row_dots[..., None])).astype(jnp.bfloat16)
            return running + score_scale * jnp.einsum(
                "shqk,kshd->qshd", grad_scores, key_rows, preferred_element_type=jnp.float32
            )

        return lax.cond(key_first <= query_last, compute, lambda running: running, state_carry)

    return fold_step


def key_grad_step(key_rows, value_rows, key_first, score_scale):

    def fold_step(state_carry, blocks, query_first):
        queries, grad_heads, log_total_tok, row_dots_tok = blocks
        query_last = query_first + queries.shape[0] - 1

        def compute(running):
            scores, allowed = masked_scores(queries, key_rows, query_first, key_first, score_scale)
            log_total = jnp.transpose(log_total_tok, (1, 2, 0))
            row_dots = jnp.transpose(row_dots_tok, (1, 2, 0))
            attn_probs = jnp.where(allowed, jnp.exp(scores - log_total[..., None]), 0.0)
            grad_value_rows = jnp.einsum(
                "shqk,qshd->kshd",
                attn_probs.astype(jnp.bfloat16),
                grad_heads,
                preferred_element_type=jnp.float32,
            )
            grad_probs = jnp.einsum(
                "qshd,kshd->shqk", grad_heads, value_rows, preferred_element_type=jnp.float32
            )
            grad_scores = (attn_probs * (grad_probs - row_dots[..., None])).astype(jnp.bfloat16)
            grad_key_rows = score_scale * jnp.einsum(
                "shqk,qshd->kshd", grad_scores, queries, preferred_element_type=jnp.float32
            )
            return (grad_key_rows, grad_value_rows)

        return lax.cond(key_first <= query_last, compute, lambda running: running, state_carry)

    return fold_step


def project_in(token_rows, weight, a_chosen, b_chosen):
    main_term = jnp.einsum("scd,dw->csw", token_rows, weight, preferred_element_type=jnp.float32)
    low_rank = jnp.einsum("scd,srd->scr", token_rows, a_chosen, preferred_element_type=jnp.float32)
    side_term = jnp.einsum(
        "scr,srw->csw", low_rank, b_chosen.astype(jnp.float32), precision=highest
    )
    return (main_term + adapt_scale * side_term, low_rank)


def project_out(middle, weight, a_chosen, b_chosen):
    main_term = jnp.einsum("csw,wd->scd", middle, weight, preferred_element_type=jnp.float32)
    low_rank = jnp.einsum("csw,srw->scr", middle, a_chosen, preferred_element_type=jnp.float32)
    side_term = jnp.einsum(
        "scr,srd->scd", low_rank, b_chosen.astype(jnp.float32), precision=highest
    )
    return (main_term + adapt_scale * side_term, low_rank)


def back_in(gradient, weight, a_chosen, b_chosen, token_rows, low_rank):
    back_rank = jnp.einsum("csw,srw->scr", gradient, b_chosen, preferred_element_type=jnp.float32)
    grad_rows = jnp.einsum("csw,dw->scd", gradient, weight, preferred_element_type=jnp.float32)
    grad_rows = grad_rows + adapt_scale * jnp.einsum(
        "scr,srd->scd", back_rank, a_chosen.astype(jnp.float32), precision=highest
    )
    grad_a = adapt_scale * jnp.einsum("scr,scd->srd", back_rank, token_rows, precision=highest)
    grad_b = adapt_scale * jnp.einsum("scr,csw->srw", low_rank, gradient, precision=highest)
    return (grad_rows, grad_a, grad_b)


def back_out(gradient, weight, a_chosen, b_chosen, middle, low_rank):
    back_rank = jnp.einsum("scd,srd->scr", gradient, b_chosen, preferred_element_type=jnp.float32)
    grad_middle = jnp.einsum("scd,wd->csw", gradient, weight, preferred_element_type=jnp.float32)
    grad_middle = grad_middle + adapt_scale * jnp.einsum(
        "scr,srw->csw", back_rank, a_chosen.astype(jnp.float32), precision=highest
    )
    grad_a = adapt_scale * jnp.einsum("scr,csw->srw", back_rank, middle, precision=highest)
    grad_b = adapt_scale * jnp.einsum("scr,scd->srd", low_rank, gradient, precision=highest)
    return (grad_middle, grad_a, grad_b)


def pick_set(onehot, set_table):
    flattened = set_table.reshape(set_table.shape[0], -1)
    chosen = jnp.dot(onehot, flattened, preferred_element_type=jnp.float32).astype(jnp.bfloat16)
    return chosen.reshape((onehot.shape[0],) + set_table.shape[1:])


def spread_sets(onehot, per_sequence):
    flattened = per_sequence.reshape(per_sequence.shape[0], -1)
    summed = jnp.dot(onehot.astype(jnp.float32).T, flattened, precision=highest)
    return summed.reshape((onehot.shape[1],) + per_sequence.shape[1:])


def per_device(
    layer_in,
    w_qkv,
    w_out,
    w_gate_up,
    w_down,
    a_in,
    b_qkv,
    b_gate_up,
    a_out,
    a_down,
    b_out_down,
    set_index,
    positions,
    cotangent,
):
    local_len = positions.shape[1]
    seq_count = positions.shape[0]
    score_scale = 1.0 / math.sqrt(HDIM)
    my_first = lax.axis_index("seq") * local_len
    onehot = (set_index[:, None] == jnp.arange(a_in.shape[0])[None, :]).astype(jnp.bfloat16)
    chosen_a_in = pick_set(onehot, a_in)
    chosen_b_qkv = pick_set(onehot, b_qkv)
    chosen_b_gate_up = pick_set(onehot, b_gate_up)
    chosen_a_out = pick_set(onehot, a_out)
    chosen_a_down = pick_set(onehot, a_down)
    chosen_b_out_down = pick_set(onehot, b_out_down)

    def to_heads(values):
        return values.reshape(local_len, seq_count, -1, HDIM)

    residual_in = layer_in.astype(jnp.float32)
    normed_attn, inverse_attn = layer_norm(residual_in)
    rows_attn = gather_rows(normed_attn.astype(jnp.bfloat16))
    projected = [
        project_in(rows_attn, w_qkv[member], chosen_a_in[:, member], chosen_b_qkv[:, member])
        for member in range(3)
    ]
    cosine_table, sine_table = rope_tables(positions)
    queries = rotate(to_heads(projected[0][0]), cosine_table, sine_table).astype(jnp.bfloat16)
    key_rows = rotate(to_heads(projected[1][0]), cosine_table, sine_table).astype(jnp.bfloat16)
    value_rows = to_heads(projected[2][0]).astype(jnp.bfloat16)
    stat_shape = (seq_count, queries.shape[2], local_len)
    initial = (
        jnp.full(stat_shape, far_below, jnp.float32),
        jnp.zeros(stat_shape, jnp.float32),
        jnp.zeros(stat_shape + (HDIM,), jnp.float32),
    )
    attend = forward_step(queries, my_first, score_scale)
    running_max, running_sum, weighted = blockwise(
        attend,
        initial,
        (
            lax.all_gather(key_rows, "seq", axis=0, tiled=True),
            lax.all_gather(value_rows, "seq", axis=0, tiled=True),
        ),
        jnp.int32(0),
    )
    log_total = running_max + jnp.log(running_sum)
    attn_output = jnp.transpose(weighted / running_sum[..., None], (2, 0, 1, 3))
    mixed = attn_output.reshape(local_len, seq_count, -1).astype(jnp.bfloat16)
    attn_term, rank_out = project_out(mixed, w_out, chosen_a_out, chosen_b_out_down[:, 0])
    residual = residual_in + scatter_rows(attn_term)
    normed_mlp, inverse_mlp = layer_norm(residual)
    rows_mlp = gather_rows(normed_mlp.astype(jnp.bfloat16))
    gate_proj, rank_gate = project_in(
        rows_mlp, w_gate_up[0], chosen_a_in[:, 3], chosen_b_gate_up[:, 0]
    )
    up_proj, rank_up = project_in(rows_mlp, w_gate_up[1], chosen_a_in[:, 4], chosen_b_gate_up[:, 1])
    sigmoid_gate = jax.nn.sigmoid(gate_proj)
    activation = (gate_proj * sigmoid_gate * up_proj).astype(jnp.bfloat16)
    down_term, rank_down = project_out(activation, w_down, chosen_a_down, chosen_b_out_down[:, 1])
    result = (residual + scatter_rows(down_term)).astype(jnp.bfloat16)
    grad_down = gather_rows(cotangent)
    grad_activation, grad_a_down, grad_b_down = back_out(
        grad_down, w_down, chosen_a_down, chosen_b_out_down[:, 1], activation, rank_down
    )
    grad_up = (grad_activation * gate_proj * sigmoid_gate).astype(jnp.bfloat16)
    grad_gate = (
        grad_activation * up_proj * sigmoid_gate * (1.0 + gate_proj * (1.0 - sigmoid_gate))
    ).astype(jnp.bfloat16)
    rows_from_gate, grad_a_gate, grad_b_gate = back_in(
        grad_gate, w_gate_up[0], chosen_a_in[:, 3], chosen_b_gate_up[:, 0], rows_mlp, rank_gate
    )
    rows_from_up, grad_a_up, grad_b_up = back_in(
        grad_up, w_gate_up[1], chosen_a_in[:, 4], chosen_b_gate_up[:, 1], rows_mlp, rank_up
    )
    grad_residual = cotangent.astype(jnp.float32) + norm_back(
        scatter_rows(rows_from_gate + rows_from_up), normed_mlp, inverse_mlp
    )
    grad_attn_rows = gather_rows(grad_residual.astype(jnp.bfloat16))
    grad_mixed, grad_a_out, grad_b_out = back_out(
        grad_attn_rows, w_out, chosen_a_out, chosen_b_out_down[:, 0], mixed, rank_out
    )
    grad_heads = to_heads(grad_mixed.astype(jnp.bfloat16))
    row_dots_tok = jnp.sum(grad_heads.astype(jnp.float32) * attn_output, axis=-1)
    row_dots = jnp.transpose(row_dots_tok, (1, 2, 0))
    log_total_tok = jnp.transpose(log_total, (2, 0, 1))
    query_step = query_grad_step(queries, grad_heads, log_total, row_dots, my_first, score_scale)
    zero_heads = jnp.zeros(queries.shape, jnp.float32)
    every_key, every_value = (
        lax.all_gather(key_rows, "seq", axis=0, tiled=True),
        lax.all_gather(value_rows, "seq", axis=0, tiled=True),
    )
    grad_queries = blockwise(query_step, zero_heads, (every_key, every_value), 0)
    block_size = 512

    def one_block(block_id):
        first_key = block_id * block_size
        block_keys = lax.dynamic_slice_in_dim(every_key, first_key, block_size, 0)
        block_values = lax.dynamic_slice_in_dim(every_value, first_key, block_size, 0)
        zero_block = jnp.zeros(block_keys.shape, jnp.float32)
        block_step = key_grad_step(block_keys, block_values, first_key, score_scale)
        grad_key_block, grad_value_block = block_step(
            (zero_block, zero_block), (queries, grad_heads, log_total_tok, row_dots_tok), my_first
        )
        return jnp.concatenate([grad_key_block, grad_value_block], axis=-1)

    stacked = lax.map(one_block, jnp.arange(local_len * lax.axis_size("seq") // block_size))
    stacked_terms = lax.psum_scatter(
        stacked.reshape((local_len * lax.axis_size("seq"),) + stacked.shape[2:]).astype(
            jnp.bfloat16
        ),
        "seq",
        scatter_dimension=0,
        tiled=True,
    ).astype(jnp.float32)
    grad_keys = stacked_terms[..., :HDIM]
    grad_values = stacked_terms[..., HDIM:]
    grad_query_raw = (
        rotate_back(grad_queries, cosine_table, sine_table)
        .astype(jnp.bfloat16)
        .reshape(local_len, seq_count, -1)
    )
    grad_key_raw = (
        rotate_back(grad_keys, cosine_table, sine_table)
        .astype(jnp.bfloat16)
        .reshape(local_len, seq_count, -1)
    )
    grad_value_raw = grad_values.astype(jnp.bfloat16).reshape(local_len, seq_count, -1)
    back_parts = [
        back_in(
            gradient,
            w_qkv[member],
            chosen_a_in[:, member],
            chosen_b_qkv[:, member],
            rows_attn,
            projected[member][1],
        )
        for member, gradient in enumerate((grad_query_raw, grad_key_raw, grad_value_raw))
    ]
    grad_rows_attn = back_parts[0][0] + back_parts[1][0] + back_parts[2][0]
    grad_in = (
        grad_residual + norm_back(scatter_rows(grad_rows_attn), normed_attn, inverse_attn)
    ).astype(jnp.bfloat16)
    per_seq_a_in = jnp.stack(
        [back_parts[0][1], back_parts[1][1], back_parts[2][1], grad_a_gate, grad_a_up], axis=1
    )
    per_seq_b_qkv = jnp.stack([bundle[2] for bundle in back_parts], axis=1)
    per_seq_b_gate_up = jnp.stack([grad_b_gate, grad_b_up], axis=1)
    per_seq_b_out_down = jnp.stack([grad_b_out, grad_b_down], axis=1)
    sums_seq = (
        lax.psum(spread_sets(onehot, per_seq_b_qkv).astype(jnp.bfloat16), "seq").astype(
            jnp.float32
        ),
        lax.psum(spread_sets(onehot, per_seq_b_gate_up).astype(jnp.bfloat16), "seq").astype(
            jnp.float32
        ),
        lax.psum(spread_sets(onehot, grad_a_out).astype(jnp.bfloat16), "seq").astype(jnp.float32),
        lax.psum(spread_sets(onehot, grad_a_down).astype(jnp.bfloat16), "seq").astype(jnp.float32),
    )
    sums_all = lax.psum(
        (spread_sets(onehot, per_seq_a_in), spread_sets(onehot, per_seq_b_out_down)), ("seq", "mp")
    )
    return (
        result,
        grad_in,
        sums_all[0],
        sums_seq[0],
        sums_seq[1],
        sums_seq[2],
        sums_seq[3],
        sums_all[1],
    )


log2e = 1.4426950408889634
attn_tile = 512
hidden_tile = 512


def dot_nt(a, b):
    return lax.dot_general(a, b, (((1,), (1,)), ((), ())), preferred_element_type=jnp.float32)


def dot_tn(a, b):
    return lax.dot_general(a, b, (((0,), (0,)), ((), ())), preferred_element_type=jnp.float32)


def dot_nn(a, b):
    return jnp.dot(a, b, preferred_element_type=jnp.float32)


def causal(block_t, first_row, first_col):
    rows = first_row + lax.broadcasted_iota(jnp.int32, block_t.shape, 0)
    cols = first_col + lax.broadcasted_iota(jnp.int32, block_t.shape, 1)
    return rows <= cols


def turn_back(gradient, packed):
    left = lax.broadcasted_iota(jnp.int32, packed.shape, 1) < HDIM // 2
    turned = pltpu.roll(packed, HDIM // 2, 1)
    cos = jnp.where(left, packed, turned)
    sin = jnp.where(left, turned, -packed)
    return gradient * cos + pltpu.roll(gradient, HDIM // 2, 1) * sin


def attend_back_kernel(
    q_ref, k_ref, v_ref, go_ref, lse_ref, dots_ref, table_ref, dq_ref, dk_ref, dv_ref, acc_ref
):
    j = pl.program_id(1)
    tile = k_ref.shape[0]
    length = q_ref.shape[0]
    scale = 1.0 / math.sqrt(HDIM)
    factor = log2e * scale
    k = k_ref[...]
    v = v_ref[...]

    @pl.when(j == 0)
    def _():
        acc_ref[...] = jnp.zeros_like(acc_ref)

    def fold(i, carry, diagonal):
        dk, dv = carry
        at = pl.ds(pl.multiple_of(i * tile, tile), tile)
        q = q_ref[at, :]
        go = go_ref[at, :]
        scores = dot_nt(k, q)
        weight = jnp.exp2(scores * factor - lse_ref[0, :, at])
        if diagonal:
            weight = jnp.where(causal(scores, 0, 0), weight, 0.0)
        grad_weight = dot_nt(v, go)
        grad_scores = (weight * (grad_weight - dots_ref[0, :, at])).astype(jnp.bfloat16)
        dv = dv + dot_nn(weight.astype(jnp.bfloat16), go)
        dk = dk + dot_nn(grad_scores, q)
        acc_ref[at, :] += dot_tn(grad_scores, k)
        return (dk, dv)

    zero = jnp.zeros((tile, HDIM), jnp.float32)
    carry = fold(j, (zero, zero), True)
    dk, dv = lax.fori_loop(j + 1, length // tile, lambda i, c: fold(i, c, False), carry)
    at = pl.ds(pl.multiple_of(j * tile, tile), tile)
    dk_ref[...] = turn_back(dk * scale, table_ref[at, :]).astype(dk_ref.dtype)
    dv_ref[...] = dv.astype(dv_ref.dtype)
    dq_ref[...] = turn_back(acc_ref[at, :] * scale, table_ref[at, :]).astype(dq_ref.dtype)


def attend_back(q, k, v, go, lse, dots, table):
    length = q.shape[0]
    heads = q.shape[1] // HDIM
    tile = attn_tile
    whole = pl.BlockSpec((length, HDIM), lambda h, j: (0, h))
    part = pl.BlockSpec((tile, HDIM), lambda h, j: (j, h))
    row = pl.BlockSpec((1, 1, length), lambda h, j: (h, 0, 0))
    rope = pl.BlockSpec((length, HDIM), lambda h, j: (0, 0))
    return pl.pallas_call(
        attend_back_kernel,
        grid=(heads, length // tile),
        in_specs=[whole, part, part, whole, row, row, rope],
        out_specs=[part, part, part],
        out_shape=[jax.ShapeDtypeStruct(q.shape, jnp.bfloat16)] * 3,
        scratch_shapes=[pltpu.VMEM((length, HDIM), jnp.float32)],
        cost_estimate=pl.CostEstimate(
            flops=5 * heads * length * length * HDIM,
            bytes_accessed=14 * length * heads * HDIM,
            transcendentals=heads * length * length // 2,
        ),
        compiler_params=pltpu.CompilerParams(vmem_limit_bytes=32 << 20),
    )(q, k, v, go, lse, dots, table)


mesh_ids = pl.DeviceIdType.MESH


def remote(src, dst, send, recv, target):
    return pltpu.make_async_remote_copy(
        src_ref=src, dst_ref=dst, send_sem=send, recv_sem=recv, device_id=target, device_id_type=mesh_ids
    )


def meet(partners):
    barrier = pltpu.get_barrier_semaphore()
    for condition, device in partners:
        if condition is None:
            pl.semaphore_signal(barrier, inc=1, device_id=device, device_id_type=mesh_ids)
        else:

            @pl.when(condition)
            def _():
                pl.semaphore_signal(barrier, inc=1, device_id=device, device_id_type=mesh_ids)

    count = 0
    for condition, device in partners:
        count = count + (1 if condition is None else condition.astype(jnp.int32))
    pl.semaphore_wait(barrier, count)


def flip(index, bit):
    return index + bit - 2 * bit * ((index // bit) % 2)


def places():
    s = lax.axis_index("seq")
    z = lax.axis_index("mp")
    return s, z


class Gather:
    def __init__(self, blocks, s, z, send, recv, half):
        self.at = blocks
        self.s = s
        self.z = z
        self.send = send
        self.recv = recv
        self.half = half

    def rows(self, part):
        return pl.ds(part * self.half, self.half)

    def copy(self, index, span, part, target):
        ref = self.at.at[span] if part is None else self.at.at[span, self.rows(part)]
        return remote(ref, ref, self.send.at[index], self.recv.at[index], (target, self.z))

    def begin(self):
        s, x, y, other = self.s, flip(self.s, 2), flip(self.s, 4), flip(self.s, 1)
        self.copies = [
            self.copy(0, s, 0, x),
            self.copy(1, s, 1, y),
            self.copy(2, s, 1, x),
            self.copy(3, s, 0, y),
            self.copy(6, s, None, other),
        ]
        for one in self.copies:
            one.start()

    def arrive_first(self):
        s, x, y = self.s, flip(self.s, 2), flip(self.s, 4)
        self.copy(0, x, 0, x).wait_recv()
        one = self.copy(4, x, 0, y)
        one.start()
        self.copy(1, y, 1, y).wait_recv()
        two = self.copy(5, y, 1, x)
        two.start()
        self.copies += [one, two]

    def arrive_neighbours(self):
        s, x, y, other = self.s, flip(self.s, 2), flip(self.s, 4), flip(self.s, 1)
        self.copy(2, x, 1, x).wait_recv()
        one = self.copy(7, x, None, other)
        one.start()
        self.copy(3, y, 0, y).wait_recv()
        two = self.copy(8, y, None, other)
        two.start()
        self.copies += [one, two]

    def arrive_diagonal(self):
        s, other = self.s, flip(self.s, 1)
        diagonal = flip(flip(s, 2), 4)
        self.copy(4, diagonal, 0, other).wait_recv()
        self.copy(5, diagonal, 1, other).wait_recv()
        one = self.copy(9, diagonal, None, other)
        one.start()
        self.copies += [one]

    def arrive_core(self, index):
        s = self.s
        other = flip(s, 1)
        span = (other, flip(other, 2), flip(other, 4), flip(flip(other, 2), 4))[index]
        self.copy(6 + index, span, None, other).wait_recv()
        return span

    def end(self):
        for one in self.copies:
            one.wait_send()


gather_sems = 10


def spend(microseconds):
    return pl.CostEstimate(flops=microseconds * 10**9, bytes_accessed=10**6, transcendentals=0)


class Line:
    def __init__(self, blocks, core, s, z, send, recv):
        self.at = blocks
        self.core = core
        self.s = s
        self.z = z
        self.send = send
        self.recv = recv

    def ref(self, j):
        return self.at.at[j] if self.core is None else self.at.at[j, self.core]

    def up(self, hop, j):
        ref = self.ref(j)
        return remote(ref, ref, self.send.at[hop], self.recv.at[hop], (self.s, self.z + 1))

    def down(self, hop, j):
        ref = self.ref(j)
        return remote(ref, ref, self.send.at[3 + hop], self.recv.at[3 + hop], (self.s, self.z - 1))

    def across(self, index, j):
        ref = self.ref(j)
        return remote(ref, ref, self.send.at[6 + index], self.recv.at[6 + index], (flip(self.s, 1), self.z))

    def begin(self):
        z = self.z

        @pl.when(z < 3)
        def _():
            self.up(0, z).start()

        @pl.when(z > 0)
        def _():
            self.down(0, z).start()

        if self.core is not None:
            self.across(0, z).start()

    def hop(self, t):
        z = self.z

        @pl.when(z >= t)
        def _():
            self.up(t - 1, z - t).wait_recv()
            if self.core is not None:
                self.across(t, z - t).start()
            if t < 3:

                @pl.when(z < 3)
                def _():
                    self.up(t, z - t).start()

        @pl.when(z + t <= 3)
        def _():
            self.down(t - 1, z + t).wait_recv()
            if self.core is not None:
                self.across(3 + t, z + t).start()
            if t < 3:

                @pl.when(z > 0)
                def _():
                    self.down(t, z + t).start()

    def arrive_core(self):
        z = self.z
        other = 1 - self.core

        def wait(index, j):
            ref = self.at.at[j, other]
            remote(ref, ref, self.send.at[6 + index], self.recv.at[6 + index], (flip(self.s, 1), z)).wait_recv()

        wait(0, z)
        for t in (1, 2, 3):

            @pl.when(z >= t)
            def _():
                wait(t, z - t)

            @pl.when(z + t <= 3)
            def _():
                wait(3 + t, z + t)

    def end(self):
        z = self.z

        @pl.when(z < 3)
        def _():
            self.up(0, z).wait_send()

        @pl.when(z > 0)
        def _():
            self.down(0, z).wait_send()

        if self.core is not None:
            self.across(0, z).wait_send()
        for t in (1, 2, 3):

            @pl.when(z >= t)
            def _():
                if self.core is not None:
                    self.across(t, z - t).wait_send()
                if t < 3:

                    @pl.when(z < 3)
                    def _():
                        self.up(t, z - t).wait_send()

            @pl.when(z + t <= 3)
            def _():
                if self.core is not None:
                    self.across(3 + t, z + t).wait_send()
                if t < 3:

                    @pl.when(z > 0)
                    def _():
                        self.down(t, z + t).wait_send()


line_sems = 13


def norm_rows(values):
    centred = values - jnp.mean(values, axis=-1, keepdims=True)
    inverse = lax.rsqrt(jnp.mean(centred * centred, axis=-1, keepdims=True) + norm_eps)
    return (centred * inverse, inverse)


class Reduce:
    def __init__(self, product, s, z, out, inn, send, recv):
        self.product = product
        self.s = s
        self.z = z
        self.out = out
        self.inn = inn
        self.send = send
        self.recv = recv
        chip = s // 2
        self.chip = chip
        self.cx = flip(chip, 1)
        self.cy = flip(chip, 2)
        self.cd = flip(self.cx, 2)

    def copy(self, index):
        target = flip(self.s, 2) if index in (0, 2, 5) else flip(self.s, 4)
        return remote(
            self.out.at[index], self.inn.at[index], self.send.at[index], self.recv.at[index], (target, self.z)
        )

    def give(self, index, chip, half, extra=None):
        value = self.product(chip, half)
        if extra is not None:
            self.copy(extra).wait_recv()
            value = value + self.inn[extra].astype(jnp.float32)
        self.out[index] = value.astype(jnp.bfloat16)
        self.copy(index).start()

    def begin(self):
        self.give(0, self.cd, 0)
        self.give(1, self.cd, 1)
        self.give(2, self.cx, 0)
        self.give(3, self.cy, 1)

    def middle(self):
        self.give(4, self.cy, 0, 0)
        self.give(5, self.cx, 1, 1)

    def finish(self, half):
        indices = (2, 4) if half == 0 else (3, 5)
        total = self.product(self.chip, half)
        for index in indices:
            self.copy(index).wait_recv()
            total = total + self.inn[index].astype(jnp.float32)
        return total

    def end(self):
        for index in range(6):
            self.copy(index).wait_send()


def front_kernel(
    x_ref, w_qkv_ref, w_out_ref, b_qkv_ref, a_out_ref, a_in_ref, b_od_ref, table_ref, cot_ref, set_ref,
    x_own_ref, m_own_ref, residual_ref, o_eff_ref, b_sel_ref, a_sel_ref, lse_ref,
    u_out, q_out, k_out, v_out, low_out, table_out, mixed_out, w_cat_out, cots_ref,
    u_ref, w_buf, w_cat, q_buf, k_buf, v_buf, low_buf, tables, mixed, o_all, o_big, sib, out_buf, in_buf,
    b_small, a_small,
    a2a_send, a2a_recv, tab_send, tab_recv, ag_send, ag_recv, w_send, w_recv, o_send, o_recv, cot_send, cot_recv,
    small_send, small_recv, sib_send, sib_recv, red_send, red_recv, local_sem, store_sem,
):
    f32 = jnp.float32
    bf16 = jnp.bfloat16
    s, z = places()
    core = s % 2
    chip = s // 2
    other = flip(s, 1)
    zs = [flip(z, 1), flip(z, 2), 3 - z]
    columns = pl.ds(pl.multiple_of(chip * HDIM, HDIM), HDIM)
    half_rows = pl.ds(pl.multiple_of(core * 1024, 1024), 1024)
    owns = [
        pltpu.make_async_copy(w_qkv_ref.at[:, half_rows, columns], w_buf.at[z, core], local_sem.at[0]),
        pltpu.make_async_copy(w_out_ref.at[columns, half_rows], o_all.at[z, core], local_sem.at[1]),
        pltpu.make_async_copy(b_qkv_ref.at[:, :, :, columns], b_small.at[z], local_sem.at[2]),
        pltpu.make_async_copy(a_out_ref.at[:, :, columns], a_small.at[z], local_sem.at[3]),
        pltpu.make_async_copy(cot_ref, cots_ref.at[z], local_sem.at[4]),
    ]
    for one in owns:
        one.start()
    tables[s] = table_ref[...]
    meet([(None, (other, z)), (None, (flip(s, 2), z)), (None, (flip(s, 4), z))] + [(None, (s, j)) for j in zs])

    swaps = [
        remote(x_ref.at[j], x_own_ref.at[z], a2a_send.at[d], a2a_recv.at[d], (s, j)) for d, j in enumerate(zs)
    ]
    for one in swaps:
        one.start()
    table_gather = Gather(tables, s, z, tab_send, tab_recv, 128)
    table_gather.begin()
    x_own_ref[z] = x_ref[z]
    table_gather.arrive_first()
    table_gather.arrive_neighbours()
    table_gather.arrive_diagonal()
    for one in owns:
        one.wait()
    for d, j in enumerate(zs):
        remote(x_ref.at[j], x_own_ref.at[j], a2a_send.at[d], a2a_recv.at[d], (s, j)).wait_recv()
    line = Line(w_buf, core, s, z, w_send, w_recv)
    line.begin()
    smalls = []
    for d, j in enumerate(zs):
        smalls.append(remote(b_small.at[z], b_small.at[z], small_send.at[d], small_recv.at[d], (s, j)))
        smalls.append(remote(a_small.at[z], a_small.at[z], small_send.at[3 + d], small_recv.at[3 + d], (s, j)))
    for one in smalls:
        one.start()
    for part in range(4):
        normed, _ = norm_rows(x_own_ref[part].astype(f32))
        u_ref[s, pl.ds(part * 64, 64), :] = normed.astype(bf16)
    gather = Gather(u_ref, s, z, ag_send, ag_recv, 128)
    gather.begin()
    gather.arrive_first()
    line.hop(1)
    gather.arrive_neighbours()
    line.hop(2)
    gather.arrive_diagonal()
    for index in range(4):
        gather.arrive_core(index)
        table_gather.arrive_core(index)
    stores = [pltpu.make_async_copy(u_ref, u_out, store_sem.at[0])]
    stores[0].start()
    mine = set_ref[z]
    a48 = a_in_ref[mine, 0:3].reshape(48, -1)

    def lows(t, _):
        low_buf[t] = (adapt_scale * dot_nt(u_ref[t], a48)).astype(bf16)
        return 0

    lax.fori_loop(0, 8, lows, 0)
    for d, j in enumerate(zs):
        remote(b_small.at[j], b_small.at[j], small_send.at[d], small_recv.at[d], (s, j)).wait_recv()
        remote(a_small.at[j], a_small.at[j], small_send.at[3 + d], small_recv.at[3 + d], (s, j)).wait_recv()
    for j in range(4):
        b_sel_ref[j] = b_small[j, mine].reshape(48, HDIM)
        a_sel_ref[j] = a_small[j, mine]

    def merge(index, _):
        j = index // 3
        part = index % 3
        head = (2 * core + j) % 4
        b_part = b_sel_ref[head, pl.ds(pl.multiple_of(part * 16, 16), 16), :]
        column = pl.multiple_of(((j // 2) * 6 + part * 2 + j % 2) * HDIM, HDIM)
        for side in range(2):
            a_part = a_in_ref[mine, part, :, pl.ds(side * 1024, 1024)]
            merged = adapt_scale * dot_tn(a_part, b_part)
            w_cat[pl.ds(side * 1024, 1024), pl.ds(column, HDIM)] = (
                w_buf[head, side, part].astype(f32) + merged
            ).astype(bf16)
        return 0

    line.hop(3)
    o_line = Line(o_all, core, s, z, o_send, o_recv)
    o_line.begin()
    cot_line = Line(cots_ref, None, s, z, cot_send, cot_recv)
    cot_line.begin()
    line.arrive_core()
    lax.fori_loop(0, 6, merge, 0)
    left = lax.broadcasted_iota(jnp.int32, (256, HDIM), 1) < HDIM // 2

    def project(t, _):
        u = u_ref[t]
        packed = tables[t]
        turned = pltpu.roll(packed, HDIM // 2, 1)
        cos = jnp.where(left, packed, turned)
        sin = jnp.where(left, turned, -packed)
        rows = pl.ds(pl.multiple_of(t * 256, 256), 256)
        for part, out in enumerate((q_buf, k_buf, v_buf)):
            raw = dot_nn(u, w_cat[:, 256 * part : 256 * part + 256])
            for head in range(2):
                piece = raw[:, HDIM * head : HDIM * head + HDIM]
                if part < 2:
                    piece = piece * cos - pltpu.roll(piece, HDIM // 2, 1) * sin
                out[rows, HDIM * head : HDIM * head + HDIM] = piece.astype(bf16)
        return 0

    lax.fori_loop(0, 3, project, 0)
    o_line.hop(1)
    lax.fori_loop(3, 6, project, 0)
    o_line.hop(2)
    lax.fori_loop(6, 8, project, 0)
    stores += [
        pltpu.make_async_copy(source, target, store_sem.at[1 + i])
        for i, (source, target) in enumerate(
            ((q_buf, q_out), (k_buf, k_out), (v_buf, v_out), (low_buf, low_out), (tables, table_out))
        )
    ]
    for one in stores[1:]:
        one.start()

    tile = attn_tile
    factor = log2e / math.sqrt(HDIM)

    def attend(index, _):
        head = index // 4
        i = index % 4
        lanes = pl.ds(pl.multiple_of(head * HDIM, HDIM), HDIM)
        here = pl.ds(pl.multiple_of(i * tile, tile), tile)
        q = q_buf[here, lanes]

        def fold(j, carry, diagonal):
            top, total, acc = carry
            at = pl.ds(pl.multiple_of(j * tile, tile), tile)
            scores = dot_nt(k_buf[at, lanes], q)
            if diagonal:
                scores = jnp.where(causal(scores, 0, 0), scores, far_below)
            new_top = jnp.maximum(top, jnp.max(scores, axis=0, keepdims=True))
            weight = jnp.exp2(scores * factor - new_top * factor)
            keep = jnp.exp2((top - new_top) * factor)
            total = total * keep + jnp.sum(weight, axis=0, keepdims=True)
            acc = acc * keep + dot_tn(v_buf[at, lanes], weight.astype(bf16))
            return (new_top, total, acc)

        carry = (
            jnp.full((1, tile), far_below, f32),
            jnp.zeros((1, tile), f32),
            jnp.zeros((HDIM, tile), f32),
        )
        carry = lax.fori_loop(0, i, lambda j, c: fold(j, c, False), carry)
        top, total, acc = fold(i, carry, True)
        mixed[here, lanes] = jnp.transpose(acc / total).astype(bf16)
        lse_ref[head, i] = top * factor + jnp.log2(total)
        return 0

    lax.fori_loop(0, 3, attend, 0)
    o_line.hop(3)
    lax.fori_loop(3, 8, attend, 0)

    def span_rows(span, first, count):
        return pl.ds(pl.multiple_of(span * 256 + first, 128), count)

    crosses = [
        remote(mixed.at[span_rows(2 * c + 1 - core, 0, 256)], sib.at[c], sib_send.at[c], sib_recv.at[c], (other, z))
        for c in range(4)
    ]
    for one in crosses:
        one.start()
    stores.append(pltpu.make_async_copy(mixed, mixed_out, store_sem.at[6]))
    stores[-1].start()
    o_line.arrive_core()
    b_row = b_od_ref[mine, 0]
    for j in range(4):
        head = (2 * core + j) % 4
        merged = adapt_scale * dot_tn(a_sel_ref[head], b_row)
        for side in range(2):
            o_big[pl.ds(j * HDIM, HDIM), pl.ds(side * 1024, 1024)] = (
                o_all[head, side].astype(f32) + merged[:, side * 1024 : side * 1024 + 1024]
            ).astype(bf16)
    o_eff_ref[...] = o_big[0 : 2 * HDIM, :]
    for one in crosses:
        one.wait_recv()

    def product(c, half):
        both = jnp.concatenate(
            [mixed[span_rows(2 * c + core, half * 128, 128), :], sib[c, pl.ds(half * 128, 128), :]], axis=1
        )
        return dot_nn(both, o_big[...])

    reduce = Reduce(product, s, z, out_buf, in_buf, red_send, red_recv)
    reduce.begin()
    cot_line.hop(1)
    lax.fori_loop(6, 8, merge, 0)
    reduce.middle()
    lax.fori_loop(8, 12, merge, 0)
    stores.append(pltpu.make_async_copy(w_cat, w_cat_out, store_sem.at[7]))
    stores[-1].start()
    cot_line.hop(2)
    for half in range(2):
        total = reduce.finish(half)
        x = x_own_ref[2 * half : 2 * half + 2].reshape(128, -1).astype(f32)
        residual = x + total
        residual_ref[pl.ds(half * 128, 128), :] = residual
        normed, _ = norm_rows(residual)
        m_own_ref[pl.ds(half * 128, 128), :] = normed.astype(bf16)
    cot_line.hop(3)
    for one in stores:
        one.wait()
    for one in swaps + smalls + crosses:
        one.wait_send()
    line.end()
    o_line.end()
    cot_line.end()
    gather.end()
    table_gather.end()
    reduce.end()


def front_layer(x, w_qkv, w_out, b_qkv, a_out, a_in, b_out_down, table, cotangent, set_index):
    bf16 = jnp.bfloat16
    f32 = jnp.float32
    vmem = pl.BlockSpec(memory_space=pltpu.VMEM)
    anywhere = pl.BlockSpec(memory_space=pl.ANY)
    width = x.shape[2]
    shape = jax.ShapeDtypeStruct
    dma = pltpu.SemaphoreType.DMA
    vm = pltpu.VMEM
    return pl.pallas_call(
        front_kernel,
        in_specs=[vmem] + [anywhere] * 4 + [vmem] * 3 + [anywhere, pl.BlockSpec(memory_space=pltpu.SMEM)],
        out_specs=[vmem] * 7 + [anywhere] * 9,
        out_shape=[
            shape((4, 64, width), bf16),
            shape((256, width), bf16),
            shape((256, width), f32),
            shape((256, width), bf16),
            shape((4, 48, HDIM), bf16),
            shape((4, 16, HDIM), bf16),
            shape((2, 4, 1, attn_tile), f32),
            shape((8, 256, width), bf16),
            shape((2048, 256), bf16),
            shape((2048, 256), bf16),
            shape((2048, 256), bf16),
            shape((8, 256, 48), bf16),
            shape((8, 256, HDIM), f32),
            shape((2048, 256), bf16),
            shape((width, 1536), bf16),
            shape((4, 4, 64, width), bf16),
        ],
        scratch_shapes=[
            vm((8, 256, width), bf16),
            vm((4, 2, 3, 1024, HDIM), bf16),
            vm((width, 1536), bf16),
            vm((2048, 256), bf16),
            vm((2048, 256), bf16),
            vm((2048, 256), bf16),
            vm((8, 256, 48), bf16),
            vm((8, 256, HDIM), f32),
            vm((2048, 256), bf16),
            vm((4, 2, HDIM, 1024), bf16),
            vm((4 * HDIM, width), bf16),
            vm((4, 256, 256), bf16),
            vm((6, 128, width), bf16),
            vm((6, 128, width), bf16),
            vm((4, 4, 3, 16, HDIM), bf16),
            vm((4, 4, 16, HDIM), bf16),
        ]
        + [
            dma((count,))
            for count in (3, 3, 10, 10, 10, 10, 13, 13, 13, 13, 13, 13, 6, 6, 4, 4, 6, 6, 5, 8)
        ],
        cost_estimate=spend(150),
        compiler_params=pltpu.CompilerParams(
            collective_id=1, has_side_effects=True, vmem_limit_bytes=58 << 20
        ),
    )(x, w_qkv, w_out, b_qkv, a_out, a_in, b_out_down, table, cotangent, set_index)


def spread_kernel(
    g_ref, o_eff_ref, mixed_ref, b_od_ref, down1_ref, down2_ref, set_ref,
    g_out, gm_ref, dots_ref, rank_ref, got1_ref, got2_ref, g_buf, send, recv, local_sem, down_send, down_recv,
):
    s, z = places()
    meet(
        [(None, (flip(s, 1), z)), (None, (flip(s, 2), z)), (None, (flip(s, 4), z))]
        + [(None, (s, flip(z, 1))), (None, (s, flip(z, 2)))]
    )
    results = [
        remote(down1_ref, got1_ref, down_send.at[0], down_recv.at[0], (s, flip(z, 1))),
        remote(down2_ref, got2_ref, down_send.at[1], down_recv.at[1], (s, flip(z, 2))),
    ]
    for one in results:
        one.start()
    g_buf[s] = g_ref[...]
    gather = Gather(g_buf, s, z, send, recv, 128)
    gather.begin()

    def store(t):
        return pltpu.make_async_copy(g_buf.at[t], g_out.at[t], local_sem.at[0])

    def work(t):
        g = g_buf[t]
        store(t).start()
        back = dot_nt(g, o_eff_ref[...]).astype(jnp.bfloat16)
        gm_ref[t] = back
        product = back.astype(jnp.float32) * mixed_ref[t].astype(jnp.float32)
        for head in range(2):
            turned = jnp.transpose(product[:, HDIM * head : HDIM * head + HDIM])
            dots_ref[head, t] = jnp.sum(turned, axis=0, keepdims=True)
        rank_ref[t] = (adapt_scale * dot_nt(g, b_od_ref[set_ref[z], 0])).astype(jnp.bfloat16)
        store(t).wait()

    work(s)
    gather.arrive_first()
    work(gather.arrive_core(0))
    gather.arrive_neighbours()
    work(flip(s, 2))
    work(flip(s, 4))
    work(gather.arrive_core(1))
    work(gather.arrive_core(2))
    gather.arrive_diagonal()
    work(flip(flip(s, 2), 4))
    work(gather.arrive_core(3))
    gather.end()
    for one in results:
        one.wait()


def spread_layer(g_own, o_eff, mixed, b_out_down, down1, down2, set_index):
    bf16 = jnp.bfloat16
    vmem = pl.BlockSpec(memory_space=pltpu.VMEM)
    anywhere = pl.BlockSpec(memory_space=pl.ANY)
    width = g_own.shape[1]
    shape = jax.ShapeDtypeStruct
    dma = pltpu.SemaphoreType.DMA
    return pl.pallas_call(
        spread_kernel,
        in_specs=[vmem] * 4 + [anywhere] * 2 + [pl.BlockSpec(memory_space=pltpu.SMEM)],
        out_specs=[anywhere, vmem, vmem, vmem, anywhere, anywhere],
        out_shape=[
            shape((8, 256, width), bf16),
            shape((8, 256, 256), bf16),
            shape((2, 8, 1, 256), jnp.float32),
            shape((8, 256, 16), bf16),
            shape(down1.shape, bf16),
            shape(down2.shape, bf16),
        ],
        scratch_shapes=[
            pltpu.VMEM((8, 256, width), bf16),
            dma((gather_sems,)),
            dma((gather_sems,)),
            dma((1,)),
            dma((2,)),
            dma((2,)),
        ],
        cost_estimate=spend(40),
        compiler_params=pltpu.CompilerParams(
            collective_id=3, has_side_effects=True, vmem_limit_bytes=48 << 20
        ),
    )(g_own, o_eff, mixed, b_out_down, down1, down2, set_index)


def mlp_line_kernel(
    m_ref, residual_ref, cots_ref, w_gu_ref, w_d_ref, a_ref, b_ref, ad_ref, bd_ref, set_ref,
    g_ref, grad_res_ref, down0_ref, down1_ref, down2_ref, down3_ref, grad_b_ref, grad_ad_ref, grad_a_ref, grad_bd_ref,
    m_buf, wg, wu, wd, cot_buf, back_acc, down_acc, ranks, slots, r1, r2, r3, r4, r5, stage,
    up_send, up_recv, dn_send, dn_recv, send1, recv1, send4, recv4, send5, recv5, send23, recv23,
    weight_sem, cot_sem, stage_sem,
):
    s, z = places()
    tiles = wg.shape[0]
    tile = wg.shape[2]
    f32 = jnp.float32
    bf16 = jnp.bfloat16
    middle = z * (3 - z) == 2
    at_end = z * (3 - z) == 0
    pair = flip(z, 1)
    opposite = 3 - z
    inner = 1 + z // 2
    high = z // 2
    ids = [z, pair, 2 - high, 3 - 3 * high]
    far = 3 - 3 * high

    loads = []
    for h in range(tiles):
        columns = pl.ds(h * tile, tile)
        loads.append(
            [
                pltpu.make_async_copy(w_gu_ref.at[0, :, columns], wg.at[h], weight_sem.at[3 * h]),
                pltpu.make_async_copy(w_gu_ref.at[1, :, columns], wu.at[h], weight_sem.at[3 * h + 1]),
                pltpu.make_async_copy(w_d_ref.at[columns, :], wd.at[h], weight_sem.at[3 * h + 2]),
            ]
        )
        for one in loads[-1]:
            one.start()

    others = [z, pair, flip(z, 2), opposite]
    down_refs = (down0_ref, down1_ref, down2_ref, down3_ref)

    def load_cot(seq):
        return [pltpu.make_async_copy(cots_ref.at[j, seq], cot_buf.at[j], cot_sem.at[j]) for j in range(4)]

    for one in load_cot(z):
        one.start()

    meet([(z < 3, (s, z + 1)), (z > 0, (s, z - 1)), (None, (s, flip(z, 2)))])
    m_buf[z] = m_ref[...]

    def up(hop, j):
        return remote(m_buf.at[j], m_buf.at[j], up_send.at[hop], up_recv.at[hop], (s, z + 1))

    def down(hop, j):
        return remote(m_buf.at[j], m_buf.at[j], dn_send.at[hop], dn_recv.at[hop], (s, z - 1))

    def begin():
        @pl.when(z < 3)
        def _():
            up(0, z).start()

        @pl.when(z > 0)
        def _():
            down(0, z).start()

    def hop(t):
        @pl.when(z >= t)
        def _():
            up(t - 1, z - t).wait_recv()
            if t < 3:

                @pl.when(z < 3)
                def _():
                    up(t, z - t).start()

        @pl.when(z + t <= 3)
        def _():
            down(t - 1, z + t).wait_recv()
            if t < 3:

                @pl.when(z > 0)
                def _():
                    down(t, z + t).start()

    def hop_end():
        @pl.when(z < 3)
        def _():
            up(0, z).wait_send()

        @pl.when(z > 0)
        def _():
            down(0, z).wait_send()

        for t in (1, 2):

            @pl.when((z >= t) & (z < 3))
            def _():
                up(t, z - t).wait_send()

            @pl.when((z + t <= 3) & (z > 0))
            def _():
                down(t, z + t).wait_send()

    def piece(p):
        return pl.ds(p * 64, 64)

    def copy1():
        return remote(slots.at[1], r1, send1.at[0], recv1.at[0], (s, pair))

    def copy2():
        return remote(slots.at[2], r2, send23.at[0], recv23.at[0], (s, opposite))

    def copy3():
        return remote(slots.at[2], r3, send23.at[1], recv23.at[1], (s, inner))

    def copy4(p):
        return remote(slots.at[3, piece(p)], r4.at[piece(p)], send4.at[p], recv4.at[p], (s, far))

    def copy5(p):
        return remote(slots.at[3, piece(p)], r5.at[piece(p)], send5.at[p], recv5.at[p], (s, inner))

    def stage_copies(seq):
        return [
            pltpu.make_async_copy(stage.at[others[d]], down_refs[d].at[seq], stage_sem.at[d]) for d in range(4)
        ]

    def in_maps(seq):
        return a_ref[set_ref[seq], 3:5].reshape(32, -1)

    def compute(slot):
        seq = ids[slot]
        member = set_ref[seq]
        rows = m_buf[seq]
        for one in load_cot(seq):
            one.wait()
        ranks[:, 0:32] = adapt_scale * dot_nt(rows, in_maps(seq))
        cot = cot_buf[...].reshape(256, -1)
        ranks[:, 32:48] = adapt_scale * dot_nt(cot, bd_ref[member, 1])
        ranks[:, 48:96] = jnp.zeros((256, 48), f32)
        back_acc[...] = jnp.zeros_like(back_acc)
        down_acc[...] = jnp.zeros_like(down_acc)

        def step(h, _):
            columns = pl.ds(pl.multiple_of(h * tile, tile), tile)
            low = ranks[...].astype(bf16)
            low_gate = low[:, 0:16]
            low_up = low[:, 16:32]
            low_cot = low[:, 32:48]
            bg = b_ref[member, 0, :, columns]
            bu = b_ref[member, 1, :, columns]
            ad = ad_ref[member, :, columns]
            rows = m_buf[seq]
            cot = cot_buf[...].reshape(256, -1)
            gate = dot_nn(rows, wg[h]) + dot_nn(low_gate, bg)
            up_value = dot_nn(rows, wu[h]) + dot_nn(low_up, bu)
            grad_act = dot_nt(cot, wd[h]) + dot_nn(low_cot, ad)
            sig = jax.nn.sigmoid(gate)
            act = (gate * sig * up_value).astype(bf16)
            grad_up = (grad_act * gate * sig).astype(bf16)
            grad_gate = (grad_act * up_value * sig * (1.0 + gate * (1.0 - sig))).astype(bf16)
            for part in range(4):
                wide = pl.ds(part * 512, 512)
                back_acc[:, wide] += dot_nt(grad_gate, wg[h, wide, :]) + dot_nt(grad_up, wu[h, wide, :])
                down_acc[:, wide] += dot_nn(act, wd[h, :, wide])
            ranks[:, 48:64] += dot_nt(act, ad)
            ranks[:, 64:80] += dot_nt(grad_gate, bg)
            ranks[:, 80:96] += dot_nt(grad_up, bu)
            grad_b_ref[seq, 0, :, columns] = dot_tn(low_gate, grad_gate)
            grad_b_ref[seq, 1, :, columns] = dot_tn(low_up, grad_up)
            grad_ad_ref[seq, :, columns] = dot_tn(low_cot, act)
            return 0

        if slot == 0:
            for h in range(tiles):
                for one in loads[h]:
                    one.wait()
        lax.fori_loop(0, tiles, step, 0)
        back_rank = (adapt_scale * ranks[:, 64:96]).astype(bf16)
        slots[slot] = (back_acc[...] + dot_nn(back_rank, in_maps(seq))).astype(bf16)

    def rest(slot):
        seq = ids[slot]
        back_rank = (adapt_scale * ranks[:, 64:96]).astype(bf16)
        low_down = (adapt_scale * ranks[:, 48:64]).astype(bf16)
        grad_a_ref[seq] = dot_tn(back_rank, m_buf[seq])
        grad_bd_ref[seq] = dot_tn(low_down, cot_buf[...].reshape(256, -1))
        if slot > 0:
            for one in stage_copies(ids[slot - 1]):
                one.wait()
        value = down_acc[...] + dot_nn(low_down, bd_ref[set_ref[seq], 1])
        if slot == 0:
            value = value + residual_ref[...]
        stage[...] = value.astype(bf16).reshape(4, 64, -1)
        for one in stage_copies(seq):
            one.start()
        following = ids[slot + 1] if slot < 3 else z
        for one in load_cot(following):
            one.start()

    def add(slot, p, extra):
        slots[slot, piece(p), :] = (
            slots[slot, piece(p), :].astype(f32) + extra[piece(p), :].astype(f32)
        ).astype(bf16)

    begin()
    compute(0)
    rest(0)
    hop(1)
    compute(1)

    @pl.when(at_end)
    def _():
        copy1().start()

    rest(1)
    hop(2)
    compute(2)

    @pl.when(at_end)
    def _():
        copy3().start()

    @pl.when(middle)
    def _():
        copy1().start()

    rest(2)
    hop(3)
    compute(3)

    @pl.when(at_end)
    def _():
        copy5(0).start()
        copy5(1).start()

    @pl.when(middle)
    def _():
        copy3().wait_recv()
        for p in range(4):
            add(2, p, r3)
        copy2().start()

    rest(3)

    @pl.when(at_end)
    def _():
        for p in (2, 3):
            copy5(p - 2).wait_send()
            copy5(p).start()

    @pl.when(middle)
    def _():
        for p in range(4):
            copy5(p).wait_recv()
            add(3, p, r5)
            copy4(p).start()

    copy1().wait_recv()
    for p in range(4):
        add(0, p, r1)

    @pl.when(middle)
    def _():
        copy2().wait_recv()
        for p in range(4):
            add(0, p, r2)

    for one in load_cot(z):
        one.wait()
    for p in range(4):

        @pl.when(at_end)
        def _():
            copy4(p).wait_recv()
            add(0, p, r4)

        grad = slots[0, piece(p), :].astype(f32)
        normed, inverse = norm_rows(residual_ref[piece(p), :])
        value = cot_buf[p].astype(f32) + norm_back(grad, normed, inverse)
        grad_res_ref[piece(p), :] = value
        g_ref[piece(p), :] = value.astype(bf16)
    for one in stage_copies(ids[3]):
        one.wait()
    hop_end()
    copy1().wait_send()

    @pl.when(at_end)
    def _():
        copy3().wait_send()
        for p in (2, 3):
            copy5(p).wait_send()

    @pl.when(middle)
    def _():
        copy2().wait_send()
        for p in range(4):
            copy4(p).wait_send()


def mlp_line(m_own, residual, cots, w_gate_up, w_down, a_in, b_gate_up, a_down, b_out_down, set_index):
    bf16 = jnp.bfloat16
    f32 = jnp.float32
    vmem = pl.BlockSpec(memory_space=pltpu.VMEM)
    anywhere = pl.BlockSpec(memory_space=pl.ANY)
    width = m_own.shape[1]
    hidden = w_down.shape[0]
    tile = hidden_tile
    tiles = hidden // tile
    shape = jax.ShapeDtypeStruct
    dma = pltpu.SemaphoreType.DMA
    vm = pltpu.VMEM
    return pl.pallas_call(
        mlp_line_kernel,
        in_specs=[vmem, vmem]
        + [anywhere] * 3
        + [vmem] * 4
        + [pl.BlockSpec(memory_space=pltpu.SMEM)],
        out_specs=[vmem, vmem] + [anywhere] * 4 + [vmem, vmem, vmem, vmem],
        out_shape=[
            shape((256, width), bf16),
            shape((256, width), f32),
        ]
        + [shape((4, 64, width), bf16)] * 4
        + [
            shape((4, 2, 16, hidden), f32),
            shape((4, 16, hidden), f32),
            shape((4, 32, width), f32),
            shape((4, 16, width), f32),
        ],
        scratch_shapes=[
            vm((4, 256, width), bf16),
            vm((tiles, width, tile), bf16),
            vm((tiles, width, tile), bf16),
            vm((tiles, tile, width), bf16),
            vm((4, 64, width), bf16),
            vm((256, width), f32),
            vm((256, width), f32),
            vm((256, 96), f32),
            vm((4, 256, width), bf16),
            vm((256, width), bf16),
            vm((256, width), bf16),
            vm((256, width), bf16),
            vm((256, width), bf16),
            vm((256, width), bf16),
            vm((4, 64, width), bf16),
        ]
        + [dma((3,))] * 4
        + [dma((4,))] * 6
        + [dma((2,))] * 2
        + [dma((3 * tiles,)), dma((4,)), dma((4,))],
        cost_estimate=spend(110),
        compiler_params=pltpu.CompilerParams(
            collective_id=5, has_side_effects=True, vmem_limit_bytes=60 << 20
        ),
    )(m_own, residual, cots, w_gate_up, w_down, a_in, b_gate_up, a_down, b_out_down, set_index)


def finish_kernel(
    dq_ref, dk_ref, dv_ref, w_ref, x_own_ref, residual_ref, u_ref, g_ref, low_ref, rank_ref, mixed_ref,
    b_sel_ref, a_sel_ref, grad_b_ref, grad_ad_ref, grad_a_ref, grad_bd_ref, down0_ref, got1_ref, got2_ref, down3_ref,
    set_ref,
    result_ref, grad_ref, pool_ref, heads_ref, got3_ref,
    own_ref, sib_q, sib_k, sib_v, out_buf, in_buf, u_buf, g_buf, a_acc, b_acc, chunk_src, chunk_sib, chunk_sum,
    chunk_in, z_src, z_in, head_src, head_in,
    a2a_send, a2a_recv, sib_send, sib_recv, send, recv, load_sem, cs_send, cs_recv, cx_send, cx_recv,
    cz_send, cz_recv, cg_send, cg_recv, hz_send, hz_recv, hg_send, hg_recv, down_send, down_recv,
):
    f32 = jnp.float32
    bf16 = jnp.bfloat16
    s, z = places()
    core = s % 2
    chip = s // 2
    other = flip(s, 1)
    sx = flip(s, 2)
    sy = flip(s, 4)
    sd = flip(sx, 4)
    zs = [flip(z, 1), flip(z, 2), 3 - z]
    meet([(None, (t, z)) for t in (other, sx, sy, sd)] + [(None, (s, j)) for j in zs])
    last_down = remote(down3_ref, got3_ref, down_send.at[0], down_recv.at[0], (s, 3 - z))
    last_down.start()
    mine = (dq_ref, dk_ref, dv_ref)
    theirs = (sib_q, sib_k, sib_v)
    swaps = [
        remote(
            mine[p].at[2 * c + 1 - core], theirs[p].at[c], sib_send.at[4 * p + c], sib_recv.at[4 * p + c], (other, z)
        )
        for c in range(4)
        for p in range(3)
    ]
    for one in swaps:
        one.start()

    def load(t):
        return [
            pltpu.make_async_copy(u_ref.at[t], u_buf.at[t % 2], load_sem.at[t % 2]),
            pltpu.make_async_copy(g_ref.at[t], g_buf.at[t % 2], load_sem.at[2 + t % 2]),
        ]

    for one in load(0):
        one.start()
    for one in swaps:
        one.wait_recv()

    def product(c, half):
        rows = pl.ds(half * 128, 128)
        both = jnp.concatenate(
            [ref[2 * c + core, rows, :] for ref in mine] + [ref[c, rows, :] for ref in theirs], axis=1
        )
        return dot_nt(both, w_ref[...])

    reduce = Reduce(product, s, z, out_buf, in_buf, send, recv)
    reduce.begin()

    b_two = [
        jnp.concatenate(
            [b_sel_ref[2 * core, 16 * p : 16 * p + 16], b_sel_ref[2 * core + 1, 16 * p : 16 * p + 16]], axis=1
        )
        for p in range(3)
    ]
    a_two = jnp.concatenate([a_sel_ref[2 * core], a_sel_ref[2 * core + 1]], axis=1)

    def adapt(t, first):
        for one in load(t):
            one.wait()
        if t < 7:
            for one in load(t + 1):
                one.start()
        back = jnp.concatenate([dot_nt(mine[p][t], b_two[p]) for p in range(3)], axis=1)
        back = (adapt_scale * back).astype(bf16)
        a_part = dot_tn(back, u_buf[t % 2])
        lows = (adapt_scale * dot_nt(mixed_ref[t], a_two)).astype(bf16)
        b_part = dot_tn(lows, g_buf[t % 2])
        if first:
            a_acc[...] = a_part
            b_acc[...] = b_part
        else:
            a_acc[...] += a_part
            b_acc[...] += b_part

    for t in range(3):
        adapt(t, t == 0)
    reduce.middle()
    for t in range(3, 8):
        adapt(t, False)
    per_head = [
        dot_tn(low_ref[...].reshape(2048, 48)[:, 16 * p : 16 * p + 16], mine[p][...].reshape(2048, 256))
        for p in range(3)
    ] + [dot_tn(rank_ref[...].reshape(2048, 16), mixed_ref[...].reshape(2048, 256))]
    for head in range(2):
        columns = slice(HDIM * head, HDIM * head + HDIM)
        head_src[head] = jnp.concatenate([part[:, columns] for part in per_head], axis=0).astype(bf16)

    keeper = (z // 2) == core

    def head_copy(head):
        return remote(head_src.at[head], head_in.at[z], hz_send.at[head], hz_recv.at[z], (s, 2 * core + head))

    for head in range(2):

        @pl.when(2 * core + head != z)
        def _():
            head_copy(head).start()

        @pl.when(2 * core + head == z)
        def _():
            head_in[z] = head_src[head]

    for member in range(4):
        whole = jnp.zeros((48, a_acc.shape[1]), f32)
        split = jnp.zeros((48, a_acc.shape[1]), f32)
        for seq in range(4):
            used = (set_ref[seq] == member).astype(f32)
            whole += used * jnp.concatenate([grad_a_ref[seq], grad_bd_ref[seq]], axis=0)
            split += used * jnp.concatenate([grad_b_ref[seq, 0], grad_b_ref[seq, 1], grad_ad_ref[seq]], axis=0)
        for part in range(2):
            i = 2 * member + part
            sequence = a_acc[8 * i : 8 * i + 8] if i < 6 else b_acc[8 * i - 48 : 8 * i - 40]
            chunk_src[i] = jnp.concatenate(
                [
                    whole[24 * part : 24 * part + 24],
                    sequence,
                    split[24 * part : 24 * part + 24],
                    jnp.zeros((8, a_acc.shape[1]), f32),
                ],
                axis=0,
            ).astype(bf16)
    crosses = [
        remote(chunk_src.at[2 * c + 1 - core], chunk_sib.at[c], cs_send.at[c], cs_recv.at[c], (other, z))
        for c in range(4)
    ]
    for one in crosses:
        one.start()
    for one in crosses:
        one.wait_recv()
    for c in range(4):
        chunk_sum[c] = (chunk_src[2 * c + core].astype(f32) + chunk_sib[c].astype(f32)).astype(bf16)
    around = [
        remote(chunk_sum.at[t // 2], chunk_in.at[d], cx_send.at[d], cx_recv.at[d], (t, z))
        for d, t in enumerate((sx, sy, sd))
    ]
    for one in around:
        one.start()

    for half in range(2):
        total = reduce.finish(half)
        x = x_own_ref[2 * half : 2 * half + 2].reshape(128, -1).astype(f32)
        normed, inverse = norm_rows(x)
        value = residual_ref[pl.ds(half * 128, 128), :] + norm_back(total, normed, inverse)
        own_ref[2 * half : 2 * half + 2] = value.astype(bf16).reshape(2, 64, -1)
    backs = [
        remote(own_ref.at[j], grad_ref.at[z], a2a_send.at[d], a2a_recv.at[d], (s, j)) for d, j in enumerate(zs)
    ]
    for one in backs:
        one.start()
    grad_ref[z] = own_ref[z]

    last_down.wait_recv()
    for part in range(4):
        result_ref[part] = (
            down0_ref[part].astype(f32)
            + got1_ref[part].astype(f32)
            + got2_ref[part].astype(f32)
            + got3_ref[part].astype(f32)
        ).astype(bf16)
    for one in around:
        one.wait_recv()
    chunk = chunk_sum[chip].astype(f32)
    for d in range(3):
        chunk += chunk_in[d].astype(f32)
    z_src[...] = chunk[0:32].astype(bf16)
    along = [remote(z_src, z_in.at[d], cz_send.at[d], cz_recv.at[d], (s, j)) for d, j in enumerate(zs)]
    for one in along:
        one.start()

    def head_spread(target, index):
        return remote(heads_ref.at[chip], heads_ref.at[chip], hg_send.at[index], hg_recv.at[index], (target, z))

    def head_pass(t, index):
        c = t // 2
        return remote(heads_ref.at[c], heads_ref.at[c], hg_send.at[index], hg_recv.at[index], (other, z))

    @pl.when(keeper)
    def _():
        for j in range(4):

            @pl.when(z != j)
            def _():
                remote(head_src.at[0], head_in.at[j], hz_send.at[0], hz_recv.at[j], (s, j)).wait_recv()

        for member in range(4):
            total = jnp.zeros((64, HDIM), f32)
            for seq in range(4):
                total += (set_ref[seq] == member).astype(f32) * head_in[seq].astype(f32)
            heads_ref[chip, pl.ds(64 * member, 64)] = total.astype(bf16)
        for index, target in enumerate((sx, sy, sd, other)):
            head_spread(target, index).start()

    for one in along:
        one.wait_recv()
    whole = chunk[0:24]
    places_z = [z] + zs
    parts = [chunk[24:32]] + [z_in[d, 24:32].astype(f32) for d in range(3)]
    for d in range(3):
        whole += z_in[d, 0:24].astype(f32)
    by_member = [
        sum((set_ref[places_z[d]] == member).astype(f32) * parts[d] for d in range(4)) for member in range(4)
    ]
    pool_ref[s] = jnp.concatenate([whole] + by_member + [chunk[32:56]], axis=0).astype(bf16)

    def pool_copy(t, index, target):
        return remote(pool_ref.at[t], pool_ref.at[t], cg_send.at[index], cg_recv.at[index], (target, z))

    gives = [pool_copy(s, index, target) for index, target in enumerate((sx, sy, sd, other))]
    for one in gives:
        one.start()

    @pl.when(keeper)
    def _():
        for index, t in enumerate((sx, sy, sd)):
            head_pass(t, index).wait_recv()
            head_pass(t, 4 + index).start()

    for index, t in enumerate((sx, sy, sd)):
        pool_copy(t, index, other).wait_recv()
        pool_copy(t, 4 + index, other).start()
    pool_copy(other, 3, other).wait_recv()
    for index, t in enumerate((sx, sy, sd)):
        pool_copy(flip(t, 1), 4 + index, other).wait_recv()

    @pl.when(z // 2 != core)
    def _():
        head_spread(other, 3).wait_recv()
        for index, t in enumerate((sx, sy, sd)):
            head_pass(t, 4 + index).wait_recv()

    for d, j in enumerate(zs):
        remote(own_ref.at[j], grad_ref.at[j], a2a_send.at[d], a2a_recv.at[d], (s, j)).wait_recv()
    for one in swaps + crosses + around + backs + along + gives + [last_down]:
        one.wait_send()
    for index, t in enumerate((sx, sy, sd)):
        pool_copy(t, 4 + index, other).wait_send()
    reduce.end()
    for head in range(2):

        @pl.when(2 * core + head != z)
        def _():
            head_copy(head).wait_send()

    @pl.when(keeper)
    def _():
        for index, target in enumerate((sx, sy, sd, other)):
            head_spread(target, index).wait_send()
        for index, t in enumerate((sx, sy, sd)):
            head_pass(t, 4 + index).wait_send()


def finish_layer(*operands):
    bf16 = jnp.bfloat16
    f32 = jnp.float32
    vmem = pl.BlockSpec(memory_space=pltpu.VMEM)
    anywhere = pl.BlockSpec(memory_space=pl.ANY)
    width = operands[4].shape[2]
    dma = pltpu.SemaphoreType.DMA
    vm = pltpu.VMEM
    shape = jax.ShapeDtypeStruct
    return pl.pallas_call(
        finish_kernel,
        in_specs=[vmem] * 6 + [anywhere] * 2 + [vmem] * 13 + [pl.BlockSpec(memory_space=pltpu.SMEM)],
        out_specs=[vmem] * 5,
        out_shape=[
            shape((4, 64, width), bf16),
            shape((4, 64, width), bf16),
            shape((8, 80, width), bf16),
            shape((4, 256, HDIM), bf16),
            shape((4, 64, width), bf16),
        ],
        scratch_shapes=[
            vm((4, 64, width), bf16),
            vm((4, 256, 256), bf16),
            vm((4, 256, 256), bf16),
            vm((4, 256, 256), bf16),
            vm((6, 128, width), bf16),
            vm((6, 128, width), bf16),
            vm((2, 256, width), bf16),
            vm((2, 256, width), bf16),
            vm((48, width), f32),
            vm((16, width), f32),
            vm((8, 64, width), bf16),
            vm((4, 64, width), bf16),
            vm((4, 64, width), bf16),
            vm((3, 64, width), bf16),
            vm((32, width), bf16),
            vm((3, 32, width), bf16),
            vm((2, 64, HDIM), bf16),
            vm((4, 64, HDIM), bf16),
        ]
        + [
            dma((count,))
            for count in (3, 3, 12, 12, 6, 6, 4, 4, 4, 3, 3, 3, 3, 7, 7, 2, 4, 7, 7, 1, 1)
        ],
        cost_estimate=spend(80),
        compiler_params=pltpu.CompilerParams(
            collective_id=4, has_side_effects=True, vmem_limit_bytes=58 << 20
        ),
    )(*operands)


def span_table(positions):
    half_dim = HDIM // 2
    frequency = jnp.exp(
        jnp.arange(half_dim, dtype=jnp.float32) * (-2.0 * math.log(rope_base) / HDIM)
    )
    angles = positions.astype(jnp.float32)[:, None] * frequency
    return jnp.concatenate([jnp.cos(angles), jnp.sin(angles)], axis=1)


def per_device_layers(
    layer_in, w_qkv, w_out, w_gate_up, w_down, a_in, b_qkv, b_gate_up, a_out, a_down, b_out_down,
    set_index, positions, cotangent,
):
    f32 = jnp.float32
    z = lax.axis_index("mp")
    sets = a_in.shape[0]
    width = layer_in.shape[2]
    rank = a_in.shape[2]
    length = 8 * 256

    table = span_table(lax.dynamic_index_in_dim(positions, z, 0, keepdims=False))
    (
        x_own, m_own, residual, o_eff, b_sel, a_sel, lse,
        u, q, k, v, low, tables, mixed, w_cat, cots,
    ) = front_layer(
        layer_in, w_qkv, w_out, b_qkv, a_out, a_in, b_out_down, table, cotangent, set_index
    )

    def spans(values):
        return values.reshape(8, 256, 256)

    (
        g_own, grad_residual, down0, down1, down2, down3,
        grad_b_mlp, grad_ad, grad_a_mlp, grad_bd,
    ) = mlp_line(
        m_own, residual, cots, w_gate_up, w_down, a_in, b_gate_up, a_down, b_out_down, set_index
    )
    g, grad_mixed, dots, out_rank, got1, got2 = spread_layer(
        g_own, o_eff, spans(mixed), b_out_down, down1, down2, set_index
    )
    dq, dk, dv = attend_back(
        q, k, v, grad_mixed.reshape(length, -1), lse.reshape(2, 1, length), dots.reshape(2, 1, length),
        tables.reshape(length, HDIM),
    )
    result, grad_in, pool, heads, _ = finish_layer(
        spans(dq), spans(dk), spans(dv), w_cat, x_own, grad_residual, u, g, low, out_rank, spans(mixed),
        b_sel, a_sel, grad_b_mlp, grad_ad, grad_a_mlp, grad_bd, down0, got1, got2, down3, set_index,
    )
    pool = pool.astype(f32)
    whole = pool[:, 0:24].reshape(sets, 48, width)
    sequence = jnp.transpose(pool[:, 24:56].reshape(8, sets, 8, width), (1, 0, 2, 3)).reshape(sets, 64, width)
    split = pool[:, 56:80].reshape(sets, 48, width)
    heads = heads.astype(f32).reshape(4, sets, 64, HDIM)
    heads = jnp.transpose(heads, (1, 2, 0, 3)).reshape(sets, 4, rank, 4 * HDIM)
    return (
        result,
        grad_in,
        jnp.concatenate([sequence[:, :48], whole[:, :32]], axis=1).reshape(sets, 5, rank, width),
        heads[:, :3],
        split[:, :32].reshape(sets, 2, rank, width),
        heads[:, 3],
        split[:, 32:],
        jnp.stack([sequence[:, 48:], whole[:, 32:]], axis=1),
    )


def solution(mesh):
    by_layers = mesh.shape["seq"] == 8 and mesh.shape["mp"] == 4
    body = per_device_layers if by_layers else per_device
    placed = (
        P(None, ("seq", "mp"), None),
        P(None, None, "mp"),
        P("mp", None),
        P(None, None, "mp"),
        P("mp", None),
        P(),
        P(None, None, None, "mp"),
        P(None, None, None, "mp"),
        P(None, None, "mp"),
        P(None, None, "mp"),
        P(),
        P(),
        P(None, "seq"),
        P(None, ("seq", "mp"), None),
    )
    return jax.shard_map(
        body,
        mesh=mesh,
        in_specs=placed,
        out_specs=(
            P(None, ("seq", "mp"), None),
            P(None, ("seq", "mp"), None),
            P(),
            P(None, None, None, "mp"),
            P(None, None, None, "mp"),
            P(None, None, "mp"),
            P(None, None, "mp"),
            P(),
        ),
        check_vma=False,
    )
```

```python
import math

import jax
import jax.numpy as jnp
from jax import lax
from jax.experimental import pallas as pl
from jax.experimental.pallas import tpu as pltpu
from jax.sharding import PartitionSpec as P

HDIM = 128


adapt_scale = 0.5
norm_eps = 1e-05
rope_base = 10000.0
far_below = -1e30
highest = lax.Precision.HIGHEST


def layer_norm(values):
    centred = values - jnp.mean(values, axis=-1, keepdims=True)
    inverse = lax.rsqrt(jnp.mean(centred * centred, axis=-1, keepdims=True) + norm_eps)
    return (centred * inverse, inverse)


def norm_back(gradient, normed, inverse):
    return inverse * (
        gradient
        - jnp.mean(gradient, axis=-1, keepdims=True)
        - normed * jnp.mean(gradient * normed, axis=-1, keepdims=True)
    )


def gather_rows(values):
    return lax.all_gather(values, "mp", axis=1, tiled=True)


def scatter_rows(values):
    return lax.psum_scatter(
        values.astype(jnp.bfloat16), "mp", scatter_dimension=1, tiled=True
    ).astype(jnp.float32)


def rope_tables(positions):
    half_dim = HDIM // 2
    frequency = jnp.exp(
        jnp.arange(half_dim, dtype=jnp.float32) * (-2.0 * math.log(rope_base) / HDIM)
    )
    angles = jnp.transpose(positions).astype(jnp.float32)[:, :, None, None] * frequency
    return (jnp.cos(angles), jnp.sin(angles))


def rotate(values, cosine_table, sine_table):
    half_dim = values.shape[-1] // 2
    first_half = values[..., :half_dim]
    second_half = values[..., half_dim:]
    return jnp.concatenate(
        [
            first_half * cosine_table - second_half * sine_table,
            second_half * cosine_table + first_half * sine_table,
        ],
        axis=-1,
    )


def rotate_back(gradient, cosine_table, sine_table):
    half_dim = gradient.shape[-1] // 2
    first_half = gradient[..., :half_dim]
    second_half = gradient[..., half_dim:]
    return jnp.concatenate(
        [
            first_half * cosine_table + second_half * sine_table,
            second_half * cosine_table - first_half * sine_table,
        ],
        axis=-1,
    )


def masked_scores(queries, key_rows, query_first, key_first, score_scale):
    raw_scores = (
        jnp.einsum("qshd,kshd->shqk", queries, key_rows, preferred_element_type=jnp.float32)
        * score_scale
    )
    query_index = query_first + jnp.arange(queries.shape[0])
    key_index = key_first + jnp.arange(key_rows.shape[0])
    return (raw_scores, key_index[None, :] <= query_index[:, None])


def blockwise(fold_step, state_carry, pieces, start_row):
    row_count = pieces[0].shape[0]
    block_size = 512

    def block_turn(block_id, running):
        blocks = tuple(
            (
                lax.dynamic_slice_in_dim(shard_piece, block_id * block_size, block_size, 0)
                for shard_piece in pieces
            )
        )
        return fold_step(running, blocks, start_row + block_id * block_size)

    return lax.fori_loop(0, row_count // block_size, block_turn, state_carry)


def forward_step(queries, query_first, score_scale):
    query_last = query_first + queries.shape[0] - 1

    def fold_step(state_carry, blocks, key_first):
        key_rows, value_rows = blocks

        def compute(running):
            running_max, running_sum, weighted = running
            scores, allowed = masked_scores(queries, key_rows, query_first, key_first, score_scale)
            new_max = jnp.maximum(
                running_max, jnp.max(jnp.where(allowed, scores, far_below), axis=-1)
            )
            exponent = jnp.where(allowed, jnp.exp(scores - new_max[..., None]), 0.0)
            factor = jnp.exp(running_max - new_max)
            running_sum = running_sum * factor + jnp.sum(exponent, axis=-1)
            weighted = weighted * factor[..., None] + jnp.einsum(
                "shqk,kshd->shqd",
                exponent.astype(jnp.bfloat16),
                value_rows,
                preferred_element_type=jnp.float32,
            )
            return (new_max, running_sum, weighted)

        return lax.cond(key_first <= query_last, compute, lambda running: running, state_carry)

    return fold_step


def query_grad_step(queries, grad_heads, log_total, row_dots, query_first, score_scale):
    query_last = query_first + queries.shape[0] - 1

    def fold_step(state_carry, blocks, key_first):
        key_rows, value_rows = blocks

        def compute(running):
            scores, allowed = masked_scores(queries, key_rows, query_first, key_first, score_scale)
            attn_probs = jnp.where(allowed, jnp.exp(scores - log_total[..., None]), 0.0)
            grad_probs = jnp.einsum(
                "qshd,kshd->shqk", grad_heads, value_rows, preferred_element_type=jnp.float32
            )
            grad_scores = (attn_probs * (grad_probs - row_dots[..., None])).astype(jnp.bfloat16)
            return running + score_scale * jnp.einsum(
                "shqk,kshd->qshd", grad_scores, key_rows, preferred_element_type=jnp.float32
            )

        return lax.cond(key_first <= query_last, compute, lambda running: running, state_carry)

    return fold_step


def key_grad_step(key_rows, value_rows, key_first, score_scale):

    def fold_step(state_carry, blocks, query_first):
        queries, grad_heads, log_total_tok, row_dots_tok = blocks
        query_last = query_first + queries.shape[0] - 1

        def compute(running):
            scores, allowed = masked_scores(queries, key_rows, query_first, key_first, score_scale)
            log_total = jnp.transpose(log_total_tok, (1, 2, 0))
            row_dots = jnp.transpose(row_dots_tok, (1, 2, 0))
            attn_probs = jnp.where(allowed, jnp.exp(scores - log_total[..., None]), 0.0)
            grad_value_rows = jnp.einsum(
                "shqk,qshd->kshd",
                attn_probs.astype(jnp.bfloat16),
                grad_heads,
                preferred_element_type=jnp.float32,
            )
            grad_probs = jnp.einsum(
                "qshd,kshd->shqk", grad_heads, value_rows, preferred_element_type=jnp.float32
            )
            grad_scores = (attn_probs * (grad_probs - row_dots[..., None])).astype(jnp.bfloat16)
            grad_key_rows = score_scale * jnp.einsum(
                "shqk,qshd->kshd", grad_scores, queries, preferred_element_type=jnp.float32
            )
            return (grad_key_rows, grad_value_rows)

        return lax.cond(key_first <= query_last, compute, lambda running: running, state_carry)

    return fold_step


def project_in(token_rows, weight, a_chosen, b_chosen):
    main_term = jnp.einsum("scd,dw->csw", token_rows, weight, preferred_element_type=jnp.float32)
    low_rank = jnp.einsum("scd,srd->scr", token_rows, a_chosen, preferred_element_type=jnp.float32)
    side_term = jnp.einsum(
        "scr,srw->csw", low_rank, b_chosen.astype(jnp.float32), precision=highest
    )
    return (main_term + adapt_scale * side_term, low_rank)


def project_out(middle, weight, a_chosen, b_chosen):
    main_term = jnp.einsum("csw,wd->scd", middle, weight, preferred_element_type=jnp.float32)
    low_rank = jnp.einsum("csw,srw->scr", middle, a_chosen, preferred_element_type=jnp.float32)
    side_term = jnp.einsum(
        "scr,srd->scd", low_rank, b_chosen.astype(jnp.float32), precision=highest
    )
    return (main_term + adapt_scale * side_term, low_rank)


def back_in(gradient, weight, a_chosen, b_chosen, token_rows, low_rank):
    back_rank = jnp.einsum("csw,srw->scr", gradient, b_chosen, preferred_element_type=jnp.float32)
    grad_rows = jnp.einsum("csw,dw->scd", gradient, weight, preferred_element_type=jnp.float32)
    grad_rows = grad_rows + adapt_scale * jnp.einsum(
        "scr,srd->scd", back_rank, a_chosen.astype(jnp.float32), precision=highest
    )
    grad_a = adapt_scale * jnp.einsum("scr,scd->srd", back_rank, token_rows, precision=highest)
    grad_b = adapt_scale * jnp.einsum("scr,csw->srw", low_rank, gradient, precision=highest)
    return (grad_rows, grad_a, grad_b)


def back_out(gradient, weight, a_chosen, b_chosen, middle, low_rank):
    back_rank = jnp.einsum("scd,srd->scr", gradient, b_chosen, preferred_element_type=jnp.float32)
    grad_middle = jnp.einsum("scd,wd->csw", gradient, weight, preferred_element_type=jnp.float32)
    grad_middle = grad_middle + adapt_scale * jnp.einsum(
        "scr,srw->csw", back_rank, a_chosen.astype(jnp.float32), precision=highest
    )
    grad_a = adapt_scale * jnp.einsum("scr,csw->srw", back_rank, middle, precision=highest)
    grad_b = adapt_scale * jnp.einsum("scr,scd->srd", low_rank, gradient, precision=highest)
    return (grad_middle, grad_a, grad_b)


def pick_set(onehot, set_table):
    flattened = set_table.reshape(set_table.shape[0], -1)
    chosen = jnp.dot(onehot, flattened, preferred_element_type=jnp.float32).astype(jnp.bfloat16)
    return chosen.reshape((onehot.shape[0],) + set_table.shape[1:])


def spread_sets(onehot, per_sequence):
    flattened = per_sequence.reshape(per_sequence.shape[0], -1)
    summed = jnp.dot(onehot.astype(jnp.float32).T, flattened, precision=highest)
    return summed.reshape((onehot.shape[1],) + per_sequence.shape[1:])


def per_device(
    layer_in,
    w_qkv,
    w_out,
    w_gate_up,
    w_down,
    a_in,
    b_qkv,
    b_gate_up,
    a_out,
    a_down,
    b_out_down,
    set_index,
    positions,
    cotangent,
):
    local_len = positions.shape[1]
    seq_count = positions.shape[0]
    score_scale = 1.0 / math.sqrt(HDIM)
    my_first = lax.axis_index("seq") * local_len
    onehot = (set_index[:, None] == jnp.arange(a_in.shape[0])[None, :]).astype(jnp.bfloat16)
    chosen_a_in = pick_set(onehot, a_in)
    chosen_b_qkv = pick_set(onehot, b_qkv)
    chosen_b_gate_up = pick_set(onehot, b_gate_up)
    chosen_a_out = pick_set(onehot, a_out)
    chosen_a_down = pick_set(onehot, a_down)
    chosen_b_out_down = pick_set(onehot, b_out_down)

    def to_heads(values):
        return values.reshape(local_len, seq_count, -1, HDIM)

    residual_in = layer_in.astype(jnp.float32)
    normed_attn, inverse_attn = layer_norm(residual_in)
    rows_attn = gather_rows(normed_attn.astype(jnp.bfloat16))
    projected = [
        project_in(rows_attn, w_qkv[member], chosen_a_in[:, member], chosen_b_qkv[:, member])
        for member in range(3)
    ]
    cosine_table, sine_table = rope_tables(positions)
    queries = rotate(to_heads(projected[0][0]), cosine_table, sine_table).astype(jnp.bfloat16)
    key_rows = rotate(to_heads(projected[1][0]), cosine_table, sine_table).astype(jnp.bfloat16)
    value_rows = to_heads(projected[2][0]).astype(jnp.bfloat16)
    stat_shape = (seq_count, queries.shape[2], local_len)
    initial = (
        jnp.full(stat_shape, far_below, jnp.float32),
        jnp.zeros(stat_shape, jnp.float32),
        jnp.zeros(stat_shape + (HDIM,), jnp.float32),
    )
    attend = forward_step(queries, my_first, score_scale)
    running_max, running_sum, weighted = blockwise(
        attend,
        initial,
        (
            lax.all_gather(key_rows, "seq", axis=0, tiled=True),
            lax.all_gather(value_rows, "seq", axis=0, tiled=True),
        ),
        jnp.int32(0),
    )
    log_total = running_max + jnp.log(running_sum)
    attn_output = jnp.transpose(weighted / running_sum[..., None], (2, 0, 1, 3))
    mixed = attn_output.reshape(local_len, seq_count, -1).astype(jnp.bfloat16)
    attn_term, rank_out = project_out(mixed, w_out, chosen_a_out, chosen_b_out_down[:, 0])
    residual = residual_in + scatter_rows(attn_term)
    normed_mlp, inverse_mlp = layer_norm(residual)
    rows_mlp = gather_rows(normed_mlp.astype(jnp.bfloat16))
    gate_proj, rank_gate = project_in(
        rows_mlp, w_gate_up[0], chosen_a_in[:, 3], chosen_b_gate_up[:, 0]
    )
    up_proj, rank_up = project_in(rows_mlp, w_gate_up[1], chosen_a_in[:, 4], chosen_b_gate_up[:, 1])
    sigmoid_gate = jax.nn.sigmoid(gate_proj)
    activation = (gate_proj * sigmoid_gate * up_proj).astype(jnp.bfloat16)
    down_term, rank_down = project_out(activation, w_down, chosen_a_down, chosen_b_out_down[:, 1])
    result = (residual + scatter_rows(down_term)).astype(jnp.bfloat16)
    grad_down = gather_rows(cotangent)
    grad_activation, grad_a_down, grad_b_down = back_out(
        grad_down, w_down, chosen_a_down, chosen_b_out_down[:, 1], activation, rank_down
    )
    grad_up = (grad_activation * gate_proj * sigmoid_gate).astype(jnp.bfloat16)
    grad_gate = (
        grad_activation * up_proj * sigmoid_gate * (1.0 + gate_proj * (1.0 - sigmoid_gate))
    ).astype(jnp.bfloat16)
    rows_from_gate, grad_a_gate, grad_b_gate = back_in(
        grad_gate, w_gate_up[0], chosen_a_in[:, 3], chosen_b_gate_up[:, 0], rows_mlp, rank_gate
    )
    rows_from_up, grad_a_up, grad_b_up = back_in(
        grad_up, w_gate_up[1], chosen_a_in[:, 4], chosen_b_gate_up[:, 1], rows_mlp, rank_up
    )
    grad_residual = cotangent.astype(jnp.float32) + norm_back(
        scatter_rows(rows_from_gate + rows_from_up), normed_mlp, inverse_mlp
    )
    grad_attn_rows = gather_rows(grad_residual.astype(jnp.bfloat16))
    grad_mixed, grad_a_out, grad_b_out = back_out(
        grad_attn_rows, w_out, chosen_a_out, chosen_b_out_down[:, 0], mixed, rank_out
    )
    grad_heads = to_heads(grad_mixed.astype(jnp.bfloat16))
    row_dots_tok = jnp.sum(grad_heads.astype(jnp.float32) * attn_output, axis=-1)
    row_dots = jnp.transpose(row_dots_tok, (1, 2, 0))
    log_total_tok = jnp.transpose(log_total, (2, 0, 1))
    query_step = query_grad_step(queries, grad_heads, log_total, row_dots, my_first, score_scale)
    zero_heads = jnp.zeros(queries.shape, jnp.float32)
    every_key, every_value = (
        lax.all_gather(key_rows, "seq", axis=0, tiled=True),
        lax.all_gather(value_rows, "seq", axis=0, tiled=True),
    )
    grad_queries = blockwise(query_step, zero_heads, (every_key, every_value), 0)
    block_size = 512

    def one_block(block_id):
        first_key = block_id * block_size
        block_keys = lax.dynamic_slice_in_dim(every_key, first_key, block_size, 0)
        block_values = lax.dynamic_slice_in_dim(every_value, first_key, block_size, 0)
        zero_block = jnp.zeros(block_keys.shape, jnp.float32)
        block_step = key_grad_step(block_keys, block_values, first_key, score_scale)
        grad_key_block, grad_value_block = block_step(
            (zero_block, zero_block), (queries, grad_heads, log_total_tok, row_dots_tok), my_first
        )
        return jnp.concatenate([grad_key_block, grad_value_block], axis=-1)

    stacked = lax.map(one_block, jnp.arange(local_len * lax.axis_size("seq") // block_size))
    stacked_terms = lax.psum_scatter(
        stacked.reshape((local_len * lax.axis_size("seq"),) + stacked.shape[2:]).astype(
            jnp.bfloat16
        ),
        "seq",
        scatter_dimension=0,
        tiled=True,
    ).astype(jnp.float32)
    grad_keys = stacked_terms[..., :HDIM]
    grad_values = stacked_terms[..., HDIM:]
    grad_query_raw = (
        rotate_back(grad_queries, cosine_table, sine_table)
        .astype(jnp.bfloat16)
        .reshape(local_len, seq_count, -1)
    )
    grad_key_raw = (
        rotate_back(grad_keys, cosine_table, sine_table)
        .astype(jnp.bfloat16)
        .reshape(local_len, seq_count, -1)
    )
    grad_value_raw = grad_values.astype(jnp.bfloat16).reshape(local_len, seq_count, -1)
    back_parts = [
        back_in(
            gradient,
            w_qkv[member],
            chosen_a_in[:, member],
            chosen_b_qkv[:, member],
            rows_attn,
            projected[member][1],
        )
        for member, gradient in enumerate((grad_query_raw, grad_key_raw, grad_value_raw))
    ]
    grad_rows_attn = back_parts[0][0] + back_parts[1][0] + back_parts[2][0]
    grad_in = (
        grad_residual + norm_back(scatter_rows(grad_rows_attn), normed_attn, inverse_attn)
    ).astype(jnp.bfloat16)
    per_seq_a_in = jnp.stack(
        [back_parts[0][1], back_parts[1][1], back_parts[2][1], grad_a_gate, grad_a_up], axis=1
    )
    per_seq_b_qkv = jnp.stack([bundle[2] for bundle in back_parts], axis=1)
    per_seq_b_gate_up = jnp.stack([grad_b_gate, grad_b_up], axis=1)
    per_seq_b_out_down = jnp.stack([grad_b_out, grad_b_down], axis=1)
    sums_seq = (
        lax.psum(spread_sets(onehot, per_seq_b_qkv).astype(jnp.bfloat16), "seq").astype(
            jnp.float32
        ),
        lax.psum(spread_sets(onehot, per_seq_b_gate_up).astype(jnp.bfloat16), "seq").astype(
            jnp.float32
        ),
        lax.psum(spread_sets(onehot, grad_a_out).astype(jnp.bfloat16), "seq").astype(jnp.float32),
        lax.psum(spread_sets(onehot, grad_a_down).astype(jnp.bfloat16), "seq").astype(jnp.float32),
    )
    sums_all = lax.psum(
        (spread_sets(onehot, per_seq_a_in), spread_sets(onehot, per_seq_b_out_down)), ("seq", "mp")
    )
    return (
        result,
        grad_in,
        sums_all[0],
        sums_seq[0],
        sums_seq[1],
        sums_seq[2],
        sums_seq[3],
        sums_all[1],
    )


log2e = 1.4426950408889634
attn_tile = 512
hidden_tile = 512


def dot_nt(a, b):
    return lax.dot_general(a, b, (((1,), (1,)), ((), ())), preferred_element_type=jnp.float32)


def dot_tn(a, b):
    return lax.dot_general(a, b, (((0,), (0,)), ((), ())), preferred_element_type=jnp.float32)


def dot_nn(a, b):
    return jnp.dot(a, b, preferred_element_type=jnp.float32)


def causal(block_t, first_row, first_col):
    rows = first_row + lax.broadcasted_iota(jnp.int32, block_t.shape, 0)
    cols = first_col + lax.broadcasted_iota(jnp.int32, block_t.shape, 1)
    return rows <= cols


mesh_ids = pl.DeviceIdType.MESH


def remote(src, dst, send, recv, target):
    return pltpu.make_async_remote_copy(
        src_ref=src, dst_ref=dst, send_sem=send, recv_sem=recv, device_id=target, device_id_type=mesh_ids
    )


def meet(partners):
    barrier = pltpu.get_barrier_semaphore()
    for condition, device in partners:
        if condition is None:
            pl.semaphore_signal(barrier, inc=1, device_id=device, device_id_type=mesh_ids)
        else:

            @pl.when(condition)
            def _():
                pl.semaphore_signal(barrier, inc=1, device_id=device, device_id_type=mesh_ids)

    count = 0
    for condition, device in partners:
        count = count + (1 if condition is None else condition.astype(jnp.int32))
    pl.semaphore_wait(barrier, count)


def flip(index, bit):
    return index + bit - 2 * bit * ((index // bit) % 2)


def places():
    s = lax.axis_index("seq")
    z = lax.axis_index("mp")
    return s, z


class Gather:
    def __init__(self, blocks, s, z, send, recv, half, base=0):
        self.at = blocks
        self.s = s
        self.z = z
        self.send = send
        self.recv = recv
        self.half = half
        self.base = base

    def rows(self, part):
        if part is None:
            return pl.ds(self.base, 2 * self.half)
        return pl.ds(self.base + part * self.half, self.half)

    def copy(self, index, span, part, target):
        ref = self.at.at[span, self.rows(part)]
        return remote(ref, ref, self.send.at[index], self.recv.at[index], (target, self.z))

    def begin(self):
        s, x, y, other = self.s, flip(self.s, 2), flip(self.s, 4), flip(self.s, 1)
        for one in (
            self.copy(0, s, 0, x),
            self.copy(1, s, 1, y),
            self.copy(2, s, 1, x),
            self.copy(3, s, 0, y),
            self.copy(6, s, None, other),
        ):
            one.start()

    def arrive_first(self):
        s, x, y = self.s, flip(self.s, 2), flip(self.s, 4)
        self.copy(0, x, 0, x).wait_recv()
        one = self.copy(4, x, 0, y)
        one.start()
        self.copy(1, y, 1, y).wait_recv()
        two = self.copy(5, y, 1, x)
        two.start()

    def arrive_neighbours(self):
        s, x, y, other = self.s, flip(self.s, 2), flip(self.s, 4), flip(self.s, 1)
        self.copy(2, x, 1, x).wait_recv()
        one = self.copy(7, x, None, other)
        one.start()
        self.copy(3, y, 0, y).wait_recv()
        two = self.copy(8, y, None, other)
        two.start()

    def arrive_diagonal(self):
        s, other = self.s, flip(self.s, 1)
        diagonal = flip(flip(s, 2), 4)
        self.copy(4, diagonal, 0, other).wait_recv()
        self.copy(5, diagonal, 1, other).wait_recv()
        one = self.copy(9, diagonal, None, other)
        one.start()

    def arrive_core(self, index):
        s = self.s
        other = flip(s, 1)
        span = (other, flip(other, 2), flip(other, 4), flip(flip(other, 2), 4))[index]
        self.copy(6 + index, span, None, other).wait_recv()
        return span

    def end(self):
        s, x, y, other = self.s, flip(self.s, 2), flip(self.s, 4), flip(self.s, 1)
        for index, span, part, target in (
            (0, s, 0, x),
            (1, s, 1, y),
            (2, s, 1, x),
            (3, s, 0, y),
            (4, x, 0, y),
            (5, y, 1, x),
            (6, s, None, other),
            (7, x, None, other),
            (8, y, None, other),
            (9, flip(x, 4), None, other),
        ):
            self.copy(index, span, part, target).wait_send()


gather_sems = 10


def spend(microseconds):
    return pl.CostEstimate(flops=microseconds * 10**9, bytes_accessed=10**6, transcendentals=0)


class Line:
    def __init__(self, blocks, core, s, z, send, recv):
        self.at = blocks
        self.core = core
        self.s = s
        self.z = z
        self.send = send
        self.recv = recv

    def ref(self, j):
        return self.at.at[j] if self.core is None else self.at.at[j, self.core]

    def up(self, hop, j):
        ref = self.ref(j)
        return remote(ref, ref, self.send.at[hop], self.recv.at[hop], (self.s, self.z + 1))

    def down(self, hop, j):
        ref = self.ref(j)
        return remote(ref, ref, self.send.at[3 + hop], self.recv.at[3 + hop], (self.s, self.z - 1))

    def across(self, index, j):
        ref = self.ref(j)
        return remote(ref, ref, self.send.at[6 + index], self.recv.at[6 + index], (flip(self.s, 1), self.z))

    def begin(self):
        z = self.z

        @pl.when(z < 3)
        def _():
            self.up(0, z).start()

        @pl.when(z > 0)
        def _():
            self.down(0, z).start()

        if self.core is not None:
            self.across(0, z).start()

    def hop(self, t):
        z = self.z

        @pl.when(z >= t)
        def _():
            self.up(t - 1, z - t).wait_recv()
            if self.core is not None:
                self.across(t, z - t).start()
            if t < 3:

                @pl.when(z < 3)
                def _():
                    self.up(t, z - t).start()

        @pl.when(z + t <= 3)
        def _():
            self.down(t - 1, z + t).wait_recv()
            if self.core is not None:
                self.across(3 + t, z + t).start()
            if t < 3:

                @pl.when(z > 0)
                def _():
                    self.down(t, z + t).start()

    def arrive_core(self):
        z = self.z
        other = 1 - self.core

        def wait(index, j):
            ref = self.at.at[j, other]
            remote(ref, ref, self.send.at[6 + index], self.recv.at[6 + index], (flip(self.s, 1), z)).wait_recv()

        wait(0, z)
        for t in (1, 2, 3):

            @pl.when(z >= t)
            def _():
                wait(t, z - t)

            @pl.when(z + t <= 3)
            def _():
                wait(3 + t, z + t)

    def end(self):
        z = self.z

        @pl.when(z < 3)
        def _():
            self.up(0, z).wait_send()

        @pl.when(z > 0)
        def _():
            self.down(0, z).wait_send()

        if self.core is not None:
            self.across(0, z).wait_send()
        for t in (1, 2, 3):

            @pl.when(z >= t)
            def _():
                if self.core is not None:
                    self.across(t, z - t).wait_send()
                if t < 3:

                    @pl.when(z < 3)
                    def _():
                        self.up(t, z - t).wait_send()

            @pl.when(z + t <= 3)
            def _():
                if self.core is not None:
                    self.across(3 + t, z + t).wait_send()
                if t < 3:

                    @pl.when(z > 0)
                    def _():
                        self.down(t, z + t).wait_send()


line_sems = 13


def norm_rows(values):
    centred = values - jnp.mean(values, axis=-1, keepdims=True)
    inverse = lax.rsqrt(jnp.mean(centred * centred, axis=-1, keepdims=True) + norm_eps)
    return (centred * inverse, inverse)


class Reduce:
    def __init__(self, rows, multiply, width, s, z, out, inn, own, send, recv):
        self.rows = rows
        self.multiply = multiply
        self.width = width
        self.s = s
        self.z = z
        self.out = out
        self.inn = inn
        self.own = own
        self.send = send
        self.recv = recv
        chip = s // 2
        self.chip = chip
        self.cx = flip(chip, 1)
        self.cy = flip(chip, 2)
        self.cd = flip(self.cx, 2)

    def copy(self, index):
        target = flip(self.s, 2) if index in (0, 2, 5) else flip(self.s, 4)
        return remote(
            self.out.at[index], self.inn.at[index], self.send.at[index], self.recv.at[index], (target, self.z)
        )

    def give(self, first, second):
        both = jnp.concatenate([self.rows(*first[1:3]), self.rows(*second[1:3])], axis=0)
        for job in (first, second):
            if job[3] is not None:
                self.copy(job[3]).wait_recv()

        def one(part, _):
            wide = pl.ds(pl.multiple_of(part * 512, 512), 512)
            value = self.multiply(both, wide)
            for job, piece in ((first, value[:128]), (second, value[128:])):
                if job[3] is not None:
                    piece = piece + self.inn[job[3], :, wide].astype(jnp.float32)
                self.out[job[0], :, wide] = piece.astype(jnp.bfloat16)
            return 0

        lax.fori_loop(0, self.width // 512, one, 0)
        self.copy(first[0]).start()
        self.copy(second[0]).start()

    def begin(self):
        self.give((0, self.cd, 0, None), (1, self.cd, 1, None))

    def second(self):
        self.give((2, self.cx, 0, None), (4, self.cy, 0, 0))

    def third(self):
        self.copy(2).wait_send()
        self.copy(4).wait_send()
        self.give((5, self.cx, 1, 1), (3, self.cy, 1, None))

    def keep(self):
        both = jnp.concatenate([self.rows(self.chip, 0), self.rows(self.chip, 1)], axis=0)

        def one(part, _):
            wide = pl.ds(pl.multiple_of(part * 512, 512), 512)
            self.own[:, wide] = self.multiply(both, wide)
            return 0

        lax.fori_loop(0, self.width // 512, one, 0)

    def finish(self, half, use):
        first, second = (2, 4) if half == 0 else (3, 5)
        self.copy(first).wait_recv()
        self.copy(second).wait_recv()

        def one(part, _):
            at = pl.ds(pl.multiple_of(part * 32, 32), 32)
            row = pl.multiple_of(part * 64 + half * 32, 32)
            total = (
                self.own[pl.ds(pl.multiple_of(half * 128 + part * 32, 32), 32), :]
                + self.inn[first, at, :].astype(jnp.float32)
                + self.inn[second, at, :].astype(jnp.float32)
            )
            use(row, total)
            return 0

        lax.fori_loop(0, 4, one, 0)

    def end(self):
        for index in (0, 1, 3, 5):
            self.copy(index).wait_send()


def some_rows(load, half):
    return jnp.concatenate([load(64 * j + 32 * half) for j in range(4)], axis=0)


def front_kernel(
    x_ref, w_qkv_ref, w_out_ref, b_qkv_ref, a_out_ref, a_in_ref, b_od_ref, table_ref, cot_ref, set_ref,
    x_own_ref, m_own_ref, residual_ref, o_eff_ref, b_sel_ref, a_sel_ref, lse_ref,
    u_out, q_out, k_out, v_out, low_out, table_out, mixed_out, w_cat_out, cots_ref,
    u_ref, w_buf, w_cat, q_buf, k_buf, v_buf, low_buf, tables, mixed, o_all, o_big, sib, out_buf, in_buf, own_sum,
    b_small, a_small,
    a2a_send, a2a_recv, tab_send, tab_recv, ag_send, ag_recv, ag2_send, ag2_recv, w_send, w_recv, o_send, o_recv, cot_send, cot_recv,
    small_send, small_recv, sib_send, sib_recv, red_send, red_recv, local_sem, store_sem,
):
    f32 = jnp.float32
    bf16 = jnp.bfloat16
    s, z = places()
    core = s % 2
    chip = s // 2
    other = flip(s, 1)
    zs = [flip(z, 1), flip(z, 2), 3 - z]
    columns = pl.ds(pl.multiple_of(chip * HDIM, HDIM), HDIM)
    half_rows = pl.ds(pl.multiple_of(core * 1024, 1024), 1024)
    owns = [
        pltpu.make_async_copy(w_qkv_ref.at[:, half_rows, columns], w_buf.at[z, core], local_sem.at[0]),
        pltpu.make_async_copy(w_out_ref.at[columns, half_rows], o_all.at[z, core], local_sem.at[1]),
        pltpu.make_async_copy(b_qkv_ref.at[:, :, :, columns], b_small.at[z], local_sem.at[2]),
        pltpu.make_async_copy(a_out_ref.at[:, :, columns], a_small.at[z], local_sem.at[3]),
        pltpu.make_async_copy(cot_ref, cots_ref.at[z], local_sem.at[4]),
    ]
    for one in owns:
        one.start()
    tables[s] = table_ref[...]
    meet([(None, (other, z)), (None, (flip(s, 2), z)), (None, (flip(s, 4), z))] + [(None, (s, j)) for j in zs])

    swaps = [
        remote(x_ref.at[j], x_own_ref.at[z], a2a_send.at[d], a2a_recv.at[d], (s, j)) for d, j in enumerate(zs)
    ]
    for one in swaps:
        one.start()
    table_gather = Gather(tables, s, z, tab_send, tab_recv, 128)
    table_gather.begin()
    x_own_ref[z] = x_ref[z]

    def arrived(d):
        j = zs[d]
        remote(x_ref.at[j], x_own_ref.at[j], a2a_send.at[d], a2a_recv.at[d], (s, j)).wait_recv()

    def normalize(j):
        def one(part, _):
            normed, _ = norm_rows(x_own_ref[j, pl.ds(pl.multiple_of(part * 32, 32), 32), :].astype(f32))
            u_ref[s, pl.ds(pl.multiple_of(j * 64 + part * 32, 32), 32), :] = normed.astype(bf16)
            return 0

        lax.fori_loop(0, 2, one, 0)

    near = Gather(u_ref, s, z, ag_send, ag_recv, 64, pl.multiple_of((z // 2) * 128, 128))
    rest = Gather(u_ref, s, z, ag2_send, ag2_recv, 64, pl.multiple_of((1 - z // 2) * 128, 128))
    arrived(0)
    normalize(z)
    normalize(zs[0])
    near.begin()
    table_gather.arrive_first()
    table_gather.arrive_neighbours()
    for one in owns:
        one.wait()
    near.arrive_first()
    arrived(1)
    arrived(2)
    line = Line(w_buf, core, s, z, w_send, w_recv)
    line.begin()
    smalls = []
    for d, j in enumerate(zs):
        smalls.append(remote(b_small.at[z], b_small.at[z], small_send.at[d], small_recv.at[d], (s, j)))
        smalls.append(remote(a_small.at[z], a_small.at[z], small_send.at[3 + d], small_recv.at[3 + d], (s, j)))
    for one in smalls:
        one.start()
    normalize(zs[1])
    normalize(zs[2])
    rest.begin()
    table_gather.arrive_diagonal()
    near.arrive_neighbours()
    near.arrive_diagonal()
    rest.arrive_first()
    line.hop(1)
    rest.arrive_neighbours()
    rest.arrive_diagonal()
    for index in range(4):
        near.arrive_core(index)
        rest.arrive_core(index)
        table_gather.arrive_core(index)
    line.hop(2)
    stores = [pltpu.make_async_copy(u_ref, u_out, store_sem.at[0])]
    stores[0].start()
    mine = set_ref[z]
    a48 = a_in_ref[mine, 0:3].reshape(48, -1)

    def lows(t, _):
        low_buf[t] = (adapt_scale * dot_nt(u_ref[t], a48)).astype(bf16)
        return 0

    lax.fori_loop(0, 8, lows, 0)
    for d, j in enumerate(zs):
        remote(b_small.at[j], b_small.at[j], small_send.at[d], small_recv.at[d], (s, j)).wait_recv()
        remote(a_small.at[j], a_small.at[j], small_send.at[3 + d], small_recv.at[3 + d], (s, j)).wait_recv()
    for j in range(4):
        b_sel_ref[j] = b_small[j, mine].reshape(48, HDIM)
        a_sel_ref[j] = a_small[j, mine]

    def merge(index, _):
        j = index // 3
        part = index % 3
        head = (2 * core + j) % 4
        b_part = b_sel_ref[head, pl.ds(pl.multiple_of(part * 16, 16), 16), :]
        column = pl.multiple_of(((j // 2) * 6 + part * 2 + j % 2) * HDIM, HDIM)
        for side in range(2):
            a_part = a_in_ref[mine, part, :, pl.ds(side * 1024, 1024)]
            merged = adapt_scale * dot_tn(a_part, b_part)
            w_cat[pl.ds(side * 1024, 1024), pl.ds(column, HDIM)] = (
                w_buf[head, side, part].astype(f32) + merged
            ).astype(bf16)
        return 0

    line.hop(3)
    o_line = Line(o_all, core, s, z, o_send, o_recv)
    o_line.begin()
    cot_line = Line(cots_ref, None, s, z, cot_send, cot_recv)
    line.arrive_core()
    lax.fori_loop(0, 6, merge, 0)
    left = lax.broadcasted_iota(jnp.int32, (256, HDIM), 1) < HDIM // 2

    def project(t, _):
        u = u_ref[t]
        packed = tables[t]
        turned = pltpu.roll(packed, HDIM // 2, 1)
        cos = jnp.where(left, packed, turned)
        sin = jnp.where(left, turned, -packed)
        rows = pl.ds(pl.multiple_of(t * 256, 256), 256)
        for part, out in enumerate((q_buf, k_buf, v_buf)):
            raw = dot_nn(u, w_cat[:, 256 * part : 256 * part + 256])
            for head in range(2):
                piece = raw[:, HDIM * head : HDIM * head + HDIM]
                if part < 2:
                    piece = piece * cos - pltpu.roll(piece, HDIM // 2, 1) * sin
                out[rows, HDIM * head : HDIM * head + HDIM] = piece.astype(bf16)
        return 0

    def project_all(t, _):
        project(t, 0)
        for step, at in ((1, 2), (2, 6)):

            @pl.when(t == at)
            def _():
                o_line.hop(step)

        return 0

    lax.fori_loop(0, 8, project_all, 0)
    cot_line.begin()
    stores += [
        pltpu.make_async_copy(source, target, store_sem.at[1 + i])
        for i, (source, target) in enumerate(
            ((q_buf, q_out), (k_buf, k_out), (v_buf, v_out), (low_buf, low_out), (tables, table_out))
        )
    ]
    for one in stores[1:]:
        one.start()

    tile = attn_tile
    factor = log2e / math.sqrt(HDIM)

    def attend(index, _):
        head = index // 4
        i = index % 4
        lanes = pl.ds(pl.multiple_of(head * HDIM, HDIM), HDIM)
        here = pl.ds(pl.multiple_of(i * tile, tile), tile)
        q = q_buf[here, lanes]

        def fold(j, carry, diagonal):
            top, total, acc = carry
            at = pl.ds(pl.multiple_of(j * tile, tile), tile)
            scores = dot_nt(k_buf[at, lanes], q)
            if diagonal:
                scores = jnp.where(causal(scores, 0, 0), scores, far_below)
            new_top = jnp.maximum(top, jnp.max(scores, axis=0, keepdims=True))
            weight = jnp.exp2(scores * factor - new_top * factor)
            keep = jnp.exp2((top - new_top) * factor)
            total = total * keep + jnp.sum(weight, axis=0, keepdims=True)
            acc = acc * keep + dot_tn(v_buf[at, lanes], weight.astype(bf16))
            return (new_top, total, acc)

        carry = (
            jnp.full((1, tile), far_below, f32),
            jnp.zeros((1, tile), f32),
            jnp.zeros((HDIM, tile), f32),
        )
        carry = lax.fori_loop(0, i, lambda j, c: fold(j, c, False), carry)
        top, total, acc = fold(i, carry, True)
        mixed[here, lanes] = jnp.transpose(acc / total).astype(bf16)
        lse_ref[head, i] = top * factor + jnp.log2(total)
        return 0

    def attend_all(index, _):
        attend(index, 0)

        @pl.when(index == 3)
        def _():
            o_line.hop(3)

        return 0

    lax.fori_loop(0, 8, attend_all, 0)

    def span_rows(span, first, count):
        return pl.ds(pl.multiple_of(span * 256 + first, 128), count)

    crosses = [
        remote(mixed.at[span_rows(2 * c + 1 - core, 0, 256)], sib.at[c], sib_send.at[c], sib_recv.at[c], (other, z))
        for c in range(4)
    ]
    for one in crosses:
        one.start()
    stores.append(pltpu.make_async_copy(mixed, mixed_out, store_sem.at[6]))
    stores[-1].start()
    o_line.arrive_core()
    b_row = b_od_ref[mine, 0]

    def merge_out(j, _):
        head = (2 * core + j) % 4
        for side in range(2):
            wide = slice(side * 1024, side * 1024 + 1024)
            merged = adapt_scale * dot_tn(a_sel_ref[head], b_row[:, wide])
            o_big[pl.ds(pl.multiple_of(j * HDIM, HDIM), HDIM), wide] = (
                o_all[head, side].astype(f32) + merged
            ).astype(bf16)
        return 0

    lax.fori_loop(0, 4, merge_out, 0)
    o_eff_ref[...] = o_big[0 : 2 * HDIM, :]
    for one in crosses:
        one.wait_recv()

    def rows_of(c, half):
        def load(row):
            at = pl.ds(pl.multiple_of((2 * c + core) * 256 + row, 32), 32)
            return jnp.concatenate([mixed[at, :], sib[c, pl.ds(row, 32), :]], axis=1)

        return some_rows(load, half)

    reduce = Reduce(
        rows_of, lambda rows, wide: dot_nn(rows, o_big[:, wide]), x_ref.shape[2], s, z,
        out_buf, in_buf, own_sum, red_send, red_recv,
    )
    reduce.begin()
    reduce.keep()
    cot_line.hop(1)
    reduce.second()
    lax.fori_loop(6, 12, merge, 0)
    stores.append(pltpu.make_async_copy(w_cat, w_cat_out, store_sem.at[7]))
    stores[-1].start()
    reduce.third()
    def settle(row, total):
        at = pl.ds(row, 32)
        x = x_own_ref[row // 64, pl.ds(pl.multiple_of(row % 64, 32), 32), :].astype(f32)
        residual = x + total
        residual_ref[at, :] = residual
        normed, _ = norm_rows(residual)
        m_own_ref[at, :] = normed.astype(bf16)

    reduce.finish(0, settle)
    cot_line.hop(2)
    reduce.finish(1, settle)
    cot_line.hop(3)
    for one in stores:
        one.wait()
    for one in swaps + smalls + crosses:
        one.wait_send()
    line.end()
    o_line.end()
    cot_line.end()
    near.end()
    rest.end()
    table_gather.end()
    reduce.end()


def front_layer(x, w_qkv, w_out, b_qkv, a_out, a_in, b_out_down, table, cotangent, set_index):
    bf16 = jnp.bfloat16
    f32 = jnp.float32
    vmem = pl.BlockSpec(memory_space=pltpu.VMEM)
    anywhere = pl.BlockSpec(memory_space=pl.ANY)
    width = x.shape[2]
    shape = jax.ShapeDtypeStruct
    dma = pltpu.SemaphoreType.DMA
    vm = pltpu.VMEM
    return pl.pallas_call(
        front_kernel,
        in_specs=[vmem] + [anywhere] * 4 + [vmem] * 3 + [anywhere, pl.BlockSpec(memory_space=pltpu.SMEM)],
        out_specs=[vmem] * 7 + [anywhere] * 9,
        out_shape=[
            shape((4, 64, width), bf16),
            shape((256, width), bf16),
            shape((256, width), f32),
            shape((256, width), bf16),
            shape((4, 48, HDIM), bf16),
            shape((4, 16, HDIM), bf16),
            shape((2, 4, 1, attn_tile), f32),
            shape((8, 256, width), bf16),
            shape((2048, 256), bf16),
            shape((2048, 256), bf16),
            shape((2048, 256), bf16),
            shape((8, 256, 48), bf16),
            shape((8, 256, HDIM), f32),
            shape((2048, 256), bf16),
            shape((width, 1536), bf16),
            shape((4, 4, 64, width), bf16),
        ],
        scratch_shapes=[
            vm((8, 256, width), bf16),
            vm((4, 2, 3, 1024, HDIM), bf16),
            vm((width, 1536), bf16),
            vm((2048, 256), bf16),
            vm((2048, 256), bf16),
            vm((2048, 256), bf16),
            vm((8, 256, 48), bf16),
            vm((8, 256, HDIM), f32),
            vm((2048, 256), bf16),
            vm((4, 2, HDIM, 1024), bf16),
            vm((4 * HDIM, width), bf16),
            vm((4, 256, 256), bf16),
            vm((6, 128, width), bf16),
            vm((6, 128, width), bf16),
            vm((256, width), f32),
            vm((4, 4, 3, 16, HDIM), bf16),
            vm((4, 4, 16, HDIM), bf16),
        ]
        + [
            dma((count,))
            for count in (3, 3, 10, 10, 10, 10, 10, 10, 13, 13, 13, 13, 13, 13, 6, 6, 4, 4, 6, 6, 5, 8)
        ],
        cost_estimate=spend(150),
        compiler_params=pltpu.CompilerParams(
            collective_id=1, has_side_effects=True, vmem_limit_bytes=58 << 20
        ),
    )(x, w_qkv, w_out, b_qkv, a_out, a_in, b_out_down, table, cotangent, set_index)


def turn_back(gradient, packed):
    left = lax.broadcasted_iota(jnp.int32, packed.shape, 1) < HDIM // 2
    turned = pltpu.roll(packed, HDIM // 2, 1)
    cos = jnp.where(left, packed, turned)
    sin = jnp.where(left, turned, -packed)
    return gradient * cos + pltpu.roll(gradient, HDIM // 2, 1) * sin


def back_kernel(
    g_ref, o_eff_ref, mixed_in, b_od_ref, q_in, k_in, v_in, lse_ref, table_in,
    grad_b_ref, grad_ad_ref, grad_a_ref, grad_bd_ref, down1_ref, down2_ref, down3_ref, set_ref,
    dq_ref, dk_ref, dv_ref, rank_ref, chunk_ref, pair_ref, g_out, got1_ref, got2_ref,
    mixed_ref, q_ref, k_ref, v_ref, table_ref, down2_buf, got3_buf, pair_sum, g_buf, gm_buf, dots, dk_acc, dv_acc, chunk_src, chunk_sib, chunk_sum, chunk_in,
    send, recv, down_send, down_recv, cs_send, cs_recv, cx_send, cx_recv, store_sem, load_sem,
):
    f32 = jnp.float32
    bf16 = jnp.bfloat16
    s, z = places()
    loads = [
        pltpu.make_async_copy(source, target, load_sem.at[i])
        for i, (source, target) in enumerate(
            (
                (mixed_in, mixed_ref),
                (q_in, q_ref),
                (k_in, k_ref),
                (v_in, v_ref),
                (table_in, table_ref),
                (down2_ref, down2_buf),
            )
        )
    ]
    for one in loads:
        one.start()
    core = s % 2
    chip = s // 2
    other = flip(s, 1)
    sx = flip(s, 2)
    sy = flip(s, 4)
    sd = flip(sx, 4)
    meet([(None, (t, z)) for t in (other, sx, sy, sd)] + [(None, (s, flip(z, 1))), (None, (s, flip(z, 2)))])
    g_buf[s] = g_ref[...]
    gather = Gather(g_buf, s, z, send, recv, 128)
    gather.begin()
    results = [
        remote(down3_ref, got3_buf, down_send.at[0], down_recv.at[0], (s, flip(z, 1))),
        remote(down1_ref, got1_ref, down_send.at[1], down_recv.at[1], (s, flip(z, 1))),
    ]
    for one in results:
        one.start()
    onward = remote(pair_sum, got2_ref, down_send.at[2], down_recv.at[2], (s, flip(z, 2)))
    member = set_ref[z]
    tile = attn_tile
    scale = 1.0 / math.sqrt(HDIM)
    factor = log2e * scale
    dk_acc[...] = jnp.zeros_like(dk_acc)
    dv_acc[...] = jnp.zeros_like(dv_acc)

    def store(t):
        return pltpu.make_async_copy(g_buf.at[t], g_out.at[t], store_sem.at[t])

    def chip_rows(c):
        here = pl.ds(pl.multiple_of(c * tile, tile), tile)

        def head_rows(part, _):
            t = 2 * c + part
            store(t).start()
            g = g_buf[t]
            back = dot_nt(g, o_eff_ref[...]).astype(bf16)
            gm_buf[pl.ds(pl.multiple_of(part * 256, 256), 256), :] = back
            product = back.astype(f32) * mixed_ref[
                pl.ds(pl.multiple_of(t * 256, 256), 256), :
            ].astype(f32)
            for head in range(2):
                turned = jnp.transpose(product[:, HDIM * head : HDIM * head + HDIM])
                dots[head, :, pl.ds(pl.multiple_of(part * 256, 256), 256)] = jnp.sum(turned, axis=0, keepdims=True)
            rank_ref[t] = (adapt_scale * dot_nt(g, b_od_ref[member, 0])).astype(bf16)
            return 0

        lax.fori_loop(0, 2, head_rows, 0)

        def one_head(head, _):
            lanes = pl.ds(pl.multiple_of(head * HDIM, HDIM), HDIM)
            q = q_ref[here, lanes]
            go = gm_buf[:, lanes]
            row_dots = dots[head]
            lse = lse_ref[head, c]

            def fold(j, dq, diagonal):
                at = pl.ds(pl.multiple_of(j * tile, tile), tile)
                k = k_ref[at, lanes]
                scores = dot_nt(k, q)
                weight = jnp.exp2(scores * factor - lse)
                if diagonal:
                    weight = jnp.where(causal(scores, 0, 0), weight, 0.0)
                grad_weight = dot_nt(v_ref[at, lanes], go)
                grad_scores = (weight * (grad_weight - row_dots)).astype(bf16)
                dv_acc[at, lanes] += dot_nn(weight.astype(bf16), go)
                dk_acc[at, lanes] += dot_nn(grad_scores, q)
                return dq + dot_tn(grad_scores, k)

            dq = lax.fori_loop(0, c, lambda j, total: fold(j, total, False), jnp.zeros((tile, HDIM), f32))
            dq = fold(c, dq, True)
            dq_ref[here, lanes] = turn_back(dq * scale, table_ref[here, :]).astype(bf16)
            return 0

        lax.fori_loop(0, 2, one_head, 0)

    def fill(one, _):
        whole = jnp.zeros((48, dk_acc.shape[0]), f32)
        split = jnp.zeros((48, dk_acc.shape[0]), f32)
        for seq in range(4):
            used = (set_ref[seq] == one).astype(f32)
            whole += used * jnp.concatenate([grad_a_ref[seq], grad_bd_ref[seq]], axis=0)
            split += used * jnp.concatenate([grad_b_ref[seq, 0], grad_b_ref[seq, 1], grad_ad_ref[seq]], axis=0)
        for part in range(2):
            rows = slice(24 * part, 24 * part + 24)
            chunk_src[2 * one + part] = jnp.concatenate([whole[rows], split[rows]], axis=0).astype(bf16)
        return 0

    lax.fori_loop(0, 4, fill, 0)
    crosses = [
        remote(chunk_src.at[2 * c + 1 - core], chunk_sib.at[c], cs_send.at[c], cs_recv.at[c], (other, z))
        for c in range(4)
    ]
    for one in crosses:
        one.start()
    for one in loads:
        one.wait()
    around = [
        remote(chunk_sum.at[t // 2], chunk_in.at[d], cx_send.at[d], cx_recv.at[d], (t, z))
        for d, t in enumerate((sx, sy, sd))
    ]

    def total_chunks(c, _):
        chunk_sum[c] = (chunk_src[2 * c + core].astype(f32) + chunk_sib[c].astype(f32)).astype(bf16)
        return 0

    def pair_rows(seq, _):
        for first, target in ((0, pair_sum), (2, pair_ref)):
            target[seq] = (
                down2_buf[first + seq].astype(f32) + got3_buf[first + seq].astype(f32)
            ).astype(bf16)
        return 0

    def visit(step, _):
        @pl.when(step == 0)
        def _():
            gather.arrive_core(0)

        @pl.when(step == 1)
        def _():
            gather.arrive_first()
            for one in crosses:
                one.wait_recv()
            lax.fori_loop(0, 4, total_chunks, 0)
            for one in around:
                one.start()
            gather.arrive_neighbours()
            results[0].wait_recv()
            lax.fori_loop(0, 2, pair_rows, 0)
            onward.start()
            gather.arrive_core(1)

        @pl.when(step == 2)
        def _():
            gather.arrive_core(2)

        @pl.when(step == 3)
        def _():
            gather.arrive_diagonal()
            gather.arrive_core(3)

        by_x = step % 2
        by_y = step // 2
        chip_rows(chip + by_x * (1 - 2 * (chip % 2)) + by_y * (2 - 4 * (chip // 2)))
        return 0

    lax.fori_loop(0, 4, visit, 0)

    def last(j, _):
        at = pl.ds(pl.multiple_of(j * tile, tile), tile)
        for head in range(2):
            lanes = slice(HDIM * head, HDIM * head + HDIM)
            dk_ref[at, lanes] = turn_back(dk_acc[at, lanes] * scale, table_ref[at, :]).astype(bf16)
            dv_ref[at, lanes] = dv_acc[at, lanes].astype(bf16)
        return 0

    lax.fori_loop(0, 4, last, 0)
    for one in around:
        one.wait_recv()
    chunk = chunk_sum[chip].astype(f32)
    for d in range(3):
        chunk += chunk_in[d].astype(f32)
    chunk_ref[...] = chunk
    for t in range(8):
        store(t).wait()
    gather.end()
    results[1].wait_recv()
    onward.wait()
    for one in crosses + around + results:
        one.wait_send()


def back_layer(*operands):
    bf16 = jnp.bfloat16
    f32 = jnp.float32
    vmem = pl.BlockSpec(memory_space=pltpu.VMEM)
    anywhere = pl.BlockSpec(memory_space=pl.ANY)
    width = operands[0].shape[1]
    shape = jax.ShapeDtypeStruct
    dma = pltpu.SemaphoreType.DMA
    vm = pltpu.VMEM
    return pl.pallas_call(
        back_kernel,
        in_specs=[vmem, vmem, anywhere, vmem, anywhere, anywhere, anywhere, vmem, anywhere]
        + [vmem] * 4
        + [anywhere] * 3
        + [pl.BlockSpec(memory_space=pltpu.SMEM)],
        out_specs=[vmem] * 6 + [anywhere] * 3,
        out_shape=[
            shape((2048, 256), bf16),
            shape((2048, 256), bf16),
            shape((2048, 256), bf16),
            shape((8, 256, 16), bf16),
            shape((48, width), f32),
            shape((2, 64, width), bf16),
            shape((8, 256, width), bf16),
            shape((4, 64, width), bf16),
            shape((2, 64, width), bf16),
        ],
        scratch_shapes=[
            vm((2048, 256), bf16),
            vm((2048, 256), bf16),
            vm((2048, 256), bf16),
            vm((2048, 256), bf16),
            vm((2048, HDIM), f32),
            vm((4, 64, width), bf16),
            vm((4, 64, width), bf16),
            vm((2, 64, width), bf16),
            vm((8, 256, width), bf16),
            vm((512, 256), bf16),
            vm((2, 1, 512), f32),
            vm((2048, 256), f32),
            vm((2048, 256), f32),
            vm((8, 48, width), bf16),
            vm((4, 48, width), bf16),
            vm((4, 48, width), bf16),
            vm((3, 48, width), bf16),
        ]
        + [dma((count,)) for count in (gather_sems, gather_sems, 3, 3, 4, 4, 3, 3, 8, 6)],
        cost_estimate=spend(60),
        compiler_params=pltpu.CompilerParams(
            collective_id=3, has_side_effects=True, vmem_limit_bytes=52 << 20
        ),
    )(*operands)


def mlp_line_kernel(
    m_ref, residual_ref, cots_ref, w_gu_ref, w_d_ref, a_ref, b_ref, ad_ref, bd_ref, set_ref,
    g_ref, grad_res_ref, down0_ref, down1_ref, down2_ref, down3_ref, grad_b_ref, grad_ad_ref, grad_a_ref, grad_bd_ref,
    m_buf, wg, wu, wd, cot_buf, back_acc, down_acc, ranks, slots, r1, r2, r3, r4, r5, stage,
    up_send, up_recv, dn_send, dn_recv, send1, recv1, send4, recv4, send5, recv5, send23, recv23,
    weight_sem, cot_sem, stage_sem,
):
    s, z = places()
    tiles = wg.shape[0]
    tile = wg.shape[2]
    f32 = jnp.float32
    bf16 = jnp.bfloat16
    middle = z * (3 - z) == 2
    at_end = z * (3 - z) == 0
    pair = flip(z, 1)
    opposite = 3 - z
    inner = 1 + z // 2
    high = z // 2
    ids = [z, pair, 2 - high, 3 - 3 * high]
    far = 3 - 3 * high

    def load_tile(h):
        columns = pl.ds(h * tile if isinstance(h, int) else pl.multiple_of(h * tile, tile), tile)
        return [
            pltpu.make_async_copy(w_gu_ref.at[0, :, columns], wg.at[h], weight_sem.at[3 * h]),
            pltpu.make_async_copy(w_gu_ref.at[1, :, columns], wu.at[h], weight_sem.at[3 * h + 1]),
            pltpu.make_async_copy(w_d_ref.at[columns, :], wd.at[h], weight_sem.at[3 * h + 2]),
        ]

    for h in range(tiles):
        for one in load_tile(h):
            one.start()

    others = [z, pair, flip(z, 2), opposite]
    down_refs = (down0_ref, down1_ref, down2_ref, down3_ref)

    def load_cot(seq):
        return [pltpu.make_async_copy(cots_ref.at[j, seq], cot_buf.at[j], cot_sem.at[j]) for j in range(4)]

    for one in load_cot(z):
        one.start()

    meet([(z < 3, (s, z + 1)), (z > 0, (s, z - 1)), (None, (s, flip(z, 2)))])
    m_buf[z] = m_ref[...]

    def up(hop, j):
        return remote(m_buf.at[j], m_buf.at[j], up_send.at[hop], up_recv.at[hop], (s, z + 1))

    def down(hop, j):
        return remote(m_buf.at[j], m_buf.at[j], dn_send.at[hop], dn_recv.at[hop], (s, z - 1))

    def begin():
        @pl.when(z < 3)
        def _():
            up(0, z).start()

        @pl.when(z > 0)
        def _():
            down(0, z).start()

    def hop(t):
        @pl.when(z >= t)
        def _():
            up(t - 1, z - t).wait_recv()
            if t < 3:

                @pl.when(z < 3)
                def _():
                    up(t, z - t).start()

        @pl.when(z + t <= 3)
        def _():
            down(t - 1, z + t).wait_recv()
            if t < 3:

                @pl.when(z > 0)
                def _():
                    down(t, z + t).start()

    def hop_end():
        @pl.when(z < 3)
        def _():
            up(0, z).wait_send()

        @pl.when(z > 0)
        def _():
            down(0, z).wait_send()

        for t in (1, 2):

            @pl.when((z >= t) & (z < 3))
            def _():
                up(t, z - t).wait_send()

            @pl.when((z + t <= 3) & (z > 0))
            def _():
                down(t, z + t).wait_send()

    def piece(p):
        return pl.ds(p * 64 if isinstance(p, int) else pl.multiple_of(p * 64, 64), 64)

    def copy1():
        return remote(slots.at[1], r1, send1.at[0], recv1.at[0], (s, pair))

    def copy2():
        return remote(slots.at[2], r2, send23.at[0], recv23.at[0], (s, opposite))

    def copy3():
        return remote(slots.at[2], r3, send23.at[1], recv23.at[1], (s, inner))

    def copy4(p):
        return remote(slots.at[3, piece(p)], r4.at[piece(p)], send4.at[p], recv4.at[p], (s, far))

    def copy5(p):
        return remote(slots.at[3, piece(p)], r5.at[piece(p)], send5.at[p], recv5.at[p], (s, inner))

    def stage_copies(seq):
        return [
            pltpu.make_async_copy(stage.at[others[d]], down_refs[d].at[seq], stage_sem.at[d]) for d in range(4)
        ]

    def in_maps(seq):
        return a_ref[set_ref[seq], 3:5].reshape(32, -1)

    def sequence(slot):
        return sum((slot == i).astype(jnp.int32) * one for i, one in enumerate(ids + [z]))

    def add(slot, extra):
        def one(p, _):
            slots[slot, piece(p), :] = (
                slots[slot, piece(p), :].astype(f32) + extra[piece(p), :].astype(f32)
            ).astype(bf16)
            return 0

        lax.fori_loop(0, 4, one, 0)

    begin()

    def chunk(slot, _):
        seq = sequence(slot)
        member = set_ref[seq]
        for one in load_cot(seq):
            one.wait()
        ranks[:, 0:32] = adapt_scale * dot_nt(m_buf[seq], in_maps(seq))
        ranks[:, 32:48] = adapt_scale * dot_nt(cot_buf[...].reshape(256, -1), bd_ref[member, 1])
        ranks[:, 48:96] = jnp.zeros((256, 48), f32)
        back_acc[...] = jnp.zeros_like(back_acc)
        down_acc[...] = jnp.zeros_like(down_acc)

        def step(h, _):
            columns = pl.ds(pl.multiple_of(h * tile, tile), tile)

            @pl.when(slot == 0)
            def _():
                for one in load_tile(h):
                    one.wait()

            @pl.when((slot == 3) & (h == 1) & middle)
            def _():
                copy1().start()

            low = ranks[...].astype(bf16)
            low_gate = low[:, 0:16]
            low_up = low[:, 16:32]
            low_cot = low[:, 32:48]
            bg = b_ref[member, 0, :, columns]
            bu = b_ref[member, 1, :, columns]
            ad = ad_ref[member, :, columns]
            rows = m_buf[seq]
            cot = cot_buf[...].reshape(256, -1)
            gate = dot_nn(rows, wg[h]) + dot_nn(low_gate, bg)
            up_value = dot_nn(rows, wu[h]) + dot_nn(low_up, bu)
            grad_act = dot_nt(cot, wd[h]) + dot_nn(low_cot, ad)
            sig = jax.nn.sigmoid(gate)
            act = (gate * sig * up_value).astype(bf16)
            grad_up = (grad_act * gate * sig).astype(bf16)
            grad_gate = (grad_act * up_value * sig * (1.0 + gate * (1.0 - sig))).astype(bf16)
            for part in range(4):
                wide = pl.ds(part * 512, 512)
                back_acc[:, wide] += dot_nt(grad_gate, wg[h, wide, :]) + dot_nt(grad_up, wu[h, wide, :])
                down_acc[:, wide] += dot_nn(act, wd[h, :, wide])
            ranks[:, 48:64] += dot_nt(act, ad)
            ranks[:, 64:80] += dot_nt(grad_gate, bg)
            ranks[:, 80:96] += dot_nt(grad_up, bu)
            grad_b_ref[seq, 0, :, columns] = dot_tn(low_gate, grad_gate)
            grad_b_ref[seq, 1, :, columns] = dot_tn(low_up, grad_up)
            grad_ad_ref[seq, :, columns] = dot_tn(low_cot, act)
            return 0

        lax.fori_loop(0, tiles, step, 0)
        for t in (1, 2, 3):

            @pl.when(slot == t - 1)
            def _():
                hop(t)

        back_rank = (adapt_scale * ranks[:, 64:96]).astype(bf16)
        slots[slot] = (back_acc[...] + dot_nn(back_rank, in_maps(seq))).astype(bf16)

        @pl.when((slot == 1) & at_end)
        def _():
            copy1().start()

        @pl.when((slot == 2) & at_end)
        def _():
            copy3().start()

        @pl.when((slot == 3) & at_end)
        def _():
            copy5(0).start()
            copy5(1).start()

        @pl.when((slot == 3) & middle)
        def _():
            copy3().wait_recv()
            add(2, r3)
            copy2().start()

        low_down = (adapt_scale * ranks[:, 48:64]).astype(bf16)
        grad_a_ref[seq] = dot_tn(back_rank, m_buf[seq])
        grad_bd_ref[seq] = dot_tn(low_down, cot_buf[...].reshape(256, -1))

        @pl.when(slot > 0)
        def _():
            for one in stage_copies(seq):
                one.wait()

        own = (slot == 0).astype(f32)
        value = down_acc[...] + dot_nn(low_down, bd_ref[member, 1]) + own * residual_ref[...]
        stage[...] = value.astype(bf16).reshape(4, 64, -1)
        for one in stage_copies(seq):
            one.start()
        for one in load_cot(sequence(slot + 1)):
            one.start()
        return 0

    lax.fori_loop(0, 4, chunk, 0)

    @pl.when(at_end)
    def _():
        for p in (2, 3):
            copy5(p - 2).wait_send()
            copy5(p).start()

    @pl.when(middle)
    def _():
        def one(p, _):
            copy5(p).wait_recv()
            slots[3, piece(p), :] = (
                slots[3, piece(p), :].astype(f32) + r5[piece(p), :].astype(f32)
            ).astype(bf16)
            copy4(p).start()
            return 0

        lax.fori_loop(0, 4, one, 0)

    copy1().wait_recv()
    add(0, r1)

    @pl.when(middle)
    def _():
        copy2().wait_recv()
        add(0, r2)

    for one in load_cot(z):
        one.wait()

    def settle(p, _):
        @pl.when(at_end)
        def _():
            copy4(p).wait_recv()
            slots[0, piece(p), :] = (
                slots[0, piece(p), :].astype(f32) + r4[piece(p), :].astype(f32)
            ).astype(bf16)

        def rows32(half, _):
            at = pl.ds(pl.multiple_of(p * 64 + half * 32, 32), 32)
            grad = slots[0, at, :].astype(f32)
            normed, inverse = norm_rows(residual_ref[at, :])
            cot = cot_buf[p, pl.ds(pl.multiple_of(half * 32, 32), 32), :].astype(f32)
            value = cot + norm_back(grad, normed, inverse)
            grad_res_ref[at, :] = value
            g_ref[at, :] = value.astype(bf16)
            return 0

        lax.fori_loop(0, 2, rows32, 0)
        return 0

    lax.fori_loop(0, 4, settle, 0)
    for one in stage_copies(z):
        one.wait()
    hop_end()
    copy1().wait_send()

    @pl.when(at_end)
    def _():
        copy3().wait_send()
        for p in (2, 3):
            copy5(p).wait_send()

    @pl.when(middle)
    def _():
        copy2().wait_send()
        for p in range(4):
            copy4(p).wait_send()


def mlp_line(m_own, residual, cots, w_gate_up, w_down, a_in, b_gate_up, a_down, b_out_down, set_index):
    bf16 = jnp.bfloat16
    f32 = jnp.float32
    vmem = pl.BlockSpec(memory_space=pltpu.VMEM)
    anywhere = pl.BlockSpec(memory_space=pl.ANY)
    width = m_own.shape[1]
    hidden = w_down.shape[0]
    tile = hidden_tile
    tiles = hidden // tile
    shape = jax.ShapeDtypeStruct
    dma = pltpu.SemaphoreType.DMA
    vm = pltpu.VMEM
    return pl.pallas_call(
        mlp_line_kernel,
        in_specs=[vmem, vmem]
        + [anywhere] * 3
        + [vmem] * 4
        + [pl.BlockSpec(memory_space=pltpu.SMEM)],
        out_specs=[vmem, vmem] + [anywhere] * 4 + [vmem, vmem, vmem, vmem],
        out_shape=[
            shape((256, width), bf16),
            shape((256, width), f32),
        ]
        + [shape((4, 64, width), bf16)] * 4
        + [
            shape((4, 2, 16, hidden), f32),
            shape((4, 16, hidden), f32),
            shape((4, 32, width), f32),
            shape((4, 16, width), f32),
        ],
        scratch_shapes=[
            vm((4, 256, width), bf16),
            vm((tiles, width, tile), bf16),
            vm((tiles, width, tile), bf16),
            vm((tiles, tile, width), bf16),
            vm((4, 64, width), bf16),
            vm((256, width), f32),
            vm((256, width), f32),
            vm((256, 96), f32),
            vm((4, 256, width), bf16),
            vm((256, width), bf16),
            vm((256, width), bf16),
            vm((256, width), bf16),
            vm((256, width), bf16),
            vm((256, width), bf16),
            vm((4, 64, width), bf16),
        ]
        + [dma((3,))] * 4
        + [dma((4,))] * 6
        + [dma((2,))] * 2
        + [dma((3 * tiles,)), dma((4,)), dma((4,))],
        cost_estimate=spend(110),
        compiler_params=pltpu.CompilerParams(
            collective_id=5, has_side_effects=True, vmem_limit_bytes=60 << 20
        ),
    )(m_own, residual, cots, w_gate_up, w_down, a_in, b_gate_up, a_down, b_out_down, set_index)


def finish_kernel(
    dq_ref, dk_ref, dv_ref, w_in, x_own_ref, residual_in, u_ref, g_ref, low_ref, rank_ref, mixed_in,
    b_sel_ref, a_sel_ref, chunk_ref, down0_in, got1_in, got2_in, pair_ref,
    set_ref,
    result_ref, grad_ref, sets_ref, pool_ref, heads_ref, got3_ref,
    w_ref, residual_ref, mixed_ref, down0_ref, got1_ref, got2_ref,
    own_ref, sib_q, sib_k, sib_v, out_buf, in_buf, own_sum, u_buf, g_buf, a_acc, b_acc, chunk_src, chunk_sib, chunk_sum,
    chunk_in, z_src, z_in, sets_src, sets_in, head_src, head_in,
    a2a_send, a2a_recv, sib_send, sib_recv, send, recv, load_sem, cs_send, cs_recv, cx_send, cx_recv,
    cz_send, cz_recv, cg_send, cg_recv, hz_send, hz_recv, hg_send, hg_recv, down_send, down_recv,
    sz_send, sz_recv, sg_send, sg_recv, late_sem,
):
    f32 = jnp.float32
    bf16 = jnp.bfloat16
    s, z = places()
    loads = [
        pltpu.make_async_copy(source, target, late_sem.at[i])
        for i, (source, target) in enumerate(
            (
                (w_in, w_ref),
                (mixed_in, mixed_ref),
                (residual_in, residual_ref),
                (down0_in, down0_ref),
                (got1_in, got1_ref),
                (got2_in, got2_ref),
            )
        )
    ]
    for one in loads[:2]:
        one.start()
    core = s % 2
    chip = s // 2
    other = flip(s, 1)
    sx = flip(s, 2)
    sy = flip(s, 4)
    sd = flip(sx, 4)
    zs = [flip(z, 1), flip(z, 2), 3 - z]
    meet([(None, (t, z)) for t in (other, sx, sy, sd)] + [(None, (s, j)) for j in zs])
    last_down = remote(pair_ref, got3_ref, down_send.at[0], down_recv.at[0], (s, flip(z, 2)))
    last_down.start()
    sets_src[...] = chunk_ref[0:32].astype(bf16)
    sets_along = [remote(sets_src, sets_in.at[d], sz_send.at[d], sz_recv.at[d], (s, j)) for d, j in enumerate(zs)]
    for one in sets_along:
        one.start()
    mine = (dq_ref, dk_ref, dv_ref)
    theirs = (sib_q, sib_k, sib_v)
    swaps = [
        remote(
            mine[p].at[2 * c + 1 - core], theirs[p].at[c], sib_send.at[4 * p + c], sib_recv.at[4 * p + c], (other, z)
        )
        for c in range(4)
        for p in range(3)
    ]
    for one in swaps:
        one.start()

    def load(t):
        return [
            pltpu.make_async_copy(u_ref.at[t], u_buf.at[t % 2], load_sem.at[t % 2]),
            pltpu.make_async_copy(g_ref.at[t], g_buf.at[t % 2], load_sem.at[2 + t % 2]),
        ]

    for one in load(0):
        one.start()
    for one in swaps:
        one.wait_recv()

    def rows_of(c, half):
        def load(row):
            at = pl.ds(row, 32)
            return jnp.concatenate(
                [ref[2 * c + core, at, :] for ref in mine] + [ref[c, at, :] for ref in theirs], axis=1
            )

        return some_rows(load, half)

    reduce = Reduce(
        rows_of, lambda rows, wide: dot_nt(rows, w_ref[wide, :]), x_own_ref.shape[2], s, z,
        out_buf, in_buf, own_sum, send, recv,
    )
    loads[0].wait()
    reduce.begin()
    for one in loads[2:]:
        one.start()
    reduce.keep()
    loads[1].wait()

    b_two = [
        jnp.concatenate(
            [b_sel_ref[2 * core, 16 * p : 16 * p + 16], b_sel_ref[2 * core + 1, 16 * p : 16 * p + 16]], axis=1
        )
        for p in range(3)
    ]
    a_two = jnp.concatenate([a_sel_ref[2 * core], a_sel_ref[2 * core + 1]], axis=1)

    a_acc[...] = jnp.zeros_like(a_acc)
    b_acc[...] = jnp.zeros_like(b_acc)

    def adapt(t, _):
        for one in load(t):
            one.wait()

        @pl.when(t < 7)
        def _():
            for one in load(t + 1):
                one.start()

        back = jnp.concatenate([dot_nt(mine[p][t], b_two[p]) for p in range(3)], axis=1)
        back = (adapt_scale * back).astype(bf16)
        lows = (adapt_scale * dot_nt(mixed_ref[t], a_two)).astype(bf16)
        u = u_buf.at[t % 2]
        g = g_buf.at[t % 2]

        def one(part, _):
            wide = pl.ds(pl.multiple_of(part * 512, 512), 512)
            a_acc[:, wide] += dot_tn(back, u[:, wide])
            b_acc[:, wide] += dot_tn(lows, g[:, wide])
            return 0

        lax.fori_loop(0, 4, one, 0)

        @pl.when(t == 2)
        def _():
            reduce.second()

        @pl.when(t == 6)
        def _():
            reduce.third()

        return 0

    lax.fori_loop(0, 8, adapt, 0)
    per_head = [
        dot_tn(low_ref[...].reshape(2048, 48)[:, 16 * p : 16 * p + 16], mine[p][...].reshape(2048, 256))
        for p in range(3)
    ] + [dot_tn(rank_ref[...].reshape(2048, 16), mixed_ref[...].reshape(2048, 256))]
    for head in range(2):
        columns = slice(HDIM * head, HDIM * head + HDIM)
        head_src[head] = jnp.concatenate([part[:, columns] for part in per_head], axis=0).astype(bf16)

    keeper = (z // 2) == core

    def head_copy(head):
        return remote(head_src.at[head], head_in.at[z], hz_send.at[head], hz_recv.at[z], (s, 2 * core + head))

    for head in range(2):

        @pl.when(2 * core + head != z)
        def _():
            head_copy(head).start()

        @pl.when(2 * core + head == z)
        def _():
            head_in[z] = head_src[head]

    for i in range(8):
        sequence = a_acc[8 * i : 8 * i + 8] if i < 6 else b_acc[8 * i - 48 : 8 * i - 40]
        chunk_src[i] = jnp.concatenate([sequence, jnp.zeros((8, a_acc.shape[1]), f32)], axis=0).astype(bf16)
    crosses = [
        remote(chunk_src.at[2 * c + 1 - core], chunk_sib.at[c], cs_send.at[c], cs_recv.at[c], (other, z))
        for c in range(4)
    ]
    for one in crosses:
        one.start()
    for one in crosses:
        one.wait_recv()
    for c in range(4):
        chunk_sum[c] = (chunk_src[2 * c + core].astype(f32) + chunk_sib[c].astype(f32)).astype(bf16)
    around = [
        remote(chunk_sum.at[t // 2], chunk_in.at[d], cx_send.at[d], cx_recv.at[d], (t, z))
        for d, t in enumerate((sx, sy, sd))
    ]
    for one in around:
        one.start()

    for one in sets_along:
        one.wait_recv()
    whole = chunk_ref[0:24]
    for d in range(3):
        whole += sets_in[d, 0:24].astype(f32)
    sets_ref[s] = jnp.concatenate([whole, chunk_ref[24:48]], axis=0).astype(bf16)

    for one in loads[2:]:
        one.wait()
    def settle(row, total):
        at = pl.ds(row, 32)
        inside = pl.ds(pl.multiple_of(row % 64, 32), 32)
        normed, inverse = norm_rows(x_own_ref[row // 64, inside, :].astype(f32))
        value = residual_ref[at, :] + norm_back(total, normed, inverse)
        own_ref[row // 64, inside, :] = value.astype(bf16)

    def back(d, half):
        rows = pl.ds(32 * half, 32)
        return remote(
            own_ref.at[zs[d], rows], grad_ref.at[z, rows], a2a_send.at[2 * d + half], a2a_recv.at[2 * d + half],
            (s, zs[d]),
        )

    backs = []
    for half in range(2):
        reduce.finish(half, settle)
        for d in range(3):
            backs.append(back(d, half))
            backs[-1].start()
        if half == 0:
            for one in around:
                one.wait_recv()
            chunk = chunk_sum[chip].astype(f32)
            for d in range(3):
                chunk += chunk_in[d].astype(f32)
            z_src[...] = chunk.astype(bf16)
            along = [remote(z_src, z_in.at[d], cz_send.at[d], cz_recv.at[d], (s, j)) for d, j in enumerate(zs)]
            for one in along:
                one.start()
    grad_ref[z] = own_ref[z]

    def sets_copy(t, index, target):
        return remote(sets_ref.at[t], sets_ref.at[t], sg_send.at[index], sg_recv.at[index], (target, z))

    sets_gives = [sets_copy(s, index, target) for index, target in enumerate((sx, sy, sd, other))]
    for one in sets_gives:
        one.start()

    last_down.wait_recv()

    def result_rows(part, _):
        for first, other_pair in ((0, got2_ref), (2, got3_ref)):
            result_ref[first + part] = (
                down0_ref[first + part].astype(f32)
                + got1_ref[first + part].astype(f32)
                + other_pair[part].astype(f32)
            ).astype(bf16)
        return 0

    lax.fori_loop(0, 2, result_rows, 0)
    def head_spread(target, index):
        return remote(heads_ref.at[chip], heads_ref.at[chip], hg_send.at[index], hg_recv.at[index], (target, z))

    def head_pass(t, index):
        c = t // 2
        return remote(heads_ref.at[c], heads_ref.at[c], hg_send.at[index], hg_recv.at[index], (other, z))

    @pl.when(keeper)
    def _():
        for j in range(4):

            @pl.when(z != j)
            def _():
                remote(head_src.at[0], head_in.at[j], hz_send.at[0], hz_recv.at[j], (s, j)).wait_recv()

        for member in range(4):
            total = jnp.zeros((64, HDIM), f32)
            for seq in range(4):
                total += (set_ref[seq] == member).astype(f32) * head_in[seq].astype(f32)
            heads_ref[chip, pl.ds(64 * member, 64)] = total.astype(bf16)
        for index, target in enumerate((sx, sy, sd, other)):
            head_spread(target, index).start()

    for one in along:
        one.wait_recv()
    places_z = [z] + zs
    parts = [chunk[0:8]] + [z_in[d, 0:8].astype(f32) for d in range(3)]
    by_member = [
        sum((set_ref[places_z[d]] == member).astype(f32) * parts[d] for d in range(4)) for member in range(4)
    ]
    pool_ref[s] = jnp.concatenate(by_member, axis=0).astype(bf16)

    def pool_copy(t, index, target):
        return remote(pool_ref.at[t], pool_ref.at[t], cg_send.at[index], cg_recv.at[index], (target, z))

    gives = [pool_copy(s, index, target) for index, target in enumerate((sx, sy, sd, other))]
    for one in gives:
        one.start()

    @pl.when(keeper)
    def _():
        for index, t in enumerate((sx, sy, sd)):
            head_pass(t, index).wait_recv()
            head_pass(t, 4 + index).start()

    for copy in (sets_copy, pool_copy):
        for index, t in enumerate((sx, sy, sd)):
            copy(t, index, other).wait_recv()
            copy(t, 4 + index, other).start()
    for copy in (sets_copy, pool_copy):
        copy(other, 3, other).wait_recv()
        for index, t in enumerate((sx, sy, sd)):
            copy(flip(t, 1), 4 + index, other).wait_recv()

    @pl.when(z // 2 != core)
    def _():
        head_spread(other, 3).wait_recv()
        for index, t in enumerate((sx, sy, sd)):
            head_pass(t, 4 + index).wait_recv()

    for d, j in enumerate(zs):
        for half in range(2):
            rows = pl.ds(32 * half, 32)
            index = 2 * d + half
            remote(
                own_ref.at[j, rows], grad_ref.at[j, rows], a2a_send.at[index], a2a_recv.at[index], (s, j)
            ).wait_recv()
    for one in swaps + crosses + around + backs + along + gives + sets_along + sets_gives + [last_down]:
        one.wait_send()
    for index, t in enumerate((sx, sy, sd)):
        pool_copy(t, 4 + index, other).wait_send()
        sets_copy(t, 4 + index, other).wait_send()
    reduce.end()
    for head in range(2):

        @pl.when(2 * core + head != z)
        def _():
            head_copy(head).wait_send()

    @pl.when(keeper)
    def _():
        for index, target in enumerate((sx, sy, sd, other)):
            head_spread(target, index).wait_send()
        for index, t in enumerate((sx, sy, sd)):
            head_pass(t, 4 + index).wait_send()


def finish_layer(*operands):
    bf16 = jnp.bfloat16
    f32 = jnp.float32
    vmem = pl.BlockSpec(memory_space=pltpu.VMEM)
    anywhere = pl.BlockSpec(memory_space=pl.ANY)
    width = operands[4].shape[2]
    dma = pltpu.SemaphoreType.DMA
    vm = pltpu.VMEM
    shape = jax.ShapeDtypeStruct
    return pl.pallas_call(
        finish_kernel,
        in_specs=[vmem] * 3
        + [anywhere, vmem, anywhere, anywhere, anywhere, vmem, vmem, anywhere]
        + [vmem] * 3
        + [anywhere] * 3
        + [vmem, pl.BlockSpec(memory_space=pltpu.SMEM)],
        out_specs=[vmem] * 6,
        out_shape=[
            shape((4, 64, width), bf16),
            shape((4, 64, width), bf16),
            shape((8, 48, width), bf16),
            shape((8, 32, width), bf16),
            shape((4, 256, HDIM), bf16),
            shape((2, 64, width), bf16),
        ],
        scratch_shapes=[
            vm((width, 1536), bf16),
            vm((256, width), f32),
            vm((8, 256, 256), bf16),
            vm((4, 64, width), bf16),
            vm((4, 64, width), bf16),
            vm((2, 64, width), bf16),
            vm((4, 64, width), bf16),
            vm((4, 256, 256), bf16),
            vm((4, 256, 256), bf16),
            vm((4, 256, 256), bf16),
            vm((6, 128, width), bf16),
            vm((6, 128, width), bf16),
            vm((256, width), f32),
            vm((2, 256, width), bf16),
            vm((2, 256, width), bf16),
            vm((48, width), f32),
            vm((16, width), f32),
            vm((8, 16, width), bf16),
            vm((4, 16, width), bf16),
            vm((4, 16, width), bf16),
            vm((3, 16, width), bf16),
            vm((16, width), bf16),
            vm((3, 16, width), bf16),
            vm((32, width), bf16),
            vm((3, 32, width), bf16),
            vm((2, 64, HDIM), bf16),
            vm((4, 64, HDIM), bf16),
        ]
        + [
            dma((count,))
            for count in (6, 6, 12, 12, 6, 6, 4, 4, 4, 3, 3, 3, 3, 7, 7, 2, 4, 7, 7, 1, 1, 3, 3, 7, 7, 6)
        ],
        cost_estimate=spend(80),
        compiler_params=pltpu.CompilerParams(
            collective_id=4, has_side_effects=True, vmem_limit_bytes=58 << 20
        ),
    )(*operands)


def span_table(positions):
    half_dim = HDIM // 2
    frequency = jnp.exp(
        jnp.arange(half_dim, dtype=jnp.float32) * (-2.0 * math.log(rope_base) / HDIM)
    )
    angles = positions.astype(jnp.float32)[:, None] * frequency
    return jnp.concatenate([jnp.cos(angles), jnp.sin(angles)], axis=1)


def per_device_layers(
    layer_in, w_qkv, w_out, w_gate_up, w_down, a_in, b_qkv, b_gate_up, a_out, a_down, b_out_down,
    set_index, positions, cotangent,
):
    f32 = jnp.float32
    z = lax.axis_index("mp")
    sets = a_in.shape[0]
    width = layer_in.shape[2]
    rank = a_in.shape[2]
    length = 8 * 256

    table = span_table(lax.dynamic_index_in_dim(positions, z, 0, keepdims=False))
    (
        x_own, m_own, residual, o_eff, b_sel, a_sel, lse,
        u, q, k, v, low, tables, mixed, w_cat, cots,
    ) = front_layer(
        layer_in, w_qkv, w_out, b_qkv, a_out, a_in, b_out_down, table, cotangent, set_index
    )

    def spans(values):
        return values.reshape(8, 256, 256)

    (
        g_own, grad_residual, down0, down1, down2, down3,
        grad_b_mlp, grad_ad, grad_a_mlp, grad_bd,
    ) = mlp_line(
        m_own, residual, cots, w_gate_up, w_down, a_in, b_gate_up, a_down, b_out_down, set_index
    )
    dq, dk, dv, out_rank, chunk, pair, g, got1, got2 = back_layer(
        g_own, o_eff, mixed, b_out_down, q, k, v, lse, tables.reshape(length, HDIM),
        grad_b_mlp, grad_ad, grad_a_mlp, grad_bd, down1, down2, down3, set_index,
    )
    result, grad_in, pooled, pool, heads, _ = finish_layer(
        spans(dq), spans(dk), spans(dv), w_cat, x_own, grad_residual, u, g, low, out_rank, spans(mixed),
        b_sel, a_sel, chunk, down0, got1, got2, pair, set_index,
    )
    pooled = pooled.astype(f32)
    whole = pooled[:, 0:24].reshape(sets, 48, width)
    split = pooled[:, 24:48].reshape(sets, 48, width)
    pool = pool.astype(f32).reshape(8, sets, 8, width)
    sequence = jnp.transpose(pool, (1, 0, 2, 3)).reshape(sets, 64, width)
    heads = heads.astype(f32).reshape(4, sets, 64, HDIM)
    heads = jnp.transpose(heads, (1, 2, 0, 3)).reshape(sets, 4, rank, 4 * HDIM)
    return (
        result,
        grad_in,
        jnp.concatenate([sequence[:, :48], whole[:, :32]], axis=1).reshape(sets, 5, rank, width),
        heads[:, :3],
        split[:, :32].reshape(sets, 2, rank, width),
        heads[:, 3],
        split[:, 32:],
        jnp.stack([sequence[:, 48:], whole[:, 32:]], axis=1),
    )


def solution(mesh):
    by_layers = mesh.shape["seq"] == 8 and mesh.shape["mp"] == 4
    body = per_device_layers if by_layers else per_device
    placed = (
        P(None, ("seq", "mp"), None),
        P(None, None, "mp"),
        P("mp", None),
        P(None, None, "mp"),
        P("mp", None),
        P(),
        P(None, None, None, "mp"),
        P(None, None, None, "mp"),
        P(None, None, "mp"),
        P(None, None, "mp"),
        P(),
        P(),
        P(None, "seq"),
        P(None, ("seq", "mp"), None),
    )
    return jax.shard_map(
        body,
        mesh=mesh,
        in_specs=placed,
        out_specs=(
            P(None, ("seq", "mp"), None),
            P(None, ("seq", "mp"), None),
            P(),
            P(None, None, None, "mp"),
            P(None, None, None, "mp"),
            P(None, None, "mp"),
            P(None, None, "mp"),
            P(),
        ),
        check_vma=False,
    )
```

```python
import math

import jax
import jax.numpy as jnp
from jax import lax
from jax.experimental import pallas as pl
from jax.experimental.pallas import tpu as pltpu
from jax.sharding import PartitionSpec as P

HDIM = 128


adapt_scale = 0.5
norm_eps = 1e-05
rope_base = 10000.0
far_below = -1e30
highest = lax.Precision.HIGHEST


def layer_norm(values):
    centred = values - jnp.mean(values, axis=-1, keepdims=True)
    inverse = lax.rsqrt(jnp.mean(centred * centred, axis=-1, keepdims=True) + norm_eps)
    return (centred * inverse, inverse)


def norm_back(gradient, normed, inverse):
    return inverse * (
        gradient
        - jnp.mean(gradient, axis=-1, keepdims=True)
        - normed * jnp.mean(gradient * normed, axis=-1, keepdims=True)
    )


def gather_rows(values):
    return lax.all_gather(values, "mp", axis=1, tiled=True)


def scatter_rows(values):
    return lax.psum_scatter(
        values.astype(jnp.bfloat16), "mp", scatter_dimension=1, tiled=True
    ).astype(jnp.float32)


def rope_tables(positions):
    half_dim = HDIM // 2
    frequency = jnp.exp(
        jnp.arange(half_dim, dtype=jnp.float32) * (-2.0 * math.log(rope_base) / HDIM)
    )
    angles = jnp.transpose(positions).astype(jnp.float32)[:, :, None, None] * frequency
    return (jnp.cos(angles), jnp.sin(angles))


def rotate(values, cosine_table, sine_table):
    half_dim = values.shape[-1] // 2
    first_half = values[..., :half_dim]
    second_half = values[..., half_dim:]
    return jnp.concatenate(
        [
            first_half * cosine_table - second_half * sine_table,
            second_half * cosine_table + first_half * sine_table,
        ],
        axis=-1,
    )


def rotate_back(gradient, cosine_table, sine_table):
    half_dim = gradient.shape[-1] // 2
    first_half = gradient[..., :half_dim]
    second_half = gradient[..., half_dim:]
    return jnp.concatenate(
        [
            first_half * cosine_table + second_half * sine_table,
            second_half * cosine_table - first_half * sine_table,
        ],
        axis=-1,
    )


def masked_scores(queries, key_rows, query_first, key_first, score_scale):
    raw_scores = (
        jnp.einsum("qshd,kshd->shqk", queries, key_rows, preferred_element_type=jnp.float32)
        * score_scale
    )
    query_index = query_first + jnp.arange(queries.shape[0])
    key_index = key_first + jnp.arange(key_rows.shape[0])
    return (raw_scores, key_index[None, :] <= query_index[:, None])


def blockwise(fold_step, state_carry, pieces, start_row):
    row_count = pieces[0].shape[0]
    block_size = 512

    def block_turn(block_id, running):
        blocks = tuple(
            (
                lax.dynamic_slice_in_dim(shard_piece, block_id * block_size, block_size, 0)
                for shard_piece in pieces
            )
        )
        return fold_step(running, blocks, start_row + block_id * block_size)

    return lax.fori_loop(0, row_count // block_size, block_turn, state_carry)


def forward_step(queries, query_first, score_scale):
    query_last = query_first + queries.shape[0] - 1

    def fold_step(state_carry, blocks, key_first):
        key_rows, value_rows = blocks

        def compute(running):
            running_max, running_sum, weighted = running
            scores, allowed = masked_scores(queries, key_rows, query_first, key_first, score_scale)
            new_max = jnp.maximum(
                running_max, jnp.max(jnp.where(allowed, scores, far_below), axis=-1)
            )
            exponent = jnp.where(allowed, jnp.exp(scores - new_max[..., None]), 0.0)
            factor = jnp.exp(running_max - new_max)
            running_sum = running_sum * factor + jnp.sum(exponent, axis=-1)
            weighted = weighted * factor[..., None] + jnp.einsum(
                "shqk,kshd->shqd",
                exponent.astype(jnp.bfloat16),
                value_rows,
                preferred_element_type=jnp.float32,
            )
            return (new_max, running_sum, weighted)

        return lax.cond(key_first <= query_last, compute, lambda running: running, state_carry)

    return fold_step


def query_grad_step(queries, grad_heads, log_total, row_dots, query_first, score_scale):
    query_last = query_first + queries.shape[0] - 1

    def fold_step(state_carry, blocks, key_first):
        key_rows, value_rows = blocks

        def compute(running):
            scores, allowed = masked_scores(queries, key_rows, query_first, key_first, score_scale)
            attn_probs = jnp.where(allowed, jnp.exp(scores - log_total[..., None]), 0.0)
            grad_probs = jnp.einsum(
                "qshd,kshd->shqk", grad_heads, value_rows, preferred_element_type=jnp.float32
            )
            grad_scores = (attn_probs * (grad_probs - row_dots[..., None])).astype(jnp.bfloat16)
            return running + score_scale * jnp.einsum(
                "shqk,kshd->qshd", grad_scores, key_rows, preferred_element_type=jnp.float32
            )

        return lax.cond(key_first <= query_last, compute, lambda running: running, state_carry)

    return fold_step


def key_grad_step(key_rows, value_rows, key_first, score_scale):

    def fold_step(state_carry, blocks, query_first):
        queries, grad_heads, log_total_tok, row_dots_tok = blocks
        query_last = query_first + queries.shape[0] - 1

        def compute(running):
            scores, allowed = masked_scores(queries, key_rows, query_first, key_first, score_scale)
            log_total = jnp.transpose(log_total_tok, (1, 2, 0))
            row_dots = jnp.transpose(row_dots_tok, (1, 2, 0))
            attn_probs = jnp.where(allowed, jnp.exp(scores - log_total[..., None]), 0.0)
            grad_value_rows = jnp.einsum(
                "shqk,qshd->kshd",
                attn_probs.astype(jnp.bfloat16),
                grad_heads,
                preferred_element_type=jnp.float32,
            )
            grad_probs = jnp.einsum(
                "qshd,kshd->shqk", grad_heads, value_rows, preferred_element_type=jnp.float32
            )
            grad_scores = (attn_probs * (grad_probs - row_dots[..., None])).astype(jnp.bfloat16)
            grad_key_rows = score_scale * jnp.einsum(
                "shqk,qshd->kshd", grad_scores, queries, preferred_element_type=jnp.float32
            )
            return (grad_key_rows, grad_value_rows)

        return lax.cond(key_first <= query_last, compute, lambda running: running, state_carry)

    return fold_step


def project_in(token_rows, weight, a_chosen, b_chosen):
    main_term = jnp.einsum("scd,dw->csw", token_rows, weight, preferred_element_type=jnp.float32)
    low_rank = jnp.einsum("scd,srd->scr", token_rows, a_chosen, preferred_element_type=jnp.float32)
    side_term = jnp.einsum(
        "scr,srw->csw", low_rank, b_chosen.astype(jnp.float32), precision=highest
    )
    return (main_term + adapt_scale * side_term, low_rank)


def project_out(middle, weight, a_chosen, b_chosen):
    main_term = jnp.einsum("csw,wd->scd", middle, weight, preferred_element_type=jnp.float32)
    low_rank = jnp.einsum("csw,srw->scr", middle, a_chosen, preferred_element_type=jnp.float32)
    side_term = jnp.einsum(
        "scr,srd->scd", low_rank, b_chosen.astype(jnp.float32), precision=highest
    )
    return (main_term + adapt_scale * side_term, low_rank)


def back_in(gradient, weight, a_chosen, b_chosen, token_rows, low_rank):
    back_rank = jnp.einsum("csw,srw->scr", gradient, b_chosen, preferred_element_type=jnp.float32)
    grad_rows = jnp.einsum("csw,dw->scd", gradient, weight, preferred_element_type=jnp.float32)
    grad_rows = grad_rows + adapt_scale * jnp.einsum(
        "scr,srd->scd", back_rank, a_chosen.astype(jnp.float32), precision=highest
    )
    grad_a = adapt_scale * jnp.einsum("scr,scd->srd", back_rank, token_rows, precision=highest)
    grad_b = adapt_scale * jnp.einsum("scr,csw->srw", low_rank, gradient, precision=highest)
    return (grad_rows, grad_a, grad_b)


def back_out(gradient, weight, a_chosen, b_chosen, middle, low_rank):
    back_rank = jnp.einsum("scd,srd->scr", gradient, b_chosen, preferred_element_type=jnp.float32)
    grad_middle = jnp.einsum("scd,wd->csw", gradient, weight, preferred_element_type=jnp.float32)
    grad_middle = grad_middle + adapt_scale * jnp.einsum(
        "scr,srw->csw", back_rank, a_chosen.astype(jnp.float32), precision=highest
    )
    grad_a = adapt_scale * jnp.einsum("scr,csw->srw", back_rank, middle, precision=highest)
    grad_b = adapt_scale * jnp.einsum("scr,scd->srd", low_rank, gradient, precision=highest)
    return (grad_middle, grad_a, grad_b)


def pick_set(onehot, set_table):
    flattened = set_table.reshape(set_table.shape[0], -1)
    chosen = jnp.dot(onehot, flattened, preferred_element_type=jnp.float32).astype(jnp.bfloat16)
    return chosen.reshape((onehot.shape[0],) + set_table.shape[1:])


def spread_sets(onehot, per_sequence):
    flattened = per_sequence.reshape(per_sequence.shape[0], -1)
    summed = jnp.dot(onehot.astype(jnp.float32).T, flattened, precision=highest)
    return summed.reshape((onehot.shape[1],) + per_sequence.shape[1:])


def per_device(
    layer_in,
    w_qkv,
    w_out,
    w_gate_up,
    w_down,
    a_in,
    b_qkv,
    b_gate_up,
    a_out,
    a_down,
    b_out_down,
    set_index,
    positions,
    cotangent,
):
    local_len = positions.shape[1]
    seq_count = positions.shape[0]
    score_scale = 1.0 / math.sqrt(HDIM)
    my_first = lax.axis_index("seq") * local_len
    onehot = (set_index[:, None] == jnp.arange(a_in.shape[0])[None, :]).astype(jnp.bfloat16)
    chosen_a_in = pick_set(onehot, a_in)
    chosen_b_qkv = pick_set(onehot, b_qkv)
    chosen_b_gate_up = pick_set(onehot, b_gate_up)
    chosen_a_out = pick_set(onehot, a_out)
    chosen_a_down = pick_set(onehot, a_down)
    chosen_b_out_down = pick_set(onehot, b_out_down)

    def to_heads(values):
        return values.reshape(local_len, seq_count, -1, HDIM)

    residual_in = layer_in.astype(jnp.float32)
    normed_attn, inverse_attn = layer_norm(residual_in)
    rows_attn = gather_rows(normed_attn.astype(jnp.bfloat16))
    projected = [
        project_in(rows_attn, w_qkv[member], chosen_a_in[:, member], chosen_b_qkv[:, member])
        for member in range(3)
    ]
    cosine_table, sine_table = rope_tables(positions)
    queries = rotate(to_heads(projected[0][0]), cosine_table, sine_table).astype(jnp.bfloat16)
    key_rows = rotate(to_heads(projected[1][0]), cosine_table, sine_table).astype(jnp.bfloat16)
    value_rows = to_heads(projected[2][0]).astype(jnp.bfloat16)
    stat_shape = (seq_count, queries.shape[2], local_len)
    initial = (
        jnp.full(stat_shape, far_below, jnp.float32),
        jnp.zeros(stat_shape, jnp.float32),
        jnp.zeros(stat_shape + (HDIM,), jnp.float32),
    )
    attend = forward_step(queries, my_first, score_scale)
    running_max, running_sum, weighted = blockwise(
        attend,
        initial,
        (
            lax.all_gather(key_rows, "seq", axis=0, tiled=True),
            lax.all_gather(value_rows, "seq", axis=0, tiled=True),
        ),
        jnp.int32(0),
    )
    log_total = running_max + jnp.log(running_sum)
    attn_output = jnp.transpose(weighted / running_sum[..., None], (2, 0, 1, 3))
    mixed = attn_output.reshape(local_len, seq_count, -1).astype(jnp.bfloat16)
    attn_term, rank_out = project_out(mixed, w_out, chosen_a_out, chosen_b_out_down[:, 0])
    residual = residual_in + scatter_rows(attn_term)
    normed_mlp, inverse_mlp = layer_norm(residual)
    rows_mlp = gather_rows(normed_mlp.astype(jnp.bfloat16))
    gate_proj, rank_gate = project_in(
        rows_mlp, w_gate_up[0], chosen_a_in[:, 3], chosen_b_gate_up[:, 0]
    )
    up_proj, rank_up = project_in(rows_mlp, w_gate_up[1], chosen_a_in[:, 4], chosen_b_gate_up[:, 1])
    sigmoid_gate = jax.nn.sigmoid(gate_proj)
    activation = (gate_proj * sigmoid_gate * up_proj).astype(jnp.bfloat16)
    down_term, rank_down = project_out(activation, w_down, chosen_a_down, chosen_b_out_down[:, 1])
    result = (residual + scatter_rows(down_term)).astype(jnp.bfloat16)
    grad_down = gather_rows(cotangent)
    grad_activation, grad_a_down, grad_b_down = back_out(
        grad_down, w_down, chosen_a_down, chosen_b_out_down[:, 1], activation, rank_down
    )
    grad_up = (grad_activation * gate_proj * sigmoid_gate).astype(jnp.bfloat16)
    grad_gate = (
        grad_activation * up_proj * sigmoid_gate * (1.0 + gate_proj * (1.0 - sigmoid_gate))
    ).astype(jnp.bfloat16)
    rows_from_gate, grad_a_gate, grad_b_gate = back_in(
        grad_gate, w_gate_up[0], chosen_a_in[:, 3], chosen_b_gate_up[:, 0], rows_mlp, rank_gate
    )
    rows_from_up, grad_a_up, grad_b_up = back_in(
        grad_up, w_gate_up[1], chosen_a_in[:, 4], chosen_b_gate_up[:, 1], rows_mlp, rank_up
    )
    grad_residual = cotangent.astype(jnp.float32) + norm_back(
        scatter_rows(rows_from_gate + rows_from_up), normed_mlp, inverse_mlp
    )
    grad_attn_rows = gather_rows(grad_residual.astype(jnp.bfloat16))
    grad_mixed, grad_a_out, grad_b_out = back_out(
        grad_attn_rows, w_out, chosen_a_out, chosen_b_out_down[:, 0], mixed, rank_out
    )
    grad_heads = to_heads(grad_mixed.astype(jnp.bfloat16))
    row_dots_tok = jnp.sum(grad_heads.astype(jnp.float32) * attn_output, axis=-1)
    row_dots = jnp.transpose(row_dots_tok, (1, 2, 0))
    log_total_tok = jnp.transpose(log_total, (2, 0, 1))
    query_step = query_grad_step(queries, grad_heads, log_total, row_dots, my_first, score_scale)
    zero_heads = jnp.zeros(queries.shape, jnp.float32)
    every_key, every_value = (
        lax.all_gather(key_rows, "seq", axis=0, tiled=True),
        lax.all_gather(value_rows, "seq", axis=0, tiled=True),
    )
    grad_queries = blockwise(query_step, zero_heads, (every_key, every_value), 0)
    block_size = 512

    def one_block(block_id):
        first_key = block_id * block_size
        block_keys = lax.dynamic_slice_in_dim(every_key, first_key, block_size, 0)
        block_values = lax.dynamic_slice_in_dim(every_value, first_key, block_size, 0)
        zero_block = jnp.zeros(block_keys.shape, jnp.float32)
        block_step = key_grad_step(block_keys, block_values, first_key, score_scale)
        grad_key_block, grad_value_block = block_step(
            (zero_block, zero_block), (queries, grad_heads, log_total_tok, row_dots_tok), my_first
        )
        return jnp.concatenate([grad_key_block, grad_value_block], axis=-1)

    stacked = lax.map(one_block, jnp.arange(local_len * lax.axis_size("seq") // block_size))
    stacked_terms = lax.psum_scatter(
        stacked.reshape((local_len * lax.axis_size("seq"),) + stacked.shape[2:]).astype(
            jnp.bfloat16
        ),
        "seq",
        scatter_dimension=0,
        tiled=True,
    ).astype(jnp.float32)
    grad_keys = stacked_terms[..., :HDIM]
    grad_values = stacked_terms[..., HDIM:]
    grad_query_raw = (
        rotate_back(grad_queries, cosine_table, sine_table)
        .astype(jnp.bfloat16)
        .reshape(local_len, seq_count, -1)
    )
    grad_key_raw = (
        rotate_back(grad_keys, cosine_table, sine_table)
        .astype(jnp.bfloat16)
        .reshape(local_len, seq_count, -1)
    )
    grad_value_raw = grad_values.astype(jnp.bfloat16).reshape(local_len, seq_count, -1)
    back_parts = [
        back_in(
            gradient,
            w_qkv[member],
            chosen_a_in[:, member],
            chosen_b_qkv[:, member],
            rows_attn,
            projected[member][1],
        )
        for member, gradient in enumerate((grad_query_raw, grad_key_raw, grad_value_raw))
    ]
    grad_rows_attn = back_parts[0][0] + back_parts[1][0] + back_parts[2][0]
    grad_in = (
        grad_residual + norm_back(scatter_rows(grad_rows_attn), normed_attn, inverse_attn)
    ).astype(jnp.bfloat16)
    per_seq_a_in = jnp.stack(
        [back_parts[0][1], back_parts[1][1], back_parts[2][1], grad_a_gate, grad_a_up], axis=1
    )
    per_seq_b_qkv = jnp.stack([bundle[2] for bundle in back_parts], axis=1)
    per_seq_b_gate_up = jnp.stack([grad_b_gate, grad_b_up], axis=1)
    per_seq_b_out_down = jnp.stack([grad_b_out, grad_b_down], axis=1)
    sums_seq = (
        lax.psum(spread_sets(onehot, per_seq_b_qkv).astype(jnp.bfloat16), "seq").astype(
            jnp.float32
        ),
        lax.psum(spread_sets(onehot, per_seq_b_gate_up).astype(jnp.bfloat16), "seq").astype(
            jnp.float32
        ),
        lax.psum(spread_sets(onehot, grad_a_out).astype(jnp.bfloat16), "seq").astype(jnp.float32),
        lax.psum(spread_sets(onehot, grad_a_down).astype(jnp.bfloat16), "seq").astype(jnp.float32),
    )
    sums_all = lax.psum(
        (spread_sets(onehot, per_seq_a_in), spread_sets(onehot, per_seq_b_out_down)), ("seq", "mp")
    )
    return (
        result,
        grad_in,
        sums_all[0],
        sums_seq[0],
        sums_seq[1],
        sums_seq[2],
        sums_seq[3],
        sums_all[1],
    )


log2e = 1.4426950408889634
attn_tile = 512
hidden_tile = 512


def dot_nt(a, b):
    return lax.dot_general(a, b, (((1,), (1,)), ((), ())), preferred_element_type=jnp.float32)


def dot_tn(a, b):
    return lax.dot_general(a, b, (((0,), (0,)), ((), ())), preferred_element_type=jnp.float32)


def dot_nn(a, b):
    return jnp.dot(a, b, preferred_element_type=jnp.float32)


def causal(block_t, first_row, first_col):
    rows = first_row + lax.broadcasted_iota(jnp.int32, block_t.shape, 0)
    cols = first_col + lax.broadcasted_iota(jnp.int32, block_t.shape, 1)
    return rows <= cols


mesh_ids = pl.DeviceIdType.MESH


def remote(src, dst, send, recv, target):
    return pltpu.make_async_remote_copy(
        src_ref=src, dst_ref=dst, send_sem=send, recv_sem=recv, device_id=target, device_id_type=mesh_ids
    )


def meet(partners):
    barrier = pltpu.get_barrier_semaphore()
    for condition, device in partners:
        if condition is None:
            pl.semaphore_signal(barrier, inc=1, device_id=device, device_id_type=mesh_ids)
        else:

            @pl.when(condition)
            def _():
                pl.semaphore_signal(barrier, inc=1, device_id=device, device_id_type=mesh_ids)

    count = 0
    for condition, device in partners:
        count = count + (1 if condition is None else condition.astype(jnp.int32))
    pl.semaphore_wait(barrier, count)


def flip(index, bit):
    return index + bit - 2 * bit * ((index // bit) % 2)


def places():
    s = lax.axis_index("seq")
    z = lax.axis_index("mp")
    return s, z


class Gather:
    def __init__(self, blocks, s, z, send, recv, half, base=0):
        self.at = blocks
        self.s = s
        self.z = z
        self.send = send
        self.recv = recv
        self.half = half
        self.base = base

    def rows(self, part):
        if part is None:
            return pl.ds(self.base, 2 * self.half)
        return pl.ds(self.base + part * self.half, self.half)

    def copy(self, index, span, part, target):
        ref = self.at.at[span, self.rows(part)]
        return remote(ref, ref, self.send.at[index], self.recv.at[index], (target, self.z))

    def begin(self):
        s, x, y, other = self.s, flip(self.s, 2), flip(self.s, 4), flip(self.s, 1)
        for one in (
            self.copy(0, s, 0, x),
            self.copy(1, s, 1, y),
            self.copy(2, s, 1, x),
            self.copy(3, s, 0, y),
            self.copy(6, s, None, other),
        ):
            one.start()

    def arrive_first(self):
        s, x, y = self.s, flip(self.s, 2), flip(self.s, 4)
        self.copy(0, x, 0, x).wait_recv()
        one = self.copy(4, x, 0, y)
        one.start()
        self.copy(1, y, 1, y).wait_recv()
        two = self.copy(5, y, 1, x)
        two.start()

    def arrive_neighbours(self):
        s, x, y, other = self.s, flip(self.s, 2), flip(self.s, 4), flip(self.s, 1)
        self.copy(2, x, 1, x).wait_recv()
        one = self.copy(7, x, None, other)
        one.start()
        self.copy(3, y, 0, y).wait_recv()
        two = self.copy(8, y, None, other)
        two.start()

    def arrive_diagonal(self):
        s, other = self.s, flip(self.s, 1)
        diagonal = flip(flip(s, 2), 4)
        self.copy(4, diagonal, 0, other).wait_recv()
        self.copy(5, diagonal, 1, other).wait_recv()
        one = self.copy(9, diagonal, None, other)
        one.start()

    def arrive_core(self, index):
        s = self.s
        other = flip(s, 1)
        span = (other, flip(other, 2), flip(other, 4), flip(flip(other, 2), 4))[index]
        self.copy(6 + index, span, None, other).wait_recv()
        return span

    def end(self):
        s, x, y, other = self.s, flip(self.s, 2), flip(self.s, 4), flip(self.s, 1)
        for index, span, part, target in (
            (0, s, 0, x),
            (1, s, 1, y),
            (2, s, 1, x),
            (3, s, 0, y),
            (4, x, 0, y),
            (5, y, 1, x),
            (6, s, None, other),
            (7, x, None, other),
            (8, y, None, other),
            (9, flip(x, 4), None, other),
        ):
            self.copy(index, span, part, target).wait_send()


gather_sems = 10


def spend(microseconds):
    return pl.CostEstimate(flops=microseconds * 10**9, bytes_accessed=10**6, transcendentals=0)


class Line:
    def __init__(self, blocks, core, s, z, send, recv):
        self.at = blocks
        self.core = core
        self.s = s
        self.z = z
        self.send = send
        self.recv = recv

    def ref(self, j):
        return self.at.at[j] if self.core is None else self.at.at[j, self.core]

    def up(self, hop, j):
        ref = self.ref(j)
        return remote(ref, ref, self.send.at[hop], self.recv.at[hop], (self.s, self.z + 1))

    def down(self, hop, j):
        ref = self.ref(j)
        return remote(ref, ref, self.send.at[3 + hop], self.recv.at[3 + hop], (self.s, self.z - 1))

    def across(self, index, j):
        ref = self.ref(j)
        return remote(ref, ref, self.send.at[6 + index], self.recv.at[6 + index], (flip(self.s, 1), self.z))

    def begin(self):
        z = self.z

        @pl.when(z < 3)
        def _():
            self.up(0, z).start()

        @pl.when(z > 0)
        def _():
            self.down(0, z).start()

        if self.core is not None:
            self.across(0, z).start()

    def hop(self, t):
        z = self.z

        def from_above(side):
            @pl.when((z + t <= 3) & side)
            def _():
                self.down(t - 1, z + t).wait_recv()
                if self.core is not None:
                    self.across(3 + t, z + t).start()
                if t < 3:

                    @pl.when(z > 0)
                    def _():
                        self.down(t, z + t).start()

        from_above(z < 2)

        @pl.when(z >= t)
        def _():
            self.up(t - 1, z - t).wait_recv()
            if self.core is not None:
                self.across(t, z - t).start()
            if t < 3:

                @pl.when(z < 3)
                def _():
                    self.up(t, z - t).start()

        from_above(z >= 2)

    def arrive_core(self):
        z = self.z
        other = 1 - self.core

        def wait(index, j):
            ref = self.at.at[j, other]
            remote(ref, ref, self.send.at[6 + index], self.recv.at[6 + index], (flip(self.s, 1), z)).wait_recv()

        wait(0, z)
        for t in (1, 2, 3):

            @pl.when(z >= t)
            def _():
                wait(t, z - t)

            @pl.when(z + t <= 3)
            def _():
                wait(3 + t, z + t)

    def end(self):
        z = self.z

        @pl.when(z < 3)
        def _():
            self.up(0, z).wait_send()

        @pl.when(z > 0)
        def _():
            self.down(0, z).wait_send()

        if self.core is not None:
            self.across(0, z).wait_send()
        for t in (1, 2, 3):

            @pl.when(z >= t)
            def _():
                if self.core is not None:
                    self.across(t, z - t).wait_send()
                if t < 3:

                    @pl.when(z < 3)
                    def _():
                        self.up(t, z - t).wait_send()

            @pl.when(z + t <= 3)
            def _():
                if self.core is not None:
                    self.across(3 + t, z + t).wait_send()
                if t < 3:

                    @pl.when(z > 0)
                    def _():
                        self.down(t, z + t).wait_send()


line_sems = 13


def norm_rows(values):
    centred = values - jnp.mean(values, axis=-1, keepdims=True)
    inverse = lax.rsqrt(jnp.mean(centred * centred, axis=-1, keepdims=True) + norm_eps)
    return (centred * inverse, inverse)


class Reduce:
    def __init__(self, rows, multiply, width, s, z, out, inn, own, send, recv):
        self.rows = rows
        self.multiply = multiply
        self.width = width
        self.s = s
        self.z = z
        self.out = out
        self.inn = inn
        self.own = own
        self.send = send
        self.recv = recv
        chip = s // 2
        self.chip = chip
        self.cx = flip(chip, 1)
        self.cy = flip(chip, 2)
        self.cd = flip(self.cx, 2)

    def copy(self, index):
        target = flip(self.s, 2) if index in (0, 2, 5) else flip(self.s, 4)
        return remote(
            self.out.at[index], self.inn.at[index], self.send.at[index], self.recv.at[index], (target, self.z)
        )

    def give(self, first, second):
        both = jnp.concatenate([self.rows(*first[1:3]), self.rows(*second[1:3])], axis=0)
        for job in (first, second):
            if job[3] is not None:
                self.copy(job[3]).wait_recv()

        def one(part, _):
            wide = pl.ds(pl.multiple_of(part * 512, 512), 512)
            value = self.multiply(both, wide)
            for job, piece in ((first, value[:128]), (second, value[128:])):
                if job[3] is not None:
                    piece = piece + self.inn[job[3], :, wide].astype(jnp.float32)
                self.out[job[0], :, wide] = piece.astype(jnp.bfloat16)
            return 0

        lax.fori_loop(0, self.width // 512, one, 0)
        self.copy(first[0]).start()
        self.copy(second[0]).start()

    def begin(self):
        self.give((0, self.cd, 0, None), (1, self.cd, 1, None))

    def second(self):
        self.give((2, self.cx, 0, None), (4, self.cy, 0, 0))

    def third(self):
        self.copy(2).wait_send()
        self.copy(4).wait_send()
        self.give((5, self.cx, 1, 1), (3, self.cy, 1, None))

    def keep(self):
        both = jnp.concatenate([self.rows(self.chip, 0), self.rows(self.chip, 1)], axis=0)

        def one(part, _):
            wide = pl.ds(pl.multiple_of(part * 512, 512), 512)
            self.own[:, wide] = self.multiply(both, wide)
            return 0

        lax.fori_loop(0, self.width // 512, one, 0)

    def finish(self, half, use):
        first, second = (2, 4) if half == 0 else (3, 5)
        self.copy(first).wait_recv()
        self.copy(second).wait_recv()

        def one(part, _):
            at = pl.ds(pl.multiple_of(part * 32, 32), 32)
            row = pl.multiple_of(part * 64 + half * 32, 32)
            total = (
                self.own[pl.ds(pl.multiple_of(half * 128 + part * 32, 32), 32), :]
                + self.inn[first, at, :].astype(jnp.float32)
                + self.inn[second, at, :].astype(jnp.float32)
            )
            use(row, total)
            return 0

        lax.fori_loop(0, 4, one, 0)

    def end(self):
        for index in (0, 1, 3, 5):
            self.copy(index).wait_send()


def some_rows(load, half):
    return jnp.concatenate([load(64 * j + 32 * half) for j in range(4)], axis=0)


def front_kernel(
    x_ref, w_qkv_ref, w_out_ref, b_qkv_ref, a_out_ref, a_in_ref, b_od_ref, table_ref, cot_ref, set_ref,
    x_own_ref, m_own_ref, residual_ref, o_eff_ref, b_sel_ref, a_sel_ref, lse_ref,
    u_out, q_out, k_out, v_out, low_out, table_out, mixed_out, w_cat_out, cots_ref,
    u_ref, w_buf, w_cat, q_buf, k_buf, v_buf, low_buf, tables, mixed, o_all, o_big, sib, out_buf, in_buf, own_sum,
    b_small, a_small,
    a2a_send, a2a_recv, tab_send, tab_recv, ag_send, ag_recv, ag2_send, ag2_recv, w_send, w_recv, o_send, o_recv, cot_send, cot_recv,
    small_send, small_recv, sib_send, sib_recv, red_send, red_recv, local_sem, store_sem,
):
    f32 = jnp.float32
    bf16 = jnp.bfloat16
    s, z = places()
    core = s % 2
    chip = s // 2
    other = flip(s, 1)
    zs = [flip(z, 1), flip(z, 2), 3 - z]
    middle = z * (3 - z) == 2
    columns = pl.ds(pl.multiple_of(chip * HDIM, HDIM), HDIM)
    half_rows = pl.ds(pl.multiple_of(core * 1024, 1024), 1024)
    owns = [
        pltpu.make_async_copy(w_qkv_ref.at[:, half_rows, columns], w_buf.at[z, core], local_sem.at[0]),
        pltpu.make_async_copy(w_out_ref.at[columns, half_rows], o_all.at[z, core], local_sem.at[1]),
        pltpu.make_async_copy(b_qkv_ref.at[:, :, :, columns], b_small.at[z], local_sem.at[2]),
        pltpu.make_async_copy(a_out_ref.at[:, :, columns], a_small.at[z], local_sem.at[3]),
        pltpu.make_async_copy(cot_ref, cots_ref.at[z], local_sem.at[4]),
    ]
    for one in owns:
        one.start()
    tables[s] = table_ref[...]
    meet([(None, (other, z)), (None, (flip(s, 2), z)), (None, (flip(s, 4), z))] + [(None, (s, j)) for j in zs])

    swaps = [
        remote(x_ref.at[j], x_own_ref.at[z], a2a_send.at[d], a2a_recv.at[d], (s, j)) for d, j in enumerate(zs)
    ]
    for one in swaps:
        one.start()
    for one in owns:
        one.wait()
    line = Line(w_buf, core, s, z, w_send, w_recv)
    line.begin()
    table_gather = Gather(tables, s, z, tab_send, tab_recv, 128)
    table_gather.begin()
    x_own_ref[z] = x_ref[z]

    def arrived(d):
        j = zs[d]
        remote(x_ref.at[j], x_own_ref.at[j], a2a_send.at[d], a2a_recv.at[d], (s, j)).wait_recv()

    def normalize(j):
        def one(part, _):
            normed, _ = norm_rows(x_own_ref[j, pl.ds(pl.multiple_of(part * 32, 32), 32), :].astype(f32))
            u_ref[s, pl.ds(pl.multiple_of(j * 64 + part * 32, 32), 32), :] = normed.astype(bf16)
            return 0

        lax.fori_loop(0, 2, one, 0)

    near = Gather(u_ref, s, z, ag_send, ag_recv, 64, pl.multiple_of((z // 2) * 128, 128))
    rest = Gather(u_ref, s, z, ag2_send, ag2_recv, 64, pl.multiple_of((1 - z // 2) * 128, 128))
    arrived(0)
    normalize(z)
    normalize(zs[0])
    near.begin()
    table_gather.arrive_first()
    table_gather.arrive_neighbours()
    near.arrive_first()
    arrived(1)
    arrived(2)
    smalls = []
    for d, j in enumerate(zs):
        smalls.append(remote(b_small.at[z], b_small.at[z], small_send.at[d], small_recv.at[d], (s, j)))
        smalls.append(remote(a_small.at[z], a_small.at[z], small_send.at[3 + d], small_recv.at[3 + d], (s, j)))
    for one in smalls:
        one.start()
    normalize(zs[1])
    normalize(zs[2])
    rest.begin()
    table_gather.arrive_diagonal()
    near.arrive_neighbours()
    near.arrive_diagonal()
    line.hop(1)
    rest.arrive_first()
    rest.arrive_neighbours()
    rest.arrive_diagonal()
    for index in range(4):
        near.arrive_core(index)
        rest.arrive_core(index)
        table_gather.arrive_core(index)
    line.hop(2)
    stores = [pltpu.make_async_copy(u_ref, u_out, store_sem.at[0])]
    stores[0].start()
    mine = set_ref[z]
    a48 = a_in_ref[mine, 0:3].reshape(48, -1)

    def lows(t, _):
        low_buf[t] = (adapt_scale * dot_nt(u_ref[t], a48)).astype(bf16)
        return 0

    lax.fori_loop(0, 8, lows, 0)
    for d, j in enumerate(zs):
        remote(b_small.at[j], b_small.at[j], small_send.at[d], small_recv.at[d], (s, j)).wait_recv()
        remote(a_small.at[j], a_small.at[j], small_send.at[3 + d], small_recv.at[3 + d], (s, j)).wait_recv()
    for j in range(4):
        b_sel_ref[j] = b_small[j, mine].reshape(48, HDIM)
        a_sel_ref[j] = a_small[j, mine]

    def merge(index, _):
        j = index // 3
        part = index % 3
        head = (2 * core + j) % 4
        b_part = b_sel_ref[head, pl.ds(pl.multiple_of(part * 16, 16), 16), :]
        column = pl.multiple_of(((j // 2) * 6 + part * 2 + j % 2) * HDIM, HDIM)
        for side in range(2):
            a_part = a_in_ref[mine, part, :, pl.ds(side * 1024, 1024)]
            merged = adapt_scale * dot_tn(a_part, b_part)
            w_cat[pl.ds(side * 1024, 1024), pl.ds(column, HDIM)] = (
                w_buf[head, side, part].astype(f32) + merged
            ).astype(bf16)
        return 0

    line.hop(3)
    o_line = Line(o_all, core, s, z, o_send, o_recv)
    o_line.begin()
    cot_line = Line(cots_ref, None, s, z, cot_send, cot_recv)
    line.arrive_core()
    lax.fori_loop(0, 6, merge, 0)
    left = lax.broadcasted_iota(jnp.int32, (256, HDIM), 1) < HDIM // 2

    def project(t, _):
        u = u_ref[t]
        packed = tables[t]
        turned = pltpu.roll(packed, HDIM // 2, 1)
        cos = jnp.where(left, packed, turned)
        sin = jnp.where(left, turned, -packed)
        rows = pl.ds(pl.multiple_of(t * 256, 256), 256)
        for part, out in enumerate((q_buf, k_buf, v_buf)):
            raw = dot_nn(u, w_cat[:, 256 * part : 256 * part + 256])
            for head in range(2):
                piece = raw[:, HDIM * head : HDIM * head + HDIM]
                if part < 2:
                    piece = piece * cos - pltpu.roll(piece, HDIM // 2, 1) * sin
                out[rows, HDIM * head : HDIM * head + HDIM] = piece.astype(bf16)
        return 0

    def project_all(t, _):
        project(t, 0)
        for step, at in ((1, 2), (2, 6)):

            @pl.when(t == at)
            def _():
                o_line.hop(step)

        return 0

    cot_line.begin()
    lax.fori_loop(0, 8, project_all, 0)
    stores += [
        pltpu.make_async_copy(source, target, store_sem.at[1 + i])
        for i, (source, target) in enumerate(
            ((q_buf, q_out), (k_buf, k_out), (v_buf, v_out), (low_buf, low_out), (tables, table_out))
        )
    ]
    for one in stores[1:]:
        one.start()

    tile = attn_tile
    factor = log2e / math.sqrt(HDIM)

    def attend(index, _):
        head = index // 4
        i = index % 4
        lanes = pl.ds(pl.multiple_of(head * HDIM, HDIM), HDIM)
        here = pl.ds(pl.multiple_of(i * tile, tile), tile)
        q = q_buf[here, lanes]

        def fold(j, carry, diagonal):
            top, total, acc = carry
            at = pl.ds(pl.multiple_of(j * tile, tile), tile)
            scores = dot_nt(k_buf[at, lanes], q)
            if diagonal:
                scores = jnp.where(causal(scores, 0, 0), scores, far_below)
            new_top = jnp.maximum(top, jnp.max(scores, axis=0, keepdims=True))
            weight = jnp.exp2(scores * factor - new_top * factor)
            keep = jnp.exp2((top - new_top) * factor)
            total = total * keep + jnp.sum(weight, axis=0, keepdims=True)
            acc = acc * keep + dot_tn(v_buf[at, lanes], weight.astype(bf16))
            return (new_top, total, acc)

        carry = (
            jnp.full((1, tile), far_below, f32),
            jnp.zeros((1, tile), f32),
            jnp.zeros((HDIM, tile), f32),
        )
        carry = lax.fori_loop(0, i, lambda j, c: fold(j, c, False), carry)
        top, total, acc = fold(i, carry, True)
        mixed[here, lanes] = jnp.transpose(acc / total).astype(bf16)
        lse_ref[head, i] = top * factor + jnp.log2(total)
        return 0

    def attend_all(index, _):
        attend(index, 0)

        @pl.when(index == 3)
        def _():
            o_line.hop(3)

        @pl.when((index == 5) & middle)
        def _():
            cot_line.hop(1)

        return 0

    lax.fori_loop(0, 8, attend_all, 0)

    def span_rows(span, first, count):
        return pl.ds(pl.multiple_of(span * 256 + first, 128), count)

    crosses = [
        remote(mixed.at[span_rows(2 * c + 1 - core, 0, 256)], sib.at[c], sib_send.at[c], sib_recv.at[c], (other, z))
        for c in range(4)
    ]
    for one in crosses:
        one.start()
    stores.append(pltpu.make_async_copy(mixed, mixed_out, store_sem.at[6]))
    stores[-1].start()
    o_line.arrive_core()
    b_row = b_od_ref[mine, 0]

    def merge_out(j, _):
        head = (2 * core + j) % 4
        for side in range(2):
            wide = slice(side * 1024, side * 1024 + 1024)
            merged = adapt_scale * dot_tn(a_sel_ref[head], b_row[:, wide])
            o_big[pl.ds(pl.multiple_of(j * HDIM, HDIM), HDIM), wide] = (
                o_all[head, side].astype(f32) + merged
            ).astype(bf16)
        return 0

    lax.fori_loop(0, 4, merge_out, 0)
    o_eff_ref[...] = o_big[0 : 2 * HDIM, :]
    for one in crosses:
        one.wait_recv()

    def rows_of(c, half):
        def load(row):
            at = pl.ds(pl.multiple_of((2 * c + core) * 256 + row, 32), 32)
            return jnp.concatenate([mixed[at, :], sib[c, pl.ds(row, 32), :]], axis=1)

        return some_rows(load, half)

    reduce = Reduce(
        rows_of, lambda rows, wide: dot_nn(rows, o_big[:, wide]), x_ref.shape[2], s, z,
        out_buf, in_buf, own_sum, red_send, red_recv,
    )
    reduce.begin()
    reduce.keep()
    reduce.second()

    @pl.when(middle)
    def _():
        cot_line.hop(2)

    lax.fori_loop(6, 12, merge, 0)
    stores.append(pltpu.make_async_copy(w_cat, w_cat_out, store_sem.at[7]))
    stores[-1].start()
    reduce.third()
    def settle(row, total):
        at = pl.ds(row, 32)
        x = x_own_ref[row // 64, pl.ds(pl.multiple_of(row % 64, 32), 32), :].astype(f32)
        residual = x + total
        residual_ref[at, :] = residual
        normed, _ = norm_rows(residual)
        m_own_ref[at, :] = normed.astype(bf16)

    reduce.finish(0, settle)
    reduce.finish(1, settle)
    @pl.when(z * (3 - z) == 0)
    def _():
        for t in (1, 2, 3):
            cot_line.hop(t)

    for one in stores:
        one.wait()
    for one in swaps + smalls + crosses:
        one.wait_send()
    line.end()
    o_line.end()
    cot_line.end()
    near.end()
    rest.end()
    table_gather.end()
    reduce.end()


def front_layer(x, w_qkv, w_out, b_qkv, a_out, a_in, b_out_down, table, cotangent, set_index):
    bf16 = jnp.bfloat16
    f32 = jnp.float32
    vmem = pl.BlockSpec(memory_space=pltpu.VMEM)
    anywhere = pl.BlockSpec(memory_space=pl.ANY)
    width = x.shape[2]
    shape = jax.ShapeDtypeStruct
    dma = pltpu.SemaphoreType.DMA
    vm = pltpu.VMEM
    return pl.pallas_call(
        front_kernel,
        in_specs=[vmem] + [anywhere] * 4 + [vmem] * 3 + [anywhere, pl.BlockSpec(memory_space=pltpu.SMEM)],
        out_specs=[vmem] * 7 + [anywhere] * 9,
        out_shape=[
            shape((4, 64, width), bf16),
            shape((256, width), bf16),
            shape((256, width), f32),
            shape((256, width), bf16),
            shape((4, 48, HDIM), bf16),
            shape((4, 16, HDIM), bf16),
            shape((2, 4, 1, attn_tile), f32),
            shape((8, 256, width), bf16),
            shape((2048, 256), bf16),
            shape((2048, 256), bf16),
            shape((2048, 256), bf16),
            shape((8, 256, 48), bf16),
            shape((8, 256, HDIM), f32),
            shape((2048, 256), bf16),
            shape((width, 1536), bf16),
            shape((4, 4, 64, width), bf16),
        ],
        scratch_shapes=[
            vm((8, 256, width), bf16),
            vm((4, 2, 3, 1024, HDIM), bf16),
            vm((width, 1536), bf16),
            vm((2048, 256), bf16),
            vm((2048, 256), bf16),
            vm((2048, 256), bf16),
            vm((8, 256, 48), bf16),
            vm((8, 256, HDIM), f32),
            vm((2048, 256), bf16),
            vm((4, 2, HDIM, 1024), bf16),
            vm((4 * HDIM, width), bf16),
            vm((4, 256, 256), bf16),
            vm((6, 128, width), bf16),
            vm((6, 128, width), bf16),
            vm((256, width), f32),
            vm((4, 4, 3, 16, HDIM), bf16),
            vm((4, 4, 16, HDIM), bf16),
        ]
        + [
            dma((count,))
            for count in (3, 3, 10, 10, 10, 10, 10, 10, 13, 13, 13, 13, 13, 13, 6, 6, 4, 4, 6, 6, 5, 8)
        ],
        cost_estimate=spend(150),
        compiler_params=pltpu.CompilerParams(
            collective_id=1, has_side_effects=True, vmem_limit_bytes=58 << 20
        ),
    )(x, w_qkv, w_out, b_qkv, a_out, a_in, b_out_down, table, cotangent, set_index)


def turn_back(gradient, packed):
    left = lax.broadcasted_iota(jnp.int32, packed.shape, 1) < HDIM // 2
    turned = pltpu.roll(packed, HDIM // 2, 1)
    cos = jnp.where(left, packed, turned)
    sin = jnp.where(left, turned, -packed)
    return gradient * cos + pltpu.roll(gradient, HDIM // 2, 1) * sin


def back_kernel(
    g_ref, o_eff_in, mixed_in, b_od_ref, q_in, k_in, v_in, lse_ref, table_in,
    grad_b_in, grad_ad_in, grad_a_in, grad_bd_in, down2_ref, down3_ref, set_ref,
    dq_ref, dk_ref, dv_ref, rank_ref, chunk_ref, pair_ref, g_out, got2_ref,
    grad_b_ref, grad_ad_ref, grad_a_ref, grad_bd_ref, o_eff_ref, mixed_ref, q_ref, k_ref, v_ref, table_ref, down2_buf, got3_buf, pair_sum, g_buf, gm_buf, dots, dk_acc, dv_acc, chunk_src, chunk_sib, chunk_sum, chunk_in,
    send, recv, down_send, down_recv, cs_send, cs_recv, cx_send, cx_recv, store_sem, load_sem,
):
    f32 = jnp.float32
    bf16 = jnp.bfloat16
    s, z = places()
    loads = [
        pltpu.make_async_copy(source, target, load_sem.at[i])
        for i, (source, target) in enumerate(
            (
                (grad_b_in, grad_b_ref),
                (grad_ad_in, grad_ad_ref),
                (grad_a_in, grad_a_ref),
                (grad_bd_in, grad_bd_ref),
                (o_eff_in, o_eff_ref),
                (mixed_in, mixed_ref),
                (q_in, q_ref),
                (k_in, k_ref),
                (v_in, v_ref),
                (table_in, table_ref),
                (down2_ref, down2_buf),
            )
        )
    ]
    for one in loads:
        one.start()
    core = s % 2
    chip = s // 2
    other = flip(s, 1)
    sx = flip(s, 2)
    sy = flip(s, 4)
    sd = flip(sx, 4)
    meet([(None, (t, z)) for t in (other, sx, sy, sd)] + [(None, (s, flip(z, 1))), (None, (s, flip(z, 2)))])
    g_buf[s] = g_ref[...]
    gather = Gather(g_buf, s, z, send, recv, 128)
    gather.begin()
    across = remote(down3_ref, got3_buf, down_send.at[0], down_recv.at[0], (s, flip(z, 1)))
    across.start()
    onward = remote(pair_sum, got2_ref, down_send.at[1], down_recv.at[1], (s, flip(z, 2)))
    member = set_ref[z]
    tile = attn_tile
    scale = 1.0 / math.sqrt(HDIM)
    factor = log2e * scale
    dk_acc[...] = jnp.zeros_like(dk_acc)
    dv_acc[...] = jnp.zeros_like(dv_acc)

    def store(t):
        return pltpu.make_async_copy(g_buf.at[t], g_out.at[t], store_sem.at[t])

    def chip_rows(c):
        here = pl.ds(pl.multiple_of(c * tile, tile), tile)

        def head_rows(part, _):
            t = 2 * c + part
            store(t).start()
            g = g_buf[t]
            back = dot_nt(g, o_eff_ref[...]).astype(bf16)
            gm_buf[pl.ds(pl.multiple_of(part * 256, 256), 256), :] = back
            product = back.astype(f32) * mixed_ref[
                pl.ds(pl.multiple_of(t * 256, 256), 256), :
            ].astype(f32)
            for head in range(2):
                turned = jnp.transpose(product[:, HDIM * head : HDIM * head + HDIM])
                dots[head, :, pl.ds(pl.multiple_of(part * 256, 256), 256)] = jnp.sum(turned, axis=0, keepdims=True)
            rank_ref[t] = (adapt_scale * dot_nt(g, b_od_ref[member, 0])).astype(bf16)
            return 0

        lax.fori_loop(0, 2, head_rows, 0)

        def one_head(head, _):
            lanes = pl.ds(pl.multiple_of(head * HDIM, HDIM), HDIM)
            q = q_ref[here, lanes]
            go = gm_buf[:, lanes]
            row_dots = dots[head]
            lse = lse_ref[head, c]

            def fold(j, dq, diagonal):
                at = pl.ds(pl.multiple_of(j * tile, tile), tile)
                k = k_ref[at, lanes]
                scores = dot_nt(k, q)
                weight = jnp.exp2(scores * factor - lse)
                if diagonal:
                    weight = jnp.where(causal(scores, 0, 0), weight, 0.0)
                grad_weight = dot_nt(v_ref[at, lanes], go)
                grad_scores = (weight * (grad_weight - row_dots)).astype(bf16)
                dv_acc[at, lanes] += dot_nn(weight.astype(bf16), go)
                dk_acc[at, lanes] += dot_nn(grad_scores, q)
                return dq + dot_tn(grad_scores, k)

            dq = lax.fori_loop(0, c, lambda j, total: fold(j, total, False), jnp.zeros((tile, HDIM), f32))
            dq = fold(c, dq, True)
            dq_ref[here, lanes] = turn_back(dq * scale, table_ref[here, :]).astype(bf16)
            return 0

        lax.fori_loop(0, 2, one_head, 0)

    def fill(one, _):
        whole = jnp.zeros((48, dk_acc.shape[0]), f32)
        split = jnp.zeros((48, dk_acc.shape[0]), f32)
        for seq in range(4):
            used = (set_ref[seq] == one).astype(f32)
            whole += used * jnp.concatenate([grad_a_ref[seq], grad_bd_ref[seq]], axis=0)
            split += used * jnp.concatenate([grad_b_ref[seq, 0], grad_b_ref[seq, 1], grad_ad_ref[seq]], axis=0)
        for part in range(2):
            rows = slice(24 * part, 24 * part + 24)
            chunk_src[2 * one + part] = jnp.concatenate([whole[rows], split[rows]], axis=0).astype(bf16)
        return 0

    for one in loads[:4]:
        one.wait()
    lax.fori_loop(0, 4, fill, 0)
    crosses = [
        remote(chunk_src.at[2 * c + 1 - core], chunk_sib.at[c], cs_send.at[c], cs_recv.at[c], (other, z))
        for c in range(4)
    ]
    for one in crosses:
        one.start()
    for one in loads[4:]:
        one.wait()
    around = [
        remote(chunk_sum.at[t // 2], chunk_in.at[d], cx_send.at[d], cx_recv.at[d], (t, z))
        for d, t in enumerate((sx, sy, sd))
    ]

    def total_chunks(c, _):
        chunk_sum[c] = (chunk_src[2 * c + core].astype(f32) + chunk_sib[c].astype(f32)).astype(bf16)
        return 0

    def pair_rows(seq, _):
        for first, target in ((0, pair_sum), (2, pair_ref)):
            target[seq] = (
                down2_buf[first + seq].astype(f32) + got3_buf[first + seq].astype(f32)
            ).astype(bf16)
        return 0

    def visit(step, _):
        @pl.when(step == 0)
        def _():
            gather.arrive_core(0)

        @pl.when(step == 1)
        def _():
            gather.arrive_first()
            for one in crosses:
                one.wait_recv()
            lax.fori_loop(0, 4, total_chunks, 0)
            for one in around:
                one.start()
            gather.arrive_neighbours()
            across.wait_recv()
            lax.fori_loop(0, 2, pair_rows, 0)
            onward.start()
            gather.arrive_core(1)

        @pl.when(step == 2)
        def _():
            gather.arrive_core(2)

        @pl.when(step == 3)
        def _():
            gather.arrive_diagonal()
            gather.arrive_core(3)

        by_x = step % 2
        by_y = step // 2
        chip_rows(chip + by_x * (1 - 2 * (chip % 2)) + by_y * (2 - 4 * (chip // 2)))
        return 0

    lax.fori_loop(0, 4, visit, 0)

    def last(j, _):
        at = pl.ds(pl.multiple_of(j * tile, tile), tile)
        for head in range(2):
            lanes = slice(HDIM * head, HDIM * head + HDIM)
            dk_ref[at, lanes] = turn_back(dk_acc[at, lanes] * scale, table_ref[at, :]).astype(bf16)
            dv_ref[at, lanes] = dv_acc[at, lanes].astype(bf16)
        return 0

    lax.fori_loop(0, 4, last, 0)
    for one in around:
        one.wait_recv()
    chunk = chunk_sum[chip].astype(f32)
    for d in range(3):
        chunk += chunk_in[d].astype(f32)
    chunk_ref[...] = chunk
    for t in range(8):
        store(t).wait()
    gather.end()
    onward.wait()
    for one in crosses + around + [across]:
        one.wait_send()


def back_layer(*operands):
    bf16 = jnp.bfloat16
    f32 = jnp.float32
    vmem = pl.BlockSpec(memory_space=pltpu.VMEM)
    anywhere = pl.BlockSpec(memory_space=pl.ANY)
    width = operands[0].shape[1]
    shape = jax.ShapeDtypeStruct
    dma = pltpu.SemaphoreType.DMA
    vm = pltpu.VMEM
    return pl.pallas_call(
        back_kernel,
        in_specs=[vmem, anywhere, anywhere, vmem, anywhere, anywhere, anywhere, vmem, anywhere]
        + [anywhere] * 6
        + [pl.BlockSpec(memory_space=pltpu.SMEM)],
        out_specs=[vmem] * 6 + [anywhere] * 2,
        out_shape=[
            shape((2048, 256), bf16),
            shape((2048, 256), bf16),
            shape((2048, 256), bf16),
            shape((8, 256, 16), bf16),
            shape((48, width), f32),
            shape((2, 64, width), bf16),
            shape((8, 256, width), bf16),
            shape((2, 64, width), bf16),
        ],
        scratch_shapes=[vm(operands[i].shape, f32) for i in (9, 10, 11, 12)]
        + [
            vm((256, width), bf16),
            vm((2048, 256), bf16),
            vm((2048, 256), bf16),
            vm((2048, 256), bf16),
            vm((2048, 256), bf16),
            vm((2048, HDIM), f32),
            vm((4, 64, width), bf16),
            vm((4, 64, width), bf16),
            vm((2, 64, width), bf16),
            vm((8, 256, width), bf16),
            vm((512, 256), bf16),
            vm((2, 1, 512), f32),
            vm((2048, 256), f32),
            vm((2048, 256), f32),
            vm((8, 48, width), bf16),
            vm((4, 48, width), bf16),
            vm((4, 48, width), bf16),
            vm((3, 48, width), bf16),
        ]
        + [dma((count,)) for count in (gather_sems, gather_sems, 2, 2, 4, 4, 3, 3, 8, 11)],
        cost_estimate=spend(60),
        compiler_params=pltpu.CompilerParams(
            collective_id=3, has_side_effects=True, vmem_limit_bytes=60 << 20
        ),
    )(*operands)


def mlp_line_kernel(
    m_ref, residual_in, cots_ref, w_gu_ref, w_d_ref, a_in, b_in, ad_in, bd_in, set_ref,
    g_ref, grad_res_ref, down0_ref, down1_ref, down2_ref, down3_ref, grad_b_ref, grad_ad_ref, grad_a_ref, grad_bd_ref,
    residual_ref, a_ref, b_ref, ad_ref, bd_ref, m_buf, wg, wu, wd, acts, grad_gates, grad_ups, cot_buf, back_acc, ranks, slots, r1, r2, r3, r5, stage,
    up_send, up_recv, dn_send, dn_recv, send1, recv1, send4, recv4, send5, recv5, send23, recv23,
    weight_sem, cot_sem, stage_sem, late_sem,
):
    s, z = places()
    late = [
        pltpu.make_async_copy(source, target, late_sem.at[i])
        for i, (source, target) in enumerate(
            (
                (a_in, a_ref),
                (b_in, b_ref),
                (ad_in, ad_ref),
                (bd_in, bd_ref),
                (residual_in, residual_ref),
            )
        )
    ]
    for one in late:
        one.start()
    tiles = wg.shape[0]
    tile = wg.shape[2]
    f32 = jnp.float32
    bf16 = jnp.bfloat16
    middle = z * (3 - z) == 2
    at_end = z * (3 - z) == 0
    pair = flip(z, 1)
    opposite = 3 - z
    inner = 1 + z // 2
    high = z // 2
    ids = [z, pair, 2 - high, 3 - 3 * high]
    far = 3 - 3 * high

    def load_tile(h):
        columns = pl.ds(h * tile if isinstance(h, int) else pl.multiple_of(h * tile, tile), tile)
        return [
            pltpu.make_async_copy(w_gu_ref.at[0, :, columns], wg.at[h], weight_sem.at[3 * h]),
            pltpu.make_async_copy(w_gu_ref.at[1, :, columns], wu.at[h], weight_sem.at[3 * h + 1]),
            pltpu.make_async_copy(w_d_ref.at[columns, :], wd.at[h], weight_sem.at[3 * h + 2]),
        ]

    for h in range(tiles):
        for one in load_tile(h):
            one.start()

    others = [z, pair, flip(z, 2), opposite]
    down_refs = (down0_ref, down1_ref, down2_ref, down3_ref)

    def load_cot(seq):
        return [pltpu.make_async_copy(cots_ref.at[j, seq], cot_buf.at[j], cot_sem.at[j]) for j in range(4)]

    for one in load_cot(z):
        one.start()

    meet([(z < 3, (s, z + 1)), (z > 0, (s, z - 1)), (None, (s, flip(z, 2)))])
    m_buf[z] = m_ref[...]

    def up(hop, j):
        return remote(m_buf.at[j], m_buf.at[j], up_send.at[hop], up_recv.at[hop], (s, z + 1))

    def down(hop, j):
        return remote(m_buf.at[j], m_buf.at[j], dn_send.at[hop], dn_recv.at[hop], (s, z - 1))

    def begin():
        @pl.when(z < 3)
        def _():
            up(0, z).start()

        @pl.when(z > 0)
        def _():
            down(0, z).start()

    def hop(t):
        def from_above(side):
            @pl.when((z + t <= 3) & side)
            def _():
                down(t - 1, z + t).wait_recv()
                if t < 3:

                    @pl.when(z > 0)
                    def _():
                        down(t, z + t).start()

        from_above(z < 2)

        @pl.when(z >= t)
        def _():
            up(t - 1, z - t).wait_recv()
            if t < 3:

                @pl.when(z < 3)
                def _():
                    up(t, z - t).start()

        from_above(z >= 2)

    def hop_end():
        @pl.when(z < 3)
        def _():
            up(0, z).wait_send()

        @pl.when(z > 0)
        def _():
            down(0, z).wait_send()

        for t in (1, 2):

            @pl.when((z >= t) & (z < 3))
            def _():
                up(t, z - t).wait_send()

            @pl.when((z + t <= 3) & (z > 0))
            def _():
                down(t, z + t).wait_send()

    def piece(p):
        return pl.ds(p * 64 if isinstance(p, int) else pl.multiple_of(p * 64, 64), 64)

    def copy1():
        return remote(slots.at[1], r1, send1.at[0], recv1.at[0], (s, pair))

    def copy2():
        return remote(slots.at[2], r2, send23.at[0], recv23.at[0], (s, opposite))

    def copy3():
        return remote(slots.at[2], r3, send23.at[1], recv23.at[1], (s, inner))

    def copy4(p):
        return remote(slots.at[3, piece(p)], r3.at[piece(p)], send4.at[p], recv4.at[p], (s, far))

    def copy5(p):
        return remote(slots.at[3, piece(p)], r5.at[piece(p)], send5.at[p], recv5.at[p], (s, inner))

    def stage_copies(seq):
        return [
            pltpu.make_async_copy(stage.at[others[d]], down_refs[d].at[seq], stage_sem.at[d]) for d in range(4)
        ]

    def in_maps(seq):
        return a_ref[set_ref[seq], 3:5].reshape(32, -1)

    def sequence(slot):
        return sum((slot == i).astype(jnp.int32) * one for i, one in enumerate(ids + [z]))

    def add(slot, extra):
        def one(p, _):
            slots[slot, piece(p), :] = (
                slots[slot, piece(p), :].astype(f32) + extra[piece(p), :].astype(f32)
            ).astype(bf16)
            return 0

        lax.fori_loop(0, 4, one, 0)

    begin()
    for one in late:
        one.wait()

    def chunk(slot, _):
        seq = sequence(slot)
        member = set_ref[seq]
        for one in load_cot(seq):
            one.wait()
        ranks[:, 0:32] = adapt_scale * dot_nt(m_buf[seq], in_maps(seq))
        ranks[:, 32:48] = adapt_scale * dot_nt(cot_buf[...].reshape(256, -1), bd_ref[member, 1])
        ranks[:, 48:96] = jnp.zeros((256, 48), f32)
        back_acc[...] = jnp.zeros_like(back_acc)

        def step(h, _):
            columns = pl.ds(pl.multiple_of(h * tile, tile), tile)

            @pl.when(slot == 0)
            def _():
                for one in load_tile(h):
                    one.wait()

            @pl.when((slot == 3) & (h == 1) & middle)
            def _():
                copy1().start()

            low = ranks[...].astype(bf16)
            low_gate = low[:, 0:16]
            low_up = low[:, 16:32]
            low_cot = low[:, 32:48]
            bg = b_ref[member, 0, :, columns]
            bu = b_ref[member, 1, :, columns]
            ad = ad_ref[member, :, columns]
            rows = m_buf[seq]
            cot = cot_buf[...].reshape(256, -1)
            gate = dot_nn(rows, wg[h]) + dot_nn(low_gate, bg)
            up_value = dot_nn(rows, wu[h]) + dot_nn(low_up, bu)
            grad_act = dot_nt(cot, wd[h]) + dot_nn(low_cot, ad)
            sig = jax.nn.sigmoid(gate)
            act = (gate * sig * up_value).astype(bf16)
            grad_up = (grad_act * gate * sig).astype(bf16)
            grad_gate = (grad_act * up_value * sig * (1.0 + gate * (1.0 - sig))).astype(bf16)
            acts[h] = act
            grad_gates[h] = grad_gate
            grad_ups[h] = grad_up
            for part in range(4):
                wide = pl.ds(part * 512, 512)
                back_acc[:, wide] += dot_nt(grad_gate, wg[h, wide, :]) + dot_nt(grad_up, wu[h, wide, :])
            ranks[:, 64:80] += dot_nt(grad_gate, bg)
            ranks[:, 80:96] += dot_nt(grad_up, bu)
            return 0

        def later(h, _):
            columns = pl.ds(pl.multiple_of(h * tile, tile), tile)
            low = ranks[:, 0:48].astype(bf16)
            act = acts[h]
            for part in range(4):
                wide = pl.ds(part * 512, 512)
                back_acc[:, wide] += dot_nn(act, wd[h, :, wide])
            ranks[:, 48:64] += dot_nt(act, ad_ref[member, :, columns])
            grad_b_ref[seq, 0, :, columns] = dot_tn(low[:, 0:16], grad_gates[h])
            grad_b_ref[seq, 1, :, columns] = dot_tn(low[:, 16:32], grad_ups[h])
            grad_ad_ref[seq, :, columns] = dot_tn(low[:, 32:48], act)
            return 0

        lax.fori_loop(0, tiles, step, 0)
        for t in (1, 2):

            @pl.when((slot == t - 1) & middle)
            def _():
                hop(t)

        back_rank = (adapt_scale * ranks[:, 64:96]).astype(bf16)
        slots[slot] = (back_acc[...] + dot_nn(back_rank, in_maps(seq))).astype(bf16)

        @pl.when((slot == 1) & at_end)
        def _():
            copy1().start()

        @pl.when((slot == 2) & at_end)
        def _():
            copy3().start()

        @pl.when((slot == 3) & at_end)
        def _():
            copy5(0).start()
            copy5(1).start()

        @pl.when((slot == 3) & middle)
        def _():
            copy3().wait_recv()
            add(2, r3)
            copy2().start()

        back_acc[...] = jnp.zeros_like(back_acc)
        lax.fori_loop(0, tiles, later, 0)
        low_down = (adapt_scale * ranks[:, 48:64]).astype(bf16)
        grad_a_ref[seq] = dot_tn(back_rank, m_buf[seq])
        grad_bd_ref[seq] = dot_tn(low_down, cot_buf[...].reshape(256, -1))

        @pl.when(slot > 0)
        def _():
            for one in stage_copies(seq):
                one.wait()

        own = (slot == 0).astype(f32)
        value = back_acc[...] + dot_nn(low_down, bd_ref[member, 1]) + own * residual_ref[...]
        stage[...] = value.astype(bf16).reshape(4, 64, -1)
        for one in stage_copies(seq):
            one.start()
        for one in load_cot(sequence(slot + 1)):
            one.start()
        for t in (1, 2, 3):

            @pl.when((slot == t - 1) & at_end)
            def _():
                hop(t)

        return 0

    lax.fori_loop(0, 4, chunk, 0)

    @pl.when(at_end)
    def _():
        for p in (2, 3):
            copy5(p - 2).wait_send()
            copy5(p).start()

    @pl.when(middle)
    def _():
        def one(p, _):
            copy5(p).wait_recv()
            slots[3, piece(p), :] = (
                slots[3, piece(p), :].astype(f32) + r5[piece(p), :].astype(f32)
            ).astype(bf16)
            copy4(p).start()
            return 0

        lax.fori_loop(0, 4, one, 0)

    copy1().wait_recv()
    add(0, r1)

    @pl.when(middle)
    def _():
        copy2().wait_recv()
        add(0, r2)

    for one in load_cot(z):
        one.wait()

    def settle(p, _):
        @pl.when(at_end)
        def _():
            copy4(p).wait_recv()
            slots[0, piece(p), :] = (
                slots[0, piece(p), :].astype(f32) + r3[piece(p), :].astype(f32)
            ).astype(bf16)

        def rows32(half, _):
            at = pl.ds(pl.multiple_of(p * 64 + half * 32, 32), 32)
            grad = slots[0, at, :].astype(f32)
            normed, inverse = norm_rows(residual_ref[at, :])
            cot = cot_buf[p, pl.ds(pl.multiple_of(half * 32, 32), 32), :].astype(f32)
            value = cot + norm_back(grad, normed, inverse)
            grad_res_ref[at, :] = value
            g_ref[at, :] = value.astype(bf16)
            return 0

        lax.fori_loop(0, 2, rows32, 0)
        return 0

    lax.fori_loop(0, 4, settle, 0)
    for one in stage_copies(z):
        one.wait()
    hop_end()
    copy1().wait_send()

    @pl.when(at_end)
    def _():
        copy3().wait_send()
        for p in (2, 3):
            copy5(p).wait_send()

    @pl.when(middle)
    def _():
        copy2().wait_send()
        for p in range(4):
            copy4(p).wait_send()


def mlp_line(m_own, residual, cots, w_gate_up, w_down, a_in, b_gate_up, a_down, b_out_down, set_index):
    bf16 = jnp.bfloat16
    f32 = jnp.float32
    vmem = pl.BlockSpec(memory_space=pltpu.VMEM)
    anywhere = pl.BlockSpec(memory_space=pl.ANY)
    width = m_own.shape[1]
    hidden = w_down.shape[0]
    tile = hidden_tile
    tiles = hidden // tile
    shape = jax.ShapeDtypeStruct
    dma = pltpu.SemaphoreType.DMA
    vm = pltpu.VMEM
    return pl.pallas_call(
        mlp_line_kernel,
        in_specs=[vmem]
        + [anywhere] * 8
        + [pl.BlockSpec(memory_space=pltpu.SMEM)],
        out_specs=[vmem, vmem] + [anywhere] * 4 + [vmem, vmem, vmem, vmem],
        out_shape=[
            shape((256, width), bf16),
            shape((256, width), f32),
        ]
        + [shape((4, 64, width), bf16)] * 4
        + [
            shape((4, 2, 16, hidden), f32),
            shape((4, 16, hidden), f32),
            shape((4, 32, width), f32),
            shape((4, 16, width), f32),
        ],
        scratch_shapes=[
            vm((256, width), f32),
            vm(a_in.shape, bf16),
            vm(b_gate_up.shape, bf16),
            vm(a_down.shape, bf16),
            vm(b_out_down.shape, bf16),
            vm((4, 256, width), bf16),
            vm((tiles, width, tile), bf16),
            vm((tiles, width, tile), bf16),
            vm((tiles, tile, width), bf16),
            vm((tiles, 256, tile), bf16),
            vm((tiles, 256, tile), bf16),
            vm((tiles, 256, tile), bf16),
            vm((4, 64, width), bf16),
            vm((256, width), f32),
            vm((256, 96), f32),
            vm((4, 256, width), bf16),
            vm((256, width), bf16),
            vm((256, width), bf16),
            vm((256, width), bf16),
            vm((256, width), bf16),
            vm((4, 64, width), bf16),
        ]
        + [dma((3,))] * 4
        + [dma((4,))] * 6
        + [dma((2,))] * 2
        + [dma((3 * tiles,)), dma((4,)), dma((4,)), dma((5,))],
        cost_estimate=spend(110),
        compiler_params=pltpu.CompilerParams(
            collective_id=5, has_side_effects=True, vmem_limit_bytes=60 << 20
        ),
    )(m_own, residual, cots, w_gate_up, w_down, a_in, b_gate_up, a_down, b_out_down, set_index)


def finish_kernel(
    dq_in, dk_in, dv_in, w_in, x_own_in, residual_in, u_ref, g_ref, low_in, rank_ref, mixed_in,
    b_sel_ref, a_sel_ref, chunk_ref, down0_in, down1_ref, got2_ref, pair_ref,
    set_ref,
    result_ref, grad_ref, whole_ref, split_ref, sequence_ref, heads_ref, got3_ref,
    sets_ref, pool_ref, dq_ref, dk_ref, dv_ref, x_own_ref, low_ref,
    w_ref, residual_ref, mixed_ref, down0_ref, got1_ref,
    own_ref, sib_q, sib_k, sib_v, out_buf, in_buf, own_sum, u_buf, g_buf, a_acc, b_acc, chunk_src, chunk_sib, chunk_sum,
    chunk_in, z_src, z_in, sets_src, sets_in, head_src, head_in,
    a2a_send, a2a_recv, sib_send, sib_recv, send, recv, load_sem, cs_send, cs_recv, cx_send, cx_recv,
    cz_send, cz_recv, cg_send, cg_recv, hz_send, hz_recv, hg_send, hg_recv, down_send, down_recv,
    sz_send, sz_recv, sg_send, sg_recv, late_sem,
):
    f32 = jnp.float32
    bf16 = jnp.bfloat16
    s, z = places()
    loads = [
        pltpu.make_async_copy(source, target, late_sem.at[i])
        for i, (source, target) in enumerate(
            (
                (dq_in, dq_ref),
                (dk_in, dk_ref),
                (dv_in, dv_ref),
                (w_in, w_ref),
                (mixed_in, mixed_ref),
                (low_in, low_ref),
                (x_own_in, x_own_ref),
                (residual_in, residual_ref),
                (down0_in, down0_ref),
            )
        )
    ]
    for one in loads[:5]:
        one.start()
    core = s % 2
    chip = s // 2
    other = flip(s, 1)
    sx = flip(s, 2)
    sy = flip(s, 4)
    sd = flip(sx, 4)
    zs = [flip(z, 1), flip(z, 2), 3 - z]
    meet([(None, (t, z)) for t in (other, sx, sy, sd)] + [(None, (s, j)) for j in zs])
    last_down = remote(pair_ref, got3_ref, down_send.at[0], down_recv.at[0], (s, flip(z, 2)))
    last_down.start()
    pair_down = remote(down1_ref, got1_ref, down_send.at[1], down_recv.at[1], (s, zs[0]))
    pair_down.start()
    sets_src[...] = chunk_ref[0:32].astype(bf16)
    sets_along = [remote(sets_src, sets_in.at[d], sz_send.at[d], sz_recv.at[d], (s, j)) for d, j in enumerate(zs)]
    for one in sets_along:
        one.start()
    mine = (dq_ref, dk_ref, dv_ref)
    sources = (dq_in, dk_in, dv_in)
    theirs = (sib_q, sib_k, sib_v)
    swaps = [
        remote(
            sources[p].at[2 * c + 1 - core], theirs[p].at[c], sib_send.at[4 * p + c], sib_recv.at[4 * p + c], (other, z)
        )
        for c in range(4)
        for p in range(3)
    ]
    for one in swaps:
        one.start()

    def load(t):
        return [
            pltpu.make_async_copy(u_ref.at[t], u_buf.at[t % 2], load_sem.at[t % 2]),
            pltpu.make_async_copy(g_ref.at[t], g_buf.at[t % 2], load_sem.at[2 + t % 2]),
        ]

    for one in load(0):
        one.start()
    for one in swaps:
        one.wait_recv()

    def rows_of(c, half):
        def load(row):
            at = pl.ds(row, 32)
            return jnp.concatenate(
                [ref[2 * c + core, at, :] for ref in mine] + [ref[c, at, :] for ref in theirs], axis=1
            )

        return some_rows(load, half)

    reduce = Reduce(
        rows_of, lambda rows, wide: dot_nt(rows, w_ref[wide, :]), x_own_ref.shape[2], s, z,
        out_buf, in_buf, own_sum, send, recv,
    )
    for one in loads[:4]:
        one.wait()
    reduce.begin()
    for one in loads[5:]:
        one.start()
    reduce.keep()
    loads[4].wait()

    b_two = [
        jnp.concatenate(
            [b_sel_ref[2 * core, 16 * p : 16 * p + 16], b_sel_ref[2 * core + 1, 16 * p : 16 * p + 16]], axis=1
        )
        for p in range(3)
    ]
    a_two = jnp.concatenate([a_sel_ref[2 * core], a_sel_ref[2 * core + 1]], axis=1)

    a_acc[...] = jnp.zeros_like(a_acc)
    b_acc[...] = jnp.zeros_like(b_acc)

    def adapt(t, _):
        for one in load(t):
            one.wait()

        @pl.when(t < 7)
        def _():
            for one in load(t + 1):
                one.start()

        back = jnp.concatenate([dot_nt(mine[p][t], b_two[p]) for p in range(3)], axis=1)
        back = (adapt_scale * back).astype(bf16)
        lows = (adapt_scale * dot_nt(mixed_ref[t], a_two)).astype(bf16)
        u = u_buf.at[t % 2]
        g = g_buf.at[t % 2]

        def one(part, _):
            wide = pl.ds(pl.multiple_of(part * 512, 512), 512)
            a_acc[:, wide] += dot_tn(back, u[:, wide])
            b_acc[:, wide] += dot_tn(lows, g[:, wide])
            return 0

        lax.fori_loop(0, 4, one, 0)

        @pl.when(t == 2)
        def _():
            reduce.second()

        @pl.when(t == 6)
        def _():
            reduce.third()

        return 0

    lax.fori_loop(0, 8, adapt, 0)
    for one in loads[5:]:
        one.wait()
    per_head = [
        dot_tn(low_ref[...].reshape(2048, 48)[:, 16 * p : 16 * p + 16], mine[p][...].reshape(2048, 256))
        for p in range(3)
    ] + [dot_tn(rank_ref[...].reshape(2048, 16), mixed_ref[...].reshape(2048, 256))]
    for head in range(2):
        columns = slice(HDIM * head, HDIM * head + HDIM)
        head_src[head] = jnp.concatenate([part[:, columns] for part in per_head], axis=0).astype(bf16)

    keeper = (z // 2) == core

    def head_copy(head):
        return remote(head_src.at[head], head_in.at[z], hz_send.at[head], hz_recv.at[z], (s, 2 * core + head))

    for head in range(2):

        @pl.when(2 * core + head != z)
        def _():
            head_copy(head).start()

        @pl.when(2 * core + head == z)
        def _():
            head_in[z] = head_src[head]

    for i in range(8):
        sequence = a_acc[8 * i : 8 * i + 8] if i < 6 else b_acc[8 * i - 48 : 8 * i - 40]
        chunk_src[i] = jnp.concatenate([sequence, jnp.zeros((8, a_acc.shape[1]), f32)], axis=0).astype(bf16)
    crosses = [
        remote(chunk_src.at[2 * c + 1 - core], chunk_sib.at[c], cs_send.at[c], cs_recv.at[c], (other, z))
        for c in range(4)
    ]
    for one in crosses:
        one.start()
    for one in crosses:
        one.wait_recv()
    for c in range(4):
        chunk_sum[c] = (chunk_src[2 * c + core].astype(f32) + chunk_sib[c].astype(f32)).astype(bf16)
    around = [
        remote(chunk_sum.at[t // 2], chunk_in.at[d], cx_send.at[d], cx_recv.at[d], (t, z))
        for d, t in enumerate((sx, sy, sd))
    ]
    for one in around:
        one.start()

    for one in sets_along:
        one.wait_recv()
    whole = chunk_ref[0:24]
    for d in range(3):
        whole += sets_in[d, 0:24].astype(f32)
    sets_ref[s] = jnp.concatenate([whole, chunk_ref[24:48]], axis=0).astype(bf16)

    def settle(row, total):
        at = pl.ds(row, 32)
        inside = pl.ds(pl.multiple_of(row % 64, 32), 32)
        normed, inverse = norm_rows(x_own_ref[row // 64, inside, :].astype(f32))
        value = residual_ref[at, :] + norm_back(total, normed, inverse)
        own_ref[row // 64, inside, :] = value.astype(bf16)

    def back(d, half):
        rows = pl.ds(32 * half, 32)
        return remote(
            own_ref.at[zs[d], rows], grad_ref.at[z, rows], a2a_send.at[2 * d + half], a2a_recv.at[2 * d + half],
            (s, zs[d]),
        )

    backs = []
    for half in range(2):
        reduce.finish(half, settle)
        for d in range(3):
            backs.append(back(d, half))
            backs[-1].start()
        if half == 0:
            for one in around:
                one.wait_recv()
            chunk = chunk_sum[chip].astype(f32)
            for d in range(3):
                chunk += chunk_in[d].astype(f32)
            z_src[...] = chunk.astype(bf16)
            along = [remote(z_src, z_in.at[d], cz_send.at[d], cz_recv.at[d], (s, j)) for d, j in enumerate(zs)]
            for one in along:
                one.start()
    grad_ref[z] = own_ref[z]

    def sets_copy(t, index, target):
        return remote(sets_ref.at[t], sets_ref.at[t], sg_send.at[index], sg_recv.at[index], (target, z))

    sets_gives = [sets_copy(s, index, target) for index, target in enumerate((sx, sy, sd, other))]
    for one in sets_gives:
        one.start()

    last_down.wait_recv()
    pair_down.wait_recv()

    def result_rows(part, _):
        for first, other_pair in ((0, got2_ref), (2, got3_ref)):
            result_ref[first + part] = (
                down0_ref[first + part].astype(f32)
                + got1_ref[first + part].astype(f32)
                + other_pair[part].astype(f32)
            ).astype(bf16)
        return 0

    lax.fori_loop(0, 2, result_rows, 0)
    def head_spread(target, index):
        return remote(heads_ref.at[chip], heads_ref.at[chip], hg_send.at[index], hg_recv.at[index], (target, z))

    def head_pass(t, index):
        c = t // 2
        return remote(heads_ref.at[c], heads_ref.at[c], hg_send.at[index], hg_recv.at[index], (other, z))

    @pl.when(keeper)
    def _():
        for j in range(4):

            @pl.when(z != j)
            def _():
                remote(head_src.at[0], head_in.at[j], hz_send.at[0], hz_recv.at[j], (s, j)).wait_recv()

        for member in range(4):
            total = jnp.zeros((64, HDIM), f32)
            for seq in range(4):
                total += (set_ref[seq] == member).astype(f32) * head_in[seq].astype(f32)
            heads_ref[chip, pl.ds(64 * member, 64)] = total.astype(bf16)
        for index, target in enumerate((sx, sy, sd, other)):
            head_spread(target, index).start()

    for one in along:
        one.wait_recv()
    places_z = [z] + zs
    parts = [chunk[0:8]] + [z_in[d, 0:8].astype(f32) for d in range(3)]
    by_member = [
        sum((set_ref[places_z[d]] == member).astype(f32) * parts[d] for d in range(4)) for member in range(4)
    ]
    pool_ref[s] = jnp.concatenate(by_member, axis=0).astype(bf16)

    def pool_copy(t, index, target):
        return remote(pool_ref.at[t], pool_ref.at[t], cg_send.at[index], cg_recv.at[index], (target, z))

    gives = [pool_copy(s, index, target) for index, target in enumerate((sx, sy, sd, other))]
    for one in gives:
        one.start()

    @pl.when(keeper)
    def _():
        for index, t in enumerate((sx, sy, sd)):
            head_pass(t, index).wait_recv()
            head_pass(t, 4 + index).start()

    for copy in (sets_copy, pool_copy):
        for index, t in enumerate((sx, sy, sd)):
            copy(t, index, other).wait_recv()
            copy(t, 4 + index, other).start()
    for copy in (sets_copy, pool_copy):
        copy(other, 3, other).wait_recv()
        for index, t in enumerate((sx, sy, sd)):
            copy(flip(t, 1), 4 + index, other).wait_recv()

    def widen(t, _):
        rows = sets_ref[t].astype(f32)
        whole_ref[t] = rows[0:24]
        split_ref[t] = rows[24:48]
        rows = pool_ref[t].astype(f32)
        for member in range(4):
            sequence_ref[member, pl.ds(pl.multiple_of(8 * t, 8), 8), :] = rows[8 * member : 8 * member + 8]
        return 0

    lax.fori_loop(0, 8, widen, 0)

    @pl.when(z // 2 != core)
    def _():
        head_spread(other, 3).wait_recv()
        for index, t in enumerate((sx, sy, sd)):
            head_pass(t, 4 + index).wait_recv()

    for d, j in enumerate(zs):
        for half in range(2):
            rows = pl.ds(32 * half, 32)
            index = 2 * d + half
            remote(
                own_ref.at[j, rows], grad_ref.at[j, rows], a2a_send.at[index], a2a_recv.at[index], (s, j)
            ).wait_recv()
    for one in swaps + crosses + around + backs + along + gives + sets_along + sets_gives + [last_down, pair_down]:
        one.wait_send()
    for index, t in enumerate((sx, sy, sd)):
        pool_copy(t, 4 + index, other).wait_send()
        sets_copy(t, 4 + index, other).wait_send()
    reduce.end()
    for head in range(2):

        @pl.when(2 * core + head != z)
        def _():
            head_copy(head).wait_send()

    @pl.when(keeper)
    def _():
        for index, target in enumerate((sx, sy, sd, other)):
            head_spread(target, index).wait_send()
        for index, t in enumerate((sx, sy, sd)):
            head_pass(t, 4 + index).wait_send()


def finish_layer(*operands):
    bf16 = jnp.bfloat16
    f32 = jnp.float32
    vmem = pl.BlockSpec(memory_space=pltpu.VMEM)
    anywhere = pl.BlockSpec(memory_space=pl.ANY)
    width = operands[4].shape[2]
    dma = pltpu.SemaphoreType.DMA
    vm = pltpu.VMEM
    shape = jax.ShapeDtypeStruct
    return pl.pallas_call(
        finish_kernel,
        in_specs=[anywhere] * 9
        + [vmem, anywhere]
        + [vmem] * 3
        + [anywhere] * 2
        + [vmem] * 2
        + [pl.BlockSpec(memory_space=pltpu.SMEM)],
        out_specs=[vmem] * 7,
        out_shape=[
            shape((4, 64, width), bf16),
            shape((4, 64, width), bf16),
            shape((8, 24, width), f32),
            shape((8, 24, width), f32),
            shape((4, 64, width), f32),
            shape((4, 256, HDIM), bf16),
            shape((2, 64, width), bf16),
        ],
        scratch_shapes=[
            vm((8, 48, width), bf16),
            vm((8, 32, width), bf16),
            vm((8, 256, 256), bf16),
            vm((8, 256, 256), bf16),
            vm((8, 256, 256), bf16),
            vm((4, 64, width), bf16),
            vm((8, 256, 48), bf16),
            vm((width, 1536), bf16),
            vm((256, width), f32),
            vm((8, 256, 256), bf16),
            vm((4, 64, width), bf16),
            vm((4, 64, width), bf16),
            vm((4, 64, width), bf16),
            vm((4, 256, 256), bf16),
            vm((4, 256, 256), bf16),
            vm((4, 256, 256), bf16),
            vm((6, 128, width), bf16),
            vm((6, 128, width), bf16),
            vm((256, width), f32),
            vm((2, 256, width), bf16),
            vm((2, 256, width), bf16),
            vm((48, width), f32),
            vm((16, width), f32),
            vm((8, 16, width), bf16),
            vm((4, 16, width), bf16),
            vm((4, 16, width), bf16),
            vm((3, 16, width), bf16),
            vm((16, width), bf16),
            vm((3, 16, width), bf16),
            vm((32, width), bf16),
            vm((3, 32, width), bf16),
            vm((2, 64, HDIM), bf16),
            vm((4, 64, HDIM), bf16),
        ]
        + [
            dma((count,))
            for count in (6, 6, 12, 12, 6, 6, 4, 4, 4, 3, 3, 3, 3, 7, 7, 2, 4, 7, 7, 2, 2, 3, 3, 7, 7, 9)
        ],
        cost_estimate=spend(80),
        compiler_params=pltpu.CompilerParams(
            collective_id=4, has_side_effects=True, vmem_limit_bytes=60 << 20
        ),
    )(*operands)


def span_table(positions):
    half_dim = HDIM // 2
    frequency = jnp.exp(
        jnp.arange(half_dim, dtype=jnp.float32) * (-2.0 * math.log(rope_base) / HDIM)
    )
    angles = positions.astype(jnp.float32)[:, None] * frequency
    return jnp.concatenate([jnp.cos(angles), jnp.sin(angles)], axis=1)


def per_device_layers(
    layer_in, w_qkv, w_out, w_gate_up, w_down, a_in, b_qkv, b_gate_up, a_out, a_down, b_out_down,
    set_index, positions, cotangent,
):
    f32 = jnp.float32
    z = lax.axis_index("mp")
    sets = a_in.shape[0]
    width = layer_in.shape[2]
    rank = a_in.shape[2]
    length = 8 * 256

    table = span_table(lax.dynamic_index_in_dim(positions, z, 0, keepdims=False))
    (
        x_own, m_own, residual, o_eff, b_sel, a_sel, lse,
        u, q, k, v, low, tables, mixed, w_cat, cots,
    ) = front_layer(
        layer_in, w_qkv, w_out, b_qkv, a_out, a_in, b_out_down, table, cotangent, set_index
    )

    def spans(values):
        return values.reshape(8, 256, 256)

    (
        g_own, grad_residual, down0, down1, down2, down3,
        grad_b_mlp, grad_ad, grad_a_mlp, grad_bd,
    ) = mlp_line(
        m_own, residual, cots, w_gate_up, w_down, a_in, b_gate_up, a_down, b_out_down, set_index
    )
    dq, dk, dv, out_rank, chunk, pair, g, got2 = back_layer(
        g_own, o_eff, mixed, b_out_down, q, k, v, lse, tables.reshape(length, HDIM),
        grad_b_mlp, grad_ad, grad_a_mlp, grad_bd, down2, down3, set_index,
    )
    result, grad_in, whole, split, sequence, heads, _ = finish_layer(
        spans(dq), spans(dk), spans(dv), w_cat, x_own, grad_residual, u, g, low, out_rank, spans(mixed),
        b_sel, a_sel, chunk, down0, down1, got2, pair, set_index,
    )
    whole = whole.reshape(sets, 48, width)
    split = split.reshape(sets, 48, width)
    heads = heads.astype(f32).reshape(4, sets, 64, HDIM)
    heads = jnp.transpose(heads, (1, 2, 0, 3)).reshape(sets, 4, rank, 4 * HDIM)
    return (
        result,
        grad_in,
        jnp.concatenate([sequence[:, :48], whole[:, :32]], axis=1).reshape(sets, 5, rank, width),
        heads[:, :3],
        split[:, :32].reshape(sets, 2, rank, width),
        heads[:, 3],
        split[:, 32:],
        jnp.stack([sequence[:, 48:], whole[:, 32:]], axis=1),
    )


def solution(mesh):
    by_layers = mesh.shape["seq"] == 8 and mesh.shape["mp"] == 4
    body = per_device_layers if by_layers else per_device
    placed = (
        P(None, ("seq", "mp"), None),
        P(None, None, "mp"),
        P("mp", None),
        P(None, None, "mp"),
        P("mp", None),
        P(),
        P(None, None, None, "mp"),
        P(None, None, None, "mp"),
        P(None, None, "mp"),
        P(None, None, "mp"),
        P(),
        P(),
        P(None, "seq"),
        P(None, ("seq", "mp"), None),
    )
    return jax.shard_map(
        body,
        mesh=mesh,
        in_specs=placed,
        out_specs=(
            P(None, ("seq", "mp"), None),
            P(None, ("seq", "mp"), None),
            P(),
            P(None, None, None, "mp"),
            P(None, None, None, "mp"),
            P(None, None, "mp"),
            P(None, None, "mp"),
            P(),
        ),
        check_vma=False,
    )
```

```python
import math

import jax
import jax.numpy as jnp
from jax import lax
from jax.experimental import pallas as pl
from jax.experimental.pallas import tpu as pltpu
from jax.sharding import PartitionSpec as P

HDIM = 128


adapt_scale = 0.5
norm_eps = 1e-05
rope_base = 10000.0
far_below = -1e30
highest = lax.Precision.HIGHEST


def layer_norm(values):
    centred = values - jnp.mean(values, axis=-1, keepdims=True)
    inverse = lax.rsqrt(jnp.mean(centred * centred, axis=-1, keepdims=True) + norm_eps)
    return (centred * inverse, inverse)


def norm_back(gradient, normed, inverse):
    return inverse * (
        gradient
        - jnp.mean(gradient, axis=-1, keepdims=True)
        - normed * jnp.mean(gradient * normed, axis=-1, keepdims=True)
    )


def gather_rows(values):
    return lax.all_gather(values, "mp", axis=1, tiled=True)


def scatter_rows(values):
    return lax.psum_scatter(
        values.astype(jnp.bfloat16), "mp", scatter_dimension=1, tiled=True
    ).astype(jnp.float32)


def rope_tables(positions):
    half_dim = HDIM // 2
    frequency = jnp.exp(
        jnp.arange(half_dim, dtype=jnp.float32) * (-2.0 * math.log(rope_base) / HDIM)
    )
    angles = jnp.transpose(positions).astype(jnp.float32)[:, :, None, None] * frequency
    return (jnp.cos(angles), jnp.sin(angles))


def rotate(values, cosine_table, sine_table):
    half_dim = values.shape[-1] // 2
    first_half = values[..., :half_dim]
    second_half = values[..., half_dim:]
    return jnp.concatenate(
        [
            first_half * cosine_table - second_half * sine_table,
            second_half * cosine_table + first_half * sine_table,
        ],
        axis=-1,
    )


def rotate_back(gradient, cosine_table, sine_table):
    half_dim = gradient.shape[-1] // 2
    first_half = gradient[..., :half_dim]
    second_half = gradient[..., half_dim:]
    return jnp.concatenate(
        [
            first_half * cosine_table + second_half * sine_table,
            second_half * cosine_table - first_half * sine_table,
        ],
        axis=-1,
    )


def masked_scores(queries, key_rows, query_first, key_first, score_scale):
    raw_scores = (
        jnp.einsum("qshd,kshd->shqk", queries, key_rows, preferred_element_type=jnp.float32)
        * score_scale
    )
    query_index = query_first + jnp.arange(queries.shape[0])
    key_index = key_first + jnp.arange(key_rows.shape[0])
    return (raw_scores, key_index[None, :] <= query_index[:, None])


def blockwise(fold_step, state_carry, pieces, start_row):
    row_count = pieces[0].shape[0]
    block_size = 512

    def block_turn(block_id, running):
        blocks = tuple(
            (
                lax.dynamic_slice_in_dim(shard_piece, block_id * block_size, block_size, 0)
                for shard_piece in pieces
            )
        )
        return fold_step(running, blocks, start_row + block_id * block_size)

    return lax.fori_loop(0, row_count // block_size, block_turn, state_carry)


def forward_step(queries, query_first, score_scale):
    query_last = query_first + queries.shape[0] - 1

    def fold_step(state_carry, blocks, key_first):
        key_rows, value_rows = blocks

        def compute(running):
            running_max, running_sum, weighted = running
            scores, allowed = masked_scores(queries, key_rows, query_first, key_first, score_scale)
            new_max = jnp.maximum(
                running_max, jnp.max(jnp.where(allowed, scores, far_below), axis=-1)
            )
            exponent = jnp.where(allowed, jnp.exp(scores - new_max[..., None]), 0.0)
            factor = jnp.exp(running_max - new_max)
            running_sum = running_sum * factor + jnp.sum(exponent, axis=-1)
            weighted = weighted * factor[..., None] + jnp.einsum(
                "shqk,kshd->shqd",
                exponent.astype(jnp.bfloat16),
                value_rows,
                preferred_element_type=jnp.float32,
            )
            return (new_max, running_sum, weighted)

        return lax.cond(key_first <= query_last, compute, lambda running: running, state_carry)

    return fold_step


def query_grad_step(queries, grad_heads, log_total, row_dots, query_first, score_scale):
    query_last = query_first + queries.shape[0] - 1

    def fold_step(state_carry, blocks, key_first):
        key_rows, value_rows = blocks

        def compute(running):
            scores, allowed = masked_scores(queries, key_rows, query_first, key_first, score_scale)
            attn_probs = jnp.where(allowed, jnp.exp(scores - log_total[..., None]), 0.0)
            grad_probs = jnp.einsum(
                "qshd,kshd->shqk", grad_heads, value_rows, preferred_element_type=jnp.float32
            )
            grad_scores = (attn_probs * (grad_probs - row_dots[..., None])).astype(jnp.bfloat16)
            return running + score_scale * jnp.einsum(
                "shqk,kshd->qshd", grad_scores, key_rows, preferred_element_type=jnp.float32
            )

        return lax.cond(key_first <= query_last, compute, lambda running: running, state_carry)

    return fold_step


def key_grad_step(key_rows, value_rows, key_first, score_scale):

    def fold_step(state_carry, blocks, query_first):
        queries, grad_heads, log_total_tok, row_dots_tok = blocks
        query_last = query_first + queries.shape[0] - 1

        def compute(running):
            scores, allowed = masked_scores(queries, key_rows, query_first, key_first, score_scale)
            log_total = jnp.transpose(log_total_tok, (1, 2, 0))
            row_dots = jnp.transpose(row_dots_tok, (1, 2, 0))
            attn_probs = jnp.where(allowed, jnp.exp(scores - log_total[..., None]), 0.0)
            grad_value_rows = jnp.einsum(
                "shqk,qshd->kshd",
                attn_probs.astype(jnp.bfloat16),
                grad_heads,
                preferred_element_type=jnp.float32,
            )
            grad_probs = jnp.einsum(
                "qshd,kshd->shqk", grad_heads, value_rows, preferred_element_type=jnp.float32
            )
            grad_scores = (attn_probs * (grad_probs - row_dots[..., None])).astype(jnp.bfloat16)
            grad_key_rows = score_scale * jnp.einsum(
                "shqk,qshd->kshd", grad_scores, queries, preferred_element_type=jnp.float32
            )
            return (grad_key_rows, grad_value_rows)

        return lax.cond(key_first <= query_last, compute, lambda running: running, state_carry)

    return fold_step


def project_in(token_rows, weight, a_chosen, b_chosen):
    main_term = jnp.einsum("scd,dw->csw", token_rows, weight, preferred_element_type=jnp.float32)
    low_rank = jnp.einsum("scd,srd->scr", token_rows, a_chosen, preferred_element_type=jnp.float32)
    side_term = jnp.einsum(
        "scr,srw->csw", low_rank, b_chosen.astype(jnp.float32), precision=highest
    )
    return (main_term + adapt_scale * side_term, low_rank)


def project_out(middle, weight, a_chosen, b_chosen):
    main_term = jnp.einsum("csw,wd->scd", middle, weight, preferred_element_type=jnp.float32)
    low_rank = jnp.einsum("csw,srw->scr", middle, a_chosen, preferred_element_type=jnp.float32)
    side_term = jnp.einsum(
        "scr,srd->scd", low_rank, b_chosen.astype(jnp.float32), precision=highest
    )
    return (main_term + adapt_scale * side_term, low_rank)


def back_in(gradient, weight, a_chosen, b_chosen, token_rows, low_rank):
    back_rank = jnp.einsum("csw,srw->scr", gradient, b_chosen, preferred_element_type=jnp.float32)
    grad_rows = jnp.einsum("csw,dw->scd", gradient, weight, preferred_element_type=jnp.float32)
    grad_rows = grad_rows + adapt_scale * jnp.einsum(
        "scr,srd->scd", back_rank, a_chosen.astype(jnp.float32), precision=highest
    )
    grad_a = adapt_scale * jnp.einsum("scr,scd->srd", back_rank, token_rows, precision=highest)
    grad_b = adapt_scale * jnp.einsum("scr,csw->srw", low_rank, gradient, precision=highest)
    return (grad_rows, grad_a, grad_b)


def back_out(gradient, weight, a_chosen, b_chosen, middle, low_rank):
    back_rank = jnp.einsum("scd,srd->scr", gradient, b_chosen, preferred_element_type=jnp.float32)
    grad_middle = jnp.einsum("scd,wd->csw", gradient, weight, preferred_element_type=jnp.float32)
    grad_middle = grad_middle + adapt_scale * jnp.einsum(
        "scr,srw->csw", back_rank, a_chosen.astype(jnp.float32), precision=highest
    )
    grad_a = adapt_scale * jnp.einsum("scr,csw->srw", back_rank, middle, precision=highest)
    grad_b = adapt_scale * jnp.einsum("scr,scd->srd", low_rank, gradient, precision=highest)
    return (grad_middle, grad_a, grad_b)


def pick_set(onehot, set_table):
    flattened = set_table.reshape(set_table.shape[0], -1)
    chosen = jnp.dot(onehot, flattened, preferred_element_type=jnp.float32).astype(jnp.bfloat16)
    return chosen.reshape((onehot.shape[0],) + set_table.shape[1:])


def spread_sets(onehot, per_sequence):
    flattened = per_sequence.reshape(per_sequence.shape[0], -1)
    summed = jnp.dot(onehot.astype(jnp.float32).T, flattened, precision=highest)
    return summed.reshape((onehot.shape[1],) + per_sequence.shape[1:])


def per_device(
    layer_in,
    w_qkv,
    w_out,
    w_gate_up,
    w_down,
    a_in,
    b_qkv,
    b_gate_up,
    a_out,
    a_down,
    b_out_down,
    set_index,
    positions,
    cotangent,
):
    local_len = positions.shape[1]
    seq_count = positions.shape[0]
    score_scale = 1.0 / math.sqrt(HDIM)
    my_first = lax.axis_index("seq") * local_len
    onehot = (set_index[:, None] == jnp.arange(a_in.shape[0])[None, :]).astype(jnp.bfloat16)
    chosen_a_in = pick_set(onehot, a_in)
    chosen_b_qkv = pick_set(onehot, b_qkv)
    chosen_b_gate_up = pick_set(onehot, b_gate_up)
    chosen_a_out = pick_set(onehot, a_out)
    chosen_a_down = pick_set(onehot, a_down)
    chosen_b_out_down = pick_set(onehot, b_out_down)

    def to_heads(values):
        return values.reshape(local_len, seq_count, -1, HDIM)

    residual_in = layer_in.astype(jnp.float32)
    normed_attn, inverse_attn = layer_norm(residual_in)
    rows_attn = gather_rows(normed_attn.astype(jnp.bfloat16))
    projected = [
        project_in(rows_attn, w_qkv[member], chosen_a_in[:, member], chosen_b_qkv[:, member])
        for member in range(3)
    ]
    cosine_table, sine_table = rope_tables(positions)
    queries = rotate(to_heads(projected[0][0]), cosine_table, sine_table).astype(jnp.bfloat16)
    key_rows = rotate(to_heads(projected[1][0]), cosine_table, sine_table).astype(jnp.bfloat16)
    value_rows = to_heads(projected[2][0]).astype(jnp.bfloat16)
    stat_shape = (seq_count, queries.shape[2], local_len)
    initial = (
        jnp.full(stat_shape, far_below, jnp.float32),
        jnp.zeros(stat_shape, jnp.float32),
        jnp.zeros(stat_shape + (HDIM,), jnp.float32),
    )
    attend = forward_step(queries, my_first, score_scale)
    running_max, running_sum, weighted = blockwise(
        attend,
        initial,
        (
            lax.all_gather(key_rows, "seq", axis=0, tiled=True),
            lax.all_gather(value_rows, "seq", axis=0, tiled=True),
        ),
        jnp.int32(0),
    )
    log_total = running_max + jnp.log(running_sum)
    attn_output = jnp.transpose(weighted / running_sum[..., None], (2, 0, 1, 3))
    mixed = attn_output.reshape(local_len, seq_count, -1).astype(jnp.bfloat16)
    attn_term, rank_out = project_out(mixed, w_out, chosen_a_out, chosen_b_out_down[:, 0])
    residual = residual_in + scatter_rows(attn_term)
    normed_mlp, inverse_mlp = layer_norm(residual)
    rows_mlp = gather_rows(normed_mlp.astype(jnp.bfloat16))
    gate_proj, rank_gate = project_in(
        rows_mlp, w_gate_up[0], chosen_a_in[:, 3], chosen_b_gate_up[:, 0]
    )
    up_proj, rank_up = project_in(rows_mlp, w_gate_up[1], chosen_a_in[:, 4], chosen_b_gate_up[:, 1])
    sigmoid_gate = jax.nn.sigmoid(gate_proj)
    activation = (gate_proj * sigmoid_gate * up_proj).astype(jnp.bfloat16)
    down_term, rank_down = project_out(activation, w_down, chosen_a_down, chosen_b_out_down[:, 1])
    result = (residual + scatter_rows(down_term)).astype(jnp.bfloat16)
    grad_down = gather_rows(cotangent)
    grad_activation, grad_a_down, grad_b_down = back_out(
        grad_down, w_down, chosen_a_down, chosen_b_out_down[:, 1], activation, rank_down
    )
    grad_up = (grad_activation * gate_proj * sigmoid_gate).astype(jnp.bfloat16)
    grad_gate = (
        grad_activation * up_proj * sigmoid_gate * (1.0 + gate_proj * (1.0 - sigmoid_gate))
    ).astype(jnp.bfloat16)
    rows_from_gate, grad_a_gate, grad_b_gate = back_in(
        grad_gate, w_gate_up[0], chosen_a_in[:, 3], chosen_b_gate_up[:, 0], rows_mlp, rank_gate
    )
    rows_from_up, grad_a_up, grad_b_up = back_in(
        grad_up, w_gate_up[1], chosen_a_in[:, 4], chosen_b_gate_up[:, 1], rows_mlp, rank_up
    )
    grad_residual = cotangent.astype(jnp.float32) + norm_back(
        scatter_rows(rows_from_gate + rows_from_up), normed_mlp, inverse_mlp
    )
    grad_attn_rows = gather_rows(grad_residual.astype(jnp.bfloat16))
    grad_mixed, grad_a_out, grad_b_out = back_out(
        grad_attn_rows, w_out, chosen_a_out, chosen_b_out_down[:, 0], mixed, rank_out
    )
    grad_heads = to_heads(grad_mixed.astype(jnp.bfloat16))
    row_dots_tok = jnp.sum(grad_heads.astype(jnp.float32) * attn_output, axis=-1)
    row_dots = jnp.transpose(row_dots_tok, (1, 2, 0))
    log_total_tok = jnp.transpose(log_total, (2, 0, 1))
    query_step = query_grad_step(queries, grad_heads, log_total, row_dots, my_first, score_scale)
    zero_heads = jnp.zeros(queries.shape, jnp.float32)
    every_key, every_value = (
        lax.all_gather(key_rows, "seq", axis=0, tiled=True),
        lax.all_gather(value_rows, "seq", axis=0, tiled=True),
    )
    grad_queries = blockwise(query_step, zero_heads, (every_key, every_value), 0)
    block_size = 512

    def one_block(block_id):
        first_key = block_id * block_size
        block_keys = lax.dynamic_slice_in_dim(every_key, first_key, block_size, 0)
        block_values = lax.dynamic_slice_in_dim(every_value, first_key, block_size, 0)
        zero_block = jnp.zeros(block_keys.shape, jnp.float32)
        block_step = key_grad_step(block_keys, block_values, first_key, score_scale)
        grad_key_block, grad_value_block = block_step(
            (zero_block, zero_block), (queries, grad_heads, log_total_tok, row_dots_tok), my_first
        )
        return jnp.concatenate([grad_key_block, grad_value_block], axis=-1)

    stacked = lax.map(one_block, jnp.arange(local_len * lax.axis_size("seq") // block_size))
    stacked_terms = lax.psum_scatter(
        stacked.reshape((local_len * lax.axis_size("seq"),) + stacked.shape[2:]).astype(
            jnp.bfloat16
        ),
        "seq",
        scatter_dimension=0,
        tiled=True,
    ).astype(jnp.float32)
    grad_keys = stacked_terms[..., :HDIM]
    grad_values = stacked_terms[..., HDIM:]
    grad_query_raw = (
        rotate_back(grad_queries, cosine_table, sine_table)
        .astype(jnp.bfloat16)
        .reshape(local_len, seq_count, -1)
    )
    grad_key_raw = (
        rotate_back(grad_keys, cosine_table, sine_table)
        .astype(jnp.bfloat16)
        .reshape(local_len, seq_count, -1)
    )
    grad_value_raw = grad_values.astype(jnp.bfloat16).reshape(local_len, seq_count, -1)
    back_parts = [
        back_in(
            gradient,
            w_qkv[member],
            chosen_a_in[:, member],
            chosen_b_qkv[:, member],
            rows_attn,
            projected[member][1],
        )
        for member, gradient in enumerate((grad_query_raw, grad_key_raw, grad_value_raw))
    ]
    grad_rows_attn = back_parts[0][0] + back_parts[1][0] + back_parts[2][0]
    grad_in = (
        grad_residual + norm_back(scatter_rows(grad_rows_attn), normed_attn, inverse_attn)
    ).astype(jnp.bfloat16)
    per_seq_a_in = jnp.stack(
        [back_parts[0][1], back_parts[1][1], back_parts[2][1], grad_a_gate, grad_a_up], axis=1
    )
    per_seq_b_qkv = jnp.stack([bundle[2] for bundle in back_parts], axis=1)
    per_seq_b_gate_up = jnp.stack([grad_b_gate, grad_b_up], axis=1)
    per_seq_b_out_down = jnp.stack([grad_b_out, grad_b_down], axis=1)
    sums_seq = (
        lax.psum(spread_sets(onehot, per_seq_b_qkv).astype(jnp.bfloat16), "seq").astype(
            jnp.float32
        ),
        lax.psum(spread_sets(onehot, per_seq_b_gate_up).astype(jnp.bfloat16), "seq").astype(
            jnp.float32
        ),
        lax.psum(spread_sets(onehot, grad_a_out).astype(jnp.bfloat16), "seq").astype(jnp.float32),
        lax.psum(spread_sets(onehot, grad_a_down).astype(jnp.bfloat16), "seq").astype(jnp.float32),
    )
    sums_all = lax.psum(
        (spread_sets(onehot, per_seq_a_in), spread_sets(onehot, per_seq_b_out_down)), ("seq", "mp")
    )
    return (
        result,
        grad_in,
        sums_all[0],
        sums_seq[0],
        sums_seq[1],
        sums_seq[2],
        sums_seq[3],
        sums_all[1],
    )


log2e = 1.4426950408889634
attn_tile = 512
hidden_tile = 512


def dot_nt(a, b):
    return lax.dot_general(a, b, (((1,), (1,)), ((), ())), preferred_element_type=jnp.float32)


def dot_tn(a, b):
    return lax.dot_general(a, b, (((0,), (0,)), ((), ())), preferred_element_type=jnp.float32)


def dot_nn(a, b):
    return jnp.dot(a, b, preferred_element_type=jnp.float32)


def causal(block_t, first_row, first_col):
    rows = first_row + lax.broadcasted_iota(jnp.int32, block_t.shape, 0)
    cols = first_col + lax.broadcasted_iota(jnp.int32, block_t.shape, 1)
    return rows <= cols


mesh_ids = pl.DeviceIdType.MESH


def remote(src, dst, send, recv, target):
    return pltpu.make_async_remote_copy(
        src_ref=src, dst_ref=dst, send_sem=send, recv_sem=recv, device_id=target, device_id_type=mesh_ids
    )


def meet(partners):
    barrier = pltpu.get_barrier_semaphore()
    for condition, device in partners:
        if condition is None:
            pl.semaphore_signal(barrier, inc=1, device_id=device, device_id_type=mesh_ids)
        else:

            @pl.when(condition)
            def _():
                pl.semaphore_signal(barrier, inc=1, device_id=device, device_id_type=mesh_ids)

    count = 0
    for condition, device in partners:
        count = count + (1 if condition is None else condition.astype(jnp.int32))
    pl.semaphore_wait(barrier, count)


def flip(index, bit):
    return index + bit - 2 * bit * ((index // bit) % 2)


def places():
    s = lax.axis_index("seq")
    z = lax.axis_index("mp")
    return s, z


class Gather:
    def __init__(self, blocks, s, z, send, recv, half, base=0):
        self.at = blocks
        self.s = s
        self.z = z
        self.send = send
        self.recv = recv
        self.half = half
        self.base = base

    def rows(self, part):
        if part is None:
            return pl.ds(self.base, 2 * self.half)
        return pl.ds(self.base + part * self.half, self.half)

    def copy(self, index, span, part, target):
        ref = self.at.at[span, self.rows(part)]
        return remote(ref, ref, self.send.at[index], self.recv.at[index], (target, self.z))

    def begin(self):
        s, x, y, other = self.s, flip(self.s, 2), flip(self.s, 4), flip(self.s, 1)
        for one in (
            self.copy(0, s, 0, x),
            self.copy(1, s, 1, y),
            self.copy(2, s, 1, x),
            self.copy(3, s, 0, y),
            self.copy(6, s, None, other),
        ):
            one.start()

    def arrive_first(self):
        s, x, y = self.s, flip(self.s, 2), flip(self.s, 4)
        self.copy(0, x, 0, x).wait_recv()
        one = self.copy(4, x, 0, y)
        one.start()
        self.copy(1, y, 1, y).wait_recv()
        two = self.copy(5, y, 1, x)
        two.start()

    def arrive_neighbours(self):
        s, x, y, other = self.s, flip(self.s, 2), flip(self.s, 4), flip(self.s, 1)
        self.copy(2, x, 1, x).wait_recv()
        one = self.copy(7, x, None, other)
        one.start()
        self.copy(3, y, 0, y).wait_recv()
        two = self.copy(8, y, None, other)
        two.start()

    def arrive_diagonal(self):
        s, other = self.s, flip(self.s, 1)
        diagonal = flip(flip(s, 2), 4)
        self.copy(4, diagonal, 0, other).wait_recv()
        self.copy(5, diagonal, 1, other).wait_recv()
        one = self.copy(9, diagonal, None, other)
        one.start()

    def arrive_core(self, index):
        s = self.s
        other = flip(s, 1)
        span = (other, flip(other, 2), flip(other, 4), flip(flip(other, 2), 4))[index]
        self.copy(6 + index, span, None, other).wait_recv()
        return span

    def end(self):
        s, x, y, other = self.s, flip(self.s, 2), flip(self.s, 4), flip(self.s, 1)
        for index, span, part, target in (
            (0, s, 0, x),
            (1, s, 1, y),
            (2, s, 1, x),
            (3, s, 0, y),
            (4, x, 0, y),
            (5, y, 1, x),
            (6, s, None, other),
            (7, x, None, other),
            (8, y, None, other),
            (9, flip(x, 4), None, other),
        ):
            self.copy(index, span, part, target).wait_send()


gather_sems = 10


def spend(microseconds):
    return pl.CostEstimate(flops=microseconds * 10**9, bytes_accessed=10**6, transcendentals=0)


class Line:
    def __init__(self, blocks, core, s, z, send, recv):
        self.at = blocks
        self.core = core
        self.s = s
        self.z = z
        self.send = send
        self.recv = recv

    def ref(self, j):
        return self.at.at[j] if self.core is None else self.at.at[j, self.core]

    def up(self, hop, j):
        ref = self.ref(j)
        return remote(ref, ref, self.send.at[hop], self.recv.at[hop], (self.s, self.z + 1))

    def down(self, hop, j):
        ref = self.ref(j)
        return remote(ref, ref, self.send.at[3 + hop], self.recv.at[3 + hop], (self.s, self.z - 1))

    def across(self, index, j):
        ref = self.ref(j)
        return remote(ref, ref, self.send.at[6 + index], self.recv.at[6 + index], (flip(self.s, 1), self.z))

    def begin(self):
        z = self.z

        @pl.when(z < 3)
        def _():
            self.up(0, z).start()

        @pl.when(z > 0)
        def _():
            self.down(0, z).start()

        if self.core is not None:
            self.across(0, z).start()

    def hop(self, t):
        z = self.z

        def from_above(side):
            @pl.when((z + t <= 3) & side)
            def _():
                self.down(t - 1, z + t).wait_recv()
                if self.core is not None:
                    self.across(3 + t, z + t).start()
                if t < 3:

                    @pl.when(z > 0)
                    def _():
                        self.down(t, z + t).start()

        from_above(z < 2)

        @pl.when(z >= t)
        def _():
            self.up(t - 1, z - t).wait_recv()
            if self.core is not None:
                self.across(t, z - t).start()
            if t < 3:

                @pl.when(z < 3)
                def _():
                    self.up(t, z - t).start()

        from_above(z >= 2)

    def arrive_core(self):
        z = self.z
        other = 1 - self.core

        def wait(index, j):
            ref = self.at.at[j, other]
            remote(ref, ref, self.send.at[6 + index], self.recv.at[6 + index], (flip(self.s, 1), z)).wait_recv()

        wait(0, z)
        for t in (1, 2, 3):

            @pl.when(z >= t)
            def _():
                wait(t, z - t)

            @pl.when(z + t <= 3)
            def _():
                wait(3 + t, z + t)

    def end(self):
        z = self.z

        @pl.when(z < 3)
        def _():
            self.up(0, z).wait_send()

        @pl.when(z > 0)
        def _():
            self.down(0, z).wait_send()

        if self.core is not None:
            self.across(0, z).wait_send()
        for t in (1, 2, 3):

            @pl.when(z >= t)
            def _():
                if self.core is not None:
                    self.across(t, z - t).wait_send()
                if t < 3:

                    @pl.when(z < 3)
                    def _():
                        self.up(t, z - t).wait_send()

            @pl.when(z + t <= 3)
            def _():
                if self.core is not None:
                    self.across(3 + t, z + t).wait_send()
                if t < 3:

                    @pl.when(z > 0)
                    def _():
                        self.down(t, z + t).wait_send()


line_sems = 13


def norm_rows(values):
    centred = values - jnp.mean(values, axis=-1, keepdims=True)
    inverse = lax.rsqrt(jnp.mean(centred * centred, axis=-1, keepdims=True) + norm_eps)
    return (centred * inverse, inverse)


class Reduce:
    def __init__(self, rows, multiply, width, s, z, out, inn, own, send, recv):
        self.rows = rows
        self.multiply = multiply
        self.width = width
        self.s = s
        self.z = z
        self.out = out
        self.inn = inn
        self.own = own
        self.send = send
        self.recv = recv
        chip = s // 2
        self.chip = chip
        self.cx = flip(chip, 1)
        self.cy = flip(chip, 2)
        self.cd = flip(self.cx, 2)

    def copy(self, index):
        target = flip(self.s, 2) if index in (0, 2, 5) else flip(self.s, 4)
        return remote(
            self.out.at[index], self.inn.at[index], self.send.at[index], self.recv.at[index], (target, self.z)
        )

    def give(self, first, second):
        both = jnp.concatenate([self.rows(*first[1:3]), self.rows(*second[1:3])], axis=0)
        for job in (first, second):
            if job[3] is not None:
                self.copy(job[3]).wait_recv()

        def one(part, _):
            wide = pl.ds(pl.multiple_of(part * 512, 512), 512)
            value = self.multiply(both, wide)
            for job, piece in ((first, value[:128]), (second, value[128:])):
                if job[3] is not None:
                    piece = piece + self.inn[job[3], :, wide].astype(jnp.float32)
                self.out[job[0], :, wide] = piece.astype(jnp.bfloat16)
            return 0

        lax.fori_loop(0, self.width // 512, one, 0)
        self.copy(first[0]).start()
        self.copy(second[0]).start()

    def begin(self):
        self.give((0, self.cd, 0, None), (1, self.cd, 1, None))

    def second(self):
        self.give((2, self.cx, 0, None), (4, self.cy, 0, 0))

    def third(self):
        self.copy(2).wait_send()
        self.copy(4).wait_send()
        self.give((5, self.cx, 1, 1), (3, self.cy, 1, None))

    def keep(self):
        both = jnp.concatenate([self.rows(self.chip, 0), self.rows(self.chip, 1)], axis=0)

        def one(part, _):
            wide = pl.ds(pl.multiple_of(part * 512, 512), 512)
            self.own[:, wide] = self.multiply(both, wide)
            return 0

        lax.fori_loop(0, self.width // 512, one, 0)

    def finish(self, half, use):
        first, second = (2, 4) if half == 0 else (3, 5)
        self.copy(first).wait_recv()
        self.copy(second).wait_recv()

        def one(part, _):
            at = pl.ds(pl.multiple_of(part * 32, 32), 32)
            row = pl.multiple_of(part * 64 + half * 32, 32)
            total = (
                self.own[pl.ds(pl.multiple_of(half * 128 + part * 32, 32), 32), :]
                + self.inn[first, at, :].astype(jnp.float32)
                + self.inn[second, at, :].astype(jnp.float32)
            )
            use(row, total)
            return 0

        lax.fori_loop(0, 4, one, 0)

    def end(self):
        for index in (0, 1, 3, 5):
            self.copy(index).wait_send()


def some_rows(load, half):
    return jnp.concatenate([load(64 * j + 32 * half) for j in range(4)], axis=0)


def front_kernel(
    x_ref, w_qkv_ref, w_out_ref, b_qkv_ref, a_out_ref, a_in_ref, b_od_ref, table_ref, cot_ref, set_ref,
    x_own_ref, m_own_ref, residual_ref, o_eff_ref, b_sel_ref, a_sel_ref, lse_ref,
    u_out, q_out, k_out, v_out, low_out, table_out, mixed_out, w_cat_out, cots_ref,
    u_ref, w_buf, w_cat, q_buf, k_buf, v_buf, low_buf, tables, mixed, o_all, o_big, sib, out_buf, in_buf, own_sum,
    b_small, a_small,
    a2a_send, a2a_recv, tab_send, tab_recv, ag_send, ag_recv, ag2_send, ag2_recv, w_send, w_recv, o_send, o_recv, cot_send, cot_recv,
    small_send, small_recv, sib_send, sib_recv, red_send, red_recv, local_sem, store_sem,
):
    f32 = jnp.float32
    bf16 = jnp.bfloat16
    s, z = places()
    core = s % 2
    chip = s // 2
    other = flip(s, 1)
    zs = [flip(z, 1), flip(z, 2), 3 - z]
    middle = z * (3 - z) == 2
    columns = pl.ds(pl.multiple_of(chip * HDIM, HDIM), HDIM)
    half_rows = pl.ds(pl.multiple_of(core * 1024, 1024), 1024)
    owns = [
        pltpu.make_async_copy(w_qkv_ref.at[:, half_rows, columns], w_buf.at[z, core], local_sem.at[0]),
        pltpu.make_async_copy(w_out_ref.at[columns, half_rows], o_all.at[z, core], local_sem.at[1]),
        pltpu.make_async_copy(b_qkv_ref.at[:, :, :, columns], b_small.at[z], local_sem.at[2]),
        pltpu.make_async_copy(a_out_ref.at[:, :, columns], a_small.at[z], local_sem.at[3]),
        pltpu.make_async_copy(cot_ref, cots_ref.at[z], local_sem.at[4]),
    ]
    for one in owns:
        one.start()
    tables[s] = table_ref[...]
    meet([(None, (other, z)), (None, (flip(s, 2), z)), (None, (flip(s, 4), z))] + [(None, (s, j)) for j in zs])

    swaps = [
        remote(x_ref.at[j], x_own_ref.at[z], a2a_send.at[d], a2a_recv.at[d], (s, j)) for d, j in enumerate(zs)
    ]
    for one in swaps:
        one.start()
    for one in owns:
        one.wait()
    line = Line(w_buf, core, s, z, w_send, w_recv)
    line.begin()
    table_gather = Gather(tables, s, z, tab_send, tab_recv, 128)
    table_gather.begin()
    x_own_ref[z] = x_ref[z]

    def arrived(d):
        j = zs[d]
        remote(x_ref.at[j], x_own_ref.at[j], a2a_send.at[d], a2a_recv.at[d], (s, j)).wait_recv()

    def normalize(j):
        def one(part, _):
            normed, _ = norm_rows(x_own_ref[j, pl.ds(pl.multiple_of(part * 32, 32), 32), :].astype(f32))
            u_ref[s, pl.ds(pl.multiple_of(j * 64 + part * 32, 32), 32), :] = normed.astype(bf16)
            return 0

        lax.fori_loop(0, 2, one, 0)

    near = Gather(u_ref, s, z, ag_send, ag_recv, 64, pl.multiple_of((z // 2) * 128, 128))
    rest = Gather(u_ref, s, z, ag2_send, ag2_recv, 64, pl.multiple_of((1 - z // 2) * 128, 128))
    arrived(0)
    normalize(z)
    normalize(zs[0])
    near.begin()
    table_gather.arrive_first()
    table_gather.arrive_neighbours()
    near.arrive_first()
    arrived(1)
    arrived(2)
    smalls = []
    for d, j in enumerate(zs):
        smalls.append(remote(b_small.at[z], b_small.at[z], small_send.at[d], small_recv.at[d], (s, j)))
        smalls.append(remote(a_small.at[z], a_small.at[z], small_send.at[3 + d], small_recv.at[3 + d], (s, j)))
    for one in smalls:
        one.start()
    normalize(zs[1])
    normalize(zs[2])
    rest.begin()
    table_gather.arrive_diagonal()
    near.arrive_neighbours()
    near.arrive_diagonal()
    line.hop(1)
    rest.arrive_first()
    rest.arrive_neighbours()
    line.hop(2)
    rest.arrive_diagonal()
    for index in range(4):
        near.arrive_core(index)
        rest.arrive_core(index)
        table_gather.arrive_core(index)
    stores = [pltpu.make_async_copy(u_ref, u_out, store_sem.at[0])]
    stores[0].start()
    mine = set_ref[z]
    a48 = a_in_ref[mine, 0:3].reshape(48, -1)

    def lows(t, _):
        low_buf[t] = (adapt_scale * dot_nt(u_ref[t], a48)).astype(bf16)
        return 0

    lax.fori_loop(0, 8, lows, 0)
    for d, j in enumerate(zs):
        remote(b_small.at[j], b_small.at[j], small_send.at[d], small_recv.at[d], (s, j)).wait_recv()
        remote(a_small.at[j], a_small.at[j], small_send.at[3 + d], small_recv.at[3 + d], (s, j)).wait_recv()
    for j in range(4):
        b_sel_ref[j] = b_small[j, mine].reshape(48, HDIM)
        a_sel_ref[j] = a_small[j, mine]

    def merge(index, _):
        j = index // 3
        part = index % 3
        head = (2 * core + j) % 4
        b_part = b_sel_ref[head, pl.ds(pl.multiple_of(part * 16, 16), 16), :]
        column = pl.multiple_of(((j // 2) * 6 + part * 2 + j % 2) * HDIM, HDIM)
        for side in range(2):
            a_part = a_in_ref[mine, part, :, pl.ds(side * 1024, 1024)]
            merged = adapt_scale * dot_tn(a_part, b_part)
            w_cat[pl.ds(side * 1024, 1024), pl.ds(column, HDIM)] = (
                w_buf[head, side, part].astype(f32) + merged
            ).astype(bf16)
        return 0

    line.hop(3)
    o_line = Line(o_all, core, s, z, o_send, o_recv)
    o_line.begin()
    cot_line = Line(cots_ref, None, s, z, cot_send, cot_recv)
    line.arrive_core()
    lax.fori_loop(0, 6, merge, 0)
    left = lax.broadcasted_iota(jnp.int32, (256, HDIM), 1) < HDIM // 2

    def project(t, _):
        u = u_ref[t]
        packed = tables[t]
        turned = pltpu.roll(packed, HDIM // 2, 1)
        cos = jnp.where(left, packed, turned)
        sin = jnp.where(left, turned, -packed)
        rows = pl.ds(pl.multiple_of(t * 256, 256), 256)
        for part, out in enumerate((q_buf, k_buf, v_buf)):
            raw = dot_nn(u, w_cat[:, 256 * part : 256 * part + 256])
            for head in range(2):
                piece = raw[:, HDIM * head : HDIM * head + HDIM]
                if part < 2:
                    piece = piece * cos - pltpu.roll(piece, HDIM // 2, 1) * sin
                out[rows, HDIM * head : HDIM * head + HDIM] = piece.astype(bf16)
        return 0

    def project_all(t, _):
        project(t, 0)
        for step, at in ((1, 2), (2, 6)):

            @pl.when(t == at)
            def _():
                o_line.hop(step)

        return 0

    lax.fori_loop(0, 8, project_all, 0)
    cot_line.begin()
    stores += [
        pltpu.make_async_copy(source, target, store_sem.at[1 + i])
        for i, (source, target) in enumerate(
            ((q_buf, q_out), (k_buf, k_out), (v_buf, v_out), (low_buf, low_out), (tables, table_out))
        )
    ]
    for one in stores[1:]:
        one.start()

    tile = attn_tile
    factor = log2e / math.sqrt(HDIM)

    def attend(index, _):
        head = index // 4
        i = index % 4
        lanes = pl.ds(pl.multiple_of(head * HDIM, HDIM), HDIM)
        here = pl.ds(pl.multiple_of(i * tile, tile), tile)
        q = q_buf[here, lanes]

        def fold(j, carry, diagonal):
            top, total, acc = carry
            at = pl.ds(pl.multiple_of(j * tile, tile), tile)
            scores = dot_nt(k_buf[at, lanes], q)
            if diagonal:
                scores = jnp.where(causal(scores, 0, 0), scores, far_below)
            new_top = jnp.maximum(top, jnp.max(scores, axis=0, keepdims=True))
            weight = jnp.exp2(scores * factor - new_top * factor)
            keep = jnp.exp2((top - new_top) * factor)
            total = total * keep + jnp.sum(weight, axis=0, keepdims=True)
            acc = acc * keep + dot_tn(v_buf[at, lanes], weight.astype(bf16))
            return (new_top, total, acc)

        carry = (
            jnp.full((1, tile), far_below, f32),
            jnp.zeros((1, tile), f32),
            jnp.zeros((HDIM, tile), f32),
        )
        carry = lax.fori_loop(0, i, lambda j, c: fold(j, c, False), carry)
        top, total, acc = fold(i, carry, True)
        mixed[here, lanes] = jnp.transpose(acc / total).astype(bf16)
        lse_ref[head, i] = top * factor + jnp.log2(total)
        return 0

    def attend_all(index, _):
        attend(index, 0)

        @pl.when(index == 3)
        def _():
            o_line.hop(3)

        return 0

    lax.fori_loop(0, 8, attend_all, 0)

    def span_rows(span, first, count):
        return pl.ds(pl.multiple_of(span * 256 + first, 128), count)

    crosses = [
        remote(mixed.at[span_rows(2 * c + 1 - core, 0, 256)], sib.at[c], sib_send.at[c], sib_recv.at[c], (other, z))
        for c in range(4)
    ]
    for one in crosses:
        one.start()
    stores.append(pltpu.make_async_copy(mixed, mixed_out, store_sem.at[6]))
    stores[-1].start()
    o_line.arrive_core()
    b_row = b_od_ref[mine, 0]

    def merge_out(j, _):
        head = (2 * core + j) % 4
        for side in range(2):
            wide = slice(side * 1024, side * 1024 + 1024)
            merged = adapt_scale * dot_tn(a_sel_ref[head], b_row[:, wide])
            o_big[pl.ds(pl.multiple_of(j * HDIM, HDIM), HDIM), wide] = (
                o_all[head, side].astype(f32) + merged
            ).astype(bf16)
        return 0

    lax.fori_loop(0, 4, merge_out, 0)
    o_eff_ref[...] = o_big[0 : 2 * HDIM, :]
    for one in crosses:
        one.wait_recv()

    def rows_of(c, half):
        def load(row):
            at = pl.ds(pl.multiple_of((2 * c + core) * 256 + row, 32), 32)
            return jnp.concatenate([mixed[at, :], sib[c, pl.ds(row, 32), :]], axis=1)

        return some_rows(load, half)

    reduce = Reduce(
        rows_of, lambda rows, wide: dot_nn(rows, o_big[:, wide]), x_ref.shape[2], s, z,
        out_buf, in_buf, own_sum, red_send, red_recv,
    )
    reduce.begin()
    reduce.keep()

    @pl.when(middle)
    def _():
        cot_line.hop(1)

    reduce.second()
    lax.fori_loop(6, 12, merge, 0)
    stores.append(pltpu.make_async_copy(w_cat, w_cat_out, store_sem.at[7]))
    stores[-1].start()
    reduce.third()
    def settle(row, total):
        at = pl.ds(row, 32)
        x = x_own_ref[row // 64, pl.ds(pl.multiple_of(row % 64, 32), 32), :].astype(f32)
        residual = x + total
        residual_ref[at, :] = residual
        normed, _ = norm_rows(residual)
        m_own_ref[at, :] = normed.astype(bf16)

    reduce.finish(0, settle)

    @pl.when(middle)
    def _():
        cot_line.hop(2)

    reduce.finish(1, settle)
    @pl.when(z * (3 - z) == 0)
    def _():
        for t in (1, 2, 3):
            cot_line.hop(t)

    for one in stores:
        one.wait()
    for one in swaps + smalls + crosses:
        one.wait_send()
    line.end()
    o_line.end()
    cot_line.end()
    near.end()
    rest.end()
    table_gather.end()
    reduce.end()


def front_layer(x, w_qkv, w_out, b_qkv, a_out, a_in, b_out_down, table, cotangent, set_index):
    bf16 = jnp.bfloat16
    f32 = jnp.float32
    vmem = pl.BlockSpec(memory_space=pltpu.VMEM)
    anywhere = pl.BlockSpec(memory_space=pl.ANY)
    width = x.shape[2]
    shape = jax.ShapeDtypeStruct
    dma = pltpu.SemaphoreType.DMA
    vm = pltpu.VMEM
    return pl.pallas_call(
        front_kernel,
        in_specs=[vmem] + [anywhere] * 4 + [vmem] * 3 + [anywhere, pl.BlockSpec(memory_space=pltpu.SMEM)],
        out_specs=[vmem] * 7 + [anywhere] * 9,
        out_shape=[
            shape((4, 64, width), bf16),
            shape((256, width), bf16),
            shape((256, width), f32),
            shape((256, width), bf16),
            shape((4, 48, HDIM), bf16),
            shape((4, 16, HDIM), bf16),
            shape((2, 4, 1, attn_tile), f32),
            shape((8, 256, width), bf16),
            shape((2048, 256), bf16),
            shape((2048, 256), bf16),
            shape((2048, 256), bf16),
            shape((8, 256, 48), bf16),
            shape((8, 256, HDIM), f32),
            shape((2048, 256), bf16),
            shape((width, 1536), bf16),
            shape((4, 4, 64, width), bf16),
        ],
        scratch_shapes=[
            vm((8, 256, width), bf16),
            vm((4, 2, 3, 1024, HDIM), bf16),
            vm((width, 1536), bf16),
            vm((2048, 256), bf16),
            vm((2048, 256), bf16),
            vm((2048, 256), bf16),
            vm((8, 256, 48), bf16),
            vm((8, 256, HDIM), f32),
            vm((2048, 256), bf16),
            vm((4, 2, HDIM, 1024), bf16),
            vm((4 * HDIM, width), bf16),
            vm((4, 256, 256), bf16),
            vm((6, 128, width), bf16),
            vm((6, 128, width), bf16),
            vm((256, width), f32),
            vm((4, 4, 3, 16, HDIM), bf16),
            vm((4, 4, 16, HDIM), bf16),
        ]
        + [
            dma((count,))
            for count in (3, 3, 10, 10, 10, 10, 10, 10, 13, 13, 13, 13, 13, 13, 6, 6, 4, 4, 6, 6, 5, 8)
        ],
        cost_estimate=spend(150),
        compiler_params=pltpu.CompilerParams(
            collective_id=1, has_side_effects=True, vmem_limit_bytes=58 << 20
        ),
    )(x, w_qkv, w_out, b_qkv, a_out, a_in, b_out_down, table, cotangent, set_index)


def turn_back(gradient, packed):
    left = lax.broadcasted_iota(jnp.int32, packed.shape, 1) < HDIM // 2
    turned = pltpu.roll(packed, HDIM // 2, 1)
    cos = jnp.where(left, packed, turned)
    sin = jnp.where(left, turned, -packed)
    return gradient * cos + pltpu.roll(gradient, HDIM // 2, 1) * sin


def back_kernel(
    g_ref, o_eff_in, mixed_in, b_od_ref, q_in, k_in, v_in, lse_ref, table_in,
    grad_b_in, grad_ad_in, grad_a_in, grad_bd_in, down2_ref, down3_ref, set_ref,
    dq_ref, dk_ref, dv_ref, rank_ref, chunk_ref, pair_ref, g_out, got2_ref,
    grad_b_ref, grad_ad_ref, grad_a_ref, grad_bd_ref, o_eff_ref, mixed_ref, q_ref, k_ref, v_ref, table_ref, down2_buf, got3_buf, pair_sum, g_buf, gm_buf, dots, dk_acc, dv_acc, chunk_src, chunk_sib, chunk_sum, chunk_in,
    send, recv, down_send, down_recv, cs_send, cs_recv, cx_send, cx_recv, store_sem, load_sem,
):
    f32 = jnp.float32
    bf16 = jnp.bfloat16
    s, z = places()
    loads = [
        pltpu.make_async_copy(source, target, load_sem.at[i])
        for i, (source, target) in enumerate(
            (
                (grad_b_in, grad_b_ref),
                (grad_ad_in, grad_ad_ref),
                (grad_a_in, grad_a_ref),
                (grad_bd_in, grad_bd_ref),
                (o_eff_in, o_eff_ref),
                (mixed_in, mixed_ref),
                (q_in, q_ref),
                (k_in, k_ref),
                (v_in, v_ref),
                (table_in, table_ref),
                (down2_ref, down2_buf),
            )
        )
    ]
    for one in loads:
        one.start()
    core = s % 2
    chip = s // 2
    other = flip(s, 1)
    sx = flip(s, 2)
    sy = flip(s, 4)
    sd = flip(sx, 4)
    meet([(None, (t, z)) for t in (other, sx, sy, sd)] + [(None, (s, flip(z, 1))), (None, (s, flip(z, 2)))])
    g_buf[s] = g_ref[...]
    gather = Gather(g_buf, s, z, send, recv, 128)
    gather.begin()
    across = remote(down3_ref, got3_buf, down_send.at[0], down_recv.at[0], (s, flip(z, 1)))
    across.start()
    onward = remote(pair_sum, got2_ref, down_send.at[1], down_recv.at[1], (s, flip(z, 2)))
    member = set_ref[z]
    tile = attn_tile
    scale = 1.0 / math.sqrt(HDIM)
    factor = log2e * scale
    dk_acc[...] = jnp.zeros_like(dk_acc)
    dv_acc[...] = jnp.zeros_like(dv_acc)

    def store(t):
        return pltpu.make_async_copy(g_buf.at[t], g_out.at[t], store_sem.at[t])

    def chip_rows(c):
        here = pl.ds(pl.multiple_of(c * tile, tile), tile)

        def head_rows(part, _):
            t = 2 * c + part
            store(t).start()
            g = g_buf[t]
            back = dot_nt(g, o_eff_ref[...]).astype(bf16)
            gm_buf[pl.ds(pl.multiple_of(part * 256, 256), 256), :] = back
            product = back.astype(f32) * mixed_ref[
                pl.ds(pl.multiple_of(t * 256, 256), 256), :
            ].astype(f32)
            for head in range(2):
                turned = jnp.transpose(product[:, HDIM * head : HDIM * head + HDIM])
                dots[head, :, pl.ds(pl.multiple_of(part * 256, 256), 256)] = jnp.sum(turned, axis=0, keepdims=True)
            rank_ref[t] = (adapt_scale * dot_nt(g, b_od_ref[member, 0])).astype(bf16)
            return 0

        lax.fori_loop(0, 2, head_rows, 0)

        def one_head(head, _):
            lanes = pl.ds(pl.multiple_of(head * HDIM, HDIM), HDIM)
            q = q_ref[here, lanes]
            go = gm_buf[:, lanes]
            row_dots = dots[head]
            lse = lse_ref[head, c]

            def fold(j, dq, diagonal):
                at = pl.ds(pl.multiple_of(j * tile, tile), tile)
                k = k_ref[at, lanes]
                scores = dot_nt(k, q)
                weight = jnp.exp2(scores * factor - lse)
                if diagonal:
                    weight = jnp.where(causal(scores, 0, 0), weight, 0.0)
                grad_weight = dot_nt(v_ref[at, lanes], go)
                grad_scores = (weight * (grad_weight - row_dots)).astype(bf16)
                dv_acc[at, lanes] += dot_nn(weight.astype(bf16), go)
                dk_acc[at, lanes] += dot_nn(grad_scores, q)
                return dq + dot_tn(grad_scores, k)

            dq = lax.fori_loop(0, c, lambda j, total: fold(j, total, False), jnp.zeros((tile, HDIM), f32))
            dq = fold(c, dq, True)
            dq_ref[here, lanes] = turn_back(dq * scale, table_ref[here, :]).astype(bf16)
            return 0

        lax.fori_loop(0, 2, one_head, 0)

    def fill(one, _):
        whole = jnp.zeros((48, dk_acc.shape[0]), f32)
        split = jnp.zeros((48, dk_acc.shape[0]), f32)
        for seq in range(4):
            used = (set_ref[seq] == one).astype(f32)
            whole += used * jnp.concatenate([grad_a_ref[seq], grad_bd_ref[seq]], axis=0)
            split += used * jnp.concatenate([grad_b_ref[seq, 0], grad_b_ref[seq, 1], grad_ad_ref[seq]], axis=0)
        for part in range(2):
            rows = slice(24 * part, 24 * part + 24)
            chunk_src[2 * one + part] = jnp.concatenate([whole[rows], split[rows]], axis=0).astype(bf16)
        return 0

    for one in loads[:4]:
        one.wait()
    lax.fori_loop(0, 4, fill, 0)
    crosses = [
        remote(chunk_src.at[2 * c + 1 - core], chunk_sib.at[c], cs_send.at[c], cs_recv.at[c], (other, z))
        for c in range(4)
    ]
    for one in crosses:
        one.start()
    for one in loads[4:]:
        one.wait()
    around = [
        remote(chunk_sum.at[t // 2], chunk_in.at[d], cx_send.at[d], cx_recv.at[d], (t, z))
        for d, t in enumerate((sx, sy, sd))
    ]

    def total_chunks(c, _):
        chunk_sum[c] = (chunk_src[2 * c + core].astype(f32) + chunk_sib[c].astype(f32)).astype(bf16)
        return 0

    def pair_rows(seq, _):
        for first, target in ((0, pair_sum), (2, pair_ref)):
            target[seq] = (
                down2_buf[first + seq].astype(f32) + got3_buf[first + seq].astype(f32)
            ).astype(bf16)
        return 0

    def visit(step, _):
        @pl.when(step == 0)
        def _():
            gather.arrive_core(0)

        @pl.when(step == 1)
        def _():
            gather.arrive_first()
            for one in crosses:
                one.wait_recv()
            lax.fori_loop(0, 4, total_chunks, 0)
            for one in around:
                one.start()
            gather.arrive_neighbours()
            across.wait_recv()
            lax.fori_loop(0, 2, pair_rows, 0)
            onward.start()
            gather.arrive_core(1)

        @pl.when(step == 2)
        def _():
            gather.arrive_core(2)

        @pl.when(step == 3)
        def _():
            gather.arrive_diagonal()
            gather.arrive_core(3)

        by_x = step % 2
        by_y = step // 2
        chip_rows(chip + by_x * (1 - 2 * (chip % 2)) + by_y * (2 - 4 * (chip // 2)))
        return 0

    lax.fori_loop(0, 4, visit, 0)

    def last(j, _):
        at = pl.ds(pl.multiple_of(j * tile, tile), tile)
        for head in range(2):
            lanes = slice(HDIM * head, HDIM * head + HDIM)
            dk_ref[at, lanes] = turn_back(dk_acc[at, lanes] * scale, table_ref[at, :]).astype(bf16)
            dv_ref[at, lanes] = dv_acc[at, lanes].astype(bf16)
        return 0

    lax.fori_loop(0, 4, last, 0)
    for one in around:
        one.wait_recv()
    chunk = chunk_sum[chip].astype(f32)
    for d in range(3):
        chunk += chunk_in[d].astype(f32)
    chunk_ref[...] = chunk
    for t in range(8):
        store(t).wait()
    gather.end()
    onward.wait()
    for one in crosses + around + [across]:
        one.wait_send()


def back_layer(*operands):
    bf16 = jnp.bfloat16
    f32 = jnp.float32
    vmem = pl.BlockSpec(memory_space=pltpu.VMEM)
    anywhere = pl.BlockSpec(memory_space=pl.ANY)
    width = operands[0].shape[1]
    shape = jax.ShapeDtypeStruct
    dma = pltpu.SemaphoreType.DMA
    vm = pltpu.VMEM
    return pl.pallas_call(
        back_kernel,
        in_specs=[vmem, anywhere, anywhere, vmem, anywhere, anywhere, anywhere, vmem, anywhere]
        + [anywhere] * 6
        + [pl.BlockSpec(memory_space=pltpu.SMEM)],
        out_specs=[vmem] * 6 + [anywhere] * 2,
        out_shape=[
            shape((2048, 256), bf16),
            shape((2048, 256), bf16),
            shape((2048, 256), bf16),
            shape((8, 256, 16), bf16),
            shape((48, width), f32),
            shape((2, 64, width), bf16),
            shape((8, 256, width), bf16),
            shape((2, 64, width), bf16),
        ],
        scratch_shapes=[vm(operands[i].shape, f32) for i in (9, 10, 11, 12)]
        + [
            vm((256, width), bf16),
            vm((2048, 256), bf16),
            vm((2048, 256), bf16),
            vm((2048, 256), bf16),
            vm((2048, 256), bf16),
            vm((2048, HDIM), f32),
            vm((4, 64, width), bf16),
            vm((4, 64, width), bf16),
            vm((2, 64, width), bf16),
            vm((8, 256, width), bf16),
            vm((512, 256), bf16),
            vm((2, 1, 512), f32),
            vm((2048, 256), f32),
            vm((2048, 256), f32),
            vm((8, 48, width), bf16),
            vm((4, 48, width), bf16),
            vm((4, 48, width), bf16),
            vm((3, 48, width), bf16),
        ]
        + [dma((count,)) for count in (gather_sems, gather_sems, 2, 2, 4, 4, 3, 3, 8, 11)],
        cost_estimate=spend(60),
        compiler_params=pltpu.CompilerParams(
            collective_id=3, has_side_effects=True, vmem_limit_bytes=60 << 20
        ),
    )(*operands)


def mlp_line_kernel(
    m_ref, residual_in, cots_ref, w_gu_ref, w_d_ref, a_in, b_in, ad_in, bd_in, set_ref,
    g_ref, grad_res_ref, down0_ref, down1_ref, down2_ref, down3_ref, grad_b_ref, grad_ad_ref, grad_a_ref, grad_bd_ref,
    residual_ref, a_ref, b_ref, ad_ref, bd_ref, m_buf, wg, wu, wd, acts, grad_gates, grad_ups, cot_buf, back_acc, ranks, slots, r1, r2, r3, r5, stage,
    up_send, up_recv, dn_send, dn_recv, send1, recv1, send4, recv4, send5, recv5, send23, recv23,
    weight_sem, cot_sem, stage_sem, late_sem,
):
    s, z = places()
    late = [
        pltpu.make_async_copy(source, target, late_sem.at[i])
        for i, (source, target) in enumerate(
            (
                (a_in, a_ref),
                (b_in, b_ref),
                (ad_in, ad_ref),
                (bd_in, bd_ref),
                (residual_in, residual_ref),
            )
        )
    ]
    for one in late:
        one.start()
    tiles = wg.shape[0]
    tile = wg.shape[2]
    f32 = jnp.float32
    bf16 = jnp.bfloat16
    middle = z * (3 - z) == 2
    at_end = z * (3 - z) == 0
    pair = flip(z, 1)
    opposite = 3 - z
    inner = 1 + z // 2
    high = z // 2
    ids = [z, pair, 2 - high, 3 - 3 * high]
    far = 3 - 3 * high

    def load_tile(h):
        columns = pl.ds(h * tile if isinstance(h, int) else pl.multiple_of(h * tile, tile), tile)
        return [
            pltpu.make_async_copy(w_gu_ref.at[0, :, columns], wg.at[h], weight_sem.at[3 * h]),
            pltpu.make_async_copy(w_gu_ref.at[1, :, columns], wu.at[h], weight_sem.at[3 * h + 1]),
            pltpu.make_async_copy(w_d_ref.at[columns, :], wd.at[h], weight_sem.at[3 * h + 2]),
        ]

    for h in range(tiles):
        for one in load_tile(h):
            one.start()

    others = [z, pair, flip(z, 2), opposite]
    down_refs = (down0_ref, down1_ref, down2_ref, down3_ref)

    def load_cot(seq):
        return [pltpu.make_async_copy(cots_ref.at[j, seq], cot_buf.at[j], cot_sem.at[j]) for j in range(4)]

    for one in load_cot(z):
        one.start()

    meet([(z < 3, (s, z + 1)), (z > 0, (s, z - 1)), (None, (s, flip(z, 2)))])
    m_buf[z] = m_ref[...]

    def up(hop, j):
        return remote(m_buf.at[j], m_buf.at[j], up_send.at[hop], up_recv.at[hop], (s, z + 1))

    def down(hop, j):
        return remote(m_buf.at[j], m_buf.at[j], dn_send.at[hop], dn_recv.at[hop], (s, z - 1))

    def begin():
        @pl.when(z < 3)
        def _():
            up(0, z).start()

        @pl.when(z > 0)
        def _():
            down(0, z).start()

    def hop(t):
        def from_above(side):
            @pl.when((z + t <= 3) & side)
            def _():
                down(t - 1, z + t).wait_recv()
                if t < 3:

                    @pl.when(z > 0)
                    def _():
                        down(t, z + t).start()

        from_above(z < 2)

        @pl.when(z >= t)
        def _():
            up(t - 1, z - t).wait_recv()
            if t < 3:

                @pl.when(z < 3)
                def _():
                    up(t, z - t).start()

        from_above(z >= 2)

    def hop_end():
        @pl.when(z < 3)
        def _():
            up(0, z).wait_send()

        @pl.when(z > 0)
        def _():
            down(0, z).wait_send()

        for t in (1, 2):

            @pl.when((z >= t) & (z < 3))
            def _():
                up(t, z - t).wait_send()

            @pl.when((z + t <= 3) & (z > 0))
            def _():
                down(t, z + t).wait_send()

    def piece(p):
        return pl.ds(p * 64 if isinstance(p, int) else pl.multiple_of(p * 64, 64), 64)

    def copy1():
        return remote(slots.at[1], r1, send1.at[0], recv1.at[0], (s, pair))

    def copy2():
        return remote(slots.at[2], r2, send23.at[0], recv23.at[0], (s, opposite))

    def copy3():
        return remote(slots.at[2], r3, send23.at[1], recv23.at[1], (s, inner))

    def copy4(p):
        return remote(slots.at[3, piece(p)], r3.at[piece(p)], send4.at[p], recv4.at[p], (s, far))

    def copy5(p):
        return remote(slots.at[3, piece(p)], r5.at[piece(p)], send5.at[p], recv5.at[p], (s, inner))

    def stage_copies(seq):
        return [
            pltpu.make_async_copy(stage.at[others[d]], down_refs[d].at[seq], stage_sem.at[d]) for d in range(4)
        ]

    def in_maps(seq):
        return a_ref[set_ref[seq], 3:5].reshape(32, -1)

    def sequence(slot):
        return sum((slot == i).astype(jnp.int32) * one for i, one in enumerate(ids + [z]))

    def add(slot, extra):
        def one(p, _):
            slots[slot, piece(p), :] = (
                slots[slot, piece(p), :].astype(f32) + extra[piece(p), :].astype(f32)
            ).astype(bf16)
            return 0

        lax.fori_loop(0, 4, one, 0)

    begin()
    for one in late:
        one.wait()

    def chunk(slot, _):
        seq = sequence(slot)
        member = set_ref[seq]
        for one in load_cot(seq):
            one.wait()
        ranks[:, 0:32] = adapt_scale * dot_nt(m_buf[seq], in_maps(seq))
        ranks[:, 32:48] = adapt_scale * dot_nt(cot_buf[...].reshape(256, -1), bd_ref[member, 1])
        ranks[:, 48:96] = jnp.zeros((256, 48), f32)
        back_acc[...] = jnp.zeros_like(back_acc)

        def step(h, _):
            columns = pl.ds(pl.multiple_of(h * tile, tile), tile)

            @pl.when(slot == 0)
            def _():
                for one in load_tile(h):
                    one.wait()

            @pl.when((slot == 3) & (h == 1) & middle)
            def _():
                copy1().start()

            low = ranks[...].astype(bf16)
            low_gate = low[:, 0:16]
            low_up = low[:, 16:32]
            low_cot = low[:, 32:48]
            bg = b_ref[member, 0, :, columns]
            bu = b_ref[member, 1, :, columns]
            ad = ad_ref[member, :, columns]
            rows = m_buf[seq]
            cot = cot_buf[...].reshape(256, -1)
            gate = dot_nn(rows, wg[h]) + dot_nn(low_gate, bg)
            up_value = dot_nn(rows, wu[h]) + dot_nn(low_up, bu)
            grad_act = dot_nt(cot, wd[h]) + dot_nn(low_cot, ad)
            sig = jax.nn.sigmoid(gate)
            act = (gate * sig * up_value).astype(bf16)
            grad_up = (grad_act * gate * sig).astype(bf16)
            grad_gate = (grad_act * up_value * sig * (1.0 + gate * (1.0 - sig))).astype(bf16)
            acts[h] = act
            grad_gates[h] = grad_gate
            grad_ups[h] = grad_up
            for part in range(4):
                wide = pl.ds(part * 512, 512)
                back_acc[:, wide] += dot_nt(grad_gate, wg[h, wide, :]) + dot_nt(grad_up, wu[h, wide, :])
            ranks[:, 64:80] += dot_nt(grad_gate, bg)
            ranks[:, 80:96] += dot_nt(grad_up, bu)
            return 0

        def later(h, _):
            columns = pl.ds(pl.multiple_of(h * tile, tile), tile)
            low = ranks[:, 0:48].astype(bf16)
            act = acts[h]
            for part in range(4):
                wide = pl.ds(part * 512, 512)
                back_acc[:, wide] += dot_nn(act, wd[h, :, wide])
            ranks[:, 48:64] += dot_nt(act, ad_ref[member, :, columns])
            grad_b_ref[seq, 0, :, columns] = dot_tn(low[:, 0:16], grad_gates[h])
            grad_b_ref[seq, 1, :, columns] = dot_tn(low[:, 16:32], grad_ups[h])
            grad_ad_ref[seq, :, columns] = dot_tn(low[:, 32:48], act)
            return 0

        lax.fori_loop(0, tiles, step, 0)
        for t in (1, 2):

            @pl.when((slot == t - 1) & middle)
            def _():
                hop(t)

        back_rank = (adapt_scale * ranks[:, 64:96]).astype(bf16)
        slots[slot] = (back_acc[...] + dot_nn(back_rank, in_maps(seq))).astype(bf16)

        @pl.when((slot == 1) & at_end)
        def _():
            copy1().start()

        @pl.when((slot == 2) & at_end)
        def _():
            copy3().start()

        @pl.when((slot == 3) & at_end)
        def _():
            copy5(0).start()
            copy5(1).start()

        @pl.when((slot == 3) & middle)
        def _():
            copy3().wait_recv()
            add(2, r3)
            copy2().start()

        back_acc[...] = jnp.zeros_like(back_acc)
        lax.fori_loop(0, tiles, later, 0)
        low_down = (adapt_scale * ranks[:, 48:64]).astype(bf16)
        grad_a_ref[seq] = dot_tn(back_rank, m_buf[seq])
        grad_bd_ref[seq] = dot_tn(low_down, cot_buf[...].reshape(256, -1))

        @pl.when(slot > 0)
        def _():
            for one in stage_copies(seq):
                one.wait()

        own = (slot == 0).astype(f32)
        value = back_acc[...] + dot_nn(low_down, bd_ref[member, 1]) + own * residual_ref[...]
        stage[...] = value.astype(bf16).reshape(4, 64, -1)
        for one in stage_copies(seq):
            one.start()
        for one in load_cot(sequence(slot + 1)):
            one.start()
        for t in (1, 2, 3):

            @pl.when((slot == t - 1) & at_end)
            def _():
                hop(t)

        return 0

    lax.fori_loop(0, 4, chunk, 0)

    @pl.when(at_end)
    def _():
        for p in (2, 3):
            copy5(p - 2).wait_send()
            copy5(p).start()

    @pl.when(middle)
    def _():
        def one(p, _):
            copy5(p).wait_recv()
            slots[3, piece(p), :] = (
                slots[3, piece(p), :].astype(f32) + r5[piece(p), :].astype(f32)
            ).astype(bf16)
            copy4(p).start()
            return 0

        lax.fori_loop(0, 4, one, 0)

    copy1().wait_recv()
    add(0, r1)

    @pl.when(middle)
    def _():
        copy2().wait_recv()
        add(0, r2)

    for one in load_cot(z):
        one.wait()

    def settle(p, _):
        @pl.when(at_end)
        def _():
            copy4(p).wait_recv()
            slots[0, piece(p), :] = (
                slots[0, piece(p), :].astype(f32) + r3[piece(p), :].astype(f32)
            ).astype(bf16)

        def rows32(half, _):
            at = pl.ds(pl.multiple_of(p * 64 + half * 32, 32), 32)
            grad = slots[0, at, :].astype(f32)
            normed, inverse = norm_rows(residual_ref[at, :])
            cot = cot_buf[p, pl.ds(pl.multiple_of(half * 32, 32), 32), :].astype(f32)
            value = cot + norm_back(grad, normed, inverse)
            grad_res_ref[at, :] = value
            g_ref[at, :] = value.astype(bf16)
            return 0

        lax.fori_loop(0, 2, rows32, 0)
        return 0

    lax.fori_loop(0, 4, settle, 0)
    for one in stage_copies(z):
        one.wait()
    hop_end()
    copy1().wait_send()

    @pl.when(at_end)
    def _():
        copy3().wait_send()
        for p in (2, 3):
            copy5(p).wait_send()

    @pl.when(middle)
    def _():
        copy2().wait_send()
        for p in range(4):
            copy4(p).wait_send()


def mlp_line(m_own, residual, cots, w_gate_up, w_down, a_in, b_gate_up, a_down, b_out_down, set_index):
    bf16 = jnp.bfloat16
    f32 = jnp.float32
    vmem = pl.BlockSpec(memory_space=pltpu.VMEM)
    anywhere = pl.BlockSpec(memory_space=pl.ANY)
    width = m_own.shape[1]
    hidden = w_down.shape[0]
    tile = hidden_tile
    tiles = hidden // tile
    shape = jax.ShapeDtypeStruct
    dma = pltpu.SemaphoreType.DMA
    vm = pltpu.VMEM
    return pl.pallas_call(
        mlp_line_kernel,
        in_specs=[vmem]
        + [anywhere] * 8
        + [pl.BlockSpec(memory_space=pltpu.SMEM)],
        out_specs=[vmem, vmem] + [anywhere] * 4 + [vmem, vmem, vmem, vmem],
        out_shape=[
            shape((256, width), bf16),
            shape((256, width), f32),
        ]
        + [shape((4, 64, width), bf16)] * 4
        + [
            shape((4, 2, 16, hidden), f32),
            shape((4, 16, hidden), f32),
            shape((4, 32, width), f32),
            shape((4, 16, width), f32),
        ],
        scratch_shapes=[
            vm((256, width), f32),
            vm(a_in.shape, bf16),
            vm(b_gate_up.shape, bf16),
            vm(a_down.shape, bf16),
            vm(b_out_down.shape, bf16),
            vm((4, 256, width), bf16),
            vm((tiles, width, tile), bf16),
            vm((tiles, width, tile), bf16),
            vm((tiles, tile, width), bf16),
            vm((tiles, 256, tile), bf16),
            vm((tiles, 256, tile), bf16),
            vm((tiles, 256, tile), bf16),
            vm((4, 64, width), bf16),
            vm((256, width), f32),
            vm((256, 96), f32),
            vm((4, 256, width), bf16),
            vm((256, width), bf16),
            vm((256, width), bf16),
            vm((256, width), bf16),
            vm((256, width), bf16),
            vm((4, 64, width), bf16),
        ]
        + [dma((3,))] * 4
        + [dma((4,))] * 6
        + [dma((2,))] * 2
        + [dma((3 * tiles,)), dma((4,)), dma((4,)), dma((5,))],
        cost_estimate=spend(110),
        compiler_params=pltpu.CompilerParams(
            collective_id=5, has_side_effects=True, vmem_limit_bytes=60 << 20
        ),
    )(m_own, residual, cots, w_gate_up, w_down, a_in, b_gate_up, a_down, b_out_down, set_index)


def finish_kernel(
    dq_in, dk_in, dv_in, w_in, x_own_in, residual_in, u_ref, g_ref, low_in, rank_ref, mixed_in,
    b_sel_ref, a_sel_ref, chunk_ref, down0_in, down1_ref, got2_ref, pair_ref,
    set_ref,
    result_ref, grad_ref, whole_ref, split_ref, sequence_ref, heads_ref, got3_ref,
    sets_ref, pool_ref, dq_ref, dk_ref, dv_ref, x_own_ref, low_ref,
    w_ref, residual_ref, mixed_ref, down0_ref, got1_ref,
    own_ref, sib_q, sib_k, sib_v, out_buf, in_buf, own_sum, u_buf, g_buf, a_acc, b_acc, chunk_src, chunk_sib, chunk_sum,
    chunk_in, z_src, z_in, sets_src, sets_in, head_src, head_in,
    a2a_send, a2a_recv, sib_send, sib_recv, send, recv, load_sem, cs_send, cs_recv, cx_send, cx_recv,
    cz_send, cz_recv, cg_send, cg_recv, hz_send, hz_recv, hg_send, hg_recv, down_send, down_recv,
    sz_send, sz_recv, sg_send, sg_recv, late_sem,
):
    f32 = jnp.float32
    bf16 = jnp.bfloat16
    s, z = places()
    loads = [
        pltpu.make_async_copy(source, target, late_sem.at[i])
        for i, (source, target) in enumerate(
            (
                (dq_in, dq_ref),
                (dk_in, dk_ref),
                (dv_in, dv_ref),
                (w_in, w_ref),
                (mixed_in, mixed_ref),
                (low_in, low_ref),
                (x_own_in, x_own_ref),
                (residual_in, residual_ref),
                (down0_in, down0_ref),
            )
        )
    ]
    for one in loads[:5]:
        one.start()
    core = s % 2
    chip = s // 2
    other = flip(s, 1)
    sx = flip(s, 2)
    sy = flip(s, 4)
    sd = flip(sx, 4)
    zs = [flip(z, 1), flip(z, 2), 3 - z]
    meet([(None, (t, z)) for t in (other, sx, sy, sd)] + [(None, (s, j)) for j in zs])
    last_down = remote(pair_ref, got3_ref, down_send.at[0], down_recv.at[0], (s, flip(z, 2)))
    last_down.start()
    pair_down = remote(down1_ref, got1_ref, down_send.at[1], down_recv.at[1], (s, zs[0]))
    pair_down.start()
    sets_src[...] = chunk_ref[0:32].astype(bf16)
    sets_along = [remote(sets_src, sets_in.at[d], sz_send.at[d], sz_recv.at[d], (s, j)) for d, j in enumerate(zs)]
    for one in sets_along:
        one.start()
    mine = (dq_ref, dk_ref, dv_ref)
    sources = (dq_in, dk_in, dv_in)
    theirs = (sib_q, sib_k, sib_v)
    swaps = [
        remote(
            sources[p].at[2 * c + 1 - core], theirs[p].at[c], sib_send.at[4 * p + c], sib_recv.at[4 * p + c], (other, z)
        )
        for c in range(4)
        for p in range(3)
    ]
    for one in swaps:
        one.start()

    def load(t):
        return [
            pltpu.make_async_copy(u_ref.at[t], u_buf.at[t % 2], load_sem.at[t % 2]),
            pltpu.make_async_copy(g_ref.at[t], g_buf.at[t % 2], load_sem.at[2 + t % 2]),
        ]

    for one in load(0):
        one.start()
    for one in swaps:
        one.wait_recv()

    def rows_of(c, half):
        def load(row):
            at = pl.ds(row, 32)
            return jnp.concatenate(
                [ref[2 * c + core, at, :] for ref in mine] + [ref[c, at, :] for ref in theirs], axis=1
            )

        return some_rows(load, half)

    reduce = Reduce(
        rows_of, lambda rows, wide: dot_nt(rows, w_ref[wide, :]), x_own_ref.shape[2], s, z,
        out_buf, in_buf, own_sum, send, recv,
    )
    for one in loads[:4]:
        one.wait()
    reduce.begin()
    for one in loads[5:]:
        one.start()
    reduce.keep()
    loads[4].wait()

    b_two = [
        jnp.concatenate(
            [b_sel_ref[2 * core, 16 * p : 16 * p + 16], b_sel_ref[2 * core + 1, 16 * p : 16 * p + 16]], axis=1
        )
        for p in range(3)
    ]
    a_two = jnp.concatenate([a_sel_ref[2 * core], a_sel_ref[2 * core + 1]], axis=1)

    a_acc[...] = jnp.zeros_like(a_acc)
    b_acc[...] = jnp.zeros_like(b_acc)

    def adapt(t, _):
        for one in load(t):
            one.wait()

        @pl.when(t < 7)
        def _():
            for one in load(t + 1):
                one.start()

        back = jnp.concatenate([dot_nt(mine[p][t], b_two[p]) for p in range(3)], axis=1)
        back = (adapt_scale * back).astype(bf16)
        lows = (adapt_scale * dot_nt(mixed_ref[t], a_two)).astype(bf16)
        u = u_buf.at[t % 2]
        g = g_buf.at[t % 2]

        def one(part, _):
            wide = pl.ds(pl.multiple_of(part * 512, 512), 512)
            a_acc[:, wide] += dot_tn(back, u[:, wide])
            b_acc[:, wide] += dot_tn(lows, g[:, wide])
            return 0

        lax.fori_loop(0, 4, one, 0)

        @pl.when(t == 2)
        def _():
            reduce.second()

        @pl.when(t == 6)
        def _():
            reduce.third()

        return 0

    lax.fori_loop(0, 8, adapt, 0)
    for one in loads[5:]:
        one.wait()
    per_head = [
        dot_tn(low_ref[...].reshape(2048, 48)[:, 16 * p : 16 * p + 16], mine[p][...].reshape(2048, 256))
        for p in range(3)
    ] + [dot_tn(rank_ref[...].reshape(2048, 16), mixed_ref[...].reshape(2048, 256))]
    for head in range(2):
        columns = slice(HDIM * head, HDIM * head + HDIM)
        head_src[head] = jnp.concatenate([part[:, columns] for part in per_head], axis=0).astype(bf16)

    keeper = (z // 2) == core

    def head_copy(head):
        return remote(head_src.at[head], head_in.at[z], hz_send.at[head], hz_recv.at[z], (s, 2 * core + head))

    for head in range(2):

        @pl.when(2 * core + head != z)
        def _():
            head_copy(head).start()

        @pl.when(2 * core + head == z)
        def _():
            head_in[z] = head_src[head]

    for i in range(8):
        sequence = a_acc[8 * i : 8 * i + 8] if i < 6 else b_acc[8 * i - 48 : 8 * i - 40]
        chunk_src[i] = jnp.concatenate([sequence, jnp.zeros((8, a_acc.shape[1]), f32)], axis=0).astype(bf16)
    crosses = [
        remote(chunk_src.at[2 * c + 1 - core], chunk_sib.at[c], cs_send.at[c], cs_recv.at[c], (other, z))
        for c in range(4)
    ]
    for one in crosses:
        one.start()
    for one in crosses:
        one.wait_recv()
    for c in range(4):
        chunk_sum[c] = (chunk_src[2 * c + core].astype(f32) + chunk_sib[c].astype(f32)).astype(bf16)
    around = [
        remote(chunk_sum.at[t // 2], chunk_in.at[d], cx_send.at[d], cx_recv.at[d], (t, z))
        for d, t in enumerate((sx, sy, sd))
    ]
    for one in around:
        one.start()

    for one in sets_along:
        one.wait_recv()
    whole = chunk_ref[0:24]
    for d in range(3):
        whole += sets_in[d, 0:24].astype(f32)
    sets_ref[s] = jnp.concatenate([whole, chunk_ref[24:48]], axis=0).astype(bf16)

    def settle(row, total):
        at = pl.ds(row, 32)
        inside = pl.ds(pl.multiple_of(row % 64, 32), 32)
        normed, inverse = norm_rows(x_own_ref[row // 64, inside, :].astype(f32))
        value = residual_ref[at, :] + norm_back(total, normed, inverse)
        own_ref[row // 64, inside, :] = value.astype(bf16)

    def back(d, half):
        rows = pl.ds(32 * half, 32)
        return remote(
            own_ref.at[zs[d], rows], grad_ref.at[z, rows], a2a_send.at[2 * d + half], a2a_recv.at[2 * d + half],
            (s, zs[d]),
        )

    backs = []
    for half in range(2):
        reduce.finish(half, settle)
        for d in range(3):
            backs.append(back(d, half))
            backs[-1].start()
        if half == 0:
            for one in around:
                one.wait_recv()
            chunk = chunk_sum[chip].astype(f32)
            for d in range(3):
                chunk += chunk_in[d].astype(f32)
            z_src[...] = chunk.astype(bf16)
            along = [remote(z_src, z_in.at[d], cz_send.at[d], cz_recv.at[d], (s, j)) for d, j in enumerate(zs)]
            for one in along:
                one.start()
    grad_ref[z] = own_ref[z]

    def sets_copy(t, index, target):
        return remote(sets_ref.at[t], sets_ref.at[t], sg_send.at[index], sg_recv.at[index], (target, z))

    sets_gives = [sets_copy(s, index, target) for index, target in enumerate((sx, sy, sd, other))]
    for one in sets_gives:
        one.start()

    last_down.wait_recv()
    pair_down.wait_recv()

    def result_rows(part, _):
        for first, other_pair in ((0, got2_ref), (2, got3_ref)):
            result_ref[first + part] = (
                down0_ref[first + part].astype(f32)
                + got1_ref[first + part].astype(f32)
                + other_pair[part].astype(f32)
            ).astype(bf16)
        return 0

    lax.fori_loop(0, 2, result_rows, 0)
    def head_spread(target, index):
        return remote(heads_ref.at[chip], heads_ref.at[chip], hg_send.at[index], hg_recv.at[index], (target, z))

    def head_pass(t, index):
        c = t // 2
        return remote(heads_ref.at[c], heads_ref.at[c], hg_send.at[index], hg_recv.at[index], (other, z))

    @pl.when(keeper)
    def _():
        for j in range(4):

            @pl.when(z != j)
            def _():
                remote(head_src.at[0], head_in.at[j], hz_send.at[0], hz_recv.at[j], (s, j)).wait_recv()

        for member in range(4):
            total = jnp.zeros((64, HDIM), f32)
            for seq in range(4):
                total += (set_ref[seq] == member).astype(f32) * head_in[seq].astype(f32)
            heads_ref[chip, pl.ds(64 * member, 64)] = total.astype(bf16)
        for index, target in enumerate((sx, sy, sd, other)):
            head_spread(target, index).start()

    for one in along:
        one.wait_recv()
    places_z = [z] + zs
    parts = [chunk[0:8]] + [z_in[d, 0:8].astype(f32) for d in range(3)]
    by_member = [
        sum((set_ref[places_z[d]] == member).astype(f32) * parts[d] for d in range(4)) for member in range(4)
    ]
    pool_ref[s] = jnp.concatenate(by_member, axis=0).astype(bf16)

    def pool_copy(t, index, target):
        return remote(pool_ref.at[t], pool_ref.at[t], cg_send.at[index], cg_recv.at[index], (target, z))

    gives = [pool_copy(s, index, target) for index, target in enumerate((sx, sy, sd, other))]
    for one in gives:
        one.start()

    @pl.when(keeper)
    def _():
        for index, t in enumerate((sx, sy, sd)):
            head_pass(t, index).wait_recv()
            head_pass(t, 4 + index).start()

    for copy in (sets_copy, pool_copy):
        for index, t in enumerate((sx, sy, sd)):
            copy(t, index, other).wait_recv()
            copy(t, 4 + index, other).start()
    for copy in (sets_copy, pool_copy):
        copy(other, 3, other).wait_recv()
        for index, t in enumerate((sx, sy, sd)):
            copy(flip(t, 1), 4 + index, other).wait_recv()

    def widen(t, _):
        rows = sets_ref[t].astype(f32)
        whole_ref[t] = rows[0:24]
        split_ref[t] = rows[24:48]
        rows = pool_ref[t].astype(f32)
        for member in range(4):
            sequence_ref[member, pl.ds(pl.multiple_of(8 * t, 8), 8), :] = rows[8 * member : 8 * member + 8]
        return 0

    lax.fori_loop(0, 8, widen, 0)

    @pl.when(z // 2 != core)
    def _():
        head_spread(other, 3).wait_recv()
        for index, t in enumerate((sx, sy, sd)):
            head_pass(t, 4 + index).wait_recv()

    for d, j in enumerate(zs):
        for half in range(2):
            rows = pl.ds(32 * half, 32)
            index = 2 * d + half
            remote(
                own_ref.at[j, rows], grad_ref.at[j, rows], a2a_send.at[index], a2a_recv.at[index], (s, j)
            ).wait_recv()
    for one in swaps + crosses + around + backs + along + gives + sets_along + sets_gives + [last_down, pair_down]:
        one.wait_send()
    for index, t in enumerate((sx, sy, sd)):
        pool_copy(t, 4 + index, other).wait_send()
        sets_copy(t, 4 + index, other).wait_send()
    reduce.end()
    for head in range(2):

        @pl.when(2 * core + head != z)
        def _():
            head_copy(head).wait_send()

    @pl.when(keeper)
    def _():
        for index, target in enumerate((sx, sy, sd, other)):
            head_spread(target, index).wait_send()
        for index, t in enumerate((sx, sy, sd)):
            head_pass(t, 4 + index).wait_send()


def finish_layer(*operands):
    bf16 = jnp.bfloat16
    f32 = jnp.float32
    vmem = pl.BlockSpec(memory_space=pltpu.VMEM)
    anywhere = pl.BlockSpec(memory_space=pl.ANY)
    width = operands[4].shape[2]
    dma = pltpu.SemaphoreType.DMA
    vm = pltpu.VMEM
    shape = jax.ShapeDtypeStruct
    return pl.pallas_call(
        finish_kernel,
        in_specs=[anywhere] * 9
        + [vmem, anywhere]
        + [vmem] * 3
        + [anywhere] * 2
        + [vmem] * 2
        + [pl.BlockSpec(memory_space=pltpu.SMEM)],
        out_specs=[vmem] * 7,
        out_shape=[
            shape((4, 64, width), bf16),
            shape((4, 64, width), bf16),
            shape((8, 24, width), f32),
            shape((8, 24, width), f32),
            shape((4, 64, width), f32),
            shape((4, 256, HDIM), bf16),
            shape((2, 64, width), bf16),
        ],
        scratch_shapes=[
            vm((8, 48, width), bf16),
            vm((8, 32, width), bf16),
            vm((8, 256, 256), bf16),
            vm((8, 256, 256), bf16),
            vm((8, 256, 256), bf16),
            vm((4, 64, width), bf16),
            vm((8, 256, 48), bf16),
            vm((width, 1536), bf16),
            vm((256, width), f32),
            vm((8, 256, 256), bf16),
            vm((4, 64, width), bf16),
            vm((4, 64, width), bf16),
            vm((4, 64, width), bf16),
            vm((4, 256, 256), bf16),
            vm((4, 256, 256), bf16),
            vm((4, 256, 256), bf16),
            vm((6, 128, width), bf16),
            vm((6, 128, width), bf16),
            vm((256, width), f32),
            vm((2, 256, width), bf16),
            vm((2, 256, width), bf16),
            vm((48, width), f32),
            vm((16, width), f32),
            vm((8, 16, width), bf16),
            vm((4, 16, width), bf16),
            vm((4, 16, width), bf16),
            vm((3, 16, width), bf16),
            vm((16, width), bf16),
            vm((3, 16, width), bf16),
            vm((32, width), bf16),
            vm((3, 32, width), bf16),
            vm((2, 64, HDIM), bf16),
            vm((4, 64, HDIM), bf16),
        ]
        + [
            dma((count,))
            for count in (6, 6, 12, 12, 6, 6, 4, 4, 4, 3, 3, 3, 3, 7, 7, 2, 4, 7, 7, 2, 2, 3, 3, 7, 7, 9)
        ],
        cost_estimate=spend(80),
        compiler_params=pltpu.CompilerParams(
            collective_id=4, has_side_effects=True, vmem_limit_bytes=60 << 20
        ),
    )(*operands)


def span_table(positions):
    half_dim = HDIM // 2
    frequency = jnp.exp(
        jnp.arange(half_dim, dtype=jnp.float32) * (-2.0 * math.log(rope_base) / HDIM)
    )
    angles = positions.astype(jnp.float32)[:, None] * frequency
    return jnp.concatenate([jnp.cos(angles), jnp.sin(angles)], axis=1)


def per_device_layers(
    layer_in, w_qkv, w_out, w_gate_up, w_down, a_in, b_qkv, b_gate_up, a_out, a_down, b_out_down,
    set_index, positions, cotangent,
):
    f32 = jnp.float32
    z = lax.axis_index("mp")
    sets = a_in.shape[0]
    width = layer_in.shape[2]
    rank = a_in.shape[2]
    length = 8 * 256

    table = span_table(lax.dynamic_index_in_dim(positions, z, 0, keepdims=False))
    (
        x_own, m_own, residual, o_eff, b_sel, a_sel, lse,
        u, q, k, v, low, tables, mixed, w_cat, cots,
    ) = front_layer(
        layer_in, w_qkv, w_out, b_qkv, a_out, a_in, b_out_down, table, cotangent, set_index
    )

    def spans(values):
        return values.reshape(8, 256, 256)

    (
        g_own, grad_residual, down0, down1, down2, down3,
        grad_b_mlp, grad_ad, grad_a_mlp, grad_bd,
    ) = mlp_line(
        m_own, residual, cots, w_gate_up, w_down, a_in, b_gate_up, a_down, b_out_down, set_index
    )
    dq, dk, dv, out_rank, chunk, pair, g, got2 = back_layer(
        g_own, o_eff, mixed, b_out_down, q, k, v, lse, tables.reshape(length, HDIM),
        grad_b_mlp, grad_ad, grad_a_mlp, grad_bd, down2, down3, set_index,
    )
    result, grad_in, whole, split, sequence, heads, _ = finish_layer(
        spans(dq), spans(dk), spans(dv), w_cat, x_own, grad_residual, u, g, low, out_rank, spans(mixed),
        b_sel, a_sel, chunk, down0, down1, got2, pair, set_index,
    )
    whole = whole.reshape(sets, 48, width)
    split = split.reshape(sets, 48, width)
    heads = heads.astype(f32).reshape(4, sets, 64, HDIM)
    heads = jnp.transpose(heads, (1, 2, 0, 3)).reshape(sets, 4, rank, 4 * HDIM)
    return (
        result,
        grad_in,
        jnp.concatenate([sequence[:, :48], whole[:, :32]], axis=1).reshape(sets, 5, rank, width),
        heads[:, :3],
        split[:, :32].reshape(sets, 2, rank, width),
        heads[:, 3],
        split[:, 32:],
        jnp.stack([sequence[:, 48:], whole[:, 32:]], axis=1),
    )


def solution(mesh):
    by_layers = mesh.shape["seq"] == 8 and mesh.shape["mp"] == 4
    body = per_device_layers if by_layers else per_device
    placed = (
        P(None, ("seq", "mp"), None),
        P(None, None, "mp"),
        P("mp", None),
        P(None, None, "mp"),
        P("mp", None),
        P(),
        P(None, None, None, "mp"),
        P(None, None, None, "mp"),
        P(None, None, "mp"),
        P(None, None, "mp"),
        P(),
        P(),
        P(None, "seq"),
        P(None, ("seq", "mp"), None),
    )
    return jax.shard_map(
        body,
        mesh=mesh,
        in_specs=placed,
        out_specs=(
            P(None, ("seq", "mp"), None),
            P(None, ("seq", "mp"), None),
            P(),
            P(None, None, None, "mp"),
            P(None, None, None, "mp"),
            P(None, None, "mp"),
            P(None, None, "mp"),
            P(),
        ),
        check_vma=False,
    )
```
